32 devices in a mesh: rep: 2 (over y), prow: 4 (over z), pcol: 4 (over x, core).
Axes of the slice: x: 2, y: 2, z: 4, core: 2. Of those that a mesh axis runs over, the one named last changes fastest.
Arguments:
- homolog_features: bfloat16 [256, 64, 64], P('rep', ('pcol', 'prow')), parts along dimension 0, may hold values from -6 to 6
- subset_homolog_positions: int32 [128], P('rep'), parts along dimension 0, may hold values from 0 to 127, as said below
- first_side_matrix: bfloat16 [64, 32], replicated, may hold values from -0.75 to 0.75
- second_side_matrix: bfloat16 [64, 32], replicated, may hold values from -0.75 to 0.75
- final_mapping_matrix: bfloat16 [1024, 128], replicated, may hold values from -1.5 to 1.5
- final_offset_vector: float32 [128], replicated, may hold values from -6 to 6
- upstream_sensitivity: bfloat16 [128, 64, 128], P(('rep', 'prow'), 'pcol'), parts along dimension 0, may hold values from -0.25 to 0.25
Outputs:
- pair_delta: bfloat16 [128, 64, 128], P(('rep', 'prow'), 'pcol'), parts along dimension 0
- alignment_gradient: bfloat16 [128, 64, 64], P('rep', ('pcol', 'prow')), parts along dimension 0
- left_weight_gradient: float32 [128, 32], P('rep'), parts along dimension 0
- right_weight_gradient: float32 [128, 32], P('rep'), parts along dimension 0
- output_weight_gradient: float32 [2048, 128], P('rep'), parts along dimension 0
The draws below stay inside these ranges and needn't reach their ends.
There are 2 independent parts, one for each index of `rep`. The reference program is written for one: setup_inputs(seed, part) draws one part's arguments, and reference() takes and returns one part's arrays. A program takes and returns all parts, laid end to end along the dimension named above; an argument that names none is the same for every part. Nothing has to cross between parts.
Inputs may be any that keep to these rules, and one draw needn't show every extreme that they name: `subset_homolog_positions`: the indices are distinct; 0 and 127 are always among them.
All inputs are finite; a program needn't handle non-finite values.
Results may differ from the reference program's by a relative error of at most 0.0075.
Values may be sent and summed in bfloat16 or wider, within the bound.
No kernel may reach another device: no remote copies, remote signals or barrier semaphores. Data moves between devices by JAX's collectives and lax.ppermute only.
A program may use at most 64 MiB of HBM per device.

```python
import jax
import jax.numpy as jnp
from jax import lax

FEATURE_DEPTH = 64
HIDDEN_WIDTH = 32
CP = 128
GROUP_SEQUENCES = 64
HOMOLOG_TOTAL = 128
RESIDUE_TOTAL = 64


def draw_subset_homolog_positions(key, part):
    key = jax.random.fold_in(key, 7)
    centered_input = jax.random.permutation(key, HOMOLOG_TOTAL - 2)[:GROUP_SEQUENCES - 2] + 1
    selected_alignment = jnp.concatenate([jnp.array([0, HOMOLOG_TOTAL - 1], jnp.int32), centered_input.astype(jnp.int32)])
    return jax.random.permutation(jax.random.fold_in(key, 1), selected_alignment)


def level_of(stream_key, dims, pieces, low, top_value):
    gain = 1.0
    for axis_at, blocks in pieces:
        draws = jax.random.uniform(jax.random.fold_in(jax.random.fold_in(stream_key, 6), axis_at), (blocks,), jnp.float32, low / len(pieces), top_value / len(pieces))
        gain = gain * jnp.repeat(jnp.exp(draws), dims[axis_at] // blocks).reshape((-1,) + (1,) * (len(dims) - 1 - axis_at))
    return gain


def noise(stream_key, dims, spread, most, shards=(), held_as=jnp.bfloat16):
    values = jax.random.normal(stream_key, dims, jnp.float32) * spread
    if len(shards) > 0:
        values = level_of(stream_key, dims, shards, -0.22, 0.18) * values
    return jnp.clip(values, min=-most, max=most).astype(held_as)


def setup_inputs(seed: int = 0, part: int = 0) -> dict:
    arg_keys = jax.random.split(jax.random.key(seed), 8)
    part_keys = jax.random.split(jax.random.fold_in(arg_keys[7], part), 8)
    homolog_features = noise(part_keys[0], (HOMOLOG_TOTAL, RESIDUE_TOTAL, FEATURE_DEPTH), 1.0, 6.0, ((1, 16),))
    subset_homolog_positions = draw_subset_homolog_positions(jax.random.fold_in(jax.random.fold_in(arg_keys[7], part), 71), part)
    first_side_matrix = noise(arg_keys[2], (FEATURE_DEPTH, HIDDEN_WIDTH), FEATURE_DEPTH ** -0.5, 0.75)
    second_side_matrix = noise(arg_keys[3], (FEATURE_DEPTH, HIDDEN_WIDTH), FEATURE_DEPTH ** -0.5, 0.75)
    final_mapping_matrix = noise(arg_keys[4], (HIDDEN_WIDTH * HIDDEN_WIDTH, CP), (HIDDEN_WIDTH // 2) ** -0.5, 1.5)
    final_offset_vector = noise(arg_keys[5], (CP,), 1.0, 6.0, (), jnp.float32)
    upstream_sensitivity = noise(part_keys[6], (RESIDUE_TOTAL, RESIDUE_TOTAL, CP), 0.03125, 0.25, ((0, 4), (1, 4)))
    return {"homolog_features": homolog_features, "subset_homolog_positions": subset_homolog_positions, "first_side_matrix": first_side_matrix, "second_side_matrix": second_side_matrix, "final_mapping_matrix": final_mapping_matrix, "final_offset_vector": final_offset_vector, "upstream_sensitivity": upstream_sensitivity}


def normalize(values):
    values = values.astype(jnp.float32)
    mean_factor = lax.optimization_barrier(jnp.mean(values, axis=-1, keepdims=True))
    centered = values - mean_factor
    variance = lax.optimization_barrier(jnp.mean(centered * centered, axis=-1, keepdims=True))
    inverse_spread = lax.rsqrt(variance + 1e-05)
    return (centered * inverse_spread, inverse_spread)

def reference(homolog_features, subset_homolog_positions, first_side_matrix, second_side_matrix, final_mapping_matrix, final_offset_vector, upstream_sensitivity):
    picked_homologs = jnp.take(homolog_features, subset_homolog_positions, axis=0)
    normalized_input, inverse_spread = normalize(picked_homologs)
    normed_low = normalized_input.astype(jnp.bfloat16)
    normed_wide = normed_low.astype(jnp.float32)
    w_a32 = first_side_matrix.astype(jnp.float32)
    w_b32 = second_side_matrix.astype(jnp.float32)
    left_proj = jnp.einsum('stc,cp->stp', normed_wide, w_a32).astype(jnp.bfloat16)
    right_proj = jnp.einsum('stc,cp->stp', normed_wide, w_b32).astype(jnp.bfloat16)
    left_wide = left_proj.astype(jnp.float32)
    right_wide = right_proj.astype(jnp.float32)
    row_block = 8
    block_count = RESIDUE_TOTAL // row_block
    left_blocks = left_wide.reshape(GROUP_SEQUENCES, block_count, row_block, HIDDEN_WIDTH).transpose(1, 0, 2, 3)
    cot_blocks = upstream_sensitivity.reshape(block_count, row_block, RESIDUE_TOTAL, CP)

    def block_step(totals, inputs):
        grad_out, grad_right = totals
        left_blk, cot_blk = inputs
        outer_mean = (jnp.einsum('sip,sjq->ijpq', left_blk, right_wide) / GROUP_SEQUENCES).astype(jnp.bfloat16)
        outer_flat = outer_mean.reshape(row_block * RESIDUE_TOTAL, HIDDEN_WIDTH * HIDDEN_WIDTH)
        update = jnp.dot(outer_flat, final_mapping_matrix, preferred_element_type=jnp.float32) + final_offset_vector
        cot_flat = cot_blk.reshape(row_block * RESIDUE_TOTAL, CP)
        grad_out = grad_out + jnp.dot(outer_flat.T, cot_flat, preferred_element_type=jnp.float32)
        grad_outer = jnp.dot(cot_flat, final_mapping_matrix.T, preferred_element_type=jnp.float32).astype(jnp.bfloat16)
        grad_outer = grad_outer.reshape(row_block, RESIDUE_TOTAL, HIDDEN_WIDTH, HIDDEN_WIDTH).astype(jnp.float32)
        grad_left_blk = jnp.einsum('ijpq,sjq->sip', grad_outer, right_wide) / GROUP_SEQUENCES
        grad_right = grad_right + jnp.einsum('ijpq,sip->sjq', grad_outer, left_blk) / GROUP_SEQUENCES
        return ((grad_out, grad_right), (update.astype(jnp.bfloat16).reshape(row_block, RESIDUE_TOTAL, CP), grad_left_blk))
    start_totals = (jnp.zeros((HIDDEN_WIDTH * HIDDEN_WIDTH, CP), jnp.float32), jnp.zeros((GROUP_SEQUENCES, RESIDUE_TOTAL, HIDDEN_WIDTH), jnp.float32))
    (output_weight_gradient, grad_right_sum), (updates, grad_left_blocks) = lax.scan(block_step, start_totals, (left_blocks, cot_blocks))
    pair_delta = updates.reshape(RESIDUE_TOTAL, RESIDUE_TOTAL, CP)
    grad_left_sum = grad_left_blocks.transpose(1, 0, 2, 3).reshape(GROUP_SEQUENCES, RESIDUE_TOTAL, HIDDEN_WIDTH)
    grad_left = grad_left_sum.astype(jnp.bfloat16).astype(jnp.float32)
    grad_right = grad_right_sum.astype(jnp.bfloat16).astype(jnp.float32)
    left_weight_gradient = jnp.einsum('stc,stp->cp', normed_wide, grad_left)
    right_weight_gradient = jnp.einsum('stc,stp->cp', normed_wide, grad_right)
    normalized_gradient = jnp.einsum('stp,cp->stc', grad_left, w_a32) + jnp.einsum('stp,cp->stc', grad_right, w_b32)
    mean_factor = lax.optimization_barrier(jnp.mean(normalized_gradient, axis=-1, keepdims=True))
    projected_outer = lax.optimization_barrier(jnp.mean(normalized_gradient * normalized_input, axis=-1, keepdims=True))
    alignment_gradient = (inverse_spread * (normalized_gradient - mean_factor - normalized_input * projected_outer)).astype(jnp.bfloat16)
    return (pair_delta, alignment_gradient, left_weight_gradient, right_weight_gradient, output_weight_gradient)
```

```python
import jax
import jax.numpy as jnp
from jax import lax
from jax.sharding import PartitionSpec as P

PAIRS_AT_ONCE = 1024


def normalize(values):
    values = values.astype(jnp.float32)
    mean_factor = jnp.mean(values, axis=-1, keepdims=True)
    centered = values - mean_factor
    variance = jnp.mean(centered * centered, axis=-1, keepdims=True)
    inverse_spread = lax.rsqrt(variance + 1e-05)
    return (centered * inverse_spread, inverse_spread)


def row_routes(rows_n, cols_n):
    routes = []
    for k in range(cols_n):
        pairs = []
        for l in range(rows_n * cols_n):
            c, r = divmod(l, rows_n)
            pairs.append((r * cols_n + c, (l // cols_n) * cols_n + (l + k) % cols_n))
        routes.append(pairs)
    return routes


def col_routes(rows_n, cols_n):
    return [
        [
            (r * cols_n + c, (r + k) % rows_n * cols_n + c)
            for r in range(rows_n)
            for c in range(cols_n)
        ]
        for k in range(rows_n)
    ]


def back(pairs):
    return [(target, source) for source, target in pairs]


def local(
    homolog_features,
    subset_homolog_positions,
    first_side_matrix,
    second_side_matrix,
    final_mapping_matrix,
    final_offset_vector,
    upstream_sensitivity,
):
    axes = ("prow", "pcol")
    rows_n, cols_n = lax.axis_size("prow"), lax.axis_size("pcol")
    devices = rows_n * cols_n
    row_index, col_index = lax.axis_index("prow"), lax.axis_index("pcol")
    seq_count = subset_homolog_positions.shape[0]
    tokens = homolog_features.shape[1]
    row_count, col_count, pair_width = upstream_sensitivity.shape
    proj = first_side_matrix.shape[1]
    flat = proj * proj

    picked = jnp.take(homolog_features, subset_homolog_positions, axis=0)
    normed, inverse_spread = normalize(picked)
    normed_low = normed.astype(jnp.bfloat16)

    def project(matrix):
        out = jnp.einsum("stc,cp->stp", normed_low, matrix, preferred_element_type=jnp.float32)
        return out.astype(jnp.bfloat16).reshape(seq_count, tokens * proj)

    left_own, right_own = project(first_side_matrix), project(second_side_matrix)
    to_rows, to_cols = row_routes(rows_n, cols_n), col_routes(rows_n, cols_n)
    left_parts = [lax.ppermute(left_own, axes, pairs) for pairs in to_rows]
    right_parts = [right_own] + [lax.ppermute(right_own, axes, pairs) for pairs in to_cols[1:]]
    left = jnp.concatenate(left_parts, axis=1).reshape(seq_count, row_count, proj)
    right = jnp.concatenate(right_parts, axis=1).reshape(seq_count, col_count, proj)

    row_order = (col_index - jnp.arange(cols_n)) % cols_n
    col_order = (row_index - jnp.arange(rows_n)) % rows_n

    def reorder(pairs):
        pairs = pairs.reshape(cols_n, tokens, rows_n, tokens, pair_width)
        return jnp.take(jnp.take(pairs, row_order, axis=0), col_order, axis=2)

    cot = reorder(upstream_sensitivity).reshape(row_count, col_count, pair_width)

    def block_step(left_blk, cot_blk):
        rows = left_blk.shape[1]
        outer = jnp.einsum("sip,sjq->ijpq", left_blk, right, preferred_element_type=jnp.float32)
        outer = (outer / seq_count).astype(jnp.bfloat16).reshape(rows * col_count, flat)
        update = jnp.dot(outer, final_mapping_matrix, preferred_element_type=jnp.float32)
        update = (update + final_offset_vector).astype(jnp.bfloat16)
        cot_flat = cot_blk.reshape(rows * col_count, pair_width)
        grad_out = jnp.dot(outer.T, cot_flat, preferred_element_type=jnp.float32)
        grad_outer = jnp.dot(cot_flat, final_mapping_matrix.T, preferred_element_type=jnp.float32)
        grad_outer = grad_outer.astype(jnp.bfloat16).reshape(rows, col_count, proj, proj)
        grad_left = jnp.einsum(
            "ijpq,sjq->sip", grad_outer, right, preferred_element_type=jnp.float32
        )
        grad_right = jnp.einsum(
            "ijpq,sip->sjq", grad_outer, left_blk, preferred_element_type=jnp.float32
        )
        return update.reshape(rows, col_count, pair_width), grad_out, grad_left, grad_right

    block = max(1, min(row_count, PAIRS_AT_ONCE // col_count))
    blocks = row_count // block
    if blocks == 1:
        update, grad_out, grad_left, grad_right = block_step(left, cot)
    else:
        def step(totals, inputs):
            update, grad_out, grad_left, grad_right = block_step(*inputs)
            return (totals[0] + grad_out, totals[1] + grad_right), (update, grad_left)

        (grad_out, grad_right), (update, grad_left) = lax.scan(
            step,
            (
                jnp.zeros((flat, pair_width), jnp.float32),
                jnp.zeros((seq_count, col_count, proj), jnp.float32),
            ),
            (
                left.reshape(seq_count, blocks, block, proj).transpose(1, 0, 2, 3),
                cot.reshape(blocks, block, col_count, pair_width),
            ),
        )
        grad_left = grad_left.transpose(1, 0, 2, 3)
    pair_delta = reorder(update).reshape(row_count, col_count, pair_width)

    shares = grad_out.astype(jnp.bfloat16).reshape(devices, flat // devices, pair_width)
    shares = lax.all_to_all(shares, axes, 0, 0)
    share = jnp.sum(shares.astype(jnp.float32), axis=0).astype(jnp.bfloat16)

    def send_back(grads, count, routes):
        grads = (grads / seq_count).astype(jnp.bfloat16).reshape(seq_count, count, tokens * proj)
        total = 0.0
        for k, pairs in enumerate(routes):
            part = grads[:, k]
            if pairs[0][0] != pairs[0][1] or any(a != b for a, b in pairs):
                part = lax.ppermute(part, axes, back(pairs))
            total = total + part.astype(jnp.float32)
        return total.astype(jnp.bfloat16).reshape(seq_count, tokens, proj)

    grad_left = send_back(grad_left, cols_n, to_rows)
    grad_right = send_back(grad_right, rows_n, to_cols)

    both = jnp.concatenate([grad_left, grad_right], axis=-1)
    side_part = jnp.einsum("stc,stp->cp", normed_low, both, preferred_element_type=jnp.float32)
    features = side_part.shape[0]
    side_rows = features * 2 * proj // pair_width
    message = jnp.concatenate(
        [share, side_part.astype(jnp.bfloat16).reshape(side_rows, pair_width)], axis=0
    )
    message = jnp.broadcast_to(message[None], (devices,) + message.shape)
    message = lax.all_to_all(message, axes, 0, 0)
    output_weight_gradient = (
        message[:, : flat // devices].reshape(flat, pair_width).astype(jnp.float32)
    )
    side = jnp.sum(message[:, flat // devices :].astype(jnp.float32), axis=0)
    side = side.reshape(features, 2 * proj)
    left_weight_gradient, right_weight_gradient = side[:, :proj], side[:, proj:]

    sides = jnp.concatenate([first_side_matrix, second_side_matrix], axis=1)
    grad_normed = jnp.einsum("stp,cp->stc", both, sides, preferred_element_type=jnp.float32)
    mean_factor = jnp.mean(grad_normed, axis=-1, keepdims=True)
    projected = jnp.mean(grad_normed * normed, axis=-1, keepdims=True)
    alignment_gradient = (
        inverse_spread * (grad_normed - mean_factor - normed * projected)
    ).astype(jnp.bfloat16)
    return (
        pair_delta,
        alignment_gradient,
        left_weight_gradient,
        right_weight_gradient,
        output_weight_gradient,
    )


def solution(mesh):
    return jax.shard_map(
        local,
        mesh=mesh,
        in_specs=(
            P("rep", ("pcol", "prow"), None),
            P("rep"),
            P(),
            P(),
            P(),
            P(),
            P(("rep", "prow"), "pcol", None),
        ),
        out_specs=(
            P(("rep", "prow"), "pcol", None),
            P("rep", ("pcol", "prow"), None),
            P("rep", None),
            P("rep", None),
            P("rep", None),
        ),
        check_vma=False,
    )
```

```python
import jax
import jax.numpy as jnp
from jax import lax
from jax.sharding import PartitionSpec as P

PAIRS_AT_ONCE = 1024


def normalize(values):
    values = values.astype(jnp.float32)
    mean_factor = jnp.mean(values, axis=-1, keepdims=True)
    centered = values - mean_factor
    variance = jnp.mean(centered * centered, axis=-1, keepdims=True)
    inverse_spread = lax.rsqrt(variance + 1e-05)
    return (centered * inverse_spread, inverse_spread)


def transposed(rows_n, cols_n):
    return [
        (r * cols_n + c, c * rows_n + r) for r in range(rows_n) for c in range(cols_n)
    ]


def spread(values, axes, count):
    return lax.all_to_all(jnp.broadcast_to(values[None], (count,) + values.shape), axes, 0, 0)


def local(
    homolog_features,
    subset_homolog_positions,
    first_side_matrix,
    second_side_matrix,
    final_mapping_matrix,
    final_offset_vector,
    upstream_sensitivity,
):
    axes = ("prow", "pcol")
    rows_n, cols_n = lax.axis_size("prow"), lax.axis_size("pcol")
    devices = rows_n * cols_n
    seq_count = subset_homolog_positions.shape[0]
    tokens, features = homolog_features.shape[1:]
    row_count, col_count, pair_width = upstream_sensitivity.shape
    proj = first_side_matrix.shape[1]
    flat = proj * proj
    to_rows = transposed(rows_n, cols_n)
    to_tokens = [(target, source) for source, target in to_rows]

    picked = jnp.take(homolog_features, subset_homolog_positions, axis=0)
    packed = picked.reshape(seq_count, tokens * features)
    row_own = lax.ppermute(packed, axes, to_rows)
    col_all = spread(packed, "prow", rows_n)
    row_all = spread(row_own, "pcol", cols_n)

    def side_of(chunks, count, matrix):
        chunks = chunks.reshape(count // tokens, seq_count, tokens, features)
        chunks = chunks.transpose(1, 0, 2, 3).reshape(seq_count, count, features)
        normed_low = normalize(chunks)[0].astype(jnp.bfloat16)
        side = jnp.einsum("stc,cp->stp", normed_low, matrix, preferred_element_type=jnp.float32)
        return normed_low, side.astype(jnp.bfloat16)

    row_normed, left = side_of(row_all, row_count, first_side_matrix)
    col_normed, right = side_of(col_all, col_count, second_side_matrix)

    def block_step(left_blk, cot_blk):
        rows = left_blk.shape[1]
        outer = jnp.einsum("sip,sjq->ijpq", left_blk, right, preferred_element_type=jnp.float32)
        outer = (outer / seq_count).astype(jnp.bfloat16).reshape(rows * col_count, flat)
        update = jnp.dot(outer, final_mapping_matrix, preferred_element_type=jnp.float32)
        update = (update + final_offset_vector).astype(jnp.bfloat16)
        cot_flat = cot_blk.reshape(rows * col_count, pair_width)
        grad_out = jnp.dot(outer.T, cot_flat, preferred_element_type=jnp.float32)
        grad_outer = jnp.dot(cot_flat, final_mapping_matrix.T, preferred_element_type=jnp.float32)
        grad_outer = grad_outer.astype(jnp.bfloat16).reshape(rows, col_count, proj, proj)
        grad_left = jnp.einsum(
            "ijpq,sjq->sip", grad_outer, right, preferred_element_type=jnp.float32
        )
        grad_right = jnp.einsum(
            "ijpq,sip->sjq", grad_outer, left_blk, preferred_element_type=jnp.float32
        )
        return update.reshape(rows, col_count, pair_width), grad_out, grad_left, grad_right

    block = max(1, min(row_count, PAIRS_AT_ONCE // col_count))
    blocks = row_count // block
    if blocks == 1:
        update, grad_out, grad_left, grad_right = block_step(left, upstream_sensitivity)
    else:
        def step(totals, inputs):
            update, grad_out, grad_left, grad_right = block_step(*inputs)
            return (totals[0] + grad_out, totals[1] + grad_right), (update, grad_left)

        (grad_out, grad_right), (update, grad_left) = lax.scan(
            step,
            (
                jnp.zeros((flat, pair_width), jnp.float32),
                jnp.zeros((seq_count, col_count, proj), jnp.float32),
            ),
            (
                left.reshape(seq_count, blocks, block, proj).transpose(1, 0, 2, 3),
                upstream_sensitivity.reshape(blocks, block, col_count, pair_width),
            ),
        )
        grad_left = grad_left.transpose(1, 0, 2, 3).reshape(seq_count, row_count, proj)
    pair_delta = update.reshape(row_count, col_count, pair_width)

    grad_left = (grad_left / seq_count).astype(jnp.bfloat16)
    grad_right = (grad_right / seq_count).astype(jnp.bfloat16)

    def weight_part(normed, grads):
        return jnp.einsum("stc,stp->cp", normed, grads, preferred_element_type=jnp.float32)

    side_part = jnp.concatenate(
        [weight_part(row_normed, grad_left), weight_part(col_normed, grad_right)], axis=1
    )
    share_rows = flat // devices
    side_rows = -(-features * 2 * proj // (pair_width * devices))
    side_flat = side_part.reshape(-1, pair_width)
    side_flat = jnp.pad(side_flat, ((0, side_rows * devices - side_flat.shape[0]), (0, 0)))
    shares = jnp.concatenate(
        [
            grad_out.reshape(devices, share_rows, pair_width),
            side_flat.reshape(devices, side_rows, pair_width),
        ],
        axis=1,
    ).astype(jnp.bfloat16)
    shares = lax.all_to_all(shares, axes, 0, 0)

    def chunks_of(grads, count):
        grads = grads.reshape(seq_count, count // tokens, tokens * proj)
        return grads.transpose(1, 0, 2)

    left_back = lax.all_to_all(chunks_of(grad_left, row_count), "pcol", 0, 0)
    right_back = lax.all_to_all(chunks_of(grad_right, col_count), "prow", 0, 0)
    left_back = jnp.sum(left_back.astype(jnp.float32), axis=0).astype(jnp.bfloat16)
    right_back = jnp.sum(right_back.astype(jnp.float32), axis=0).astype(jnp.bfloat16)
    left_back = lax.ppermute(left_back, axes, to_tokens)

    share = jnp.sum(shares.astype(jnp.float32), axis=0).astype(jnp.bfloat16)
    message = spread(share, axes, devices)
    output_weight_gradient = (
        message[:, :share_rows].reshape(flat, pair_width).astype(jnp.float32)
    )
    side = message[:, share_rows:].reshape(-1, pair_width).astype(jnp.float32)
    side = side[: features * 2 * proj // pair_width].reshape(features, 2 * proj)
    left_weight_gradient, right_weight_gradient = side[:, :proj], side[:, proj:]

    normed, inverse_spread = normalize(picked)
    both = jnp.concatenate(
        [
            left_back.reshape(seq_count, tokens, proj),
            right_back.reshape(seq_count, tokens, proj),
        ],
        axis=-1,
    )
    sides = jnp.concatenate([first_side_matrix, second_side_matrix], axis=1)
    grad_normed = jnp.einsum("stp,cp->stc", both, sides, preferred_element_type=jnp.float32)
    mean_factor = jnp.mean(grad_normed, axis=-1, keepdims=True)
    projected = jnp.mean(grad_normed * normed, axis=-1, keepdims=True)
    alignment_gradient = (
        inverse_spread * (grad_normed - mean_factor - normed * projected)
    ).astype(jnp.bfloat16)
    return (
        pair_delta,
        alignment_gradient,
        left_weight_gradient,
        right_weight_gradient,
        output_weight_gradient,
    )


def solution(mesh):
    return jax.shard_map(
        local,
        mesh=mesh,
        in_specs=(
            P("rep", ("pcol", "prow"), None),
            P("rep"),
            P(),
            P(),
            P(),
            P(),
            P(("rep", "prow"), "pcol", None),
        ),
        out_specs=(
            P(("rep", "prow"), "pcol", None),
            P("rep", ("pcol", "prow"), None),
            P("rep", None),
            P("rep", None),
            P("rep", None),
        ),
        check_vma=False,
    )
```

```python
import functools

import jax
import jax.numpy as jnp
from jax import lax
from jax.experimental import pallas as pl
from jax.experimental.pallas import tpu as pltpu
from jax.sharding import Mesh
from jax.sharding import PartitionSpec as P

BF16, F32 = jnp.bfloat16, jnp.float32
LANES = 128
GATHERED_PAIRS = 4096

PAIRS_AT_ONCE = 1024


def normalize(values):
    values = values.astype(jnp.float32)
    mean_factor = jnp.mean(values, axis=-1, keepdims=True)
    centered = values - mean_factor
    variance = jnp.mean(centered * centered, axis=-1, keepdims=True)
    inverse_spread = lax.rsqrt(variance + 1e-05)
    return (centered * inverse_spread, inverse_spread)


def transposed(rows_n, cols_n):
    return [
        (r * cols_n + c, c * rows_n + r) for r in range(rows_n) for c in range(cols_n)
    ]


def spread(values, axes, count):
    return lax.all_to_all(jnp.broadcast_to(values[None], (count,) + values.shape), axes, 0, 0)


def local_phased(
    homolog_features,
    subset_homolog_positions,
    first_side_matrix,
    second_side_matrix,
    final_mapping_matrix,
    final_offset_vector,
    upstream_sensitivity,
):
    axes = ("prow", "pcol")
    rows_n, cols_n = lax.axis_size("prow"), lax.axis_size("pcol")
    devices = rows_n * cols_n
    seq_count = subset_homolog_positions.shape[0]
    tokens, features = homolog_features.shape[1:]
    row_count, col_count, pair_width = upstream_sensitivity.shape
    proj = first_side_matrix.shape[1]
    flat = proj * proj
    to_rows = transposed(rows_n, cols_n)
    to_tokens = [(target, source) for source, target in to_rows]

    picked = jnp.take(homolog_features, subset_homolog_positions, axis=0)
    packed = picked.reshape(seq_count, tokens * features)
    row_own = lax.ppermute(packed, axes, to_rows)
    col_all = spread(packed, "prow", rows_n)
    row_all = spread(row_own, "pcol", cols_n)

    def side_of(chunks, count, matrix):
        chunks = chunks.reshape(count // tokens, seq_count, tokens, features)
        chunks = chunks.transpose(1, 0, 2, 3).reshape(seq_count, count, features)
        normed_low = normalize(chunks)[0].astype(jnp.bfloat16)
        side = jnp.einsum("stc,cp->stp", normed_low, matrix, preferred_element_type=jnp.float32)
        return normed_low, side.astype(jnp.bfloat16)

    row_normed, left = side_of(row_all, row_count, first_side_matrix)
    col_normed, right = side_of(col_all, col_count, second_side_matrix)

    def block_step(left_blk, cot_blk):
        rows = left_blk.shape[1]
        outer = jnp.einsum("sip,sjq->ijpq", left_blk, right, preferred_element_type=jnp.float32)
        outer = (outer / seq_count).astype(jnp.bfloat16).reshape(rows * col_count, flat)
        update = jnp.dot(outer, final_mapping_matrix, preferred_element_type=jnp.float32)
        update = (update + final_offset_vector).astype(jnp.bfloat16)
        cot_flat = cot_blk.reshape(rows * col_count, pair_width)
        grad_out = jnp.dot(outer.T, cot_flat, preferred_element_type=jnp.float32)
        grad_outer = jnp.dot(cot_flat, final_mapping_matrix.T, preferred_element_type=jnp.float32)
        grad_outer = grad_outer.astype(jnp.bfloat16).reshape(rows, col_count, proj, proj)
        grad_left = jnp.einsum(
            "ijpq,sjq->sip", grad_outer, right, preferred_element_type=jnp.float32
        )
        grad_right = jnp.einsum(
            "ijpq,sip->sjq", grad_outer, left_blk, preferred_element_type=jnp.float32
        )
        return update.reshape(rows, col_count, pair_width), grad_out, grad_left, grad_right

    block = max(1, min(row_count, PAIRS_AT_ONCE // col_count))
    blocks = row_count // block
    if blocks == 1:
        update, grad_out, grad_left, grad_right = block_step(left, upstream_sensitivity)
    else:
        def step(totals, inputs):
            update, grad_out, grad_left, grad_right = block_step(*inputs)
            return (totals[0] + grad_out, totals[1] + grad_right), (update, grad_left)

        (grad_out, grad_right), (update, grad_left) = lax.scan(
            step,
            (
                jnp.zeros((flat, pair_width), jnp.float32),
                jnp.zeros((seq_count, col_count, proj), jnp.float32),
            ),
            (
                left.reshape(seq_count, blocks, block, proj).transpose(1, 0, 2, 3),
                upstream_sensitivity.reshape(blocks, block, col_count, pair_width),
            ),
        )
        grad_left = grad_left.transpose(1, 0, 2, 3).reshape(seq_count, row_count, proj)
    pair_delta = update.reshape(row_count, col_count, pair_width)

    grad_left = (grad_left / seq_count).astype(jnp.bfloat16)
    grad_right = (grad_right / seq_count).astype(jnp.bfloat16)

    def weight_part(normed, grads):
        return jnp.einsum("stc,stp->cp", normed, grads, preferred_element_type=jnp.float32)

    side_part = jnp.concatenate(
        [weight_part(row_normed, grad_left), weight_part(col_normed, grad_right)], axis=1
    )
    share_rows = flat // devices
    side_rows = -(-features * 2 * proj // (pair_width * devices))
    side_flat = side_part.reshape(-1, pair_width)
    side_flat = jnp.pad(side_flat, ((0, side_rows * devices - side_flat.shape[0]), (0, 0)))
    shares = jnp.concatenate(
        [
            grad_out.reshape(devices, share_rows, pair_width),
            side_flat.reshape(devices, side_rows, pair_width),
        ],
        axis=1,
    ).astype(jnp.bfloat16)
    shares = lax.all_to_all(shares, axes, 0, 0)

    def chunks_of(grads, count):
        grads = grads.reshape(seq_count, count // tokens, tokens * proj)
        return grads.transpose(1, 0, 2)

    left_back = lax.all_to_all(chunks_of(grad_left, row_count), "pcol", 0, 0)
    right_back = lax.all_to_all(chunks_of(grad_right, col_count), "prow", 0, 0)
    left_back = jnp.sum(left_back.astype(jnp.float32), axis=0).astype(jnp.bfloat16)
    right_back = jnp.sum(right_back.astype(jnp.float32), axis=0).astype(jnp.bfloat16)
    left_back = lax.ppermute(left_back, axes, to_tokens)

    share = jnp.sum(shares.astype(jnp.float32), axis=0).astype(jnp.bfloat16)
    message = spread(share, axes, devices)
    output_weight_gradient = (
        message[:, :share_rows].reshape(flat, pair_width).astype(jnp.float32)
    )
    side = message[:, share_rows:].reshape(-1, pair_width).astype(jnp.float32)
    side = side[: features * 2 * proj // pair_width].reshape(features, 2 * proj)
    left_weight_gradient, right_weight_gradient = side[:, :proj], side[:, proj:]

    normed, inverse_spread = normalize(picked)
    both = jnp.concatenate(
        [
            left_back.reshape(seq_count, tokens, proj),
            right_back.reshape(seq_count, tokens, proj),
        ],
        axis=-1,
    )
    sides = jnp.concatenate([first_side_matrix, second_side_matrix], axis=1)
    grad_normed = jnp.einsum("stp,cp->stc", both, sides, preferred_element_type=jnp.float32)
    mean_factor = jnp.mean(grad_normed, axis=-1, keepdims=True)
    projected = jnp.mean(grad_normed * normed, axis=-1, keepdims=True)
    alignment_gradient = (
        inverse_spread * (grad_normed - mean_factor - normed * projected)
    ).astype(jnp.bfloat16)
    return (
        pair_delta,
        alignment_gradient,
        left_weight_gradient,
        right_weight_gradient,
        output_weight_gradient,
    )


def dot(x, y, contract=(1, 0), precision=None):
    return lax.dot_general(
        x, y, (((contract[0],), (contract[1],)), ((), ())),
        precision=precision, preferred_element_type=F32,
    )


def lane_ids(shape):
    return lax.broadcasted_iota(jnp.int32, shape, len(shape) - 1)


def fold_lanes(x, width):
    shift = LANES // 2
    while shift >= width:
        x = x + pltpu.roll(x, shift, x.ndim - 1)
        shift //= 2
    return x


def group_mean(x, group, precision):
    lanes = x.shape[1]
    rows_id = lax.broadcasted_iota(jnp.int32, (lanes, lanes), 0) // group
    cols_id = lax.broadcasted_iota(jnp.int32, (lanes, lanes), 1) // group
    block = jnp.where(rows_id == cols_id, 1.0 / group, 0.0).astype(x.dtype)
    return dot(x, block, precision=precision)


def pick_kernel(group, positions_ref, features_ref, normed_ref, inverse_ref, sent_ref):
    heads = features_ref.shape[0]
    seqs = normed_ref.shape[0]
    wanted = positions_ref[...] == lax.broadcasted_iota(jnp.int32, (heads, seqs), 0)
    chosen = dot(wanted.astype(BF16), features_ref[...], contract=(0, 0))
    mean_factor = group_mean(chosen.astype(BF16), group, None)
    centered = chosen - mean_factor
    variance = group_mean(centered * centered, group, lax.Precision.HIGHEST)
    inverse = lax.rsqrt(variance + 1e-05)
    normed = centered * inverse
    normed_ref[...] = normed
    inverse_ref[...] = inverse
    sent_ref[...] = jnp.broadcast_to(normed.astype(BF16)[None], sent_ref.shape)


def pair_kernel(
    place_ref,
    rows_ref,
    cot_ref,
    mapping_ref,
    left_ref,
    right_ref,
    offset_ref,
    pair_ref,
    grads_ref,
    message_ref,
    expanded,
    outer,
    pulled,
    left_back,
    right_back,
    turned,
    swapped,
    sums,
    weights,
):
    owners, seqs, packed = rows_ref.shape
    prow_n, groups, block_rows, block_cols, pair_width = cot_ref.shape
    tokens = left_ref.shape[1] // LANES
    proj = LANES // tokens
    highs = proj // tokens
    span = highs * block_cols
    own_row, own_group, core = place_ref[0], place_ref[1], place_ref[2]

    def token_owner(group, row, parity):
        return (2 * group + parity) * prow_n + row

    rows_all = rows_ref[...].reshape(owners * seqs, packed)
    expanded[...] = dot(rows_all, left_ref[...]).astype(BF16).reshape(expanded.shape)

    side_rows = []
    for g in range(groups):
        chunks = [rows_ref[token_owner(g, r, core)] for r in range(prow_n)]
        side_rows.append(
            jnp.concatenate([dot(x, right_ref[...]).astype(BF16) for x in chunks], axis=1)
        )
    right = jnp.concatenate(side_rows, axis=0)
    wide = right.shape[1]
    source = lax.broadcasted_iota(jnp.int32, (wide, wide), 0)
    target = lax.broadcasted_iota(jnp.int32, (wide, wide), 1)
    jj, qh, ql = target % block_cols, target // block_cols % highs, target // span
    shuffle = (source == jj * proj + qh * tokens + ql).astype(BF16)
    right = dot(right, shuffle)
    for g in range(groups):
        for l in range(tokens):
            swapped[l * seqs : (l + 1) * seqs, g * span : (g + 1) * span] = right[
                g * seqs : (g + 1) * seqs, l * span : (l + 1) * span
            ].astype(BF16)
    turned[...] = swapped[...].astype(F32).T.astype(BF16)

    sums[...] = jnp.zeros_like(sums)
    weights[...] = jnp.zeros_like(weights)
    step_tokens = outer.shape[0] // (groups * block_cols)
    step_owners = step_tokens // tokens
    steps_a_block = block_rows // step_tokens

    def step(m, carry):
        row, part = m // steps_a_block, m % steps_a_block
        ahead = jnp.concatenate(
            [expanded[m * step_owners + o] for o in range(step_owners)], axis=1
        )
        low = lane_ids(ahead.shape) % LANES // proj
        block = jnp.concatenate(
            [jnp.where(low == l, ahead, jnp.zeros_like(ahead)) for l in range(tokens)], axis=0
        )
        cot = jnp.concatenate(
            [
                cot_ref[row, g, pl.ds(part * step_tokens, step_tokens)].reshape(
                    step_tokens * block_cols, pair_width
                )
                for g in range(groups)
            ],
            axis=0,
        )
        made = dot(turned[...], block) * (1.0 / seqs)
        grad = dot(cot, mapping_ref[...], contract=(1, 1))
        for g in range(groups):
            for t in range(step_tokens):
                here = slice((g * step_tokens + t) * block_cols, (g * step_tokens + t + 1) * block_cols)
                lanes = slice(t * LANES, (t + 1) * LANES)
                for h in range(highs):
                    there = slice((g * highs + h) * block_cols, (g * highs + h + 1) * block_cols)
                    cols = slice(h * LANES, (h + 1) * LANES)
                    outer[here, cols] = made[there, lanes].astype(BF16)
                    pulled[there, lanes] = grad[here, cols].astype(BF16)
        weights[...] += dot(cot, outer[...], contract=(0, 0))
        back = dot(swapped[...], pulled[...])
        back = functools.reduce(
            jnp.add,
            [
                jnp.where(low == l, back[l * seqs : (l + 1) * seqs], 0.0)
                for l in range(tokens)
            ],
        )
        slot = lane_ids((seqs, LANES)) // proj
        for o in range(step_owners):
            total = jnp.zeros((seqs, LANES), F32)
            for t in range(tokens):
                at = (o * tokens + t) * LANES
                total = jnp.where(slot == t, fold_lanes(back[:, at : at + LANES], proj), total)
            left_back[m * step_owners + o] = (total * (1.0 / seqs)).astype(BF16)
        sums[...] += dot(pulled[...], block, contract=(1, 1))

        @pl.when(row == own_row)
        def _():
            half = step_tokens * block_cols
            mine = outer[pl.ds(pl.multiple_of(own_group * half, half), half)]
            update = dot(mine, mapping_ref[...]) + offset_ref[...]
            pair_ref[pl.ds(part * step_tokens, step_tokens)] = update.astype(BF16).reshape(
                step_tokens, block_cols, pair_width
            )

        return carry

    lax.fori_loop(0, prow_n * steps_a_block, step, 0)

    back = (sums[...].T * (1.0 / seqs)).astype(BF16)
    back = jnp.concatenate(
        [
            jnp.concatenate(
                [
                    back[l * seqs : (l + 1) * seqs, g * span : (g + 1) * span]
                    for l in range(tokens)
                ],
                axis=1,
            )
            for g in range(groups)
        ],
        axis=0,
    )
    back = dot(back, shuffle, contract=(1, 1)).astype(BF16)
    column_rows = []
    for g in range(groups):
        for r in range(prow_n):
            right_back[g * prow_n + r] = back[
                g * seqs : (g + 1) * seqs, r * LANES : (r + 1) * LANES
            ]
            column_rows.append(rows_ref[token_owner(g, r, core)])

    def side(rows, grads):
        total = dot(rows, grads, contract=(0, 0))
        features = packed // tokens
        slot = lane_ids((features, LANES)) // proj
        kept = functools.reduce(
            jnp.add,
            [
                jnp.where(slot == t, total[t * features : (t + 1) * features], 0.0)
                for t in range(tokens)
            ],
        )
        return fold_lanes(kept, proj)

    left_side = side(rows_all, left_back[...].reshape(owners * seqs, LANES))
    right_side = side(
        jnp.concatenate(column_rows, axis=0), right_back[...].reshape(-1, LANES)
    )
    both = jnp.where(lane_ids(left_side.shape) < proj, left_side, right_side)

    flat = weights.shape[1]
    outer_f = weights[...].T
    weight_rows = outer_f.reshape(proj, proj, pair_width).swapaxes(0, 1).reshape(flat, pair_width)

    features = packed // tokens
    message_ref[:flat] = weight_rows.astype(BF16)
    message_ref[flat : flat + features] = both.astype(BF16)
    message_ref[flat + features :] = left_back[token_owner(own_group, own_row, 1 - core)]
    grads_ref[0] = left_back[token_owner(own_group, own_row, core)]
    grads_ref[1] = right_back[own_group * prow_n + own_row]


def close_kernel(
    grads_ref,
    own_ref,
    message_ref,
    normed_ref,
    inverse_ref,
    left_ref,
    right_ref,
    out_ref,
    left_out_ref,
    right_out_ref,
    rows_out_ref,
):
    flat = out_ref.shape[0]
    features, proj = left_out_ref.shape
    out_ref[...] = own_ref[:flat].astype(F32) + message_ref[:flat].astype(F32)
    both = own_ref[flat : flat + features].astype(F32)
    both = both + message_ref[flat : flat + features].astype(F32)
    left_out_ref[...] = both[:, :proj]
    right_out_ref[...] = both[:, proj : 2 * proj]
    left_back = grads_ref[0].astype(F32) + message_ref[flat + features :].astype(F32)
    grad_normed = dot(left_back.astype(BF16), left_ref[...], contract=(1, 1))
    grad_normed = grad_normed + dot(grads_ref[1], right_ref[...], contract=(1, 1))
    normed = normed_ref[...]
    mean_factor = group_mean(grad_normed, features, lax.Precision.HIGHEST)
    projected = group_mean(grad_normed * normed, features, lax.Precision.HIGHEST)
    rows_out_ref[...] = (
        inverse_ref[...] * (grad_normed - mean_factor - normed * projected)
    ).astype(BF16)


def local_gathered(
    homolog_features,
    subset_homolog_positions,
    first_side_matrix,
    second_side_matrix,
    final_mapping_matrix,
    final_offset_vector,
    upstream_sensitivity,
):
    prow_n, groups = lax.axis_size("prow"), lax.axis_size("px")
    owners = prow_n * groups * 2
    heads, tokens, features = homolog_features.shape
    seqs = subset_homolog_positions.shape[0]
    block_rows, block_cols, pair_width = upstream_sensitivity.shape
    proj = first_side_matrix.shape[1]
    flat = proj * proj
    packed = tokens * features
    step_tokens = 2 * tokens
    shape = jax.ShapeDtypeStruct
    vmem = pl.BlockSpec(memory_space=pltpu.VMEM)
    smem = pl.BlockSpec(memory_space=pltpu.SMEM)
    params = pltpu.CompilerParams(vmem_limit_bytes=48 * 1024 * 1024)

    cot = lax.all_to_all(
        jnp.broadcast_to(upstream_sensitivity[None], (prow_n * groups,) + upstream_sensitivity.shape),
        ("prow", "px"), 0, 0,
    ).reshape((prow_n, groups) + upstream_sensitivity.shape)

    normed, inverse, sent = pl.pallas_call(
        functools.partial(pick_kernel, features),
        out_shape=(
            shape((seqs, packed), F32),
            shape((seqs, packed), F32),
            shape((owners, seqs, packed), BF16),
        ),
        in_specs=[vmem] * 2,
        out_specs=(vmem,) * 3,
        compiler_params=params,
        name="pick_rows",
    )(subset_homolog_positions.reshape(1, seqs), homolog_features.reshape(heads, packed))
    rows = lax.all_to_all(sent, ("px", "pc", "prow"), 0, 0)

    one = jnp.eye(tokens, dtype=BF16)
    left_one = jnp.kron(one, first_side_matrix)
    left_wide = jnp.kron(one, jnp.tile(first_side_matrix, (1, tokens)))
    right_one = jnp.kron(one, second_side_matrix)
    mapping = final_mapping_matrix.reshape(proj, proj, pair_width)
    mapping = mapping.swapaxes(0, 1).reshape(flat, pair_width)
    place = jnp.stack([lax.axis_index("prow"), lax.axis_index("px"), lax.axis_index("pc")])

    pairs = step_tokens * groups * block_cols
    pair_delta, grads, message = pl.pallas_call(
        pair_kernel,
        out_shape=(
            shape(upstream_sensitivity.shape, BF16),
            shape((2, seqs, LANES), BF16),
            shape((flat + features + seqs, LANES), BF16),
        ),
        in_specs=[smem] + [vmem] * 6,
        out_specs=(vmem,) * 3,
        scratch_shapes=[
            pltpu.VMEM((owners, seqs, tokens * LANES), BF16),
            pltpu.VMEM((pairs, flat), BF16),
            pltpu.VMEM((groups * proj // tokens * block_cols, step_tokens * LANES), BF16),
            pltpu.VMEM((owners, seqs, LANES), BF16),
            pltpu.VMEM((groups * prow_n, seqs, LANES), BF16),
            pltpu.VMEM((groups * proj // tokens * block_cols, tokens * seqs), BF16),
            pltpu.VMEM((tokens * seqs, groups * proj // tokens * block_cols), BF16),
            pltpu.VMEM((groups * proj // tokens * block_cols, tokens * seqs), F32),
            pltpu.VMEM((pair_width, flat), F32),
        ],
        compiler_params=params,
        name="pair_work",
    )(place, rows, cot, mapping, left_wide, right_one, final_offset_vector.reshape(1, pair_width))

    theirs = lax.ppermute(message, "pc", [(0, 1), (1, 0)])
    output_weight_gradient, left_weight_gradient, right_weight_gradient, alignment = pl.pallas_call(
        close_kernel,
        out_shape=(
            shape((flat, pair_width), F32),
            shape((features, proj), F32),
            shape((features, proj), F32),
            shape((seqs, packed), BF16),
        ),
        in_specs=[vmem] * 7,
        out_specs=(vmem,) * 4,
        compiler_params=params,
        name="close",
    )(grads, message, theirs, normed, inverse, left_one, right_one)
    return (
        pair_delta,
        alignment.reshape(seqs, tokens, features),
        left_weight_gradient,
        right_weight_gradient,
        output_weight_gradient,
    )


def shapes_allow_gathering(
    mesh_shape, features, positions, first_side, second_side, mapping, offset, cot
):
    rows_n, cols_n = mesh_shape["prow"], mesh_shape["pcol"]
    parts = mesh_shape["rep"]
    tokens = features.shape[1] // (rows_n * cols_n)
    block_rows, block_cols = cot.shape[0] // (parts * rows_n), cot.shape[1] // cols_n
    proj, width = first_side.shape[1], cot.shape[2]
    return (
        cols_n % 2 == 0
        and cot.shape[1] * cot.shape[1] <= GATHERED_PAIRS
        and tokens * proj == LANES
        and proj % tokens == 0
        and block_rows % (2 * tokens) == 0
        and block_cols == rows_n * tokens == 16
        and width % LANES == 0
        and positions.shape[0] // parts % 16 == 0
        and features.shape[2] * tokens % LANES == 0
    )


def solution(mesh):
    def run(local, over, columns, *args):
        tokens_split = P("rep", columns + ("prow",), None)
        pairs_split = P(("rep", "prow"), columns, None)
        return jax.shard_map(
            local,
            mesh=over,
            in_specs=(tokens_split, P("rep"), P(), P(), P(), P(), pairs_split),
            out_specs=(pairs_split, tokens_split, P("rep", None), P("rep", None), P("rep", None)),
            check_vma=False,
        )(*args)

    def program(*args):
        if not shapes_allow_gathering(mesh.shape, *args):
            return run(local_phased, mesh, ("pcol",), *args)
        reps, rows_n, cols_n = (mesh.shape[name] for name in ("rep", "prow", "pcol"))
        chips = Mesh(
            mesh.devices.reshape(reps, rows_n, cols_n // 2, 2), ("rep", "prow", "px", "pc")
        )
        return run(local_gathered, chips, ("px", "pc"), *args)

    return program
```

```python
import functools

import jax
import jax.numpy as jnp
from jax import lax
from jax.experimental import pallas as pl
from jax.experimental.pallas import tpu as pltpu
from jax.sharding import Mesh
from jax.sharding import PartitionSpec as P

BF16, F32 = jnp.bfloat16, jnp.float32
LANES = 128
GATHERED_PAIRS = 4096

PAIRS_AT_ONCE = 1024


def normalize(values):
    values = values.astype(jnp.float32)
    mean_factor = jnp.mean(values, axis=-1, keepdims=True)
    centered = values - mean_factor
    variance = jnp.mean(centered * centered, axis=-1, keepdims=True)
    inverse_spread = lax.rsqrt(variance + 1e-05)
    return (centered * inverse_spread, inverse_spread)


def transposed(rows_n, cols_n):
    return [
        (r * cols_n + c, c * rows_n + r) for r in range(rows_n) for c in range(cols_n)
    ]


def spread(values, axes, count):
    return lax.all_to_all(jnp.broadcast_to(values[None], (count,) + values.shape), axes, 0, 0)


def local_phased(
    homolog_features,
    subset_homolog_positions,
    first_side_matrix,
    second_side_matrix,
    final_mapping_matrix,
    final_offset_vector,
    upstream_sensitivity,
):
    axes = ("prow", "pcol")
    rows_n, cols_n = lax.axis_size("prow"), lax.axis_size("pcol")
    devices = rows_n * cols_n
    seq_count = subset_homolog_positions.shape[0]
    tokens, features = homolog_features.shape[1:]
    row_count, col_count, pair_width = upstream_sensitivity.shape
    proj = first_side_matrix.shape[1]
    flat = proj * proj
    to_rows = transposed(rows_n, cols_n)
    to_tokens = [(target, source) for source, target in to_rows]

    picked = jnp.take(homolog_features, subset_homolog_positions, axis=0)
    packed = picked.reshape(seq_count, tokens * features)
    row_own = lax.ppermute(packed, axes, to_rows)
    col_all = spread(packed, "prow", rows_n)
    row_all = spread(row_own, "pcol", cols_n)

    def side_of(chunks, count, matrix):
        chunks = chunks.reshape(count // tokens, seq_count, tokens, features)
        chunks = chunks.transpose(1, 0, 2, 3).reshape(seq_count, count, features)
        normed_low = normalize(chunks)[0].astype(jnp.bfloat16)
        side = jnp.einsum("stc,cp->stp", normed_low, matrix, preferred_element_type=jnp.float32)
        return normed_low, side.astype(jnp.bfloat16)

    row_normed, left = side_of(row_all, row_count, first_side_matrix)
    col_normed, right = side_of(col_all, col_count, second_side_matrix)

    def block_step(left_blk, cot_blk):
        rows = left_blk.shape[1]
        outer = jnp.einsum("sip,sjq->ijpq", left_blk, right, preferred_element_type=jnp.float32)
        outer = (outer / seq_count).astype(jnp.bfloat16).reshape(rows * col_count, flat)
        update = jnp.dot(outer, final_mapping_matrix, preferred_element_type=jnp.float32)
        update = (update + final_offset_vector).astype(jnp.bfloat16)
        cot_flat = cot_blk.reshape(rows * col_count, pair_width)
        grad_out = jnp.dot(outer.T, cot_flat, preferred_element_type=jnp.float32)
        grad_outer = jnp.dot(cot_flat, final_mapping_matrix.T, preferred_element_type=jnp.float32)
        grad_outer = grad_outer.astype(jnp.bfloat16).reshape(rows, col_count, proj, proj)
        grad_left = jnp.einsum(
            "ijpq,sjq->sip", grad_outer, right, preferred_element_type=jnp.float32
        )
        grad_right = jnp.einsum(
            "ijpq,sip->sjq", grad_outer, left_blk, preferred_element_type=jnp.float32
        )
        return update.reshape(rows, col_count, pair_width), grad_out, grad_left, grad_right

    block = max(1, min(row_count, PAIRS_AT_ONCE // col_count))
    blocks = row_count // block
    if blocks == 1:
        update, grad_out, grad_left, grad_right = block_step(left, upstream_sensitivity)
    else:
        def step(totals, inputs):
            update, grad_out, grad_left, grad_right = block_step(*inputs)
            return (totals[0] + grad_out, totals[1] + grad_right), (update, grad_left)

        (grad_out, grad_right), (update, grad_left) = lax.scan(
            step,
            (
                jnp.zeros((flat, pair_width), jnp.float32),
                jnp.zeros((seq_count, col_count, proj), jnp.float32),
            ),
            (
                left.reshape(seq_count, blocks, block, proj).transpose(1, 0, 2, 3),
                upstream_sensitivity.reshape(blocks, block, col_count, pair_width),
            ),
        )
        grad_left = grad_left.transpose(1, 0, 2, 3).reshape(seq_count, row_count, proj)
    pair_delta = update.reshape(row_count, col_count, pair_width)

    grad_left = (grad_left / seq_count).astype(jnp.bfloat16)
    grad_right = (grad_right / seq_count).astype(jnp.bfloat16)

    def weight_part(normed, grads):
        return jnp.einsum("stc,stp->cp", normed, grads, preferred_element_type=jnp.float32)

    side_part = jnp.concatenate(
        [weight_part(row_normed, grad_left), weight_part(col_normed, grad_right)], axis=1
    )
    share_rows = flat // devices
    side_rows = -(-features * 2 * proj // (pair_width * devices))
    side_flat = side_part.reshape(-1, pair_width)
    side_flat = jnp.pad(side_flat, ((0, side_rows * devices - side_flat.shape[0]), (0, 0)))
    shares = jnp.concatenate(
        [
            grad_out.reshape(devices, share_rows, pair_width),
            side_flat.reshape(devices, side_rows, pair_width),
        ],
        axis=1,
    ).astype(jnp.bfloat16)
    shares = lax.all_to_all(shares, axes, 0, 0)

    def chunks_of(grads, count):
        grads = grads.reshape(seq_count, count // tokens, tokens * proj)
        return grads.transpose(1, 0, 2)

    left_back = lax.all_to_all(chunks_of(grad_left, row_count), "pcol", 0, 0)
    right_back = lax.all_to_all(chunks_of(grad_right, col_count), "prow", 0, 0)
    left_back = jnp.sum(left_back.astype(jnp.float32), axis=0).astype(jnp.bfloat16)
    right_back = jnp.sum(right_back.astype(jnp.float32), axis=0).astype(jnp.bfloat16)
    left_back = lax.ppermute(left_back, axes, to_tokens)

    share = jnp.sum(shares.astype(jnp.float32), axis=0).astype(jnp.bfloat16)
    message = spread(share, axes, devices)
    output_weight_gradient = (
        message[:, :share_rows].reshape(flat, pair_width).astype(jnp.float32)
    )
    side = message[:, share_rows:].reshape(-1, pair_width).astype(jnp.float32)
    side = side[: features * 2 * proj // pair_width].reshape(features, 2 * proj)
    left_weight_gradient, right_weight_gradient = side[:, :proj], side[:, proj:]

    normed, inverse_spread = normalize(picked)
    both = jnp.concatenate(
        [
            left_back.reshape(seq_count, tokens, proj),
            right_back.reshape(seq_count, tokens, proj),
        ],
        axis=-1,
    )
    sides = jnp.concatenate([first_side_matrix, second_side_matrix], axis=1)
    grad_normed = jnp.einsum("stp,cp->stc", both, sides, preferred_element_type=jnp.float32)
    mean_factor = jnp.mean(grad_normed, axis=-1, keepdims=True)
    projected = jnp.mean(grad_normed * normed, axis=-1, keepdims=True)
    alignment_gradient = (
        inverse_spread * (grad_normed - mean_factor - normed * projected)
    ).astype(jnp.bfloat16)
    return (
        pair_delta,
        alignment_gradient,
        left_weight_gradient,
        right_weight_gradient,
        output_weight_gradient,
    )


def dot(x, y, contract=(1, 0), precision=None):
    return lax.dot_general(
        x, y, (((contract[0],), (contract[1],)), ((), ())),
        precision=precision, preferred_element_type=F32,
    )


def lane_ids(shape):
    return lax.broadcasted_iota(jnp.int32, shape, len(shape) - 1)


def fold_lanes(x, width):
    shift = LANES // 2
    while shift >= width:
        x = x + pltpu.roll(x, shift, x.ndim - 1)
        shift //= 2
    return x


def group_mean(x, group, precision):
    lanes = x.shape[1]
    rows_id = lax.broadcasted_iota(jnp.int32, (lanes, lanes), 0) // group
    cols_id = lax.broadcasted_iota(jnp.int32, (lanes, lanes), 1) // group
    block = jnp.where(rows_id == cols_id, 1.0 / group, 0.0).astype(x.dtype)
    return dot(x, block, precision=precision)


def pick_kernel(group, positions_ref, features_ref, cot_ref, normed_ref, inverse_ref, sent_ref):
    heads = features_ref.shape[1]
    seqs, packed = normed_ref.shape
    wanted = positions_ref[...] == lax.broadcasted_iota(jnp.int32, (heads, seqs), 0)
    chosen = dot(wanted.astype(BF16), features_ref[...], contract=(0, 1))
    mean_factor = group_mean(chosen.astype(BF16), group, None)
    centered = chosen - mean_factor
    variance = group_mean(centered * centered, group, lax.Precision.HIGHEST)
    inverse = lax.rsqrt(variance + 1e-05)
    normed = centered * inverse
    normed_ref[...] = normed
    inverse_ref[...] = inverse
    pairs = cot_ref.shape[0]
    low = normed.astype(BF16)
    for k in range(sent_ref.shape[0]):
        sent_ref[k, :pairs] = cot_ref[...]
        for n in range(packed // LANES):
            at = pairs + n * seqs
            sent_ref[k, at : at + seqs] = low[:, n * LANES : (n + 1) * LANES]


def pair_kernel(
    place_ref,
    mine_ref,
    theirs_ref,
    mapping_ref,
    left_ref,
    right_ref,
    offset_ref,
    pair_ref,
    grads_ref,
    message_ref,
    expanded,
    outer,
    pulled,
    left_back,
    right_back,
    turned,
    swapped,
    sums,
    weights,
):
    prow_n, groups = mine_ref.shape[:2]
    block_rows, block_cols, pair_width = pair_ref.shape
    pairs = block_rows * block_cols
    owners, seqs = left_back.shape[:2]
    packed = left_ref.shape[0]
    tokens = left_ref.shape[1] // LANES
    proj = LANES // tokens
    highs = proj // tokens
    span = highs * block_cols
    own_row, own_group, core = place_ref[0], place_ref[1], place_ref[2]

    def token_owner(group, row, parity):
        return (2 * group + parity) * prow_n + row

    def rows_of(ref, g, r, start):
        return jnp.concatenate(
            [
                ref[r, g, start + n * seqs : start + (n + 1) * seqs]
                for n in range(packed // LANES)
            ],
            axis=1,
        )

    places = [(g, r) for g in range(groups) for r in range(prow_n)]
    order = [token_owner(g, r, core) for g, r in places]
    order = order + [token_owner(g, r, 1 - core) for g, r in places]
    rows_mine = [rows_of(mine_ref, g, r, pairs) for g, r in places]
    rows_all = jnp.concatenate(
        rows_mine + [rows_of(theirs_ref, g, r, 0) for g, r in places], axis=0
    )
    wide_left = dot(rows_all, left_ref[...]).astype(BF16)
    for n, owner in enumerate(order):
        expanded[owner] = wide_left[n * seqs : (n + 1) * seqs]

    side_rows = []
    for g in range(groups):
        chunks = rows_mine[g * prow_n : (g + 1) * prow_n]
        side_rows.append(
            jnp.concatenate([dot(x, right_ref[...]).astype(BF16) for x in chunks], axis=1)
        )
    right = jnp.concatenate(side_rows, axis=0)
    wide = right.shape[1]
    source = lax.broadcasted_iota(jnp.int32, (wide, wide), 0)
    target = lax.broadcasted_iota(jnp.int32, (wide, wide), 1)
    jj, qh, ql = target % block_cols, target // block_cols % highs, target // span
    shuffle = (source == jj * proj + qh * tokens + ql).astype(BF16)
    right = dot(right, shuffle)
    for g in range(groups):
        for l in range(tokens):
            swapped[l * seqs : (l + 1) * seqs, g * span : (g + 1) * span] = right[
                g * seqs : (g + 1) * seqs, l * span : (l + 1) * span
            ].astype(BF16)
    turned[...] = swapped[...].astype(F32).T.astype(BF16)

    sums[...] = jnp.zeros_like(sums)
    weights[...] = jnp.zeros_like(weights)
    step_tokens = outer.shape[0] // (groups * block_cols)
    step_owners = step_tokens // tokens
    steps_a_block = block_rows // step_tokens
    share = step_tokens * block_cols

    def step(m, carry):
        row, part = m // steps_a_block, m % steps_a_block
        ahead = jnp.concatenate(
            [expanded[m * step_owners + o] for o in range(step_owners)], axis=1
        )
        low = lane_ids(ahead.shape) % LANES // proj
        block = jnp.concatenate(
            [jnp.where(low == l, ahead, jnp.zeros_like(ahead)) for l in range(tokens)], axis=0
        )
        cot = jnp.concatenate(
            [
                mine_ref[row, g, pl.ds(pl.multiple_of(part * share, share), share)]
                for g in range(groups)
            ],
            axis=0,
        )
        made = dot(turned[...], block) * (1.0 / seqs)
        grad = dot(cot, mapping_ref[...], contract=(1, 1))
        for g in range(groups):
            for t in range(step_tokens):
                here = slice((g * step_tokens + t) * block_cols, (g * step_tokens + t + 1) * block_cols)
                lanes = slice(t * LANES, (t + 1) * LANES)
                for h in range(highs):
                    there = slice((g * highs + h) * block_cols, (g * highs + h + 1) * block_cols)
                    cols = slice(h * LANES, (h + 1) * LANES)
                    outer[here, cols] = made[there, lanes].astype(BF16)
                    pulled[there, lanes] = grad[here, cols].astype(BF16)
        weights[...] += dot(cot, outer[...], contract=(0, 0))
        back = dot(swapped[...], pulled[...])
        back = functools.reduce(
            jnp.add,
            [
                jnp.where(low == l, back[l * seqs : (l + 1) * seqs], 0.0)
                for l in range(tokens)
            ],
        )
        slot = lane_ids((seqs, LANES)) // proj
        for o in range(step_owners):
            total = jnp.zeros((seqs, LANES), F32)
            for t in range(tokens):
                at = (o * tokens + t) * LANES
                total = jnp.where(slot == t, fold_lanes(back[:, at : at + LANES], proj), total)
            left_back[m * step_owners + o] = (total * (1.0 / seqs)).astype(BF16)
        sums[...] += dot(pulled[...], block, contract=(1, 1))

        @pl.when(row == own_row)
        def _():
            mine = outer[pl.ds(pl.multiple_of(own_group * share, share), share)]
            update = dot(mine, mapping_ref[...]) + offset_ref[...]
            pair_ref[pl.ds(part * step_tokens, step_tokens)] = update.astype(BF16).reshape(
                step_tokens, block_cols, pair_width
            )

        return carry

    lax.fori_loop(0, prow_n * steps_a_block, step, 0)

    back = (sums[...].T * (1.0 / seqs)).astype(BF16)
    back = jnp.concatenate(
        [
            jnp.concatenate(
                [
                    back[l * seqs : (l + 1) * seqs, g * span : (g + 1) * span]
                    for l in range(tokens)
                ],
                axis=1,
            )
            for g in range(groups)
        ],
        axis=0,
    )
    back = dot(back, shuffle, contract=(1, 1)).astype(BF16)
    for g, r in places:
        right_back[g * prow_n + r] = back[g * seqs : (g + 1) * seqs, r * LANES : (r + 1) * LANES]

    def side(grads, rows):
        total = dot(grads, rows, contract=(0, 0))
        features = packed // tokens
        return functools.reduce(
            jnp.add,
            [
                total[t * proj : (t + 1) * proj, t * features : (t + 1) * features]
                for t in range(tokens)
            ],
        )

    left_side = side(jnp.concatenate([left_back[owner] for owner in order], axis=0), rows_all)
    right_side = side(
        right_back[...].reshape(-1, LANES), jnp.concatenate(rows_mine, axis=0)
    )
    both = jnp.concatenate([left_side, right_side], axis=0).astype(BF16)
    both = jnp.concatenate([both, jnp.zeros_like(both)], axis=1)

    flat = weights.shape[1]
    outer_f = weights[...].T
    weight_rows = outer_f.reshape(proj, proj, pair_width).swapaxes(0, 1).reshape(flat, pair_width)

    message_ref[:flat] = weight_rows.astype(BF16)
    message_ref[flat : flat + 2 * proj] = both
    message_ref[flat + 2 * proj :] = left_back[token_owner(own_group, own_row, 1 - core)]
    grads_ref[0] = left_back[token_owner(own_group, own_row, core)]
    grads_ref[1] = right_back[own_group * prow_n + own_row]


def close_kernel(
    grads_ref,
    own_ref,
    message_ref,
    normed_ref,
    inverse_ref,
    left_ref,
    right_ref,
    out_ref,
    left_out_ref,
    right_out_ref,
    rows_out_ref,
):
    flat = out_ref.shape[0]
    proj, features = left_out_ref.shape
    out_ref[...] = own_ref[:flat].astype(F32) + message_ref[:flat].astype(F32)
    sides = slice(flat, flat + 2 * proj)
    both = own_ref[sides, :features].astype(F32) + message_ref[sides, :features].astype(F32)
    left_out_ref[...] = both[:proj]
    right_out_ref[...] = both[proj:]
    left_back = grads_ref[0].astype(F32) + message_ref[flat + 2 * proj :].astype(F32)
    grad_normed = dot(left_back.astype(BF16), left_ref[...], contract=(1, 1))
    grad_normed = grad_normed + dot(grads_ref[1], right_ref[...], contract=(1, 1))
    normed = normed_ref[...]
    mean_factor = group_mean(grad_normed, features, lax.Precision.HIGHEST)
    projected = group_mean(grad_normed * normed, features, lax.Precision.HIGHEST)
    result = inverse_ref[...] * (grad_normed - mean_factor - normed * projected)
    rows_out_ref[...] = jnp.stack(
        [result[:, t * features : (t + 1) * features] for t in range(rows_out_ref.shape[1])],
        axis=1,
    ).astype(BF16)


def local_gathered(
    homolog_features,
    subset_homolog_positions,
    first_side_matrix,
    second_side_matrix,
    final_mapping_matrix,
    final_offset_vector,
    upstream_sensitivity,
):
    prow_n, groups = lax.axis_size("prow"), lax.axis_size("px")
    owners = prow_n * groups * 2
    heads, tokens, features = homolog_features.shape
    seqs = subset_homolog_positions.shape[0]
    block_rows, block_cols, pair_width = upstream_sensitivity.shape
    proj = first_side_matrix.shape[1]
    flat = proj * proj
    packed = tokens * features
    step_tokens = 2 * tokens
    shape = jax.ShapeDtypeStruct
    vmem = pl.BlockSpec(memory_space=pltpu.VMEM)
    smem = pl.BlockSpec(memory_space=pltpu.SMEM)
    params = pltpu.CompilerParams(vmem_limit_bytes=48 * 1024 * 1024)

    receivers = prow_n * groups
    pairs = block_rows * block_cols
    length = pairs + seqs * packed // LANES
    normed, inverse, sent = pl.pallas_call(
        functools.partial(pick_kernel, features),
        out_shape=(
            shape((seqs, packed), F32),
            shape((seqs, packed), F32),
            shape((receivers, length, LANES), BF16),
        ),
        in_specs=[vmem] * 3,
        out_specs=(vmem,) * 3,
        compiler_params=params,
        name="pick_rows",
    )(
        subset_homolog_positions.reshape(1, seqs),
        homolog_features.transpose(1, 2, 0).reshape(packed, heads),
        upstream_sensitivity.reshape(pairs, pair_width),
    )
    mine = lax.all_to_all(sent, ("prow", "px"), 0, 0).reshape(prow_n, groups, length, LANES)
    theirs = lax.ppermute(mine[:, :, pairs:], "pc", [(0, 1), (1, 0)])

    one = jnp.eye(tokens, dtype=BF16)
    left_one = jnp.kron(one, first_side_matrix)
    left_wide = jnp.kron(one, jnp.tile(first_side_matrix, (1, tokens)))
    right_one = jnp.kron(one, second_side_matrix)
    mapping = final_mapping_matrix.reshape(proj, proj, pair_width)
    mapping = mapping.swapaxes(0, 1).reshape(flat, pair_width)
    place = jnp.stack([lax.axis_index("prow"), lax.axis_index("px"), lax.axis_index("pc")])

    pair_delta, grads, message = pl.pallas_call(
        pair_kernel,
        out_shape=(
            shape(upstream_sensitivity.shape, BF16),
            shape((2, seqs, LANES), BF16),
            shape((flat + 2 * proj + seqs, LANES), BF16),
        ),
        in_specs=[smem] + [vmem] * 6,
        out_specs=(vmem,) * 3,
        scratch_shapes=[
            pltpu.VMEM((owners, seqs, tokens * LANES), BF16),
            pltpu.VMEM((step_tokens * groups * block_cols, flat), BF16),
            pltpu.VMEM((groups * proj // tokens * block_cols, step_tokens * LANES), BF16),
            pltpu.VMEM((owners, seqs, LANES), BF16),
            pltpu.VMEM((groups * prow_n, seqs, LANES), BF16),
            pltpu.VMEM((groups * proj // tokens * block_cols, tokens * seqs), BF16),
            pltpu.VMEM((tokens * seqs, groups * proj // tokens * block_cols), BF16),
            pltpu.VMEM((groups * proj // tokens * block_cols, tokens * seqs), F32),
            pltpu.VMEM((pair_width, flat), F32),
        ],
        compiler_params=params,
        name="pair_work",
    )(place, mine, theirs, mapping, left_wide, right_one, final_offset_vector.reshape(1, pair_width))

    theirs = lax.ppermute(message, "pc", [(0, 1), (1, 0)])
    output_weight_gradient, left_weight_gradient, right_weight_gradient, alignment = pl.pallas_call(
        close_kernel,
        out_shape=(
            shape((flat, pair_width), F32),
            shape((proj, features), F32),
            shape((proj, features), F32),
            shape((seqs, tokens, features), BF16),
        ),
        in_specs=[vmem] * 7,
        out_specs=(vmem,) * 4,
        compiler_params=params,
        name="close",
    )(grads, message, theirs, normed, inverse, left_one, right_one)
    return (
        pair_delta,
        alignment,
        left_weight_gradient.T,
        right_weight_gradient.T,
        output_weight_gradient,
    )


def shapes_allow_gathering(
    mesh_shape, features, positions, first_side, second_side, mapping, offset, cot
):
    rows_n, cols_n = mesh_shape["prow"], mesh_shape["pcol"]
    parts = mesh_shape["rep"]
    tokens = features.shape[1] // (rows_n * cols_n)
    block_rows, block_cols = cot.shape[0] // (parts * rows_n), cot.shape[1] // cols_n
    proj, width = first_side.shape[1], cot.shape[2]
    return (
        cols_n % 2 == 0
        and cot.shape[1] * cot.shape[1] <= GATHERED_PAIRS
        and tokens * proj == LANES
        and proj % tokens == 0
        and block_rows % (2 * tokens) == 0
        and block_cols == rows_n * tokens == 16
        and width == LANES
        and features.shape[2] >= 2 * proj
        and positions.shape[0] // parts % 16 == 0
        and features.shape[2] * tokens % LANES == 0
    )


def solution(mesh):
    def run(local, over, columns, *args):
        tokens_split = P("rep", columns + ("prow",), None)
        pairs_split = P(("rep", "prow"), columns, None)
        return jax.shard_map(
            local,
            mesh=over,
            in_specs=(tokens_split, P("rep"), P(), P(), P(), P(), pairs_split),
            out_specs=(pairs_split, tokens_split, P("rep", None), P("rep", None), P("rep", None)),
            check_vma=False,
        )(*args)

    def program(*args):
        if not shapes_allow_gathering(mesh.shape, *args):
            return run(local_phased, mesh, ("pcol",), *args)
        reps, rows_n, cols_n = (mesh.shape[name] for name in ("rep", "prow", "pcol"))
        chips = Mesh(
            mesh.devices.reshape(reps, rows_n, cols_n // 2, 2), ("rep", "prow", "px", "pc")
        )
        return run(local_gathered, chips, ("px", "pc"), *args)

    return program
```

```python
import functools

import jax
import jax.numpy as jnp
from jax import lax
from jax.experimental import pallas as pl
from jax.experimental.pallas import tpu as pltpu
from jax.sharding import Mesh
from jax.sharding import PartitionSpec as P

BF16, F32 = jnp.bfloat16, jnp.float32
LANES = 128
GATHERED_PAIRS = 4096

PAIRS_AT_ONCE = 1024


def normalize(values):
    values = values.astype(jnp.float32)
    mean_factor = jnp.mean(values, axis=-1, keepdims=True)
    centered = values - mean_factor
    variance = jnp.mean(centered * centered, axis=-1, keepdims=True)
    inverse_spread = lax.rsqrt(variance + 1e-05)
    return (centered * inverse_spread, inverse_spread)


def transposed(rows_n, cols_n):
    return [
        (r * cols_n + c, c * rows_n + r) for r in range(rows_n) for c in range(cols_n)
    ]


def spread(values, axes, count):
    return lax.all_to_all(jnp.broadcast_to(values[None], (count,) + values.shape), axes, 0, 0)


def local_phased(
    homolog_features,
    subset_homolog_positions,
    first_side_matrix,
    second_side_matrix,
    final_mapping_matrix,
    final_offset_vector,
    upstream_sensitivity,
):
    axes = ("prow", "pcol")
    rows_n, cols_n = lax.axis_size("prow"), lax.axis_size("pcol")
    devices = rows_n * cols_n
    seq_count = subset_homolog_positions.shape[0]
    tokens, features = homolog_features.shape[1:]
    row_count, col_count, pair_width = upstream_sensitivity.shape
    proj = first_side_matrix.shape[1]
    flat = proj * proj
    to_rows = transposed(rows_n, cols_n)
    to_tokens = [(target, source) for source, target in to_rows]

    picked = jnp.take(homolog_features, subset_homolog_positions, axis=0)
    packed = picked.reshape(seq_count, tokens * features)
    row_own = lax.ppermute(packed, axes, to_rows)
    col_all = spread(packed, "prow", rows_n)
    row_all = spread(row_own, "pcol", cols_n)

    def side_of(chunks, count, matrix):
        chunks = chunks.reshape(count // tokens, seq_count, tokens, features)
        chunks = chunks.transpose(1, 0, 2, 3).reshape(seq_count, count, features)
        normed_low = normalize(chunks)[0].astype(jnp.bfloat16)
        side = jnp.einsum("stc,cp->stp", normed_low, matrix, preferred_element_type=jnp.float32)
        return normed_low, side.astype(jnp.bfloat16)

    row_normed, left = side_of(row_all, row_count, first_side_matrix)
    col_normed, right = side_of(col_all, col_count, second_side_matrix)

    def block_step(left_blk, cot_blk):
        rows = left_blk.shape[1]
        outer = jnp.einsum("sip,sjq->ijpq", left_blk, right, preferred_element_type=jnp.float32)
        outer = (outer / seq_count).astype(jnp.bfloat16).reshape(rows * col_count, flat)
        update = jnp.dot(outer, final_mapping_matrix, preferred_element_type=jnp.float32)
        update = (update + final_offset_vector).astype(jnp.bfloat16)
        cot_flat = cot_blk.reshape(rows * col_count, pair_width)
        grad_out = jnp.dot(outer.T, cot_flat, preferred_element_type=jnp.float32)
        grad_outer = jnp.dot(cot_flat, final_mapping_matrix.T, preferred_element_type=jnp.float32)
        grad_outer = grad_outer.astype(jnp.bfloat16).reshape(rows, col_count, proj, proj)
        grad_left = jnp.einsum(
            "ijpq,sjq->sip", grad_outer, right, preferred_element_type=jnp.float32
        )
        grad_right = jnp.einsum(
            "ijpq,sip->sjq", grad_outer, left_blk, preferred_element_type=jnp.float32
        )
        return update.reshape(rows, col_count, pair_width), grad_out, grad_left, grad_right

    block = max(1, min(row_count, PAIRS_AT_ONCE // col_count))
    blocks = row_count // block
    if blocks == 1:
        update, grad_out, grad_left, grad_right = block_step(left, upstream_sensitivity)
    else:
        def step(totals, inputs):
            update, grad_out, grad_left, grad_right = block_step(*inputs)
            return (totals[0] + grad_out, totals[1] + grad_right), (update, grad_left)

        (grad_out, grad_right), (update, grad_left) = lax.scan(
            step,
            (
                jnp.zeros((flat, pair_width), jnp.float32),
                jnp.zeros((seq_count, col_count, proj), jnp.float32),
            ),
            (
                left.reshape(seq_count, blocks, block, proj).transpose(1, 0, 2, 3),
                upstream_sensitivity.reshape(blocks, block, col_count, pair_width),
            ),
        )
        grad_left = grad_left.transpose(1, 0, 2, 3).reshape(seq_count, row_count, proj)
    pair_delta = update.reshape(row_count, col_count, pair_width)

    grad_left = (grad_left / seq_count).astype(jnp.bfloat16)
    grad_right = (grad_right / seq_count).astype(jnp.bfloat16)

    def weight_part(normed, grads):
        return jnp.einsum("stc,stp->cp", normed, grads, preferred_element_type=jnp.float32)

    side_part = jnp.concatenate(
        [weight_part(row_normed, grad_left), weight_part(col_normed, grad_right)], axis=1
    )
    share_rows = flat // devices
    side_rows = -(-features * 2 * proj // (pair_width * devices))
    side_flat = side_part.reshape(-1, pair_width)
    side_flat = jnp.pad(side_flat, ((0, side_rows * devices - side_flat.shape[0]), (0, 0)))
    shares = jnp.concatenate(
        [
            grad_out.reshape(devices, share_rows, pair_width),
            side_flat.reshape(devices, side_rows, pair_width),
        ],
        axis=1,
    ).astype(jnp.bfloat16)
    shares = lax.all_to_all(shares, axes, 0, 0)

    def chunks_of(grads, count):
        grads = grads.reshape(seq_count, count // tokens, tokens * proj)
        return grads.transpose(1, 0, 2)

    left_back = lax.all_to_all(chunks_of(grad_left, row_count), "pcol", 0, 0)
    right_back = lax.all_to_all(chunks_of(grad_right, col_count), "prow", 0, 0)
    left_back = jnp.sum(left_back.astype(jnp.float32), axis=0).astype(jnp.bfloat16)
    right_back = jnp.sum(right_back.astype(jnp.float32), axis=0).astype(jnp.bfloat16)
    left_back = lax.ppermute(left_back, axes, to_tokens)

    share = jnp.sum(shares.astype(jnp.float32), axis=0).astype(jnp.bfloat16)
    message = spread(share, axes, devices)
    output_weight_gradient = (
        message[:, :share_rows].reshape(flat, pair_width).astype(jnp.float32)
    )
    side = message[:, share_rows:].reshape(-1, pair_width).astype(jnp.float32)
    side = side[: features * 2 * proj // pair_width].reshape(features, 2 * proj)
    left_weight_gradient, right_weight_gradient = side[:, :proj], side[:, proj:]

    normed, inverse_spread = normalize(picked)
    both = jnp.concatenate(
        [
            left_back.reshape(seq_count, tokens, proj),
            right_back.reshape(seq_count, tokens, proj),
        ],
        axis=-1,
    )
    sides = jnp.concatenate([first_side_matrix, second_side_matrix], axis=1)
    grad_normed = jnp.einsum("stp,cp->stc", both, sides, preferred_element_type=jnp.float32)
    mean_factor = jnp.mean(grad_normed, axis=-1, keepdims=True)
    projected = jnp.mean(grad_normed * normed, axis=-1, keepdims=True)
    alignment_gradient = (
        inverse_spread * (grad_normed - mean_factor - normed * projected)
    ).astype(jnp.bfloat16)
    return (
        pair_delta,
        alignment_gradient,
        left_weight_gradient,
        right_weight_gradient,
        output_weight_gradient,
    )


def dot(x, y, contract=(1, 0), precision=None):
    return lax.dot_general(
        x, y, (((contract[0],), (contract[1],)), ((), ())),
        precision=precision, preferred_element_type=F32,
    )


def lane_ids(shape):
    return lax.broadcasted_iota(jnp.int32, shape, len(shape) - 1)


def fold_tokens(parts):
    quarter = LANES // 4
    chunk = lane_ids(parts[0].shape) // quarter
    first, even = chunk < 2, chunk % 2 == 0
    halves = [
        jnp.where(first, parts[t], parts[t + 2])
        + pltpu.roll(jnp.where(first, parts[t + 2], parts[t]), 2 * quarter, 1)
        for t in range(2)
    ]
    other = jnp.where(even, halves[1], halves[0])
    moved = jnp.where(even, pltpu.roll(other, 3 * quarter, 1), pltpu.roll(other, quarter, 1))
    return jnp.where(even, halves[0], halves[1]) + moved


def group_mean(x, group, precision):
    lanes = x.shape[1]
    rows_id = lax.broadcasted_iota(jnp.int32, (lanes, lanes), 0) // group
    cols_id = lax.broadcasted_iota(jnp.int32, (lanes, lanes), 1) // group
    block = jnp.where(rows_id == cols_id, 1.0 / group, 0.0).astype(x.dtype)
    return dot(x, block, precision=precision)


def pick_kernel(
    positions_ref,
    features_ref,
    cot_ref,
    left_ref,
    right_ref,
    offset_ref,
    normed_ref,
    inverse_ref,
    left_wide_ref,
    left_one_ref,
    right_one_ref,
    offset_out_ref,
    sent_ref,
    positions,
    features,
    left,
    right,
    low,
    in_sems,
    cot_sems,
    low_sems,
):
    inputs = [
        pltpu.make_async_copy(source, target, in_sems.at[n])
        for n, (source, target) in enumerate(
            [
                (positions_ref, positions),
                (features_ref, features),
                (left_ref, left),
                (right_ref, right),
                (offset_ref, offset_out_ref),
            ]
        )
    ]
    for copy in inputs:
        copy.start()
    receivers = sent_ref.shape[0]
    pairs = cot_ref.shape[0]
    cot_copies = [
        pltpu.make_async_copy(cot_ref, sent_ref.at[k, pl.ds(0, pairs)], cot_sems.at[k])
        for k in range(receivers)
    ]
    for copy in cot_copies:
        copy.start()

    heads = features_ref.shape[1]
    seqs, packed = normed_ref.shape
    proj, channels = left_ref.shape
    tokens = packed // channels
    for copy in inputs:
        copy.wait()
    wanted = positions[...] == lax.broadcasted_iota(jnp.int32, (heads, seqs), 0)
    chosen = dot(wanted.astype(BF16), features[...], contract=(0, 1))
    mean_factor = group_mean(chosen.astype(BF16), channels, None)
    centered = chosen - mean_factor
    variance = group_mean(centered * centered, channels, lax.Precision.HIGHEST)
    inverse = lax.rsqrt(variance + 1e-05)
    normed = centered * inverse
    pieces = packed // LANES
    for n in range(pieces):
        low[n * seqs : (n + 1) * seqs] = normed[:, n * LANES : (n + 1) * LANES].astype(BF16)
    low_copies = [
        pltpu.make_async_copy(low, sent_ref.at[k, pl.ds(pairs, pieces * seqs)], low_sems.at[k])
        for k in range(receivers)
    ]
    for copy in low_copies:
        copy.start()
    normed_ref[...] = normed
    inverse_ref[...] = inverse

    repeat = lane_ids((proj, LANES)) % proj
    repeat = (repeat == lax.broadcasted_iota(jnp.int32, (proj, LANES), 0)).astype(BF16)
    left_row = dot(left[...], repeat, contract=(0, 0))
    right_row = dot(right[...], repeat, contract=(0, 0))
    slot = lane_ids(left_row.shape) // proj
    nothing = jnp.zeros(left_row.shape, BF16)
    for t in range(tokens):
        here = slice(t * channels, (t + 1) * channels)
        left_one_ref[here] = jnp.where(slot == t, left_row, 0.0).astype(BF16)
        right_one_ref[here] = jnp.where(slot == t, right_row, 0.0).astype(BF16)
        for other in range(tokens):
            left_wide_ref[here, other * LANES : (other + 1) * LANES] = (
                left_row.astype(BF16) if other == t else nothing
            )
    for copy in cot_copies + low_copies:
        copy.wait()


def pair_kernel(
    place_ref,
    mine_ref,
    theirs_ref,
    mapping_ref,
    turned_mapping_ref,
    left_ref,
    right_ref,
    offset_ref,
    pair_ref,
    grads_ref,
    message_ref,
    expanded,
    outer,
    pulled,
    left_back,
    right_back,
    turned,
    swapped,
    sums,
    weights,
):
    prow_n, groups = mine_ref.shape[:2]
    block_rows, block_cols, pair_width = pair_ref.shape
    pairs = block_rows * block_cols
    owners, seqs = left_back.shape[:2]
    packed = left_ref.shape[0]
    tokens = left_ref.shape[1] // LANES
    proj = LANES // tokens
    highs = proj // tokens
    span = highs * block_cols
    own_row, own_group, core = place_ref[0], place_ref[1], place_ref[2]

    def token_owner(group, row, parity):
        return (2 * group + parity) * prow_n + row

    def rows_of(ref, g, r, start):
        return jnp.concatenate(
            [
                ref[r, g, start + n * seqs : start + (n + 1) * seqs]
                for n in range(packed // LANES)
            ],
            axis=1,
        )

    places = [(g, r) for g in range(groups) for r in range(prow_n)]
    order = [token_owner(g, r, core) for g, r in places]
    order = order + [token_owner(g, r, 1 - core) for g, r in places]
    rows_mine = [rows_of(mine_ref, g, r, pairs) for g, r in places]
    rows_all = jnp.concatenate(
        rows_mine + [rows_of(theirs_ref, g, r, 0) for g, r in places], axis=0
    )
    wide_left = dot(rows_all, left_ref[...]).astype(BF16)
    for n, owner in enumerate(order):
        expanded[owner] = wide_left[n * seqs : (n + 1) * seqs]

    side_rows = []
    for g in range(groups):
        chunks = rows_mine[g * prow_n : (g + 1) * prow_n]
        side_rows.append(
            jnp.concatenate([dot(x, right_ref[...]).astype(BF16) for x in chunks], axis=1)
        )
    right = jnp.concatenate(side_rows, axis=0)
    wide = right.shape[1]
    source = lax.broadcasted_iota(jnp.int32, (wide, wide), 0)
    target = lax.broadcasted_iota(jnp.int32, (wide, wide), 1)
    jj, qh, ql = target % block_cols, target // block_cols % highs, target // span
    shuffle = (source == jj * proj + qh * tokens + ql).astype(BF16)
    right = dot(right, shuffle)
    for g in range(groups):
        for l in range(tokens):
            swapped[l * seqs : (l + 1) * seqs, g * span : (g + 1) * span] = (
                right[g * seqs : (g + 1) * seqs, l * span : (l + 1) * span] * (1.0 / seqs)
            ).astype(BF16)
    turned[...] = swapped[...].astype(F32).T.astype(BF16)

    sums[...] = jnp.zeros_like(sums)
    weights[...] = jnp.zeros_like(weights)
    step_tokens = outer.shape[0] // (groups * block_cols)
    step_owners = step_tokens // tokens
    steps_a_block = block_rows // step_tokens
    share = step_tokens * block_cols

    def step(m, carry):
        row, part = m // steps_a_block, m % steps_a_block
        ahead = jnp.concatenate(
            [expanded[m * step_owners + o] for o in range(step_owners)], axis=1
        )
        low = lane_ids(ahead.shape) % LANES // proj
        block = jnp.concatenate(
            [jnp.where(low == l, ahead, jnp.zeros_like(ahead)) for l in range(tokens)], axis=0
        )
        cot = jnp.concatenate(
            [
                mine_ref[row, g, pl.ds(pl.multiple_of(part * share, share), share)]
                for g in range(groups)
            ],
            axis=0,
        )
        made = dot(turned[...], block)
        grad = dot(cot, turned_mapping_ref[...])
        for g in range(groups):
            for t in range(step_tokens):
                here = slice((g * step_tokens + t) * block_cols, (g * step_tokens + t + 1) * block_cols)
                lanes = slice(t * LANES, (t + 1) * LANES)
                for h in range(highs):
                    there = slice((g * highs + h) * block_cols, (g * highs + h + 1) * block_cols)
                    cols = slice(h * LANES, (h + 1) * LANES)
                    outer[here, cols] = made[there, lanes].astype(BF16)
                    pulled[there, lanes] = grad[here, cols].astype(BF16)
        weights[...] += dot(cot, outer[...], contract=(0, 0))
        back = dot(swapped[...], pulled[...])
        back = functools.reduce(
            jnp.add,
            [
                jnp.where(low == l, back[l * seqs : (l + 1) * seqs], 0.0)
                for l in range(tokens)
            ],
        )
        for o in range(step_owners):
            parts = [
                back[:, (o * tokens + t) * LANES : (o * tokens + t + 1) * LANES]
                for t in range(tokens)
            ]
            left_back[m * step_owners + o] = fold_tokens(parts).astype(BF16)
        sums[...] += dot(pulled[...], block, contract=(1, 1))

        @pl.when(row == own_row)
        def _():
            mine = outer[pl.ds(pl.multiple_of(own_group * share, share), share)]
            update = dot(mine, mapping_ref[...]) + offset_ref[...]
            pair_ref[pl.ds(part * step_tokens, step_tokens)] = update.astype(BF16).reshape(
                step_tokens, block_cols, pair_width
            )

        return carry

    lax.fori_loop(0, prow_n * steps_a_block, step, 0)

    back = (sums[...].T * (1.0 / seqs)).astype(BF16)
    back = jnp.concatenate(
        [
            jnp.concatenate(
                [
                    back[l * seqs : (l + 1) * seqs, g * span : (g + 1) * span]
                    for l in range(tokens)
                ],
                axis=1,
            )
            for g in range(groups)
        ],
        axis=0,
    )
    back = dot(back, shuffle, contract=(1, 1)).astype(BF16)
    for g, r in places:
        right_back[g * prow_n + r] = back[g * seqs : (g + 1) * seqs, r * LANES : (r + 1) * LANES]

    def side(grads, rows):
        total = dot(grads, rows, contract=(0, 0))
        features = packed // tokens
        return functools.reduce(
            jnp.add,
            [
                total[t * proj : (t + 1) * proj, t * features : (t + 1) * features]
                for t in range(tokens)
            ],
        )

    left_side = side(jnp.concatenate([left_back[owner] for owner in order], axis=0), rows_all)
    right_side = side(
        right_back[...].reshape(-1, LANES), jnp.concatenate(rows_mine, axis=0)
    )
    both = jnp.concatenate([left_side, right_side], axis=0).astype(BF16)
    both = jnp.concatenate([both, jnp.zeros_like(both)], axis=1)

    flat = weights.shape[1]
    outer_f = weights[...].T
    weight_rows = outer_f.reshape(proj, proj, pair_width).swapaxes(0, 1).reshape(flat, pair_width)

    message_ref[:flat] = weight_rows.astype(BF16)
    message_ref[flat : flat + 2 * proj] = both
    message_ref[flat + 2 * proj :] = left_back[token_owner(own_group, own_row, 1 - core)]
    grads_ref[0] = left_back[token_owner(own_group, own_row, core)]
    grads_ref[1] = right_back[own_group * prow_n + own_row]


def close_kernel(
    grads_ref,
    own_ref,
    message_ref,
    normed_ref,
    inverse_ref,
    left_ref,
    right_ref,
    out_ref,
    left_out_ref,
    right_out_ref,
    rows_out_ref,
):
    flat = out_ref.shape[0]
    proj, features = left_out_ref.shape
    out_ref[...] = own_ref[:flat].astype(F32) + message_ref[:flat].astype(F32)
    sides = slice(flat, flat + 2 * proj)
    both = own_ref[sides, :features].astype(F32) + message_ref[sides, :features].astype(F32)
    left_out_ref[...] = both[:proj]
    right_out_ref[...] = both[proj:]
    left_back = grads_ref[0].astype(F32) + message_ref[flat + 2 * proj :].astype(F32)
    grad_normed = dot(left_back.astype(BF16), left_ref[...], contract=(1, 1))
    grad_normed = grad_normed + dot(grads_ref[1], right_ref[...], contract=(1, 1))
    normed = normed_ref[...]
    mean_factor = group_mean(grad_normed, features, lax.Precision.HIGHEST)
    projected = group_mean(grad_normed * normed, features, lax.Precision.HIGHEST)
    result = inverse_ref[...] * (grad_normed - mean_factor - normed * projected)
    rows_out_ref[...] = jnp.stack(
        [result[:, t * features : (t + 1) * features] for t in range(rows_out_ref.shape[1])],
        axis=1,
    ).astype(BF16)


def local_gathered(
    homolog_features,
    subset_homolog_positions,
    first_side_matrix,
    second_side_matrix,
    final_mapping_matrix,
    final_offset_vector,
    upstream_sensitivity,
):
    prow_n, groups = lax.axis_size("prow"), lax.axis_size("px")
    owners = prow_n * groups * 2
    heads, tokens, features = homolog_features.shape
    seqs = subset_homolog_positions.shape[0]
    block_rows, block_cols, pair_width = upstream_sensitivity.shape
    proj = first_side_matrix.shape[1]
    flat = proj * proj
    packed = tokens * features
    step_tokens = block_rows
    shape = jax.ShapeDtypeStruct
    vmem = pl.BlockSpec(memory_space=pltpu.VMEM)
    smem = pl.BlockSpec(memory_space=pltpu.SMEM)
    params = pltpu.CompilerParams(vmem_limit_bytes=48 * 1024 * 1024)

    receivers = prow_n * groups
    pairs = block_rows * block_cols
    length = pairs + seqs * packed // LANES
    hbm = pl.BlockSpec(memory_space=pltpu.HBM)
    normed, inverse, left_wide, left_one, right_one, offset, sent = pl.pallas_call(
        pick_kernel,
        out_shape=(
            shape((seqs, packed), F32),
            shape((seqs, packed), F32),
            shape((packed, tokens * LANES), BF16),
            shape((packed, LANES), BF16),
            shape((packed, LANES), BF16),
            shape((1, pair_width), F32),
            shape((receivers, length, LANES), BF16),
        ),
        in_specs=[hbm] * 6,
        out_specs=(vmem,) * 6 + (hbm,),
        scratch_shapes=[
            pltpu.VMEM((1, seqs), jnp.int32),
            pltpu.VMEM((packed, heads), BF16),
            pltpu.VMEM((proj, features), BF16),
            pltpu.VMEM((proj, features), BF16),
            pltpu.VMEM((seqs * packed // LANES, LANES), BF16),
            pltpu.SemaphoreType.DMA((5,)),
            pltpu.SemaphoreType.DMA((receivers,)),
            pltpu.SemaphoreType.DMA((receivers,)),
        ],
        compiler_params=params,
        name="pick_rows",
    )(
        subset_homolog_positions.reshape(1, seqs),
        homolog_features.transpose(1, 2, 0).reshape(packed, heads),
        upstream_sensitivity.reshape(pairs, pair_width),
        first_side_matrix.T,
        second_side_matrix.T,
        final_offset_vector.reshape(1, pair_width),
    )
    mine = lax.all_to_all(sent, ("prow", "px"), 0, 0).reshape(prow_n, groups, length, LANES)
    theirs = lax.ppermute(mine[:, :, pairs:], "pc", [(0, 1), (1, 0)])

    mapping = final_mapping_matrix.reshape(proj, proj, pair_width)
    mapping = mapping.swapaxes(0, 1).reshape(flat, pair_width)
    place = jnp.stack([lax.axis_index("prow"), lax.axis_index("px"), lax.axis_index("pc")])

    pair_delta, grads, message = pl.pallas_call(
        pair_kernel,
        out_shape=(
            shape(upstream_sensitivity.shape, BF16),
            shape((2, seqs, LANES), BF16),
            shape((flat + 2 * proj + seqs, LANES), BF16),
        ),
        in_specs=[smem] + [vmem] * 7,
        out_specs=(vmem,) * 3,
        scratch_shapes=[
            pltpu.VMEM((owners, seqs, tokens * LANES), BF16),
            pltpu.VMEM((step_tokens * groups * block_cols, flat), BF16),
            pltpu.VMEM((groups * proj // tokens * block_cols, step_tokens * LANES), BF16),
            pltpu.VMEM((owners, seqs, LANES), BF16),
            pltpu.VMEM((groups * prow_n, seqs, LANES), BF16),
            pltpu.VMEM((groups * proj // tokens * block_cols, tokens * seqs), BF16),
            pltpu.VMEM((tokens * seqs, groups * proj // tokens * block_cols), BF16),
            pltpu.VMEM((groups * proj // tokens * block_cols, tokens * seqs), F32),
            pltpu.VMEM((pair_width, flat), F32),
        ],
        compiler_params=params,
        name="pair_work",
    )(place, mine, theirs, mapping, mapping.T, left_wide, right_one, offset)

    theirs = lax.ppermute(message, "pc", [(0, 1), (1, 0)])
    output_weight_gradient, left_weight_gradient, right_weight_gradient, alignment = pl.pallas_call(
        close_kernel,
        out_shape=(
            shape((flat, pair_width), F32),
            shape((proj, features), F32),
            shape((proj, features), F32),
            shape((seqs, tokens, features), BF16),
        ),
        in_specs=[vmem] * 7,
        out_specs=(vmem,) * 4,
        compiler_params=params,
        name="close",
    )(grads, message, theirs, normed, inverse, left_one, right_one)
    return (
        pair_delta,
        alignment,
        left_weight_gradient.T,
        right_weight_gradient.T,
        output_weight_gradient,
    )


def shapes_allow_gathering(
    mesh_shape, features, positions, first_side, second_side, mapping, offset, cot
):
    rows_n, cols_n = mesh_shape["prow"], mesh_shape["pcol"]
    parts = mesh_shape["rep"]
    tokens = features.shape[1] // (rows_n * cols_n)
    block_rows, block_cols = cot.shape[0] // (parts * rows_n), cot.shape[1] // cols_n
    proj, width = first_side.shape[1], cot.shape[2]
    return (
        cols_n % 2 == 0
        and cot.shape[1] * cot.shape[1] <= GATHERED_PAIRS
        and tokens * proj == LANES
        and tokens == 4
        and block_rows % tokens == 0
        and block_cols == rows_n * tokens == 16
        and width == LANES
        and features.shape[2] >= 2 * proj
        and positions.shape[0] // parts % 16 == 0
        and features.shape[2] * tokens % LANES == 0
    )


def solution(mesh):
    def run(local, over, columns, *args):
        tokens_split = P("rep", columns + ("prow",), None)
        pairs_split = P(("rep", "prow"), columns, None)
        return jax.shard_map(
            local,
            mesh=over,
            in_specs=(tokens_split, P("rep"), P(), P(), P(), P(), pairs_split),
            out_specs=(pairs_split, tokens_split, P("rep", None), P("rep", None), P("rep", None)),
            check_vma=False,
        )(*args)

    def program(*args):
        if not shapes_allow_gathering(mesh.shape, *args):
            return run(local_phased, mesh, ("pcol",), *args)
        reps, rows_n, cols_n = (mesh.shape[name] for name in ("rep", "prow", "pcol"))
        chips = Mesh(
            mesh.devices.reshape(reps, rows_n, cols_n // 2, 2), ("rep", "prow", "px", "pc")
        )
        return run(local_gathered, chips, ("px", "pc"), *args)

    return program
```

```python
import functools

import jax
import jax.numpy as jnp
from jax import lax
from jax.experimental import pallas as pl
from jax.experimental.pallas import tpu as pltpu
from jax.sharding import Mesh
from jax.sharding import PartitionSpec as P

BF16, F32 = jnp.bfloat16, jnp.float32
LANES = 128
GATHERED_PAIRS = 4096

PAIRS_AT_ONCE = 1024


def normalize(values):
    values = values.astype(jnp.float32)
    mean_factor = jnp.mean(values, axis=-1, keepdims=True)
    centered = values - mean_factor
    variance = jnp.mean(centered * centered, axis=-1, keepdims=True)
    inverse_spread = lax.rsqrt(variance + 1e-05)
    return (centered * inverse_spread, inverse_spread)


def transposed(rows_n, cols_n):
    return [
        (r * cols_n + c, c * rows_n + r) for r in range(rows_n) for c in range(cols_n)
    ]


def spread(values, axes, count):
    return lax.all_to_all(jnp.broadcast_to(values[None], (count,) + values.shape), axes, 0, 0)


def local_phased(
    homolog_features,
    subset_homolog_positions,
    first_side_matrix,
    second_side_matrix,
    final_mapping_matrix,
    final_offset_vector,
    upstream_sensitivity,
):
    axes = ("prow", "pcol")
    rows_n, cols_n = lax.axis_size("prow"), lax.axis_size("pcol")
    devices = rows_n * cols_n
    seq_count = subset_homolog_positions.shape[0]
    tokens, features = homolog_features.shape[1:]
    row_count, col_count, pair_width = upstream_sensitivity.shape
    proj = first_side_matrix.shape[1]
    flat = proj * proj
    to_rows = transposed(rows_n, cols_n)
    to_tokens = [(target, source) for source, target in to_rows]

    picked = jnp.take(homolog_features, subset_homolog_positions, axis=0)
    packed = picked.reshape(seq_count, tokens * features)
    row_own = lax.ppermute(packed, axes, to_rows)
    col_all = spread(packed, "prow", rows_n)
    row_all = spread(row_own, "pcol", cols_n)

    def side_of(chunks, count, matrix):
        chunks = chunks.reshape(count // tokens, seq_count, tokens, features)
        chunks = chunks.transpose(1, 0, 2, 3).reshape(seq_count, count, features)
        normed_low = normalize(chunks)[0].astype(jnp.bfloat16)
        side = jnp.einsum("stc,cp->stp", normed_low, matrix, preferred_element_type=jnp.float32)
        return normed_low, side.astype(jnp.bfloat16)

    row_normed, left = side_of(row_all, row_count, first_side_matrix)
    col_normed, right = side_of(col_all, col_count, second_side_matrix)

    def block_step(left_blk, cot_blk):
        rows = left_blk.shape[1]
        outer = jnp.einsum("sip,sjq->ijpq", left_blk, right, preferred_element_type=jnp.float32)
        outer = (outer / seq_count).astype(jnp.bfloat16).reshape(rows * col_count, flat)
        update = jnp.dot(outer, final_mapping_matrix, preferred_element_type=jnp.float32)
        update = (update + final_offset_vector).astype(jnp.bfloat16)
        cot_flat = cot_blk.reshape(rows * col_count, pair_width)
        grad_out = jnp.dot(outer.T, cot_flat, preferred_element_type=jnp.float32)
        grad_outer = jnp.dot(cot_flat, final_mapping_matrix.T, preferred_element_type=jnp.float32)
        grad_outer = grad_outer.astype(jnp.bfloat16).reshape(rows, col_count, proj, proj)
        grad_left = jnp.einsum(
            "ijpq,sjq->sip", grad_outer, right, preferred_element_type=jnp.float32
        )
        grad_right = jnp.einsum(
            "ijpq,sip->sjq", grad_outer, left_blk, preferred_element_type=jnp.float32
        )
        return update.reshape(rows, col_count, pair_width), grad_out, grad_left, grad_right

    block = max(1, min(row_count, PAIRS_AT_ONCE // col_count))
    blocks = row_count // block
    if blocks == 1:
        update, grad_out, grad_left, grad_right = block_step(left, upstream_sensitivity)
    else:
        def step(totals, inputs):
            update, grad_out, grad_left, grad_right = block_step(*inputs)
            return (totals[0] + grad_out, totals[1] + grad_right), (update, grad_left)

        (grad_out, grad_right), (update, grad_left) = lax.scan(
            step,
            (
                jnp.zeros((flat, pair_width), jnp.float32),
                jnp.zeros((seq_count, col_count, proj), jnp.float32),
            ),
            (
                left.reshape(seq_count, blocks, block, proj).transpose(1, 0, 2, 3),
                upstream_sensitivity.reshape(blocks, block, col_count, pair_width),
            ),
        )
        grad_left = grad_left.transpose(1, 0, 2, 3).reshape(seq_count, row_count, proj)
    pair_delta = update.reshape(row_count, col_count, pair_width)

    grad_left = (grad_left / seq_count).astype(jnp.bfloat16)
    grad_right = (grad_right / seq_count).astype(jnp.bfloat16)

    def weight_part(normed, grads):
        return jnp.einsum("stc,stp->cp", normed, grads, preferred_element_type=jnp.float32)

    side_part = jnp.concatenate(
        [weight_part(row_normed, grad_left), weight_part(col_normed, grad_right)], axis=1
    )
    share_rows = flat // devices
    side_rows = -(-features * 2 * proj // (pair_width * devices))
    side_flat = side_part.reshape(-1, pair_width)
    side_flat = jnp.pad(side_flat, ((0, side_rows * devices - side_flat.shape[0]), (0, 0)))
    shares = jnp.concatenate(
        [
            grad_out.reshape(devices, share_rows, pair_width),
            side_flat.reshape(devices, side_rows, pair_width),
        ],
        axis=1,
    ).astype(jnp.bfloat16)
    shares = lax.all_to_all(shares, axes, 0, 0)

    def chunks_of(grads, count):
        grads = grads.reshape(seq_count, count // tokens, tokens * proj)
        return grads.transpose(1, 0, 2)

    left_back = lax.all_to_all(chunks_of(grad_left, row_count), "pcol", 0, 0)
    right_back = lax.all_to_all(chunks_of(grad_right, col_count), "prow", 0, 0)
    left_back = jnp.sum(left_back.astype(jnp.float32), axis=0).astype(jnp.bfloat16)
    right_back = jnp.sum(right_back.astype(jnp.float32), axis=0).astype(jnp.bfloat16)
    left_back = lax.ppermute(left_back, axes, to_tokens)

    share = jnp.sum(shares.astype(jnp.float32), axis=0).astype(jnp.bfloat16)
    message = spread(share, axes, devices)
    output_weight_gradient = (
        message[:, :share_rows].reshape(flat, pair_width).astype(jnp.float32)
    )
    side = message[:, share_rows:].reshape(-1, pair_width).astype(jnp.float32)
    side = side[: features * 2 * proj // pair_width].reshape(features, 2 * proj)
    left_weight_gradient, right_weight_gradient = side[:, :proj], side[:, proj:]

    normed, inverse_spread = normalize(picked)
    both = jnp.concatenate(
        [
            left_back.reshape(seq_count, tokens, proj),
            right_back.reshape(seq_count, tokens, proj),
        ],
        axis=-1,
    )
    sides = jnp.concatenate([first_side_matrix, second_side_matrix], axis=1)
    grad_normed = jnp.einsum("stp,cp->stc", both, sides, preferred_element_type=jnp.float32)
    mean_factor = jnp.mean(grad_normed, axis=-1, keepdims=True)
    projected = jnp.mean(grad_normed * normed, axis=-1, keepdims=True)
    alignment_gradient = (
        inverse_spread * (grad_normed - mean_factor - normed * projected)
    ).astype(jnp.bfloat16)
    return (
        pair_delta,
        alignment_gradient,
        left_weight_gradient,
        right_weight_gradient,
        output_weight_gradient,
    )


def dot(x, y, contract=(1, 0), precision=None):
    return lax.dot_general(
        x, y, (((contract[0],), (contract[1],)), ((), ())),
        precision=precision, preferred_element_type=F32,
    )


def lane_ids(shape):
    return lax.broadcasted_iota(jnp.int32, shape, len(shape) - 1)


def fold_tokens(parts):
    quarter = LANES // 4
    chunk = lane_ids(parts[0].shape) // quarter
    first, even = chunk < 2, chunk % 2 == 0
    halves = [
        jnp.where(first, parts[t], parts[t + 2])
        + pltpu.roll(jnp.where(first, parts[t + 2], parts[t]), 2 * quarter, 1)
        for t in range(2)
    ]
    other = jnp.where(even, halves[1], halves[0])
    moved = jnp.where(even, pltpu.roll(other, 3 * quarter, 1), pltpu.roll(other, quarter, 1))
    return jnp.where(even, halves[0], halves[1]) + moved


def group_mean(x, group, precision):
    lanes = x.shape[1]
    rows_id = lax.broadcasted_iota(jnp.int32, (lanes, lanes), 0) // group
    cols_id = lax.broadcasted_iota(jnp.int32, (lanes, lanes), 1) // group
    block = jnp.where(rows_id == cols_id, 1.0 / group, 0.0).astype(x.dtype)
    return dot(x, block, precision=precision)


def pick_kernel(
    positions_ref,
    features_ref,
    left_ref,
    right_ref,
    offset_ref,
    normed_ref,
    inverse_ref,
    left_wide_ref,
    left_one_ref,
    right_one_ref,
    offset_out_ref,
    low_ref,
    positions,
    features,
    left,
    right,
    in_sems,
):
    inputs = [
        pltpu.make_async_copy(source, target, in_sems.at[n])
        for n, (source, target) in enumerate(
            [
                (positions_ref, positions),
                (features_ref, features),
                (left_ref, left),
                (right_ref, right),
                (offset_ref, offset_out_ref),
            ]
        )
    ]
    for copy in inputs:
        copy.start()
    heads = features_ref.shape[1]
    seqs, packed = normed_ref.shape
    proj, channels = left_ref.shape
    tokens = packed // channels
    for copy in inputs:
        copy.wait()
    wanted = positions[...] == lax.broadcasted_iota(jnp.int32, (heads, seqs), 0)
    chosen = dot(wanted.astype(BF16), features[...], contract=(0, 1))
    mean_factor = group_mean(chosen.astype(BF16), channels, None)
    centered = chosen - mean_factor
    variance = group_mean(centered * centered, channels, lax.Precision.HIGHEST)
    inverse = lax.rsqrt(variance + 1e-05)
    normed = centered * inverse
    pieces = packed // LANES
    for n in range(pieces):
        low_ref[0, n * seqs : (n + 1) * seqs] = normed[:, n * LANES : (n + 1) * LANES].astype(
            BF16
        )
    normed_ref[...] = normed
    inverse_ref[...] = inverse

    repeat = lane_ids((proj, LANES)) % proj
    repeat = (repeat == lax.broadcasted_iota(jnp.int32, (proj, LANES), 0)).astype(BF16)
    left_row = dot(left[...], repeat, contract=(0, 0))
    right_row = dot(right[...], repeat, contract=(0, 0))
    slot = lane_ids(left_row.shape) // proj
    nothing = jnp.zeros(left_row.shape, BF16)
    for t in range(tokens):
        here = slice(t * channels, (t + 1) * channels)
        left_one_ref[here] = jnp.where(slot == t, left_row, 0.0).astype(BF16)
        right_one_ref[here] = jnp.where(slot == t, right_row, 0.0).astype(BF16)
        for other in range(tokens):
            left_wide_ref[here, other * LANES : (other + 1) * LANES] = (
                left_row.astype(BF16) if other == t else nothing
            )


def place_blocks(place_ref, offsets, refs, out_ref):
    blocks = [(ref, n) for ref in refs for n in range(ref.shape[0])]
    for (down, across), (ref, n) in zip(offsets, blocks, strict=True):
        out_ref[place_ref[0] ^ down, place_ref[1] ^ across] = ref[n]


def pull_kernel(offsets, place_ref, mapping_ref, *refs):
    *cot_refs, cot_ref, pulled_ref = refs
    prow_n, groups, pairs, pair_width = cot_ref.shape
    highs = mapping_ref.shape[1] // LANES
    block_rows = pulled_ref.shape[2] // LANES
    block_cols = pairs // block_rows
    place_blocks(place_ref, offsets, cot_refs, cot_ref)

    def step(r, carry):
        grad = dot(cot_ref[r].reshape(groups * pairs, pair_width), mapping_ref[...])
        for g in range(groups):
            for t in range(block_rows):
                start = (g * block_rows + t) * block_cols
                lanes = slice(t * LANES, (t + 1) * LANES)
                for h in range(highs):
                    there = slice((g * highs + h) * block_cols, (g * highs + h + 1) * block_cols)
                    pulled_ref[r, there, lanes] = grad[
                        start : start + block_cols, h * LANES : (h + 1) * LANES
                    ].astype(BF16)
        return carry

    lax.fori_loop(0, prow_n, step, 0)


def pair_kernel(offsets, pieces, place_ref, theirs_from_ref, *refs):
    *rest, mine_ref, theirs_ref = refs
    place_blocks(place_ref, offsets, refs[:pieces], mine_ref)
    place_blocks(place_ref, offsets, [theirs_from_ref], theirs_ref)
    pair_work(place_ref, mine_ref, theirs_ref, *rest[pieces:])


def pair_work(
    place_ref,
    mine_ref,
    theirs_ref,
    cot_ref,
    pulled_ref,
    mapping_ref,
    left_ref,
    right_ref,
    offset_ref,
    pair_ref,
    grads_ref,
    message_ref,
    expanded,
    outer,
    left_back,
    right_back,
    turned,
    swapped,
    sums,
    weights,
):
    prow_n, groups = mine_ref.shape[:2]
    block_rows, block_cols, pair_width = pair_ref.shape
    owners, seqs = left_back.shape[:2]
    packed = left_ref.shape[0]
    tokens = left_ref.shape[1] // LANES
    proj = LANES // tokens
    highs = proj // tokens
    span = highs * block_cols
    own_row, own_group, core = place_ref[0], place_ref[1], place_ref[2]

    def token_owner(group, row, parity):
        return (2 * group + parity) * prow_n + row

    def rows_of(ref, g, r):
        return jnp.concatenate(
            [ref[r, g, n * seqs : (n + 1) * seqs] for n in range(packed // LANES)], axis=1
        )

    places = [(g, r) for g in range(groups) for r in range(prow_n)]
    order = [token_owner(g, r, core) for g, r in places]
    order = order + [token_owner(g, r, 1 - core) for g, r in places]
    rows_mine = [rows_of(mine_ref, g, r) for g, r in places]
    rows_all = jnp.concatenate(
        rows_mine + [rows_of(theirs_ref, g, r) for g, r in places], axis=0
    )
    wide_left = dot(rows_all, left_ref[...]).astype(BF16)
    for n, owner in enumerate(order):
        expanded[owner] = wide_left[n * seqs : (n + 1) * seqs]

    side_rows = []
    for g in range(groups):
        chunks = rows_mine[g * prow_n : (g + 1) * prow_n]
        side_rows.append(
            jnp.concatenate([dot(x, right_ref[...]).astype(BF16) for x in chunks], axis=1)
        )
    right = jnp.concatenate(side_rows, axis=0)
    wide = right.shape[1]
    source = lax.broadcasted_iota(jnp.int32, (wide, wide), 0)
    target = lax.broadcasted_iota(jnp.int32, (wide, wide), 1)
    jj, qh, ql = target % block_cols, target // block_cols % highs, target // span
    shuffle = (source == jj * proj + qh * tokens + ql).astype(BF16)
    right = dot(right, shuffle)
    for g in range(groups):
        for l in range(tokens):
            swapped[l * seqs : (l + 1) * seqs, g * span : (g + 1) * span] = (
                right[g * seqs : (g + 1) * seqs, l * span : (l + 1) * span] * (1.0 / seqs)
            ).astype(BF16)
    turned[...] = swapped[...].astype(F32).T.astype(BF16)

    sums[...] = jnp.zeros_like(sums)
    weights[...] = jnp.zeros_like(weights)
    step_tokens = outer.shape[0] // (groups * block_cols)
    step_owners = step_tokens // tokens
    steps_a_block = block_rows // step_tokens
    share = step_tokens * block_cols

    def step(m, carry):
        row, part = m // steps_a_block, m % steps_a_block
        ahead = jnp.concatenate(
            [expanded[m * step_owners + o] for o in range(step_owners)], axis=1
        )
        low = lane_ids(ahead.shape) % LANES // proj
        block = jnp.concatenate(
            [jnp.where(low == l, ahead, jnp.zeros_like(ahead)) for l in range(tokens)], axis=0
        )
        cot = jnp.concatenate(
            [
                cot_ref[row, g, pl.ds(pl.multiple_of(part * share, share), share)]
                for g in range(groups)
            ],
            axis=0,
        )
        made = dot(turned[...], block)
        for g in range(groups):
            for t in range(step_tokens):
                here = slice((g * step_tokens + t) * block_cols, (g * step_tokens + t + 1) * block_cols)
                lanes = slice(t * LANES, (t + 1) * LANES)
                for h in range(highs):
                    there = slice((g * highs + h) * block_cols, (g * highs + h + 1) * block_cols)
                    cols = slice(h * LANES, (h + 1) * LANES)
                    outer[here, cols] = made[there, lanes].astype(BF16)
        weights[...] += dot(cot, outer[...], contract=(0, 0))
        pulled = pulled_ref[row]
        back = dot(swapped[...], pulled)
        back = functools.reduce(
            jnp.add,
            [
                jnp.where(low == l, back[l * seqs : (l + 1) * seqs], 0.0)
                for l in range(tokens)
            ],
        )
        for o in range(step_owners):
            parts = [
                back[:, (o * tokens + t) * LANES : (o * tokens + t + 1) * LANES]
                for t in range(tokens)
            ]
            left_back[m * step_owners + o] = fold_tokens(parts).astype(BF16)
        sums[...] += dot(pulled, block, contract=(1, 1))

        @pl.when(row == own_row)
        def _():
            mine = outer[pl.ds(pl.multiple_of(own_group * share, share), share)]
            update = dot(mine, mapping_ref[...]) + offset_ref[...]
            pair_ref[pl.ds(part * step_tokens, step_tokens)] = update.astype(BF16).reshape(
                step_tokens, block_cols, pair_width
            )

        return carry

    lax.fori_loop(0, prow_n * steps_a_block, step, 0)

    back = (sums[...].T * (1.0 / seqs)).astype(BF16)
    back = jnp.concatenate(
        [
            jnp.concatenate(
                [
                    back[l * seqs : (l + 1) * seqs, g * span : (g + 1) * span]
                    for l in range(tokens)
                ],
                axis=1,
            )
            for g in range(groups)
        ],
        axis=0,
    )
    back = dot(back, shuffle, contract=(1, 1)).astype(BF16)
    for g, r in places:
        right_back[g * prow_n + r] = back[g * seqs : (g + 1) * seqs, r * LANES : (r + 1) * LANES]

    def side(grads, rows):
        total = dot(grads, rows, contract=(0, 0))
        features = packed // tokens
        return functools.reduce(
            jnp.add,
            [
                total[t * proj : (t + 1) * proj, t * features : (t + 1) * features]
                for t in range(tokens)
            ],
        )

    left_side = side(jnp.concatenate([left_back[owner] for owner in order], axis=0), rows_all)
    right_side = side(
        right_back[...].reshape(-1, LANES), jnp.concatenate(rows_mine, axis=0)
    )
    both = jnp.concatenate([left_side, right_side], axis=0).astype(BF16)
    both = jnp.concatenate([both, jnp.zeros_like(both)], axis=1)

    flat = weights.shape[1]
    outer_f = weights[...].T
    weight_rows = outer_f.reshape(proj, proj, pair_width).swapaxes(0, 1).reshape(flat, pair_width)

    message_ref[:flat] = weight_rows.astype(BF16)
    message_ref[flat : flat + 2 * proj] = both
    message_ref[flat + 2 * proj :] = left_back[token_owner(own_group, own_row, 1 - core)]
    grads_ref[0] = left_back[token_owner(own_group, own_row, core)]
    grads_ref[1] = right_back[own_group * prow_n + own_row]


def close_kernel(
    grads_ref,
    own_ref,
    message_ref,
    normed_ref,
    inverse_ref,
    left_ref,
    right_ref,
    out_ref,
    left_out_ref,
    right_out_ref,
    rows_out_ref,
):
    flat = out_ref.shape[0]
    proj, features = left_out_ref.shape
    out_ref[...] = own_ref[:flat].astype(F32) + message_ref[:flat].astype(F32)
    sides = slice(flat, flat + 2 * proj)
    both = own_ref[sides, :features].astype(F32) + message_ref[sides, :features].astype(F32)
    left_out_ref[...] = both[:proj]
    right_out_ref[...] = both[proj:]
    left_back = grads_ref[0].astype(F32) + message_ref[flat + 2 * proj :].astype(F32)
    grad_normed = dot(left_back.astype(BF16), left_ref[...], contract=(1, 1))
    grad_normed = grad_normed + dot(grads_ref[1], right_ref[...], contract=(1, 1))
    normed = normed_ref[...]
    mean_factor = group_mean(grad_normed, features, lax.Precision.HIGHEST)
    projected = group_mean(grad_normed * normed, features, lax.Precision.HIGHEST)
    result = inverse_ref[...] * (grad_normed - mean_factor - normed * projected)
    rows_out_ref[...] = jnp.stack(
        [result[:, t * features : (t + 1) * features] for t in range(rows_out_ref.shape[1])],
        axis=1,
    ).astype(BF16)


def local_gathered(
    homolog_features,
    subset_homolog_positions,
    first_side_matrix,
    second_side_matrix,
    final_mapping_matrix,
    final_offset_vector,
    upstream_sensitivity,
):
    prow_n, groups = lax.axis_size("prow"), lax.axis_size("px")
    owners = prow_n * groups * 2
    heads, tokens, features = homolog_features.shape
    seqs = subset_homolog_positions.shape[0]
    block_rows, block_cols, pair_width = upstream_sensitivity.shape
    proj = first_side_matrix.shape[1]
    flat = proj * proj
    packed = tokens * features
    step_tokens = block_rows
    shape = jax.ShapeDtypeStruct
    vmem = pl.BlockSpec(memory_space=pltpu.VMEM)
    smem = pl.BlockSpec(memory_space=pltpu.SMEM)
    params = pltpu.CompilerParams(vmem_limit_bytes=40 * 1024 * 1024)

    pairs = block_rows * block_cols
    length = seqs * packed // LANES
    hbm = pl.BlockSpec(memory_space=pltpu.HBM)
    normed, inverse, left_wide, left_one, right_one, offset, low = pl.pallas_call(
        pick_kernel,
        out_shape=(
            shape((seqs, packed), F32),
            shape((seqs, packed), F32),
            shape((packed, tokens * LANES), BF16),
            shape((packed, LANES), BF16),
            shape((packed, LANES), BF16),
            shape((1, pair_width), F32),
            shape((1, length, LANES), BF16),
        ),
        in_specs=[hbm] * 5,
        out_specs=(vmem,) * 7,
        scratch_shapes=[
            pltpu.VMEM((1, seqs), jnp.int32),
            pltpu.VMEM((packed, heads), BF16),
            pltpu.VMEM((proj, features), BF16),
            pltpu.VMEM((proj, features), BF16),
            pltpu.SemaphoreType.DMA((5,)),
        ],
        compiler_params=pltpu.CompilerParams(vmem_limit_bytes=60 * 1024 * 1024),
        name="pick_rows",
    )(
        subset_homolog_positions.reshape(1, seqs),
        homolog_features.transpose(1, 2, 0).reshape(packed, heads),
        first_side_matrix.T,
        second_side_matrix.T,
        final_offset_vector.reshape(1, pair_width),
    )

    def gathered(own, order):
        pieces, offsets = [own], [(0, 0)]
        for axis, size in order:
            for bit in range(size.bit_length() - 1):
                swap = [(n, n ^ (1 << bit)) for n in range(size)]
                held = pieces[0] if len(pieces) == 1 else jnp.concatenate(pieces, axis=0)
                pieces.append(lax.ppermute(held, axis, swap))
                step = (1 << bit, 0) if axis == "prow" else (0, 1 << bit)
                offsets += [(down + step[0], across + step[1]) for down, across in offsets]
        return pieces, offsets

    along, across = ("prow", prow_n), ("px", groups)
    cots, cot_offsets = gathered(
        upstream_sensitivity.reshape(1, pairs, pair_width), (along, across)
    )
    rows, row_offsets = gathered(low, (across, along))
    theirs = lax.ppermute(jnp.concatenate(rows, axis=0), "pc", [(0, 1), (1, 0)])

    mapping = final_mapping_matrix.reshape(proj, proj, pair_width)
    mapping = mapping.swapaxes(0, 1).reshape(flat, pair_width)
    place = jnp.stack([lax.axis_index("prow"), lax.axis_index("px"), lax.axis_index("pc")])

    columns = groups * proj // tokens * block_cols
    cot, pulled = pl.pallas_call(
        functools.partial(pull_kernel, cot_offsets),
        out_shape=(
            shape((prow_n, groups, pairs, pair_width), BF16),
            shape((prow_n, columns, block_rows * LANES), BF16),
        ),
        in_specs=[smem] + [vmem] * (1 + len(cots)),
        out_specs=(vmem,) * 2,
        compiler_params=params,
        cost_estimate=pl.CostEstimate(
            flops=2 * prow_n * groups * pairs * pair_width * flat,
            bytes_accessed=2 * prow_n * groups * pairs * (2 * pair_width + flat),
            transcendentals=0,
        ),
        name="pull_back",
    )(place, mapping.T, *cots)

    pair_delta, grads, message = pl.pallas_call(
        functools.partial(pair_kernel, row_offsets, len(rows)),
        out_shape=(
            shape(upstream_sensitivity.shape, BF16),
            shape((2, seqs, LANES), BF16),
            shape((flat + 2 * proj + seqs, LANES), BF16),
        ),
        in_specs=[smem] + [vmem] * (7 + len(rows)),
        out_specs=(vmem,) * 3,
        scratch_shapes=[
            pltpu.VMEM((owners, seqs, tokens * LANES), BF16),
            pltpu.VMEM((step_tokens * groups * block_cols, flat), BF16),
            pltpu.VMEM((owners, seqs, LANES), BF16),
            pltpu.VMEM((groups * prow_n, seqs, LANES), BF16),
            pltpu.VMEM((columns, tokens * seqs), BF16),
            pltpu.VMEM((tokens * seqs, columns), BF16),
            pltpu.VMEM((columns, tokens * seqs), F32),
            pltpu.VMEM((pair_width, flat), F32),
            pltpu.VMEM((prow_n, groups, length, LANES), BF16),
            pltpu.VMEM((prow_n, groups, length, LANES), BF16),
        ],
        compiler_params=params,
        name="pair_work",
    )(place, theirs, *rows, cot, pulled, mapping, left_wide, right_one, offset)

    theirs = lax.ppermute(message, "pc", [(0, 1), (1, 0)])
    output_weight_gradient, left_weight_gradient, right_weight_gradient, alignment = pl.pallas_call(
        close_kernel,
        out_shape=(
            shape((flat, pair_width), F32),
            shape((proj, features), F32),
            shape((proj, features), F32),
            shape((seqs, tokens, features), BF16),
        ),
        in_specs=[vmem] * 7,
        out_specs=(vmem,) * 4,
        compiler_params=params,
        name="close",
    )(grads, message, theirs, normed, inverse, left_one, right_one)
    return (
        pair_delta,
        alignment,
        left_weight_gradient.T,
        right_weight_gradient.T,
        output_weight_gradient,
    )


def shapes_allow_gathering(
    mesh_shape, features, positions, first_side, second_side, mapping, offset, cot
):
    rows_n, cols_n = mesh_shape["prow"], mesh_shape["pcol"]
    parts = mesh_shape["rep"]
    tokens = features.shape[1] // (rows_n * cols_n)
    block_rows, block_cols = cot.shape[0] // (parts * rows_n), cot.shape[1] // cols_n
    proj, width = first_side.shape[1], cot.shape[2]
    return (
        cols_n % 2 == 0
        and cot.shape[1] * cot.shape[1] <= GATHERED_PAIRS
        and tokens * proj == LANES
        and tokens == 4
        and block_rows % tokens == 0
        and block_cols == rows_n * tokens == 16
        and rows_n & (rows_n - 1) == 0
        and cols_n & (cols_n - 1) == 0
        and width == LANES
        and features.shape[2] >= 2 * proj
        and positions.shape[0] // parts % 16 == 0
        and features.shape[2] * tokens % LANES == 0
    )


def solution(mesh):
    def run(local, over, columns, *args):
        tokens_split = P("rep", columns + ("prow",), None)
        pairs_split = P(("rep", "prow"), columns, None)
        return jax.shard_map(
            local,
            mesh=over,
            in_specs=(tokens_split, P("rep"), P(), P(), P(), P(), pairs_split),
            out_specs=(pairs_split, tokens_split, P("rep", None), P("rep", None), P("rep", None)),
            check_vma=False,
        )(*args)

    def program(*args):
        if not shapes_allow_gathering(mesh.shape, *args):
            return run(local_phased, mesh, ("pcol",), *args)
        reps, rows_n, cols_n = (mesh.shape[name] for name in ("rep", "prow", "pcol"))
        chips = Mesh(
            mesh.devices.reshape(reps, rows_n, cols_n // 2, 2), ("rep", "prow", "px", "pc")
        )
        return run(local_gathered, chips, ("px", "pc"), *args)

    return program
```

```python
import functools

import jax
import jax.numpy as jnp
from jax import lax
from jax.experimental import pallas as pl
from jax.experimental.pallas import tpu as pltpu
from jax.sharding import Mesh
from jax.sharding import PartitionSpec as P

BF16, F32 = jnp.bfloat16, jnp.float32
LANES = 128
GATHERED_PAIRS = 4096

PAIRS_AT_ONCE = 1024


def normalize(values):
    values = values.astype(jnp.float32)
    mean_factor = jnp.mean(values, axis=-1, keepdims=True)
    centered = values - mean_factor
    variance = jnp.mean(centered * centered, axis=-1, keepdims=True)
    inverse_spread = lax.rsqrt(variance + 1e-05)
    return (centered * inverse_spread, inverse_spread)


def transposed(rows_n, cols_n):
    return [
        (r * cols_n + c, c * rows_n + r) for r in range(rows_n) for c in range(cols_n)
    ]


def spread(values, axes, count):
    return lax.all_to_all(jnp.broadcast_to(values[None], (count,) + values.shape), axes, 0, 0)


def local_phased(
    homolog_features,
    subset_homolog_positions,
    first_side_matrix,
    second_side_matrix,
    final_mapping_matrix,
    final_offset_vector,
    upstream_sensitivity,
):
    axes = ("prow", "pcol")
    rows_n, cols_n = lax.axis_size("prow"), lax.axis_size("pcol")
    devices = rows_n * cols_n
    seq_count = subset_homolog_positions.shape[0]
    tokens, features = homolog_features.shape[1:]
    row_count, col_count, pair_width = upstream_sensitivity.shape
    proj = first_side_matrix.shape[1]
    flat = proj * proj
    to_rows = transposed(rows_n, cols_n)
    to_tokens = [(target, source) for source, target in to_rows]

    picked = jnp.take(homolog_features, subset_homolog_positions, axis=0)
    packed = picked.reshape(seq_count, tokens * features)
    row_own = lax.ppermute(packed, axes, to_rows)
    col_all = spread(packed, "prow", rows_n)
    row_all = spread(row_own, "pcol", cols_n)

    def side_of(chunks, count, matrix):
        chunks = chunks.reshape(count // tokens, seq_count, tokens, features)
        chunks = chunks.transpose(1, 0, 2, 3).reshape(seq_count, count, features)
        normed_low = normalize(chunks)[0].astype(jnp.bfloat16)
        side = jnp.einsum("stc,cp->stp", normed_low, matrix, preferred_element_type=jnp.float32)
        return normed_low, side.astype(jnp.bfloat16)

    row_normed, left = side_of(row_all, row_count, first_side_matrix)
    col_normed, right = side_of(col_all, col_count, second_side_matrix)

    def block_step(left_blk, cot_blk):
        rows = left_blk.shape[1]
        outer = jnp.einsum("sip,sjq->ijpq", left_blk, right, preferred_element_type=jnp.float32)
        outer = (outer / seq_count).astype(jnp.bfloat16).reshape(rows * col_count, flat)
        update = jnp.dot(outer, final_mapping_matrix, preferred_element_type=jnp.float32)
        update = (update + final_offset_vector).astype(jnp.bfloat16)
        cot_flat = cot_blk.reshape(rows * col_count, pair_width)
        grad_out = jnp.dot(outer.T, cot_flat, preferred_element_type=jnp.float32)
        grad_outer = jnp.dot(cot_flat, final_mapping_matrix.T, preferred_element_type=jnp.float32)
        grad_outer = grad_outer.astype(jnp.bfloat16).reshape(rows, col_count, proj, proj)
        grad_left = jnp.einsum(
            "ijpq,sjq->sip", grad_outer, right, preferred_element_type=jnp.float32
        )
        grad_right = jnp.einsum(
            "ijpq,sip->sjq", grad_outer, left_blk, preferred_element_type=jnp.float32
        )
        return update.reshape(rows, col_count, pair_width), grad_out, grad_left, grad_right

    block = max(1, min(row_count, PAIRS_AT_ONCE // col_count))
    blocks = row_count // block
    if blocks == 1:
        update, grad_out, grad_left, grad_right = block_step(left, upstream_sensitivity)
    else:
        def step(totals, inputs):
            update, grad_out, grad_left, grad_right = block_step(*inputs)
            return (totals[0] + grad_out, totals[1] + grad_right), (update, grad_left)

        (grad_out, grad_right), (update, grad_left) = lax.scan(
            step,
            (
                jnp.zeros((flat, pair_width), jnp.float32),
                jnp.zeros((seq_count, col_count, proj), jnp.float32),
            ),
            (
                left.reshape(seq_count, blocks, block, proj).transpose(1, 0, 2, 3),
                upstream_sensitivity.reshape(blocks, block, col_count, pair_width),
            ),
        )
        grad_left = grad_left.transpose(1, 0, 2, 3).reshape(seq_count, row_count, proj)
    pair_delta = update.reshape(row_count, col_count, pair_width)

    grad_left = (grad_left / seq_count).astype(jnp.bfloat16)
    grad_right = (grad_right / seq_count).astype(jnp.bfloat16)

    def weight_part(normed, grads):
        return jnp.einsum("stc,stp->cp", normed, grads, preferred_element_type=jnp.float32)

    side_part = jnp.concatenate(
        [weight_part(row_normed, grad_left), weight_part(col_normed, grad_right)], axis=1
    )
    share_rows = flat // devices
    side_rows = -(-features * 2 * proj // (pair_width * devices))
    side_flat = side_part.reshape(-1, pair_width)
    side_flat = jnp.pad(side_flat, ((0, side_rows * devices - side_flat.shape[0]), (0, 0)))
    shares = jnp.concatenate(
        [
            grad_out.reshape(devices, share_rows, pair_width),
            side_flat.reshape(devices, side_rows, pair_width),
        ],
        axis=1,
    ).astype(jnp.bfloat16)
    shares = lax.all_to_all(shares, axes, 0, 0)

    def chunks_of(grads, count):
        grads = grads.reshape(seq_count, count // tokens, tokens * proj)
        return grads.transpose(1, 0, 2)

    left_back = lax.all_to_all(chunks_of(grad_left, row_count), "pcol", 0, 0)
    right_back = lax.all_to_all(chunks_of(grad_right, col_count), "prow", 0, 0)
    left_back = jnp.sum(left_back.astype(jnp.float32), axis=0).astype(jnp.bfloat16)
    right_back = jnp.sum(right_back.astype(jnp.float32), axis=0).astype(jnp.bfloat16)
    left_back = lax.ppermute(left_back, axes, to_tokens)

    share = jnp.sum(shares.astype(jnp.float32), axis=0).astype(jnp.bfloat16)
    message = spread(share, axes, devices)
    output_weight_gradient = (
        message[:, :share_rows].reshape(flat, pair_width).astype(jnp.float32)
    )
    side = message[:, share_rows:].reshape(-1, pair_width).astype(jnp.float32)
    side = side[: features * 2 * proj // pair_width].reshape(features, 2 * proj)
    left_weight_gradient, right_weight_gradient = side[:, :proj], side[:, proj:]

    normed, inverse_spread = normalize(picked)
    both = jnp.concatenate(
        [
            left_back.reshape(seq_count, tokens, proj),
            right_back.reshape(seq_count, tokens, proj),
        ],
        axis=-1,
    )
    sides = jnp.concatenate([first_side_matrix, second_side_matrix], axis=1)
    grad_normed = jnp.einsum("stp,cp->stc", both, sides, preferred_element_type=jnp.float32)
    mean_factor = jnp.mean(grad_normed, axis=-1, keepdims=True)
    projected = jnp.mean(grad_normed * normed, axis=-1, keepdims=True)
    alignment_gradient = (
        inverse_spread * (grad_normed - mean_factor - normed * projected)
    ).astype(jnp.bfloat16)
    return (
        pair_delta,
        alignment_gradient,
        left_weight_gradient,
        right_weight_gradient,
        output_weight_gradient,
    )


def dot(x, y, contract=(1, 0), precision=None):
    return lax.dot_general(
        x, y, (((contract[0],), (contract[1],)), ((), ())),
        precision=precision, preferred_element_type=F32,
    )


def lane_ids(shape):
    return lax.broadcasted_iota(jnp.int32, shape, len(shape) - 1)


def fold_tokens(parts):
    quarter = LANES // 4
    chunk = lane_ids(parts[0].shape) // quarter
    first, even = chunk < 2, chunk % 2 == 0
    halves = [
        jnp.where(first, parts[t], parts[t + 2])
        + pltpu.roll(jnp.where(first, parts[t + 2], parts[t]), 2 * quarter, 1)
        for t in range(2)
    ]
    other = jnp.where(even, halves[1], halves[0])
    moved = jnp.where(even, pltpu.roll(other, 3 * quarter, 1), pltpu.roll(other, quarter, 1))
    return jnp.where(even, halves[0], halves[1]) + moved


def group_mean(x, group, precision):
    lanes = x.shape[1]
    rows_id = lax.broadcasted_iota(jnp.int32, (lanes, lanes), 0) // group
    cols_id = lax.broadcasted_iota(jnp.int32, (lanes, lanes), 1) // group
    block = jnp.where(rows_id == cols_id, 1.0 / group, 0.0).astype(x.dtype)
    return dot(x, block, precision=precision)


def pick_kernel(
    positions_ref,
    features_ref,
    left_ref,
    right_ref,
    offset_ref,
    cot_ref,
    normed_ref,
    inverse_ref,
    left_wide_ref,
    left_one_ref,
    right_one_ref,
    offset_out_ref,
    message_ref,
    positions,
    features,
    left,
    right,
    in_sems,
):
    pairs = cot_ref.shape[0]
    inputs = [
        pltpu.make_async_copy(source, target, in_sems.at[n])
        for n, (source, target) in enumerate(
            [
                (positions_ref, positions),
                (features_ref, features),
                (left_ref, left),
                (right_ref, right),
                (offset_ref, offset_out_ref),
                (cot_ref, message_ref.at[pl.ds(0, pairs)]),
            ]
        )
    ]
    for copy in inputs:
        copy.start()
    heads = features_ref.shape[1]
    seqs, packed = normed_ref.shape
    proj, channels = left_ref.shape
    tokens = packed // channels
    for copy in inputs:
        copy.wait()
    wanted = positions[...] == lax.broadcasted_iota(jnp.int32, (heads, seqs), 0)
    chosen = dot(wanted.astype(BF16), features[...], contract=(0, 1))
    mean_factor = group_mean(chosen.astype(BF16), channels, None)
    centered = chosen - mean_factor
    variance = group_mean(centered * centered, channels, lax.Precision.HIGHEST)
    inverse = lax.rsqrt(variance + 1e-05)
    normed = centered * inverse
    pieces = packed // LANES
    for n in range(pieces):
        message_ref[pairs + n * seqs : pairs + (n + 1) * seqs] = normed[
            :, n * LANES : (n + 1) * LANES
        ].astype(BF16)
    normed_ref[...] = normed
    inverse_ref[...] = inverse

    repeat = lane_ids((proj, LANES)) % proj
    repeat = (repeat == lax.broadcasted_iota(jnp.int32, (proj, LANES), 0)).astype(BF16)
    left_row = dot(left[...], repeat, contract=(0, 0))
    right_row = dot(right[...], repeat, contract=(0, 0))
    slot = lane_ids(left_row.shape) // proj
    nothing = jnp.zeros(left_row.shape, BF16)
    for t in range(tokens):
        here = slice(t * channels, (t + 1) * channels)
        left_one_ref[here] = jnp.where(slot == t, left_row, 0.0).astype(BF16)
        right_one_ref[here] = jnp.where(slot == t, right_row, 0.0).astype(BF16)
        for other in range(tokens):
            left_wide_ref[here, other * LANES : (other + 1) * LANES] = (
                left_row.astype(BF16) if other == t else nothing
            )


def place_blocks(place_ref, offsets, refs, out_ref):
    blocks = [(ref, n) for ref in refs for n in range(ref.shape[0])]
    for (down, across), (ref, n) in zip(offsets, blocks, strict=True):
        out_ref[place_ref[0] ^ down, place_ref[1] ^ across] = ref[n]


def pull_kernel(offsets, place_ref, mapping_ref, *refs):
    *cot_refs, cot_ref, pulled_ref = refs
    prow_n, groups, pairs, pair_width = cot_ref.shape
    highs = mapping_ref.shape[1] // LANES
    block_rows = pulled_ref.shape[2] // LANES
    block_cols = pairs // block_rows
    place_blocks(place_ref, offsets, cot_refs, cot_ref)

    def step(r, carry):
        grad = dot(cot_ref[r].reshape(groups * pairs, pair_width), mapping_ref[...])
        for g in range(groups):
            for t in range(block_rows):
                start = (g * block_rows + t) * block_cols
                lanes = slice(t * LANES, (t + 1) * LANES)
                for h in range(highs):
                    there = slice((g * highs + h) * block_cols, (g * highs + h + 1) * block_cols)
                    pulled_ref[r, there, lanes] = grad[
                        start : start + block_cols, h * LANES : (h + 1) * LANES
                    ].astype(BF16)
        return carry

    lax.fori_loop(0, prow_n, step, 0)


def outer_kernel(
    offsets,
    place_ref,
    mine_from_ref,
    theirs_from_ref,
    mapping_ref,
    left_ref,
    right_ref,
    offset_ref,
    rows_ref,
    expanded,
    swapped,
    outer_ref,
    pair_ref,
    mine_ref,
    theirs_ref,
    turned,
):
    place_blocks(place_ref, offsets, [mine_from_ref], mine_ref)
    place_blocks(place_ref, offsets, [theirs_from_ref], theirs_ref)
    prow_n, groups = mine_ref.shape[:2]
    block_rows, block_cols, pair_width = pair_ref.shape
    owners, seqs = expanded.shape[:2]
    packed = left_ref.shape[0]
    tokens = left_ref.shape[1] // LANES
    proj = LANES // tokens
    highs = proj // tokens
    span = highs * block_cols
    own_row, own_group, core = place_ref[0], place_ref[1], place_ref[2]

    def rows_of(ref, g, r):
        return jnp.concatenate(
            [ref[r, g, n * seqs : (n + 1) * seqs] for n in range(packed // LANES)], axis=1
        )

    places = [(g, r) for g in range(groups) for r in range(prow_n)]
    rows_mine = [rows_of(mine_ref, g, r) for g, r in places]
    rows_all = jnp.concatenate(
        rows_mine + [rows_of(theirs_ref, g, r) for g, r in places], axis=0
    )
    rows_ref[...] = rows_all
    wide_left = dot(rows_all, left_ref[...]).astype(BF16)
    for n, owner in enumerate(owner_order(places, prow_n, core)):
        expanded[owner] = wide_left[n * seqs : (n + 1) * seqs]

    side_rows = []
    for g in range(groups):
        chunks = rows_mine[g * prow_n : (g + 1) * prow_n]
        side_rows.append(
            jnp.concatenate([dot(x, right_ref[...]).astype(BF16) for x in chunks], axis=1)
        )
    right = dot(jnp.concatenate(side_rows, axis=0), shuffle_matrix(block_cols, proj, tokens))
    for g in range(groups):
        for l in range(tokens):
            swapped[l * seqs : (l + 1) * seqs, g * span : (g + 1) * span] = (
                right[g * seqs : (g + 1) * seqs, l * span : (l + 1) * span] * (1.0 / seqs)
            ).astype(BF16)
    turned[...] = swapped[...].astype(F32).T.astype(BF16)

    def step(row, carry):
        made = dot(turned[...], left_block(expanded, row, owners // prow_n, tokens))
        for g in range(groups):
            for t in range(block_rows):
                start = (g * block_rows + t) * block_cols
                lanes = slice(t * LANES, (t + 1) * LANES)
                for h in range(highs):
                    there = slice((g * highs + h) * block_cols, (g * highs + h + 1) * block_cols)
                    outer_ref[row, start : start + block_cols, h * LANES : (h + 1) * LANES] = made[
                        there, lanes
                    ].astype(BF16)
        return carry

    lax.fori_loop(0, prow_n, step, 0)
    share = block_rows * block_cols
    mine = outer_ref[own_row, pl.ds(pl.multiple_of(own_group * share, share), share)]
    update = dot(mine, mapping_ref[...]) + offset_ref[...]
    pair_ref[...] = update.astype(BF16).reshape(pair_ref.shape)


def owner_order(places, prow_n, core):
    mine = [(2 * g + core) * prow_n + r for g, r in places]
    return mine + [(2 * g + 1 - core) * prow_n + r for g, r in places]


def shuffle_matrix(block_cols, proj, tokens):
    wide, highs = block_cols * proj, proj // tokens
    source = lax.broadcasted_iota(jnp.int32, (wide, wide), 0)
    target = lax.broadcasted_iota(jnp.int32, (wide, wide), 1)
    jj, qh = target % block_cols, target // block_cols % highs
    ql = target // (highs * block_cols)
    return (source == jj * proj + qh * tokens + ql).astype(BF16)


def left_block(expanded, row, step_owners, tokens):
    ahead = jnp.concatenate([expanded[row * step_owners + o] for o in range(step_owners)], axis=1)
    low = lane_ids(ahead.shape) % LANES // (LANES // tokens)
    return jnp.concatenate(
        [jnp.where(low == l, ahead, jnp.zeros_like(ahead)) for l in range(tokens)], axis=0
    )


def back_kernel(
    place_ref,
    rows_ref,
    expanded,
    swapped,
    outer_ref,
    cot_ref,
    pulled_ref,
    grads_ref,
    message_ref,
    left_back,
    right_back,
    sums,
    weights,
):
    prow_n, groups, pairs, pair_width = cot_ref.shape
    owners, seqs = left_back.shape[:2]
    tokens = swapped.shape[0] // seqs
    proj = LANES // tokens
    highs = proj // tokens
    span = swapped.shape[1] // groups
    block_cols = span // highs
    step_owners = owners // prow_n
    own_row, own_group, core = place_ref[0], place_ref[1], place_ref[2]
    places = [(g, r) for g in range(groups) for r in range(prow_n)]
    order = owner_order(places, prow_n, core)

    sums[...] = jnp.zeros_like(sums)
    weights[...] = jnp.zeros_like(weights)

    def step(row, carry):
        block = left_block(expanded, row, step_owners, tokens)
        cot = cot_ref[row].reshape(groups * pairs, pair_width)
        weights[...] += dot(cot, outer_ref[row], contract=(0, 0))
        pulled = pulled_ref[row]
        back = dot(swapped[...], pulled)
        low = lane_ids((seqs, back.shape[1])) % LANES // proj
        back = functools.reduce(
            jnp.add,
            [
                jnp.where(low == l, back[l * seqs : (l + 1) * seqs], 0.0)
                for l in range(tokens)
            ],
        )
        for o in range(step_owners):
            parts = [
                back[:, (o * tokens + t) * LANES : (o * tokens + t + 1) * LANES]
                for t in range(tokens)
            ]
            left_back[row * step_owners + o] = fold_tokens(parts).astype(BF16)
        sums[...] += dot(pulled, block, contract=(1, 1))
        return carry

    lax.fori_loop(0, prow_n, step, 0)

    back = (sums[...].T * (1.0 / seqs)).astype(BF16)
    back = jnp.concatenate(
        [
            jnp.concatenate(
                [
                    back[l * seqs : (l + 1) * seqs, g * span : (g + 1) * span]
                    for l in range(tokens)
                ],
                axis=1,
            )
            for g in range(groups)
        ],
        axis=0,
    )
    shuffle = shuffle_matrix(block_cols, proj, tokens)
    back = dot(back, shuffle, contract=(1, 1)).astype(BF16)
    for g, r in places:
        right_back[g * prow_n + r] = back[g * seqs : (g + 1) * seqs, r * LANES : (r + 1) * LANES]

    def side(grads, rows):
        total = dot(grads, rows, contract=(0, 0))
        features = rows.shape[1] // tokens
        return functools.reduce(
            jnp.add,
            [
                total[t * proj : (t + 1) * proj, t * features : (t + 1) * features]
                for t in range(tokens)
            ],
        )

    left_side = side(
        jnp.concatenate([left_back[owner] for owner in order], axis=0), rows_ref[...]
    )
    columns = groups * prow_n * seqs
    right_side = side(right_back[...].reshape(columns, LANES), rows_ref[:columns])
    both = jnp.concatenate([left_side, right_side], axis=0).astype(BF16)
    both = jnp.concatenate([both, jnp.zeros_like(both)], axis=1)

    flat = weights.shape[1]
    outer_f = weights[...].T
    weight_rows = outer_f.reshape(proj, proj, pair_width).swapaxes(0, 1).reshape(flat, pair_width)

    message_ref[:flat] = weight_rows.astype(BF16)
    message_ref[flat : flat + 2 * proj] = both
    message_ref[flat + 2 * proj :] = left_back[(2 * own_group + 1 - core) * prow_n + own_row]
    grads_ref[0] = left_back[(2 * own_group + core) * prow_n + own_row]
    grads_ref[1] = right_back[own_group * prow_n + own_row]


def close_kernel(
    grads_ref,
    own_ref,
    message_ref,
    normed_ref,
    inverse_ref,
    left_ref,
    right_ref,
    out_ref,
    left_out_ref,
    right_out_ref,
    rows_out_ref,
):
    flat = out_ref.shape[0]
    proj, features = left_out_ref.shape
    out_ref[...] = own_ref[:flat].astype(F32) + message_ref[:flat].astype(F32)
    sides = slice(flat, flat + 2 * proj)
    both = own_ref[sides, :features].astype(F32) + message_ref[sides, :features].astype(F32)
    left_out_ref[...] = both[:proj]
    right_out_ref[...] = both[proj:]
    left_back = grads_ref[0].astype(F32) + message_ref[flat + 2 * proj :].astype(F32)
    grad_normed = dot(left_back.astype(BF16), left_ref[...], contract=(1, 1))
    grad_normed = grad_normed + dot(grads_ref[1], right_ref[...], contract=(1, 1))
    normed = normed_ref[...]
    mean_factor = group_mean(grad_normed, features, lax.Precision.HIGHEST)
    projected = group_mean(grad_normed * normed, features, lax.Precision.HIGHEST)
    result = inverse_ref[...] * (grad_normed - mean_factor - normed * projected)
    rows_out_ref[...] = jnp.stack(
        [result[:, t * features : (t + 1) * features] for t in range(rows_out_ref.shape[1])],
        axis=1,
    ).astype(BF16)


def local_gathered(
    homolog_features,
    subset_homolog_positions,
    first_side_matrix,
    second_side_matrix,
    final_mapping_matrix,
    final_offset_vector,
    upstream_sensitivity,
):
    prow_n, groups = lax.axis_size("prow"), lax.axis_size("px")
    owners = prow_n * groups * 2
    heads, tokens, features = homolog_features.shape
    seqs = subset_homolog_positions.shape[0]
    block_rows, block_cols, pair_width = upstream_sensitivity.shape
    proj = first_side_matrix.shape[1]
    flat = proj * proj
    packed = tokens * features
    shape = jax.ShapeDtypeStruct
    vmem = pl.BlockSpec(memory_space=pltpu.VMEM)
    smem = pl.BlockSpec(memory_space=pltpu.SMEM)
    params = pltpu.CompilerParams(vmem_limit_bytes=36 * 1024 * 1024)

    pairs = block_rows * block_cols
    length = seqs * packed // LANES
    hbm = pl.BlockSpec(memory_space=pltpu.HBM)
    normed, inverse, left_wide, left_one, right_one, offset, sent = pl.pallas_call(
        pick_kernel,
        out_shape=(
            shape((seqs, packed), F32),
            shape((seqs, packed), F32),
            shape((packed, tokens * LANES), BF16),
            shape((packed, LANES), BF16),
            shape((packed, LANES), BF16),
            shape((1, pair_width), F32),
            shape((pairs + length, LANES), BF16),
        ),
        in_specs=[hbm] * 6,
        out_specs=(vmem,) * 7,
        scratch_shapes=[
            pltpu.VMEM((1, seqs), jnp.int32),
            pltpu.VMEM((packed, heads), BF16),
            pltpu.VMEM((proj, features), BF16),
            pltpu.VMEM((proj, features), BF16),
            pltpu.SemaphoreType.DMA((6,)),
        ],
        compiler_params=pltpu.CompilerParams(vmem_limit_bytes=60 * 1024 * 1024),
        name="pick_rows",
    )(
        subset_homolog_positions.reshape(1, seqs),
        homolog_features.transpose(1, 2, 0).reshape(packed, heads),
        first_side_matrix.T,
        second_side_matrix.T,
        final_offset_vector.reshape(1, pair_width),
        upstream_sensitivity.reshape(pairs, pair_width),
    )

    messages = [sent] + [
        lax.ppermute(sent, "prow", [(n, n ^ down) for n in range(prow_n)])
        for down in range(1, prow_n)
    ]
    offsets = [(down, 0) for down in range(prow_n)]
    rows = jnp.stack([one[pairs:] for one in messages])
    cots = [jnp.stack([one[:pairs] for one in messages])]
    for bit in range(groups.bit_length() - 1):
        swap = [(n, n ^ (1 << bit)) for n in range(groups)]
        rows = jnp.concatenate([rows, lax.ppermute(rows, "px", swap)], axis=0)
        held = cots[0] if bit == 0 else jnp.concatenate(cots, axis=0)
        cots.append(lax.ppermute(held, "px", swap))
        offsets += [(down, across + (1 << bit)) for down, across in offsets]
    theirs = lax.ppermute(rows, "pc", [(0, 1), (1, 0)])

    mapping = final_mapping_matrix.reshape(proj, proj, pair_width)
    mapping = mapping.swapaxes(0, 1).reshape(flat, pair_width)
    place = jnp.stack([lax.axis_index("prow"), lax.axis_index("px"), lax.axis_index("pc")])

    columns = groups * proj // tokens * block_cols
    cot, pulled = pl.pallas_call(
        functools.partial(pull_kernel, offsets),
        out_shape=(
            shape((prow_n, groups, pairs, pair_width), BF16),
            shape((prow_n, columns, block_rows * LANES), BF16),
        ),
        in_specs=[smem] + [vmem] * (1 + len(cots)),
        out_specs=(vmem,) * 2,
        compiler_params=params,
        cost_estimate=pl.CostEstimate(
            flops=2 * prow_n * groups * pairs * pair_width * flat,
            bytes_accessed=2 * prow_n * groups * pairs * (2 * pair_width + flat),
            transcendentals=0,
        ),
        name="pull_back",
    )(place, mapping.T, *cots)

    rows_all, expanded, swapped, outer, pair_delta = pl.pallas_call(
        functools.partial(outer_kernel, offsets),
        out_shape=(
            shape((owners * seqs, packed), BF16),
            shape((owners, seqs, tokens * LANES), BF16),
            shape((tokens * seqs, columns), BF16),
            shape((prow_n, groups * pairs, flat), BF16),
            shape(upstream_sensitivity.shape, BF16),
        ),
        in_specs=[smem] + [vmem] * 6,
        out_specs=(vmem,) * 5,
        scratch_shapes=[
            pltpu.VMEM((prow_n, groups, length, LANES), BF16),
            pltpu.VMEM((prow_n, groups, length, LANES), BF16),
            pltpu.VMEM((columns, tokens * seqs), BF16),
        ],
        compiler_params=params,
        cost_estimate=pl.CostEstimate(
            flops=2 * prow_n * groups * pairs * tokens * seqs * flat,
            bytes_accessed=2 * prow_n * groups * pairs * flat,
            transcendentals=0,
        ),
        name="outer_products",
    )(place, rows, theirs, mapping, left_wide, right_one, offset)
    grads, message = pl.pallas_call(
        back_kernel,
        out_shape=(
            shape((2, seqs, LANES), BF16),
            shape((flat + 2 * proj + seqs, LANES), BF16),
        ),
        in_specs=[smem] + [vmem] * 6,
        out_specs=(vmem,) * 2,
        scratch_shapes=[
            pltpu.VMEM((owners, seqs, LANES), BF16),
            pltpu.VMEM((groups * prow_n, seqs, LANES), BF16),
            pltpu.VMEM((columns, tokens * seqs), F32),
            pltpu.VMEM((pair_width, flat), F32),
        ],
        compiler_params=params,
        name="pull_further",
    )(place, rows_all, expanded, swapped, outer, cot, pulled)

    theirs = lax.ppermute(message, "pc", [(0, 1), (1, 0)])
    output_weight_gradient, left_weight_gradient, right_weight_gradient, alignment = pl.pallas_call(
        close_kernel,
        out_shape=(
            shape((flat, pair_width), F32),
            shape((proj, features), F32),
            shape((proj, features), F32),
            shape((seqs, tokens, features), BF16),
        ),
        in_specs=[vmem] * 7,
        out_specs=(vmem,) * 4,
        compiler_params=params,
        name="close",
    )(grads, message, theirs, normed, inverse, left_one, right_one)
    return (
        pair_delta,
        alignment,
        left_weight_gradient.T,
        right_weight_gradient.T,
        output_weight_gradient,
    )


def shapes_allow_gathering(
    mesh_shape, features, positions, first_side, second_side, mapping, offset, cot
):
    rows_n, cols_n = mesh_shape["prow"], mesh_shape["pcol"]
    parts = mesh_shape["rep"]
    tokens = features.shape[1] // (rows_n * cols_n)
    block_rows, block_cols = cot.shape[0] // (parts * rows_n), cot.shape[1] // cols_n
    proj, width = first_side.shape[1], cot.shape[2]
    return (
        cols_n % 2 == 0
        and cot.shape[1] * cot.shape[1] <= GATHERED_PAIRS
        and tokens * proj == LANES
        and tokens == 4
        and block_rows % tokens == 0
        and block_cols == rows_n * tokens == 16
        and rows_n & (rows_n - 1) == 0
        and cols_n & (cols_n - 1) == 0
        and width == LANES
        and features.shape[2] >= 2 * proj
        and positions.shape[0] // parts % 16 == 0
        and features.shape[2] * tokens % LANES == 0
    )


def solution(mesh):
    def run(local, over, columns, *args):
        tokens_split = P("rep", columns + ("prow",), None)
        pairs_split = P(("rep", "prow"), columns, None)
        return jax.shard_map(
            local,
            mesh=over,
            in_specs=(tokens_split, P("rep"), P(), P(), P(), P(), pairs_split),
            out_specs=(pairs_split, tokens_split, P("rep", None), P("rep", None), P("rep", None)),
            check_vma=False,
        )(*args)

    def program(*args):
        if not shapes_allow_gathering(mesh.shape, *args):
            return run(local_phased, mesh, ("pcol",), *args)
        reps, rows_n, cols_n = (mesh.shape[name] for name in ("rep", "prow", "pcol"))
        chips = Mesh(
            mesh.devices.reshape(reps, rows_n, cols_n // 2, 2), ("rep", "prow", "px", "pc")
        )
        return run(local_gathered, chips, ("px", "pc"), *args)

    return program
```

```python
import functools

import jax
import jax.numpy as jnp
from jax import lax
from jax.experimental import pallas as pl
from jax.experimental.pallas import tpu as pltpu
from jax.sharding import Mesh
from jax.sharding import PartitionSpec as P

BF16, F32 = jnp.bfloat16, jnp.float32
LANES = 128
GATHERED_PAIRS = 4096

PAIRS_AT_ONCE = 1024


def normalize(values):
    values = values.astype(jnp.float32)
    mean_factor = jnp.mean(values, axis=-1, keepdims=True)
    centered = values - mean_factor
    variance = jnp.mean(centered * centered, axis=-1, keepdims=True)
    inverse_spread = lax.rsqrt(variance + 1e-05)
    return (centered * inverse_spread, inverse_spread)


def transposed(rows_n, cols_n):
    return [
        (r * cols_n + c, c * rows_n + r) for r in range(rows_n) for c in range(cols_n)
    ]


def spread(values, axes, count):
    return lax.all_to_all(jnp.broadcast_to(values[None], (count,) + values.shape), axes, 0, 0)


def local_phased(
    homolog_features,
    subset_homolog_positions,
    first_side_matrix,
    second_side_matrix,
    final_mapping_matrix,
    final_offset_vector,
    upstream_sensitivity,
):
    axes = ("prow", "pcol")
    rows_n, cols_n = lax.axis_size("prow"), lax.axis_size("pcol")
    devices = rows_n * cols_n
    seq_count = subset_homolog_positions.shape[0]
    tokens, features = homolog_features.shape[1:]
    row_count, col_count, pair_width = upstream_sensitivity.shape
    proj = first_side_matrix.shape[1]
    flat = proj * proj
    to_rows = transposed(rows_n, cols_n)
    to_tokens = [(target, source) for source, target in to_rows]

    picked = jnp.take(homolog_features, subset_homolog_positions, axis=0)
    packed = picked.reshape(seq_count, tokens * features)
    row_own = lax.ppermute(packed, axes, to_rows)
    col_all = spread(packed, "prow", rows_n)
    row_all = spread(row_own, "pcol", cols_n)

    def side_of(chunks, count, matrix):
        chunks = chunks.reshape(count // tokens, seq_count, tokens, features)
        chunks = chunks.transpose(1, 0, 2, 3).reshape(seq_count, count, features)
        normed_low = normalize(chunks)[0].astype(jnp.bfloat16)
        side = jnp.einsum("stc,cp->stp", normed_low, matrix, preferred_element_type=jnp.float32)
        return normed_low, side.astype(jnp.bfloat16)

    row_normed, left = side_of(row_all, row_count, first_side_matrix)
    col_normed, right = side_of(col_all, col_count, second_side_matrix)

    def block_step(left_blk, cot_blk):
        rows = left_blk.shape[1]
        outer = jnp.einsum("sip,sjq->ijpq", left_blk, right, preferred_element_type=jnp.float32)
        outer = (outer / seq_count).astype(jnp.bfloat16).reshape(rows * col_count, flat)
        update = jnp.dot(outer, final_mapping_matrix, preferred_element_type=jnp.float32)
        update = (update + final_offset_vector).astype(jnp.bfloat16)
        cot_flat = cot_blk.reshape(rows * col_count, pair_width)
        grad_out = jnp.dot(outer.T, cot_flat, preferred_element_type=jnp.float32)
        grad_outer = jnp.dot(cot_flat, final_mapping_matrix.T, preferred_element_type=jnp.float32)
        grad_outer = grad_outer.astype(jnp.bfloat16).reshape(rows, col_count, proj, proj)
        grad_left = jnp.einsum(
            "ijpq,sjq->sip", grad_outer, right, preferred_element_type=jnp.float32
        )
        grad_right = jnp.einsum(
            "ijpq,sip->sjq", grad_outer, left_blk, preferred_element_type=jnp.float32
        )
        return update.reshape(rows, col_count, pair_width), grad_out, grad_left, grad_right

    block = max(1, min(row_count, PAIRS_AT_ONCE // col_count))
    blocks = row_count // block
    if blocks == 1:
        update, grad_out, grad_left, grad_right = block_step(left, upstream_sensitivity)
    else:
        def step(totals, inputs):
            update, grad_out, grad_left, grad_right = block_step(*inputs)
            return (totals[0] + grad_out, totals[1] + grad_right), (update, grad_left)

        (grad_out, grad_right), (update, grad_left) = lax.scan(
            step,
            (
                jnp.zeros((flat, pair_width), jnp.float32),
                jnp.zeros((seq_count, col_count, proj), jnp.float32),
            ),
            (
                left.reshape(seq_count, blocks, block, proj).transpose(1, 0, 2, 3),
                upstream_sensitivity.reshape(blocks, block, col_count, pair_width),
            ),
        )
        grad_left = grad_left.transpose(1, 0, 2, 3).reshape(seq_count, row_count, proj)
    pair_delta = update.reshape(row_count, col_count, pair_width)

    grad_left = (grad_left / seq_count).astype(jnp.bfloat16)
    grad_right = (grad_right / seq_count).astype(jnp.bfloat16)

    def weight_part(normed, grads):
        return jnp.einsum("stc,stp->cp", normed, grads, preferred_element_type=jnp.float32)

    side_part = jnp.concatenate(
        [weight_part(row_normed, grad_left), weight_part(col_normed, grad_right)], axis=1
    )
    share_rows = flat // devices
    side_rows = -(-features * 2 * proj // (pair_width * devices))
    side_flat = side_part.reshape(-1, pair_width)
    side_flat = jnp.pad(side_flat, ((0, side_rows * devices - side_flat.shape[0]), (0, 0)))
    shares = jnp.concatenate(
        [
            grad_out.reshape(devices, share_rows, pair_width),
            side_flat.reshape(devices, side_rows, pair_width),
        ],
        axis=1,
    ).astype(jnp.bfloat16)
    shares = lax.all_to_all(shares, axes, 0, 0)

    def chunks_of(grads, count):
        grads = grads.reshape(seq_count, count // tokens, tokens * proj)
        return grads.transpose(1, 0, 2)

    left_back = lax.all_to_all(chunks_of(grad_left, row_count), "pcol", 0, 0)
    right_back = lax.all_to_all(chunks_of(grad_right, col_count), "prow", 0, 0)
    left_back = jnp.sum(left_back.astype(jnp.float32), axis=0).astype(jnp.bfloat16)
    right_back = jnp.sum(right_back.astype(jnp.float32), axis=0).astype(jnp.bfloat16)
    left_back = lax.ppermute(left_back, axes, to_tokens)

    share = jnp.sum(shares.astype(jnp.float32), axis=0).astype(jnp.bfloat16)
    message = spread(share, axes, devices)
    output_weight_gradient = (
        message[:, :share_rows].reshape(flat, pair_width).astype(jnp.float32)
    )
    side = message[:, share_rows:].reshape(-1, pair_width).astype(jnp.float32)
    side = side[: features * 2 * proj // pair_width].reshape(features, 2 * proj)
    left_weight_gradient, right_weight_gradient = side[:, :proj], side[:, proj:]

    normed, inverse_spread = normalize(picked)
    both = jnp.concatenate(
        [
            left_back.reshape(seq_count, tokens, proj),
            right_back.reshape(seq_count, tokens, proj),
        ],
        axis=-1,
    )
    sides = jnp.concatenate([first_side_matrix, second_side_matrix], axis=1)
    grad_normed = jnp.einsum("stp,cp->stc", both, sides, preferred_element_type=jnp.float32)
    mean_factor = jnp.mean(grad_normed, axis=-1, keepdims=True)
    projected = jnp.mean(grad_normed * normed, axis=-1, keepdims=True)
    alignment_gradient = (
        inverse_spread * (grad_normed - mean_factor - normed * projected)
    ).astype(jnp.bfloat16)
    return (
        pair_delta,
        alignment_gradient,
        left_weight_gradient,
        right_weight_gradient,
        output_weight_gradient,
    )


def dot(x, y, contract=(1, 0), precision=None):
    return lax.dot_general(
        x, y, (((contract[0],), (contract[1],)), ((), ())),
        precision=precision, preferred_element_type=F32,
    )


def lane_ids(shape):
    return lax.broadcasted_iota(jnp.int32, shape, len(shape) - 1)


def fold_tokens(parts):
    quarter = LANES // 4
    chunk = lane_ids(parts[0].shape) // quarter
    first, even = chunk < 2, chunk % 2 == 0
    halves = [
        jnp.where(first, parts[t], parts[t + 2])
        + pltpu.roll(jnp.where(first, parts[t + 2], parts[t]), 2 * quarter, 1)
        for t in range(2)
    ]
    other = jnp.where(even, halves[1], halves[0])
    moved = jnp.where(even, pltpu.roll(other, 3 * quarter, 1), pltpu.roll(other, quarter, 1))
    return jnp.where(even, halves[0], halves[1]) + moved


def group_mean(x, group, precision):
    lanes = x.shape[1]
    rows_id = lax.broadcasted_iota(jnp.int32, (lanes, lanes), 0) // group
    cols_id = lax.broadcasted_iota(jnp.int32, (lanes, lanes), 1) // group
    block = jnp.where(rows_id == cols_id, 1.0 / group, 0.0).astype(x.dtype)
    return dot(x, block, precision=precision)


def pick_kernel(
    positions_ref,
    features_ref,
    cot_ref,
    normed_ref,
    inverse_ref,
    message_ref,
    positions,
    features,
    in_sems,
):
    pairs = cot_ref.shape[0]
    inputs = [
        pltpu.make_async_copy(source, target, in_sems.at[n])
        for n, (source, target) in enumerate(
            [
                (positions_ref, positions),
                (features_ref, features),
                (cot_ref, message_ref.at[pl.ds(0, pairs)]),
            ]
        )
    ]
    for copy in inputs:
        copy.start()
    heads = features_ref.shape[1]
    seqs, packed = normed_ref.shape
    channels = packed // 4
    for copy in inputs:
        copy.wait()
    wanted = positions[...] == lax.broadcasted_iota(jnp.int32, (heads, seqs), 0)
    chosen = dot(wanted.astype(BF16), features[...], contract=(0, 1))
    mean_factor = group_mean(chosen.astype(BF16), channels, None)
    centered = chosen - mean_factor
    variance = group_mean(centered * centered, channels, lax.Precision.HIGHEST)
    inverse = lax.rsqrt(variance + 1e-05)
    normed = centered * inverse
    for n in range(packed // LANES):
        message_ref[pairs + n * seqs : pairs + (n + 1) * seqs] = normed[
            :, n * LANES : (n + 1) * LANES
        ].astype(BF16)
    normed_ref[...] = normed
    inverse_ref[...] = inverse


def place_blocks(place_ref, offsets, refs, out_ref):
    blocks = [(ref, n) for ref in refs for n in range(ref.shape[0])]
    for (down, across), (ref, n) in zip(offsets, blocks, strict=True):
        out_ref[place_ref[0] ^ down, place_ref[1] ^ across] = ref[n]


def pull_kernel(offsets, place_ref, mapping_ref, *refs):
    *cot_refs, cot_ref, pulled_ref = refs
    prow_n, groups, pairs, pair_width = cot_ref.shape
    highs = mapping_ref.shape[1] // LANES
    block_rows = pulled_ref.shape[2] // LANES
    block_cols = pairs // block_rows
    place_blocks(place_ref, offsets, cot_refs, cot_ref)

    def step(r, carry):
        grad = dot(cot_ref[r].reshape(groups * pairs, pair_width), mapping_ref[...])
        for g in range(groups):
            for t in range(block_rows):
                start = (g * block_rows + t) * block_cols
                lanes = slice(t * LANES, (t + 1) * LANES)
                for h in range(highs):
                    there = slice((g * highs + h) * block_cols, (g * highs + h + 1) * block_cols)
                    pulled_ref[r, there, lanes] = grad[
                        start : start + block_cols, h * LANES : (h + 1) * LANES
                    ].astype(BF16)
        return carry

    lax.fori_loop(0, prow_n, step, 0)


def rows_of(ref, g, r):
    half = ref.shape[2] // 2
    return jnp.concatenate([ref[r, g, :half], ref[r, g, half:]], axis=1)


def prepare_kernel(
    offsets,
    place_ref,
    mine_from_ref,
    left_ref,
    right_ref,
    rows_ref,
    ahead_ref,
    swapped,
    turned,
    left_wide,
    left_one_ref,
    right_one_ref,
    mine_ref,
):
    place_blocks(place_ref, offsets, [mine_from_ref], mine_ref)
    prow_n, groups = mine_ref.shape[:2]
    seqs = ahead_ref.shape[1]
    proj, channels = left_ref.shape
    tokens = LANES // proj
    highs = proj // tokens
    block_cols = prow_n * tokens
    span = highs * block_cols

    repeat = lane_ids((proj, LANES)) % proj
    repeat = (repeat == lax.broadcasted_iota(jnp.int32, (proj, LANES), 0)).astype(BF16)
    left_row = dot(left_ref[...], repeat, contract=(0, 0))
    right_row = dot(right_ref[...], repeat, contract=(0, 0))
    slot = lane_ids(left_row.shape) // proj
    nothing = jnp.zeros(left_row.shape, BF16)
    for t in range(tokens):
        here = slice(t * channels, (t + 1) * channels)
        left_one_ref[here] = jnp.where(slot == t, left_row, 0.0).astype(BF16)
        right_one_ref[here] = jnp.where(slot == t, right_row, 0.0).astype(BF16)
        for other in range(tokens):
            left_wide[here, other * LANES : (other + 1) * LANES] = (
                left_row.astype(BF16) if other == t else nothing
            )

    rows = jnp.concatenate(
        [rows_of(mine_ref, g, r) for g in range(groups) for r in range(prow_n)], axis=0
    )
    rows_ref[...] = rows
    ahead_ref[...] = dot(rows, left_wide[...]).astype(BF16).reshape(ahead_ref.shape)

    right = dot(rows, right_one_ref[...]).astype(BF16)
    right = jnp.concatenate(
        [
            jnp.concatenate(
                [
                    right[(g * prow_n + r) * seqs : (g * prow_n + r + 1) * seqs]
                    for r in range(prow_n)
                ],
                axis=1,
            )
            for g in range(groups)
        ],
        axis=0,
    )
    right = dot(right, shuffle_matrix(block_cols, proj, tokens))
    for g in range(groups):
        for l in range(tokens):
            swapped[l * seqs : (l + 1) * seqs, g * span : (g + 1) * span] = (
                right[g * seqs : (g + 1) * seqs, l * span : (l + 1) * span] * (1.0 / seqs)
            ).astype(BF16)
    turned[...] = swapped[...].astype(F32).T.astype(BF16)


def shuffle_matrix(block_cols, proj, tokens):
    wide, highs = block_cols * proj, proj // tokens
    source = lax.broadcasted_iota(jnp.int32, (wide, wide), 0)
    target = lax.broadcasted_iota(jnp.int32, (wide, wide), 1)
    jj, qh = target % block_cols, target // block_cols % highs
    ql = target // (highs * block_cols)
    return (source == jj * proj + qh * tokens + ql).astype(BF16)


def left_block(place_ref, prow_n, mine_ref, theirs_ref, row, tokens):
    columns_n = 2 * (mine_ref.shape[0] // prow_n)
    parts = []
    for o in range(columns_n):
        owner = row * columns_n + o
        column, at = owner // prow_n, lax.rem(owner, prow_n)
        at = column // 2 * prow_n + at
        parts.append(
            jnp.where(lax.rem(column, 2) == place_ref[2], mine_ref[at], theirs_ref[at])
        )
    ahead = jnp.concatenate(parts, axis=1)
    low = lane_ids(ahead.shape) % LANES // (LANES // tokens)
    return jnp.concatenate(
        [jnp.where(low == l, ahead, jnp.zeros_like(ahead)) for l in range(tokens)], axis=0
    )


def grads_kernel(
    offsets,
    place_ref,
    theirs_from_ref,
    rows_ref,
    mine_ahead,
    left_wide,
    swapped,
    pulled_ref,
    grads_ref,
    message_ref,
    theirs_ahead,
    theirs_ref,
    left_back,
    right_back,
    sums,
):
    place_blocks(place_ref, offsets, [theirs_from_ref], theirs_ref)
    prow_n, groups = theirs_ref.shape[:2]
    seqs = mine_ahead.shape[1]
    tokens = swapped.shape[0] // seqs
    proj = LANES // tokens
    highs = proj // tokens
    span = swapped.shape[1] // groups
    block_cols = span // highs
    columns_n = 2 * groups
    own_row, own_group, core = place_ref[0], place_ref[1], place_ref[2]
    theirs_rows = jnp.concatenate(
        [rows_of(theirs_ref, g, r) for g in range(groups) for r in range(prow_n)], axis=0
    )
    theirs_ahead[...] = dot(theirs_rows, left_wide[...]).astype(BF16).reshape(theirs_ahead.shape)
    sums[...] = jnp.zeros_like(sums)

    def step(row, carry):
        block = left_block(place_ref, prow_n, mine_ahead, theirs_ahead, row, tokens)
        pulled = pulled_ref[row]
        back = dot(swapped[...], pulled)
        low = lane_ids((seqs, back.shape[1])) % LANES // proj
        back = functools.reduce(
            jnp.add,
            [jnp.where(low == l, back[l * seqs : (l + 1) * seqs], 0.0) for l in range(tokens)],
        )
        for o in range(columns_n):
            parts = [
                back[:, (o * tokens + t) * LANES : (o * tokens + t + 1) * LANES]
                for t in range(tokens)
            ]
            owner = row * columns_n + o
            column, at = owner // prow_n, lax.rem(owner, prow_n)
            other = jnp.where(lax.rem(column, 2) == core, 0, 1)
            left_back[other, column // 2 * prow_n + at] = fold_tokens(parts).astype(BF16)
        sums[...] += dot(pulled, block, contract=(1, 1))
        return carry

    lax.fori_loop(0, prow_n, step, 0)

    back = (sums[...].T * (1.0 / seqs)).astype(BF16)
    back = jnp.concatenate(
        [
            jnp.concatenate(
                [
                    back[l * seqs : (l + 1) * seqs, g * span : (g + 1) * span]
                    for l in range(tokens)
                ],
                axis=1,
            )
            for g in range(groups)
        ],
        axis=0,
    )
    shuffle = shuffle_matrix(block_cols, proj, tokens)
    back = dot(back, shuffle, contract=(1, 1)).astype(BF16)
    for g, r in [(g, r) for g in range(groups) for r in range(prow_n)]:
        right_back[g * prow_n + r] = back[g * seqs : (g + 1) * seqs, r * LANES : (r + 1) * LANES]

    def side(grads, rows):
        total = dot(grads, rows, contract=(0, 0))
        features = rows.shape[1] // tokens
        return functools.reduce(
            jnp.add,
            [
                total[t * proj : (t + 1) * proj, t * features : (t + 1) * features]
                for t in range(tokens)
            ],
        )

    count = groups * prow_n * seqs
    left_side = side(
        left_back[...].reshape(2 * count, LANES),
        jnp.concatenate([rows_ref[...], theirs_rows], axis=0),
    )
    right_side = side(right_back[...].reshape(count, LANES), rows_ref[...])
    both = jnp.concatenate([left_side, right_side], axis=0).astype(BF16)
    message_ref[: 2 * proj] = jnp.concatenate([both, jnp.zeros_like(both)], axis=1)
    own = own_group * prow_n + own_row
    message_ref[2 * proj :] = left_back[1, own]
    grads_ref[0] = left_back[0, own]
    grads_ref[1] = right_back[own]


def weights_kernel(
    place_ref,
    mine_ahead,
    theirs_ahead,
    turned,
    cot_ref,
    mapping_ref,
    offset_ref,
    pair_ref,
    message_ref,
    outer,
    weights,
):
    prow_n, groups, pairs, pair_width = cot_ref.shape
    block_rows, block_cols, _ = pair_ref.shape
    seqs = mine_ahead.shape[1]
    tokens = turned.shape[1] // seqs
    proj = LANES // tokens
    highs = proj // tokens
    own_row, own_group = place_ref[0], place_ref[1]
    weights[...] = jnp.zeros_like(weights)

    def step(row, carry):
        block = left_block(place_ref, prow_n, mine_ahead, theirs_ahead, row, tokens)
        made = dot(turned[...], block)
        for g in range(groups):
            for t in range(block_rows):
                start = (g * block_rows + t) * block_cols
                lanes = slice(t * LANES, (t + 1) * LANES)
                for h in range(highs):
                    there = slice((g * highs + h) * block_cols, (g * highs + h + 1) * block_cols)
                    outer[start : start + block_cols, h * LANES : (h + 1) * LANES] = made[
                        there, lanes
                    ].astype(BF16)
        cot = cot_ref[row].reshape(groups * pairs, pair_width)
        weights[...] += dot(cot, outer[...], contract=(0, 0))

        @pl.when(row == own_row)
        def _():
            mine = outer[pl.ds(pl.multiple_of(own_group * pairs, pairs), pairs)]
            update = dot(mine, mapping_ref[...]) + offset_ref[...]
            pair_ref[...] = update.astype(BF16).reshape(pair_ref.shape)

        return carry

    lax.fori_loop(0, prow_n, step, 0)

    flat = weights.shape[1]
    turned_back = weights[...].T.reshape(proj, proj, pair_width)
    message_ref[...] = turned_back.swapaxes(0, 1).reshape(flat, pair_width).astype(BF16)


def close_kernel(
    grads_ref,
    own_ref,
    message_ref,
    normed_ref,
    inverse_ref,
    left_ref,
    right_ref,
    left_out_ref,
    right_out_ref,
    rows_out_ref,
):
    proj, features = left_out_ref.shape
    sides = slice(0, 2 * proj)
    both = own_ref[sides, :features].astype(F32) + message_ref[sides, :features].astype(F32)
    left_out_ref[...] = both[:proj]
    right_out_ref[...] = both[proj:]
    left_back = grads_ref[0].astype(F32) + message_ref[2 * proj :].astype(F32)
    grad_normed = dot(left_back.astype(BF16), left_ref[...], contract=(1, 1))
    grad_normed = grad_normed + dot(grads_ref[1], right_ref[...], contract=(1, 1))
    normed = normed_ref[...]
    mean_factor = group_mean(grad_normed, features, lax.Precision.HIGHEST)
    projected = group_mean(grad_normed * normed, features, lax.Precision.HIGHEST)
    result = inverse_ref[...] * (grad_normed - mean_factor - normed * projected)
    rows_out_ref[...] = jnp.stack(
        [result[:, t * features : (t + 1) * features] for t in range(rows_out_ref.shape[1])],
        axis=1,
    ).astype(BF16)


def local_gathered(
    homolog_features,
    subset_homolog_positions,
    first_side_matrix,
    second_side_matrix,
    final_mapping_matrix,
    final_offset_vector,
    upstream_sensitivity,
):
    prow_n, groups = lax.axis_size("prow"), lax.axis_size("px")
    owners = prow_n * groups * 2
    heads, tokens, features = homolog_features.shape
    seqs = subset_homolog_positions.shape[0]
    block_rows, block_cols, pair_width = upstream_sensitivity.shape
    proj = first_side_matrix.shape[1]
    flat = proj * proj
    packed = tokens * features
    shape = jax.ShapeDtypeStruct
    vmem = pl.BlockSpec(memory_space=pltpu.VMEM)
    smem = pl.BlockSpec(memory_space=pltpu.SMEM)
    params = pltpu.CompilerParams(vmem_limit_bytes=36 * 1024 * 1024)

    pairs = block_rows * block_cols
    length = seqs * packed // LANES
    hbm = pl.BlockSpec(memory_space=pltpu.HBM)
    normed, inverse, sent = pl.pallas_call(
        pick_kernel,
        out_shape=(
            shape((seqs, packed), F32),
            shape((seqs, packed), F32),
            shape((pairs + length, LANES), BF16),
        ),
        in_specs=[hbm] * 3,
        out_specs=(vmem,) * 3,
        scratch_shapes=[
            pltpu.VMEM((1, seqs), jnp.int32),
            pltpu.VMEM((packed, heads), BF16),
            pltpu.SemaphoreType.DMA((3,)),
        ],
        compiler_params=pltpu.CompilerParams(vmem_limit_bytes=60 * 1024 * 1024),
        name="pick_rows",
    )(
        subset_homolog_positions.reshape(1, seqs),
        homolog_features.transpose(1, 2, 0).reshape(packed, heads),
        upstream_sensitivity.reshape(pairs, pair_width),
    )

    downs = list(range(prow_n // 2, prow_n)) + list(range(1, prow_n // 2))
    messages = [sent] + [
        lax.ppermute(sent, "prow", [(n, n ^ down) for n in range(prow_n)]) for down in downs
    ]
    offsets = [(down, 0) for down in [0] + downs]
    rows = jnp.stack([one[pairs:] for one in messages])
    cots = [jnp.stack([one[:pairs] for one in messages])]
    for bit in range(groups.bit_length() - 1):
        swap = [(n, n ^ (1 << bit)) for n in range(groups)]
        rows = jnp.concatenate([rows, lax.ppermute(rows, "px", swap)], axis=0)
        held = cots[0] if bit == 0 else jnp.concatenate(cots, axis=0)
        cots.append(lax.ppermute(held, "px", swap))
        offsets += [(down, across + (1 << bit)) for down, across in offsets]
    theirs = lax.ppermute(rows, "pc", [(0, 1), (1, 0)])

    mapping = final_mapping_matrix.reshape(proj, proj, pair_width)
    mapping = mapping.swapaxes(0, 1).reshape(flat, pair_width)
    place = jnp.stack([lax.axis_index("prow"), lax.axis_index("px"), lax.axis_index("pc")])

    columns = groups * proj // tokens * block_cols
    cot, pulled = pl.pallas_call(
        functools.partial(pull_kernel, offsets),
        out_shape=(
            shape((prow_n, groups, pairs, pair_width), BF16),
            shape((prow_n, columns, block_rows * LANES), BF16),
        ),
        in_specs=[smem] + [vmem] * (1 + len(cots)),
        out_specs=(vmem,) * 2,
        compiler_params=params,
        cost_estimate=pl.CostEstimate(
            flops=2 * prow_n * groups * pairs * pair_width * flat,
            bytes_accessed=2 * prow_n * groups * pairs * (2 * pair_width + flat),
            transcendentals=0,
        ),
        name="pull_back",
    )(place, mapping.T, *cots)

    sided = groups * prow_n
    rows_mine, mine_ahead, swapped, turned, left_wide, left_one, right_one = pl.pallas_call(
        functools.partial(prepare_kernel, offsets),
        out_shape=(
            shape((sided * seqs, packed), BF16),
            shape((sided, seqs, tokens * LANES), BF16),
            shape((tokens * seqs, columns), BF16),
            shape((columns, tokens * seqs), BF16),
            shape((packed, tokens * LANES), BF16),
            shape((packed, LANES), BF16),
            shape((packed, LANES), BF16),
        ),
        in_specs=[smem] + [vmem] * 3,
        out_specs=(vmem,) * 7,
        scratch_shapes=[pltpu.VMEM((prow_n, groups, length, LANES), BF16)],
        compiler_params=params,
        cost_estimate=pl.CostEstimate(
            flops=2 * sided * seqs * packed * tokens * LANES,
            bytes_accessed=4 * sided * seqs * packed,
            transcendentals=0,
        ),
        name="prepare",
    )(place, rows, first_side_matrix.T, second_side_matrix.T)
    grads, side_message, theirs_ahead = pl.pallas_call(
        functools.partial(grads_kernel, offsets),
        out_shape=(
            shape((2, seqs, LANES), BF16),
            shape((2 * proj + seqs, LANES), BF16),
            shape((sided, seqs, tokens * LANES), BF16),
        ),
        in_specs=[smem] + [vmem] * 6,
        out_specs=(vmem,) * 3,
        scratch_shapes=[
            pltpu.VMEM((prow_n, groups, length, LANES), BF16),
            pltpu.VMEM((2, sided, seqs, LANES), BF16),
            pltpu.VMEM((sided, seqs, LANES), BF16),
            pltpu.VMEM((columns, tokens * seqs), F32),
        ],
        compiler_params=params,
        name="projection_grads",
    )(place, theirs, rows_mine, mine_ahead, left_wide, swapped, pulled)
    side_theirs = lax.ppermute(side_message, "pc", [(0, 1), (1, 0)])
    pair_delta, message = pl.pallas_call(
        weights_kernel,
        out_shape=(
            shape(upstream_sensitivity.shape, BF16),
            shape((flat, pair_width), BF16),
        ),
        in_specs=[smem] + [vmem] * 6,
        out_specs=(vmem,) * 2,
        scratch_shapes=[
            pltpu.VMEM((groups * pairs, flat), BF16),
            pltpu.VMEM((pair_width, flat), F32),
        ],
        compiler_params=params,
        cost_estimate=pl.CostEstimate(
            flops=4 * prow_n * groups * pairs * tokens * seqs * flat,
            bytes_accessed=2 * prow_n * groups * pairs * flat,
            transcendentals=0,
        ),
        name="outer_products",
    )(
        place, mine_ahead, theirs_ahead, turned, cot, mapping,
        final_offset_vector.reshape(1, pair_width),
    )
    theirs = lax.ppermute(message, "pc", [(0, 1), (1, 0)])
    left_weight_gradient, right_weight_gradient, alignment = pl.pallas_call(
        close_kernel,
        out_shape=(
            shape((proj, features), F32),
            shape((proj, features), F32),
            shape((seqs, tokens, features), BF16),
        ),
        in_specs=[vmem] * 7,
        out_specs=(vmem,) * 3,
        compiler_params=params,
        name="row_gradient",
    )(grads, side_message, side_theirs, normed, inverse, left_one, right_one)
    output_weight_gradient = message.astype(F32) + theirs.astype(F32)
    return (
        pair_delta,
        alignment,
        left_weight_gradient.T,
        right_weight_gradient.T,
        output_weight_gradient,
    )


def shapes_allow_gathering(
    mesh_shape, features, positions, first_side, second_side, mapping, offset, cot
):
    rows_n, cols_n = mesh_shape["prow"], mesh_shape["pcol"]
    parts = mesh_shape["rep"]
    tokens = features.shape[1] // (rows_n * cols_n)
    block_rows, block_cols = cot.shape[0] // (parts * rows_n), cot.shape[1] // cols_n
    proj, width = first_side.shape[1], cot.shape[2]
    return (
        cols_n % 2 == 0
        and cot.shape[1] * cot.shape[1] <= GATHERED_PAIRS
        and tokens * proj == LANES
        and tokens == 4
        and block_rows % tokens == 0
        and block_cols == rows_n * tokens == 16
        and rows_n & (rows_n - 1) == 0
        and cols_n & (cols_n - 1) == 0
        and width == LANES
        and features.shape[2] >= 2 * proj
        and positions.shape[0] // parts % 16 == 0
        and features.shape[2] * tokens % LANES == 0
    )


def solution(mesh):
    def run(local, over, columns, *args):
        tokens_split = P("rep", columns + ("prow",), None)
        pairs_split = P(("rep", "prow"), columns, None)
        return jax.shard_map(
            local,
            mesh=over,
            in_specs=(tokens_split, P("rep"), P(), P(), P(), P(), pairs_split),
            out_specs=(pairs_split, tokens_split, P("rep", None), P("rep", None), P("rep", None)),
            check_vma=False,
        )(*args)

    def program(*args):
        if not shapes_allow_gathering(mesh.shape, *args):
            return run(local_phased, mesh, ("pcol",), *args)
        reps, rows_n, cols_n = (mesh.shape[name] for name in ("rep", "prow", "pcol"))
        chips = Mesh(
            mesh.devices.reshape(reps, rows_n, cols_n // 2, 2), ("rep", "prow", "px", "pc")
        )
        return run(local_gathered, chips, ("px", "pc"), *args)

    return program
```

```python
import functools

import jax
import jax.numpy as jnp
from jax import lax
from jax.experimental import pallas as pl
from jax.experimental.pallas import tpu as pltpu
from jax.sharding import Mesh
from jax.sharding import PartitionSpec as P

BF16, F32 = jnp.bfloat16, jnp.float32
LANES = 128
GATHERED_PAIRS = 4096

PAIRS_AT_ONCE = 1024


def normalize(values):
    values = values.astype(jnp.float32)
    mean_factor = jnp.mean(values, axis=-1, keepdims=True)
    centered = values - mean_factor
    variance = jnp.mean(centered * centered, axis=-1, keepdims=True)
    inverse_spread = lax.rsqrt(variance + 1e-05)
    return (centered * inverse_spread, inverse_spread)


def transposed(rows_n, cols_n):
    return [
        (r * cols_n + c, c * rows_n + r) for r in range(rows_n) for c in range(cols_n)
    ]


def spread(values, axes, count):
    return lax.all_to_all(jnp.broadcast_to(values[None], (count,) + values.shape), axes, 0, 0)


def local_phased(
    homolog_features,
    subset_homolog_positions,
    first_side_matrix,
    second_side_matrix,
    final_mapping_matrix,
    final_offset_vector,
    upstream_sensitivity,
):
    axes = ("prow", "pcol")
    rows_n, cols_n = lax.axis_size("prow"), lax.axis_size("pcol")
    devices = rows_n * cols_n
    seq_count = subset_homolog_positions.shape[0]
    tokens, features = homolog_features.shape[1:]
    row_count, col_count, pair_width = upstream_sensitivity.shape
    proj = first_side_matrix.shape[1]
    flat = proj * proj
    to_rows = transposed(rows_n, cols_n)
    to_tokens = [(target, source) for source, target in to_rows]

    picked = jnp.take(homolog_features, subset_homolog_positions, axis=0)
    packed = picked.reshape(seq_count, tokens * features)
    row_own = lax.ppermute(packed, axes, to_rows)
    col_all = spread(packed, "prow", rows_n)
    row_all = spread(row_own, "pcol", cols_n)

    def side_of(chunks, count, matrix):
        chunks = chunks.reshape(count // tokens, seq_count, tokens, features)
        chunks = chunks.transpose(1, 0, 2, 3).reshape(seq_count, count, features)
        normed_low = normalize(chunks)[0].astype(jnp.bfloat16)
        side = jnp.einsum("stc,cp->stp", normed_low, matrix, preferred_element_type=jnp.float32)
        return normed_low, side.astype(jnp.bfloat16)

    row_normed, left = side_of(row_all, row_count, first_side_matrix)
    col_normed, right = side_of(col_all, col_count, second_side_matrix)

    def block_step(left_blk, cot_blk):
        rows = left_blk.shape[1]
        outer = jnp.einsum("sip,sjq->ijpq", left_blk, right, preferred_element_type=jnp.float32)
        outer = (outer / seq_count).astype(jnp.bfloat16).reshape(rows * col_count, flat)
        update = jnp.dot(outer, final_mapping_matrix, preferred_element_type=jnp.float32)
        update = (update + final_offset_vector).astype(jnp.bfloat16)
        cot_flat = cot_blk.reshape(rows * col_count, pair_width)
        grad_out = jnp.dot(outer.T, cot_flat, preferred_element_type=jnp.float32)
        grad_outer = jnp.dot(cot_flat, final_mapping_matrix.T, preferred_element_type=jnp.float32)
        grad_outer = grad_outer.astype(jnp.bfloat16).reshape(rows, col_count, proj, proj)
        grad_left = jnp.einsum(
            "ijpq,sjq->sip", grad_outer, right, preferred_element_type=jnp.float32
        )
        grad_right = jnp.einsum(
            "ijpq,sip->sjq", grad_outer, left_blk, preferred_element_type=jnp.float32
        )
        return update.reshape(rows, col_count, pair_width), grad_out, grad_left, grad_right

    block = max(1, min(row_count, PAIRS_AT_ONCE // col_count))
    blocks = row_count // block
    if blocks == 1:
        update, grad_out, grad_left, grad_right = block_step(left, upstream_sensitivity)
    else:
        def step(totals, inputs):
            update, grad_out, grad_left, grad_right = block_step(*inputs)
            return (totals[0] + grad_out, totals[1] + grad_right), (update, grad_left)

        (grad_out, grad_right), (update, grad_left) = lax.scan(
            step,
            (
                jnp.zeros((flat, pair_width), jnp.float32),
                jnp.zeros((seq_count, col_count, proj), jnp.float32),
            ),
            (
                left.reshape(seq_count, blocks, block, proj).transpose(1, 0, 2, 3),
                upstream_sensitivity.reshape(blocks, block, col_count, pair_width),
            ),
        )
        grad_left = grad_left.transpose(1, 0, 2, 3).reshape(seq_count, row_count, proj)
    pair_delta = update.reshape(row_count, col_count, pair_width)

    grad_left = (grad_left / seq_count).astype(jnp.bfloat16)
    grad_right = (grad_right / seq_count).astype(jnp.bfloat16)

    def weight_part(normed, grads):
        return jnp.einsum("stc,stp->cp", normed, grads, preferred_element_type=jnp.float32)

    side_part = jnp.concatenate(
        [weight_part(row_normed, grad_left), weight_part(col_normed, grad_right)], axis=1
    )
    share_rows = flat // devices
    side_rows = -(-features * 2 * proj // (pair_width * devices))
    side_flat = side_part.reshape(-1, pair_width)
    side_flat = jnp.pad(side_flat, ((0, side_rows * devices - side_flat.shape[0]), (0, 0)))
    shares = jnp.concatenate(
        [
            grad_out.reshape(devices, share_rows, pair_width),
            side_flat.reshape(devices, side_rows, pair_width),
        ],
        axis=1,
    ).astype(jnp.bfloat16)
    shares = lax.all_to_all(shares, axes, 0, 0)

    def chunks_of(grads, count):
        grads = grads.reshape(seq_count, count // tokens, tokens * proj)
        return grads.transpose(1, 0, 2)

    left_back = lax.all_to_all(chunks_of(grad_left, row_count), "pcol", 0, 0)
    right_back = lax.all_to_all(chunks_of(grad_right, col_count), "prow", 0, 0)
    left_back = jnp.sum(left_back.astype(jnp.float32), axis=0).astype(jnp.bfloat16)
    right_back = jnp.sum(right_back.astype(jnp.float32), axis=0).astype(jnp.bfloat16)
    left_back = lax.ppermute(left_back, axes, to_tokens)

    share = jnp.sum(shares.astype(jnp.float32), axis=0).astype(jnp.bfloat16)
    message = spread(share, axes, devices)
    output_weight_gradient = (
        message[:, :share_rows].reshape(flat, pair_width).astype(jnp.float32)
    )
    side = message[:, share_rows:].reshape(-1, pair_width).astype(jnp.float32)
    side = side[: features * 2 * proj // pair_width].reshape(features, 2 * proj)
    left_weight_gradient, right_weight_gradient = side[:, :proj], side[:, proj:]

    normed, inverse_spread = normalize(picked)
    both = jnp.concatenate(
        [
            left_back.reshape(seq_count, tokens, proj),
            right_back.reshape(seq_count, tokens, proj),
        ],
        axis=-1,
    )
    sides = jnp.concatenate([first_side_matrix, second_side_matrix], axis=1)
    grad_normed = jnp.einsum("stp,cp->stc", both, sides, preferred_element_type=jnp.float32)
    mean_factor = jnp.mean(grad_normed, axis=-1, keepdims=True)
    projected = jnp.mean(grad_normed * normed, axis=-1, keepdims=True)
    alignment_gradient = (
        inverse_spread * (grad_normed - mean_factor - normed * projected)
    ).astype(jnp.bfloat16)
    return (
        pair_delta,
        alignment_gradient,
        left_weight_gradient,
        right_weight_gradient,
        output_weight_gradient,
    )


def dot(x, y, contract=(1, 0), precision=None):
    return lax.dot_general(
        x, y, (((contract[0],), (contract[1],)), ((), ())),
        precision=precision, preferred_element_type=F32,
    )


def lane_ids(shape):
    return lax.broadcasted_iota(jnp.int32, shape, len(shape) - 1)


def fold_tokens(parts):
    quarter = LANES // 4
    chunk = lane_ids(parts[0].shape) // quarter
    first, even = chunk < 2, chunk % 2 == 0
    halves = [
        jnp.where(first, parts[t], parts[t + 2])
        + pltpu.roll(jnp.where(first, parts[t + 2], parts[t]), 2 * quarter, 1)
        for t in range(2)
    ]
    other = jnp.where(even, halves[1], halves[0])
    moved = jnp.where(even, pltpu.roll(other, 3 * quarter, 1), pltpu.roll(other, quarter, 1))
    return jnp.where(even, halves[0], halves[1]) + moved


def group_mean(x, group, precision):
    lanes = x.shape[1]
    rows_id = lax.broadcasted_iota(jnp.int32, (lanes, lanes), 0) // group
    cols_id = lax.broadcasted_iota(jnp.int32, (lanes, lanes), 1) // group
    block = jnp.where(rows_id == cols_id, 1.0 / group, 0.0).astype(x.dtype)
    return dot(x, block, precision=precision)


def pick_kernel(
    positions_ref,
    features_ref,
    left_ref,
    right_ref,
    offset_ref,
    cot_ref,
    normed_ref,
    inverse_ref,
    left_wide_ref,
    left_one_ref,
    right_one_ref,
    offset_out_ref,
    message_ref,
    positions,
    features,
    left,
    right,
    in_sems,
):
    pairs = cot_ref.shape[0]
    inputs = [
        pltpu.make_async_copy(source, target, in_sems.at[n])
        for n, (source, target) in enumerate(
            [
                (positions_ref, positions),
                (features_ref, features),
                (left_ref, left),
                (right_ref, right),
                (offset_ref, offset_out_ref),
                (cot_ref, message_ref.at[pl.ds(0, pairs)]),
            ]
        )
    ]
    for copy in inputs:
        copy.start()
    heads = features_ref.shape[1]
    seqs, packed = normed_ref.shape
    proj, channels = left_ref.shape
    tokens = packed // channels
    for copy in inputs:
        copy.wait()
    wanted = positions[...] == lax.broadcasted_iota(jnp.int32, (heads, seqs), 0)
    chosen = dot(wanted.astype(BF16), features[...], contract=(0, 1))
    mean_factor = group_mean(chosen.astype(BF16), channels, None)
    centered = chosen - mean_factor
    variance = group_mean(centered * centered, channels, lax.Precision.HIGHEST)
    inverse = lax.rsqrt(variance + 1e-05)
    normed = centered * inverse
    pieces = packed // LANES
    for n in range(pieces):
        message_ref[pairs + n * seqs : pairs + (n + 1) * seqs] = normed[
            :, n * LANES : (n + 1) * LANES
        ].astype(BF16)
    normed_ref[...] = normed
    inverse_ref[...] = inverse

    repeat = lane_ids((proj, LANES)) % proj
    repeat = (repeat == lax.broadcasted_iota(jnp.int32, (proj, LANES), 0)).astype(BF16)
    left_row = dot(left[...], repeat, contract=(0, 0))
    right_row = dot(right[...], repeat, contract=(0, 0))
    slot = lane_ids(left_row.shape) // proj
    nothing = jnp.zeros(left_row.shape, BF16)
    for t in range(tokens):
        here = slice(t * channels, (t + 1) * channels)
        left_one_ref[here] = jnp.where(slot == t, left_row, 0.0).astype(BF16)
        right_one_ref[here] = jnp.where(slot == t, right_row, 0.0).astype(BF16)
        for other in range(tokens):
            left_wide_ref[here, other * LANES : (other + 1) * LANES] = (
                left_row.astype(BF16) if other == t else nothing
            )


def place_blocks(place_ref, offsets, blocks, out_ref):
    for (down, across), block in zip(offsets, blocks, strict=True):
        out_ref[place_ref[0] ^ down, place_ref[1] ^ across] = block


def pull_kernel(offsets, place_ref, mapping_ref, *refs):
    *message_refs, cot_ref, pulled_ref = refs
    prow_n, groups, pairs, pair_width = cot_ref.shape
    highs = mapping_ref.shape[1] // LANES
    block_rows = pulled_ref.shape[2] // LANES
    block_cols = pairs // block_rows
    place_blocks(place_ref, offsets, [ref[:pairs] for ref in message_refs], cot_ref)

    def step(r, carry):
        grad = dot(cot_ref[r].reshape(groups * pairs, pair_width), mapping_ref[...])
        for g in range(groups):
            for t in range(block_rows):
                start = (g * block_rows + t) * block_cols
                lanes = slice(t * LANES, (t + 1) * LANES)
                for h in range(highs):
                    there = slice((g * highs + h) * block_cols, (g * highs + h + 1) * block_cols)
                    pulled_ref[r, there, lanes] = grad[
                        start : start + block_cols, h * LANES : (h + 1) * LANES
                    ].astype(BF16)
        return carry

    lax.fori_loop(0, prow_n, step, 0)


def outer_kernel(
    offsets,
    place_ref,
    mine_from_ref,
    theirs_from_ref,
    mapping_ref,
    left_ref,
    right_ref,
    offset_ref,
    rows_ref,
    expanded,
    swapped,
    outer_ref,
    pair_ref,
    mine_ref,
    theirs_ref,
    turned,
):
    for source, target in ((mine_from_ref, mine_ref), (theirs_from_ref, theirs_ref)):
        place_blocks(place_ref, offsets, [source[n] for n in range(source.shape[0])], target)
    prow_n, groups = mine_ref.shape[:2]
    block_rows, block_cols, pair_width = pair_ref.shape
    owners, seqs = expanded.shape[:2]
    packed = left_ref.shape[0]
    tokens = left_ref.shape[1] // LANES
    proj = LANES // tokens
    highs = proj // tokens
    span = highs * block_cols
    own_row, own_group, core = place_ref[0], place_ref[1], place_ref[2]

    def rows_of(ref, g, r):
        return jnp.concatenate(
            [ref[r, g, n * seqs : (n + 1) * seqs] for n in range(packed // LANES)], axis=1
        )

    places = [(g, r) for g in range(groups) for r in range(prow_n)]
    rows_mine = [rows_of(mine_ref, g, r) for g, r in places]
    rows_all = jnp.concatenate(
        rows_mine + [rows_of(theirs_ref, g, r) for g, r in places], axis=0
    )
    rows_ref[...] = rows_all
    wide_left = dot(rows_all, left_ref[...]).astype(BF16)
    for n, owner in enumerate(owner_order(places, prow_n, core)):
        expanded[owner] = wide_left[n * seqs : (n + 1) * seqs]

    side_rows = []
    for g in range(groups):
        chunks = rows_mine[g * prow_n : (g + 1) * prow_n]
        side_rows.append(
            jnp.concatenate([dot(x, right_ref[...]).astype(BF16) for x in chunks], axis=1)
        )
    right = dot(jnp.concatenate(side_rows, axis=0), shuffle_matrix(block_cols, proj, tokens))
    for g in range(groups):
        for l in range(tokens):
            swapped[l * seqs : (l + 1) * seqs, g * span : (g + 1) * span] = (
                right[g * seqs : (g + 1) * seqs, l * span : (l + 1) * span] * (1.0 / seqs)
            ).astype(BF16)
    turned[...] = swapped[...].astype(F32).T.astype(BF16)

    def step(row, carry):
        made = dot(turned[...], left_block(expanded, row, owners // prow_n, tokens))
        for g in range(groups):
            for t in range(block_rows):
                start = (g * block_rows + t) * block_cols
                lanes = slice(t * LANES, (t + 1) * LANES)
                for h in range(highs):
                    there = slice((g * highs + h) * block_cols, (g * highs + h + 1) * block_cols)
                    outer_ref[row, start : start + block_cols, h * LANES : (h + 1) * LANES] = made[
                        there, lanes
                    ].astype(BF16)
        return carry

    lax.fori_loop(0, prow_n, step, 0)
    share = block_rows * block_cols
    mine = outer_ref[own_row, pl.ds(pl.multiple_of(own_group * share, share), share)]
    update = dot(mine, mapping_ref[...]) + offset_ref[...]
    pair_ref[...] = update.astype(BF16).reshape(pair_ref.shape)


def owner_order(places, prow_n, core):
    mine = [(2 * g + core) * prow_n + r for g, r in places]
    return mine + [(2 * g + 1 - core) * prow_n + r for g, r in places]


def shuffle_matrix(block_cols, proj, tokens):
    wide, highs = block_cols * proj, proj // tokens
    source = lax.broadcasted_iota(jnp.int32, (wide, wide), 0)
    target = lax.broadcasted_iota(jnp.int32, (wide, wide), 1)
    jj, qh = target % block_cols, target // block_cols % highs
    ql = target // (highs * block_cols)
    return (source == jj * proj + qh * tokens + ql).astype(BF16)


def left_block(expanded, row, step_owners, tokens):
    ahead = jnp.concatenate([expanded[row * step_owners + o] for o in range(step_owners)], axis=1)
    low = lane_ids(ahead.shape) % LANES // (LANES // tokens)
    return jnp.concatenate(
        [jnp.where(low == l, ahead, jnp.zeros_like(ahead)) for l in range(tokens)], axis=0
    )


def back_kernel(
    place_ref,
    rows_ref,
    expanded,
    swapped,
    outer_ref,
    cot_ref,
    pulled_ref,
    grads_ref,
    message_ref,
    left_back,
    right_back,
    sums,
    weights,
):
    prow_n, groups, pairs, pair_width = cot_ref.shape
    owners, seqs = left_back.shape[:2]
    tokens = swapped.shape[0] // seqs
    proj = LANES // tokens
    highs = proj // tokens
    span = swapped.shape[1] // groups
    block_cols = span // highs
    step_owners = owners // prow_n
    own_row, own_group, core = place_ref[0], place_ref[1], place_ref[2]
    places = [(g, r) for g in range(groups) for r in range(prow_n)]
    order = owner_order(places, prow_n, core)

    sums[...] = jnp.zeros_like(sums)
    weights[...] = jnp.zeros_like(weights)

    def step(row, carry):
        block = left_block(expanded, row, step_owners, tokens)
        cot = cot_ref[row].reshape(groups * pairs, pair_width)
        weights[...] += dot(cot, outer_ref[row], contract=(0, 0))
        pulled = pulled_ref[row]
        back = dot(swapped[...], pulled)
        low = lane_ids((seqs, back.shape[1])) % LANES // proj
        back = functools.reduce(
            jnp.add,
            [
                jnp.where(low == l, back[l * seqs : (l + 1) * seqs], 0.0)
                for l in range(tokens)
            ],
        )
        for o in range(step_owners):
            parts = [
                back[:, (o * tokens + t) * LANES : (o * tokens + t + 1) * LANES]
                for t in range(tokens)
            ]
            left_back[row * step_owners + o] = fold_tokens(parts).astype(BF16)
        sums[...] += dot(pulled, block, contract=(1, 1))
        return carry

    lax.fori_loop(0, prow_n, step, 0)

    back = (sums[...].T * (1.0 / seqs)).astype(BF16)
    back = jnp.concatenate(
        [
            jnp.concatenate(
                [
                    back[l * seqs : (l + 1) * seqs, g * span : (g + 1) * span]
                    for l in range(tokens)
                ],
                axis=1,
            )
            for g in range(groups)
        ],
        axis=0,
    )
    shuffle = shuffle_matrix(block_cols, proj, tokens)
    back = dot(back, shuffle, contract=(1, 1)).astype(BF16)
    for g, r in places:
        right_back[g * prow_n + r] = back[g * seqs : (g + 1) * seqs, r * LANES : (r + 1) * LANES]

    def side(grads, rows):
        total = dot(grads, rows, contract=(0, 0))
        features = rows.shape[1] // tokens
        return functools.reduce(
            jnp.add,
            [
                total[t * proj : (t + 1) * proj, t * features : (t + 1) * features]
                for t in range(tokens)
            ],
        )

    left_side = side(
        jnp.concatenate([left_back[owner] for owner in order], axis=0), rows_ref[...]
    )
    columns = groups * prow_n * seqs
    right_side = side(right_back[...].reshape(columns, LANES), rows_ref[:columns])
    both = jnp.concatenate([left_side, right_side], axis=0).astype(BF16)
    both = jnp.concatenate([both, jnp.zeros_like(both)], axis=1)

    flat = weights.shape[1]
    outer_f = weights[...].T
    weight_rows = outer_f.reshape(proj, proj, pair_width).swapaxes(0, 1).reshape(flat, pair_width)

    message_ref[:flat] = weight_rows.astype(BF16)
    message_ref[flat : flat + 2 * proj] = both
    message_ref[flat + 2 * proj :] = left_back[(2 * own_group + 1 - core) * prow_n + own_row]
    grads_ref[0] = left_back[(2 * own_group + core) * prow_n + own_row]
    grads_ref[1] = right_back[own_group * prow_n + own_row]


def close_kernel(
    grads_ref,
    own_ref,
    message_ref,
    normed_ref,
    inverse_ref,
    left_ref,
    right_ref,
    out_ref,
    left_out_ref,
    right_out_ref,
    rows_out_ref,
):
    flat = out_ref.shape[0]
    proj, features = left_out_ref.shape
    out_ref[...] = own_ref[:flat].astype(F32) + message_ref[:flat].astype(F32)
    sides = slice(flat, flat + 2 * proj)
    both = own_ref[sides, :features].astype(F32) + message_ref[sides, :features].astype(F32)
    left_out_ref[...] = both[:proj]
    right_out_ref[...] = both[proj:]
    left_back = grads_ref[0].astype(F32) + message_ref[flat + 2 * proj :].astype(F32)
    grad_normed = dot(left_back.astype(BF16), left_ref[...], contract=(1, 1))
    grad_normed = grad_normed + dot(grads_ref[1], right_ref[...], contract=(1, 1))
    normed = normed_ref[...]
    mean_factor = group_mean(grad_normed, features, lax.Precision.HIGHEST)
    projected = group_mean(grad_normed * normed, features, lax.Precision.HIGHEST)
    result = inverse_ref[...] * (grad_normed - mean_factor - normed * projected)
    rows_out_ref[...] = jnp.stack(
        [result[:, t * features : (t + 1) * features] for t in range(rows_out_ref.shape[1])],
        axis=1,
    ).astype(BF16)


def local_gathered(
    homolog_features,
    subset_homolog_positions,
    first_side_matrix,
    second_side_matrix,
    final_mapping_matrix,
    final_offset_vector,
    upstream_sensitivity,
):
    prow_n, groups = lax.axis_size("prow"), lax.axis_size("px")
    owners = prow_n * groups * 2
    heads, tokens, features = homolog_features.shape
    seqs = subset_homolog_positions.shape[0]
    block_rows, block_cols, pair_width = upstream_sensitivity.shape
    proj = first_side_matrix.shape[1]
    flat = proj * proj
    packed = tokens * features
    shape = jax.ShapeDtypeStruct
    vmem = pl.BlockSpec(memory_space=pltpu.VMEM)
    smem = pl.BlockSpec(memory_space=pltpu.SMEM)
    params = pltpu.CompilerParams(vmem_limit_bytes=36 * 1024 * 1024)

    pairs = block_rows * block_cols
    length = seqs * packed // LANES
    hbm = pl.BlockSpec(memory_space=pltpu.HBM)
    normed, inverse, left_wide, left_one, right_one, offset, sent = pl.pallas_call(
        pick_kernel,
        out_shape=(
            shape((seqs, packed), F32),
            shape((seqs, packed), F32),
            shape((packed, tokens * LANES), BF16),
            shape((packed, LANES), BF16),
            shape((packed, LANES), BF16),
            shape((1, pair_width), F32),
            shape((pairs + length, LANES), BF16),
        ),
        in_specs=[hbm] * 6,
        out_specs=(vmem,) * 7,
        scratch_shapes=[
            pltpu.VMEM((1, seqs), jnp.int32),
            pltpu.VMEM((packed, heads), BF16),
            pltpu.VMEM((proj, features), BF16),
            pltpu.VMEM((proj, features), BF16),
            pltpu.SemaphoreType.DMA((6,)),
        ],
        compiler_params=pltpu.CompilerParams(vmem_limit_bytes=60 * 1024 * 1024),
        name="pick_rows",
    )(
        subset_homolog_positions.reshape(1, seqs),
        homolog_features.transpose(1, 2, 0).reshape(packed, heads),
        first_side_matrix.T,
        second_side_matrix.T,
        final_offset_vector.reshape(1, pair_width),
        upstream_sensitivity.reshape(pairs, pair_width),
    )

    def swapped_with(values, axis, size, mask):
        return lax.ppermute(values, axis, [(n, n ^ mask) for n in range(size)])

    messages = [sent] + [
        swapped_with(sent, "prow", prow_n, down) for down in range(1, prow_n)
    ]
    messages += [
        swapped_with(one, "px", groups, across) for across in range(1, groups) for one in messages
    ]
    offsets = [(down, across) for across in range(groups) for down in range(prow_n)]
    rows = jnp.stack([one[pairs:] for one in messages])
    theirs = lax.ppermute(rows, "pc", [(0, 1), (1, 0)])

    mapping = final_mapping_matrix.reshape(proj, proj, pair_width)
    mapping = mapping.swapaxes(0, 1).reshape(flat, pair_width)
    place = jnp.stack([lax.axis_index("prow"), lax.axis_index("px"), lax.axis_index("pc")])

    columns = groups * proj // tokens * block_cols
    cot, pulled = pl.pallas_call(
        functools.partial(pull_kernel, offsets),
        out_shape=(
            shape((prow_n, groups, pairs, pair_width), BF16),
            shape((prow_n, columns, block_rows * LANES), BF16),
        ),
        in_specs=[smem] + [vmem] * (1 + len(messages)),
        out_specs=(vmem,) * 2,
        compiler_params=params,
        cost_estimate=pl.CostEstimate(
            flops=2 * prow_n * groups * pairs * pair_width * flat,
            bytes_accessed=2 * prow_n * groups * pairs * (2 * pair_width + flat),
            transcendentals=0,
        ),
        name="pull_back",
    )(place, mapping.T, *messages)

    rows_all, expanded, swapped, outer, pair_delta = pl.pallas_call(
        functools.partial(outer_kernel, offsets),
        out_shape=(
            shape((owners * seqs, packed), BF16),
            shape((owners, seqs, tokens * LANES), BF16),
            shape((tokens * seqs, columns), BF16),
            shape((prow_n, groups * pairs, flat), BF16),
            shape(upstream_sensitivity.shape, BF16),
        ),
        in_specs=[smem] + [vmem] * 6,
        out_specs=(vmem,) * 5,
        scratch_shapes=[
            pltpu.VMEM((prow_n, groups, length, LANES), BF16),
            pltpu.VMEM((prow_n, groups, length, LANES), BF16),
            pltpu.VMEM((columns, tokens * seqs), BF16),
        ],
        compiler_params=params,
        cost_estimate=pl.CostEstimate(
            flops=2 * prow_n * groups * pairs * tokens * seqs * flat,
            bytes_accessed=2 * prow_n * groups * pairs * flat,
            transcendentals=0,
        ),
        name="outer_products",
    )(place, rows, theirs, mapping, left_wide, right_one, offset)
    grads, message = pl.pallas_call(
        back_kernel,
        out_shape=(
            shape((2, seqs, LANES), BF16),
            shape((flat + 2 * proj + seqs, LANES), BF16),
        ),
        in_specs=[smem] + [vmem] * 6,
        out_specs=(vmem,) * 2,
        scratch_shapes=[
            pltpu.VMEM((owners, seqs, LANES), BF16),
            pltpu.VMEM((groups * prow_n, seqs, LANES), BF16),
            pltpu.VMEM((columns, tokens * seqs), F32),
            pltpu.VMEM((pair_width, flat), F32),
        ],
        compiler_params=params,
        name="pull_further",
    )(place, rows_all, expanded, swapped, outer, cot, pulled)

    theirs = lax.ppermute(message, "pc", [(0, 1), (1, 0)])
    output_weight_gradient, left_weight_gradient, right_weight_gradient, alignment = pl.pallas_call(
        close_kernel,
        out_shape=(
            shape((flat, pair_width), F32),
            shape((proj, features), F32),
            shape((proj, features), F32),
            shape((seqs, tokens, features), BF16),
        ),
        in_specs=[vmem] * 7,
        out_specs=(vmem,) * 4,
        compiler_params=params,
        name="close",
    )(grads, message, theirs, normed, inverse, left_one, right_one)
    return (
        pair_delta,
        alignment,
        left_weight_gradient.T,
        right_weight_gradient.T,
        output_weight_gradient,
    )


def shapes_allow_gathering(
    mesh_shape, features, positions, first_side, second_side, mapping, offset, cot
):
    rows_n, cols_n = mesh_shape["prow"], mesh_shape["pcol"]
    parts = mesh_shape["rep"]
    tokens = features.shape[1] // (rows_n * cols_n)
    block_rows, block_cols = cot.shape[0] // (parts * rows_n), cot.shape[1] // cols_n
    proj, width = first_side.shape[1], cot.shape[2]
    return (
        cols_n % 2 == 0
        and cot.shape[1] * cot.shape[1] <= GATHERED_PAIRS
        and tokens * proj == LANES
        and tokens == 4
        and block_rows % tokens == 0
        and block_cols == rows_n * tokens == 16
        and rows_n & (rows_n - 1) == 0
        and cols_n & (cols_n - 1) == 0
        and width == LANES
        and features.shape[2] >= 2 * proj
        and positions.shape[0] // parts % 16 == 0
        and features.shape[2] * tokens % LANES == 0
    )


def solution(mesh):
    def run(local, over, columns, *args):
        tokens_split = P("rep", columns + ("prow",), None)
        pairs_split = P(("rep", "prow"), columns, None)
        return jax.shard_map(
            local,
            mesh=over,
            in_specs=(tokens_split, P("rep"), P(), P(), P(), P(), pairs_split),
            out_specs=(pairs_split, tokens_split, P("rep", None), P("rep", None), P("rep", None)),
            check_vma=False,
        )(*args)

    def program(*args):
        if not shapes_allow_gathering(mesh.shape, *args):
            return run(local_phased, mesh, ("pcol",), *args)
        reps, rows_n, cols_n = (mesh.shape[name] for name in ("rep", "prow", "pcol"))
        chips = Mesh(
            mesh.devices.reshape(reps, rows_n, cols_n // 2, 2), ("rep", "prow", "px", "pc")
        )
        return run(local_gathered, chips, ("px", "pc"), *args)

    return program
```

```python
import functools

import jax
import jax.numpy as jnp
from jax import lax
from jax.experimental import pallas as pl
from jax.experimental.pallas import tpu as pltpu
from jax.sharding import Mesh
from jax.sharding import PartitionSpec as P

BF16, F32 = jnp.bfloat16, jnp.float32
LANES = 128
GATHERED_PAIRS = 4096

PAIRS_AT_ONCE = 1024


def normalize(values):
    values = values.astype(jnp.float32)
    mean_factor = jnp.mean(values, axis=-1, keepdims=True)
    centered = values - mean_factor
    variance = jnp.mean(centered * centered, axis=-1, keepdims=True)
    inverse_spread = lax.rsqrt(variance + 1e-05)
    return (centered * inverse_spread, inverse_spread)


def transposed(rows_n, cols_n):
    return [
        (r * cols_n + c, c * rows_n + r) for r in range(rows_n) for c in range(cols_n)
    ]


def spread(values, axes, count):
    return lax.all_to_all(jnp.broadcast_to(values[None], (count,) + values.shape), axes, 0, 0)


def local_phased(
    homolog_features,
    subset_homolog_positions,
    first_side_matrix,
    second_side_matrix,
    final_mapping_matrix,
    final_offset_vector,
    upstream_sensitivity,
):
    axes = ("prow", "pcol")
    rows_n, cols_n = lax.axis_size("prow"), lax.axis_size("pcol")
    devices = rows_n * cols_n
    seq_count = subset_homolog_positions.shape[0]
    tokens, features = homolog_features.shape[1:]
    row_count, col_count, pair_width = upstream_sensitivity.shape
    proj = first_side_matrix.shape[1]
    flat = proj * proj
    to_rows = transposed(rows_n, cols_n)
    to_tokens = [(target, source) for source, target in to_rows]

    picked = jnp.take(homolog_features, subset_homolog_positions, axis=0)
    packed = picked.reshape(seq_count, tokens * features)
    row_own = lax.ppermute(packed, axes, to_rows)
    col_all = spread(packed, "prow", rows_n)
    row_all = spread(row_own, "pcol", cols_n)

    def side_of(chunks, count, matrix):
        chunks = chunks.reshape(count // tokens, seq_count, tokens, features)
        chunks = chunks.transpose(1, 0, 2, 3).reshape(seq_count, count, features)
        normed_low = normalize(chunks)[0].astype(jnp.bfloat16)
        side = jnp.einsum("stc,cp->stp", normed_low, matrix, preferred_element_type=jnp.float32)
        return normed_low, side.astype(jnp.bfloat16)

    row_normed, left = side_of(row_all, row_count, first_side_matrix)
    col_normed, right = side_of(col_all, col_count, second_side_matrix)

    def block_step(left_blk, cot_blk):
        rows = left_blk.shape[1]
        outer = jnp.einsum("sip,sjq->ijpq", left_blk, right, preferred_element_type=jnp.float32)
        outer = (outer / seq_count).astype(jnp.bfloat16).reshape(rows * col_count, flat)
        update = jnp.dot(outer, final_mapping_matrix, preferred_element_type=jnp.float32)
        update = (update + final_offset_vector).astype(jnp.bfloat16)
        cot_flat = cot_blk.reshape(rows * col_count, pair_width)
        grad_out = jnp.dot(outer.T, cot_flat, preferred_element_type=jnp.float32)
        grad_outer = jnp.dot(cot_flat, final_mapping_matrix.T, preferred_element_type=jnp.float32)
        grad_outer = grad_outer.astype(jnp.bfloat16).reshape(rows, col_count, proj, proj)
        grad_left = jnp.einsum(
            "ijpq,sjq->sip", grad_outer, right, preferred_element_type=jnp.float32
        )
        grad_right = jnp.einsum(
            "ijpq,sip->sjq", grad_outer, left_blk, preferred_element_type=jnp.float32
        )
        return update.reshape(rows, col_count, pair_width), grad_out, grad_left, grad_right

    block = max(1, min(row_count, PAIRS_AT_ONCE // col_count))
    blocks = row_count // block
    if blocks == 1:
        update, grad_out, grad_left, grad_right = block_step(left, upstream_sensitivity)
    else:
        def step(totals, inputs):
            update, grad_out, grad_left, grad_right = block_step(*inputs)
            return (totals[0] + grad_out, totals[1] + grad_right), (update, grad_left)

        (grad_out, grad_right), (update, grad_left) = lax.scan(
            step,
            (
                jnp.zeros((flat, pair_width), jnp.float32),
                jnp.zeros((seq_count, col_count, proj), jnp.float32),
            ),
            (
                left.reshape(seq_count, blocks, block, proj).transpose(1, 0, 2, 3),
                upstream_sensitivity.reshape(blocks, block, col_count, pair_width),
            ),
        )
        grad_left = grad_left.transpose(1, 0, 2, 3).reshape(seq_count, row_count, proj)
    pair_delta = update.reshape(row_count, col_count, pair_width)

    grad_left = (grad_left / seq_count).astype(jnp.bfloat16)
    grad_right = (grad_right / seq_count).astype(jnp.bfloat16)

    def weight_part(normed, grads):
        return jnp.einsum("stc,stp->cp", normed, grads, preferred_element_type=jnp.float32)

    side_part = jnp.concatenate(
        [weight_part(row_normed, grad_left), weight_part(col_normed, grad_right)], axis=1
    )
    share_rows = flat // devices
    side_rows = -(-features * 2 * proj // (pair_width * devices))
    side_flat = side_part.reshape(-1, pair_width)
    side_flat = jnp.pad(side_flat, ((0, side_rows * devices - side_flat.shape[0]), (0, 0)))
    shares = jnp.concatenate(
        [
            grad_out.reshape(devices, share_rows, pair_width),
            side_flat.reshape(devices, side_rows, pair_width),
        ],
        axis=1,
    ).astype(jnp.bfloat16)
    shares = lax.all_to_all(shares, axes, 0, 0)

    def chunks_of(grads, count):
        grads = grads.reshape(seq_count, count // tokens, tokens * proj)
        return grads.transpose(1, 0, 2)

    left_back = lax.all_to_all(chunks_of(grad_left, row_count), "pcol", 0, 0)
    right_back = lax.all_to_all(chunks_of(grad_right, col_count), "prow", 0, 0)
    left_back = jnp.sum(left_back.astype(jnp.float32), axis=0).astype(jnp.bfloat16)
    right_back = jnp.sum(right_back.astype(jnp.float32), axis=0).astype(jnp.bfloat16)
    left_back = lax.ppermute(left_back, axes, to_tokens)

    share = jnp.sum(shares.astype(jnp.float32), axis=0).astype(jnp.bfloat16)
    message = spread(share, axes, devices)
    output_weight_gradient = (
        message[:, :share_rows].reshape(flat, pair_width).astype(jnp.float32)
    )
    side = message[:, share_rows:].reshape(-1, pair_width).astype(jnp.float32)
    side = side[: features * 2 * proj // pair_width].reshape(features, 2 * proj)
    left_weight_gradient, right_weight_gradient = side[:, :proj], side[:, proj:]

    normed, inverse_spread = normalize(picked)
    both = jnp.concatenate(
        [
            left_back.reshape(seq_count, tokens, proj),
            right_back.reshape(seq_count, tokens, proj),
        ],
        axis=-1,
    )
    sides = jnp.concatenate([first_side_matrix, second_side_matrix], axis=1)
    grad_normed = jnp.einsum("stp,cp->stc", both, sides, preferred_element_type=jnp.float32)
    mean_factor = jnp.mean(grad_normed, axis=-1, keepdims=True)
    projected = jnp.mean(grad_normed * normed, axis=-1, keepdims=True)
    alignment_gradient = (
        inverse_spread * (grad_normed - mean_factor - normed * projected)
    ).astype(jnp.bfloat16)
    return (
        pair_delta,
        alignment_gradient,
        left_weight_gradient,
        right_weight_gradient,
        output_weight_gradient,
    )


def dot(x, y, contract=(1, 0), precision=None):
    return lax.dot_general(
        x, y, (((contract[0],), (contract[1],)), ((), ())),
        precision=precision, preferred_element_type=F32,
    )


def lane_ids(shape):
    return lax.broadcasted_iota(jnp.int32, shape, len(shape) - 1)


def fold_tokens(parts):
    quarter = LANES // 4
    chunk = lane_ids(parts[0].shape) // quarter
    first, even = chunk < 2, chunk % 2 == 0
    halves = [
        jnp.where(first, parts[t], parts[t + 2])
        + pltpu.roll(jnp.where(first, parts[t + 2], parts[t]), 2 * quarter, 1)
        for t in range(2)
    ]
    other = jnp.where(even, halves[1], halves[0])
    moved = jnp.where(even, pltpu.roll(other, 3 * quarter, 1), pltpu.roll(other, quarter, 1))
    return jnp.where(even, halves[0], halves[1]) + moved


def group_mean(x, group, precision):
    lanes = x.shape[1]
    rows_id = lax.broadcasted_iota(jnp.int32, (lanes, lanes), 0) // group
    cols_id = lax.broadcasted_iota(jnp.int32, (lanes, lanes), 1) // group
    block = jnp.where(rows_id == cols_id, 1.0 / group, 0.0).astype(x.dtype)
    return dot(x, block, precision=precision)


def pick_kernel(
    positions_ref,
    features_ref,
    cot_ref,
    normed_ref,
    inverse_ref,
    message_ref,
    positions,
    features,
    in_sems,
):
    pairs = cot_ref.shape[0]
    inputs = [
        pltpu.make_async_copy(source, target, in_sems.at[n])
        for n, (source, target) in enumerate(
            [
                (positions_ref, positions),
                (features_ref, features),
                (cot_ref, message_ref.at[pl.ds(0, pairs)]),
            ]
        )
    ]
    for copy in inputs:
        copy.start()
    heads = features_ref.shape[1]
    seqs, packed = normed_ref.shape
    channels = packed // 4
    for copy in inputs:
        copy.wait()
    wanted = positions[...] == lax.broadcasted_iota(jnp.int32, (heads, seqs), 0)
    chosen = dot(wanted.astype(BF16), features[...], contract=(0, 1))
    mean_factor = group_mean(chosen.astype(BF16), channels, None)
    centered = chosen - mean_factor
    variance = group_mean(centered * centered, channels, lax.Precision.HIGHEST)
    inverse = lax.rsqrt(variance + 1e-05)
    normed = centered * inverse
    for n in range(packed // LANES):
        message_ref[pairs + n * seqs : pairs + (n + 1) * seqs] = normed[
            :, n * LANES : (n + 1) * LANES
        ].astype(BF16)
    normed_ref[...] = normed
    inverse_ref[...] = inverse


def setup_kernel(
    first_ref,
    own_ref,
    mapping_ref,
    turned_mapping_ref,
    left_ref,
    right_ref,
    offset_ref,
    first_out_ref,
    own_out_ref,
    left_wide_ref,
    left_one_ref,
    right_one_ref,
    offset_out_ref,
):
    del mapping_ref, turned_mapping_ref
    first_out_ref[...] = first_ref[...]
    own_out_ref[...] = own_ref[...]
    offset_out_ref[...] = offset_ref[...]
    proj, channels = left_ref.shape
    tokens = left_one_ref.shape[0] // channels
    repeat = lane_ids((proj, LANES)) % proj
    repeat = (repeat == lax.broadcasted_iota(jnp.int32, (proj, LANES), 0)).astype(BF16)
    left_row = dot(left_ref[...], repeat, contract=(0, 0))
    right_row = dot(right_ref[...], repeat, contract=(0, 0))
    slot = lane_ids(left_row.shape) // proj
    nothing = jnp.zeros(left_row.shape, BF16)
    for t in range(tokens):
        here = slice(t * channels, (t + 1) * channels)
        left_one_ref[here] = jnp.where(slot == t, left_row, 0.0).astype(BF16)
        right_one_ref[here] = jnp.where(slot == t, right_row, 0.0).astype(BF16)
        for other in range(tokens):
            left_wide_ref[here, other * LANES : (other + 1) * LANES] = (
                left_row.astype(BF16) if other == t else nothing
            )


def place_blocks(place_ref, offsets, blocks, out_ref):
    for (down, across), block in zip(offsets, blocks, strict=True):
        out_ref[place_ref[0] ^ down, place_ref[1] ^ across] = block


def pull_kernel(offsets, place_ref, mapping_ref, *refs):
    *message_refs, cot_ref, pulled_ref = refs
    prow_n, groups, pairs, pair_width = cot_ref.shape
    highs = mapping_ref.shape[1] // LANES
    block_rows = pulled_ref.shape[2] // LANES
    block_cols = pairs // block_rows
    place_blocks(place_ref, offsets, [ref[:pairs] for ref in message_refs], cot_ref)

    def step(r, carry):
        grad = dot(cot_ref[r].reshape(groups * pairs, pair_width), mapping_ref[...])
        for g in range(groups):
            for t in range(block_rows):
                start = (g * block_rows + t) * block_cols
                lanes = slice(t * LANES, (t + 1) * LANES)
                for h in range(highs):
                    there = slice((g * highs + h) * block_cols, (g * highs + h + 1) * block_cols)
                    pulled_ref[r, there, lanes] = grad[
                        start : start + block_cols, h * LANES : (h + 1) * LANES
                    ].astype(BF16)
        return carry

    lax.fori_loop(0, prow_n, step, 0)


def outer_kernel(
    offsets,
    place_ref,
    mine_from_ref,
    theirs_from_ref,
    mapping_ref,
    left_ref,
    right_ref,
    offset_ref,
    rows_ref,
    expanded,
    swapped,
    outer_ref,
    pair_ref,
    mine_ref,
    theirs_ref,
    turned,
):
    for source, target in ((mine_from_ref, mine_ref), (theirs_from_ref, theirs_ref)):
        place_blocks(place_ref, offsets, [source[n] for n in range(source.shape[0])], target)
    prow_n, groups = mine_ref.shape[:2]
    block_rows, block_cols, pair_width = pair_ref.shape
    owners, seqs = expanded.shape[:2]
    packed = left_ref.shape[0]
    tokens = left_ref.shape[1] // LANES
    proj = LANES // tokens
    highs = proj // tokens
    span = highs * block_cols
    own_row, own_group, core = place_ref[0], place_ref[1], place_ref[2]

    def rows_of(ref, g, r):
        return jnp.concatenate(
            [ref[r, g, n * seqs : (n + 1) * seqs] for n in range(packed // LANES)], axis=1
        )

    places = [(g, r) for g in range(groups) for r in range(prow_n)]
    rows_mine = [rows_of(mine_ref, g, r) for g, r in places]
    rows_all = jnp.concatenate(
        rows_mine + [rows_of(theirs_ref, g, r) for g, r in places], axis=0
    )
    rows_ref[...] = rows_all
    wide_left = dot(rows_all, left_ref[...]).astype(BF16)
    for n, owner in enumerate(owner_order(places, prow_n, core)):
        expanded[owner] = wide_left[n * seqs : (n + 1) * seqs]

    side_rows = []
    for g in range(groups):
        chunks = rows_mine[g * prow_n : (g + 1) * prow_n]
        side_rows.append(
            jnp.concatenate([dot(x, right_ref[...]).astype(BF16) for x in chunks], axis=1)
        )
    right = dot(jnp.concatenate(side_rows, axis=0), shuffle_matrix(block_cols, proj, tokens))
    for g in range(groups):
        for l in range(tokens):
            swapped[l * seqs : (l + 1) * seqs, g * span : (g + 1) * span] = (
                right[g * seqs : (g + 1) * seqs, l * span : (l + 1) * span] * (1.0 / seqs)
            ).astype(BF16)
    turned[...] = swapped[...].astype(F32).T.astype(BF16)

    def step(row, carry):
        made = dot(turned[...], left_block(expanded, row, owners // prow_n, tokens))
        for g in range(groups):
            for t in range(block_rows):
                start = (g * block_rows + t) * block_cols
                lanes = slice(t * LANES, (t + 1) * LANES)
                for h in range(highs):
                    there = slice((g * highs + h) * block_cols, (g * highs + h + 1) * block_cols)
                    outer_ref[row, start : start + block_cols, h * LANES : (h + 1) * LANES] = made[
                        there, lanes
                    ].astype(BF16)
        return carry

    lax.fori_loop(0, prow_n, step, 0)
    share = block_rows * block_cols
    mine = outer_ref[own_row, pl.ds(pl.multiple_of(own_group * share, share), share)]
    update = dot(mine, mapping_ref[...]) + offset_ref[...]
    pair_ref[...] = update.astype(BF16).reshape(pair_ref.shape)


def owner_order(places, prow_n, core):
    mine = [(2 * g + core) * prow_n + r for g, r in places]
    return mine + [(2 * g + 1 - core) * prow_n + r for g, r in places]


def shuffle_matrix(block_cols, proj, tokens):
    wide, highs = block_cols * proj, proj // tokens
    source = lax.broadcasted_iota(jnp.int32, (wide, wide), 0)
    target = lax.broadcasted_iota(jnp.int32, (wide, wide), 1)
    jj, qh = target % block_cols, target // block_cols % highs
    ql = target // (highs * block_cols)
    return (source == jj * proj + qh * tokens + ql).astype(BF16)


def left_block(expanded, row, step_owners, tokens):
    ahead = jnp.concatenate([expanded[row * step_owners + o] for o in range(step_owners)], axis=1)
    low = lane_ids(ahead.shape) % LANES // (LANES // tokens)
    return jnp.concatenate(
        [jnp.where(low == l, ahead, jnp.zeros_like(ahead)) for l in range(tokens)], axis=0
    )


def back_kernel(
    place_ref,
    rows_ref,
    expanded,
    swapped,
    outer_ref,
    cot_ref,
    pulled_ref,
    grads_ref,
    message_ref,
    left_back,
    right_back,
    sums,
    weights,
):
    prow_n, groups, pairs, pair_width = cot_ref.shape
    owners, seqs = left_back.shape[:2]
    tokens = swapped.shape[0] // seqs
    proj = LANES // tokens
    highs = proj // tokens
    span = swapped.shape[1] // groups
    block_cols = span // highs
    step_owners = owners // prow_n
    own_row, own_group, core = place_ref[0], place_ref[1], place_ref[2]
    places = [(g, r) for g in range(groups) for r in range(prow_n)]
    order = owner_order(places, prow_n, core)

    sums[...] = jnp.zeros_like(sums)
    weights[...] = jnp.zeros_like(weights)

    def step(row, carry):
        block = left_block(expanded, row, step_owners, tokens)
        cot = cot_ref[row].reshape(groups * pairs, pair_width)
        weights[...] += dot(cot, outer_ref[row], contract=(0, 0))
        pulled = pulled_ref[row]
        back = dot(swapped[...], pulled)
        low = lane_ids((seqs, back.shape[1])) % LANES // proj
        back = functools.reduce(
            jnp.add,
            [
                jnp.where(low == l, back[l * seqs : (l + 1) * seqs], 0.0)
                for l in range(tokens)
            ],
        )
        for o in range(step_owners):
            parts = [
                back[:, (o * tokens + t) * LANES : (o * tokens + t + 1) * LANES]
                for t in range(tokens)
            ]
            left_back[row * step_owners + o] = fold_tokens(parts).astype(BF16)
        sums[...] += dot(pulled, block, contract=(1, 1))
        return carry

    lax.fori_loop(0, prow_n, step, 0)

    back = (sums[...].T * (1.0 / seqs)).astype(BF16)
    back = jnp.concatenate(
        [
            jnp.concatenate(
                [
                    back[l * seqs : (l + 1) * seqs, g * span : (g + 1) * span]
                    for l in range(tokens)
                ],
                axis=1,
            )
            for g in range(groups)
        ],
        axis=0,
    )
    shuffle = shuffle_matrix(block_cols, proj, tokens)
    back = dot(back, shuffle, contract=(1, 1)).astype(BF16)
    for g, r in places:
        right_back[g * prow_n + r] = back[g * seqs : (g + 1) * seqs, r * LANES : (r + 1) * LANES]

    def side(grads, rows):
        total = dot(grads, rows, contract=(0, 0))
        features = rows.shape[1] // tokens
        return functools.reduce(
            jnp.add,
            [
                total[t * proj : (t + 1) * proj, t * features : (t + 1) * features]
                for t in range(tokens)
            ],
        )

    left_side = side(
        jnp.concatenate([left_back[owner] for owner in order], axis=0), rows_ref[...]
    )
    columns = groups * prow_n * seqs
    right_side = side(right_back[...].reshape(columns, LANES), rows_ref[:columns])
    both = jnp.concatenate([left_side, right_side], axis=0).astype(BF16)
    both = jnp.concatenate([both, jnp.zeros_like(both)], axis=1)

    flat = weights.shape[1]
    outer_f = weights[...].T
    weight_rows = outer_f.reshape(proj, proj, pair_width).swapaxes(0, 1).reshape(flat, pair_width)

    message_ref[:flat] = weight_rows.astype(BF16)
    message_ref[flat : flat + 2 * proj] = both
    message_ref[flat + 2 * proj :] = left_back[(2 * own_group + 1 - core) * prow_n + own_row]
    grads_ref[0] = left_back[(2 * own_group + core) * prow_n + own_row]
    grads_ref[1] = right_back[own_group * prow_n + own_row]


def close_kernel(
    grads_ref,
    own_ref,
    message_ref,
    normed_ref,
    inverse_ref,
    left_ref,
    right_ref,
    out_ref,
    left_out_ref,
    right_out_ref,
    rows_out_ref,
):
    flat = out_ref.shape[0]
    proj, features = left_out_ref.shape
    out_ref[...] = own_ref[:flat].astype(F32) + message_ref[:flat].astype(F32)
    sides = slice(flat, flat + 2 * proj)
    both = own_ref[sides, :features].astype(F32) + message_ref[sides, :features].astype(F32)
    left_out_ref[...] = both[:proj]
    right_out_ref[...] = both[proj:]
    left_back = grads_ref[0].astype(F32) + message_ref[flat + 2 * proj :].astype(F32)
    grad_normed = dot(left_back.astype(BF16), left_ref[...], contract=(1, 1))
    grad_normed = grad_normed + dot(grads_ref[1], right_ref[...], contract=(1, 1))
    normed = normed_ref[...]
    mean_factor = group_mean(grad_normed, features, lax.Precision.HIGHEST)
    projected = group_mean(grad_normed * normed, features, lax.Precision.HIGHEST)
    result = inverse_ref[...] * (grad_normed - mean_factor - normed * projected)
    rows_out_ref[...] = jnp.stack(
        [result[:, t * features : (t + 1) * features] for t in range(rows_out_ref.shape[1])],
        axis=1,
    ).astype(BF16)


def local_gathered(
    homolog_features,
    subset_homolog_positions,
    first_side_matrix,
    second_side_matrix,
    final_mapping_matrix,
    final_offset_vector,
    upstream_sensitivity,
):
    prow_n, groups = lax.axis_size("prow"), lax.axis_size("px")
    owners = prow_n * groups * 2
    heads, tokens, features = homolog_features.shape
    seqs = subset_homolog_positions.shape[0]
    block_rows, block_cols, pair_width = upstream_sensitivity.shape
    proj = first_side_matrix.shape[1]
    flat = proj * proj
    packed = tokens * features
    shape = jax.ShapeDtypeStruct
    vmem = pl.BlockSpec(memory_space=pltpu.VMEM)
    smem = pl.BlockSpec(memory_space=pltpu.SMEM)
    params = pltpu.CompilerParams(vmem_limit_bytes=36 * 1024 * 1024)

    pairs = block_rows * block_cols
    length = seqs * packed // LANES
    hbm = pl.BlockSpec(memory_space=pltpu.HBM)
    normed, inverse, sent = pl.pallas_call(
        pick_kernel,
        out_shape=(
            shape((seqs, packed), F32),
            shape((seqs, packed), F32),
            shape((pairs + length, LANES), BF16),
        ),
        in_specs=[hbm] * 3,
        out_specs=(vmem,) * 3,
        scratch_shapes=[
            pltpu.VMEM((1, seqs), jnp.int32),
            pltpu.VMEM((packed, heads), BF16),
            pltpu.SemaphoreType.DMA((3,)),
        ],
        compiler_params=pltpu.CompilerParams(vmem_limit_bytes=60 * 1024 * 1024),
        name="pick_rows",
    )(
        subset_homolog_positions.reshape(1, seqs),
        homolog_features.transpose(1, 2, 0).reshape(packed, heads),
        upstream_sensitivity.reshape(pairs, pair_width),
    )

    mapping = final_mapping_matrix.reshape(proj, proj, pair_width)
    mapping = mapping.swapaxes(0, 1).reshape(flat, pair_width)
    turned_mapping = mapping.T

    def swapped_with(values, axis, size, mask):
        return lax.ppermute(values, axis, [(n, n ^ mask) for n in range(size)])

    messages = [sent] + [
        swapped_with(sent, "prow", prow_n, down) for down in range(1, prow_n)
    ]
    messages[1], own, left_wide, left_one, right_one, offset = pl.pallas_call(
        setup_kernel,
        out_shape=(
            shape(sent.shape, BF16),
            shape(sent.shape, BF16),
            shape((packed, tokens * LANES), BF16),
            shape((packed, LANES), BF16),
            shape((packed, LANES), BF16),
            shape((1, pair_width), F32),
        ),
        in_specs=[vmem] * 7,
        out_specs=(vmem,) * 6,
        compiler_params=params,
        name="setup",
    )(
        messages[1],
        sent,
        mapping,
        turned_mapping,
        first_side_matrix.T,
        second_side_matrix.T,
        final_offset_vector.reshape(1, pair_width),
    )
    messages += [
        swapped_with(one, "px", groups, across) for across in range(1, groups) for one in messages
    ]
    messages[0] = own
    offsets = [(down, across) for across in range(groups) for down in range(prow_n)]
    rows = jnp.stack([one[pairs:] for one in messages])
    theirs = lax.ppermute(rows, "pc", [(0, 1), (1, 0)])

    place = jnp.stack([lax.axis_index("prow"), lax.axis_index("px"), lax.axis_index("pc")])

    columns = groups * proj // tokens * block_cols
    cot, pulled = pl.pallas_call(
        functools.partial(pull_kernel, offsets),
        out_shape=(
            shape((prow_n, groups, pairs, pair_width), BF16),
            shape((prow_n, columns, block_rows * LANES), BF16),
        ),
        in_specs=[smem] + [vmem] * (1 + len(messages)),
        out_specs=(vmem,) * 2,
        compiler_params=params,
        cost_estimate=pl.CostEstimate(
            flops=2 * prow_n * groups * pairs * pair_width * flat,
            bytes_accessed=2 * prow_n * groups * pairs * (2 * pair_width + flat),
            transcendentals=0,
        ),
        name="pull_back",
    )(place, turned_mapping, *messages)

    rows_all, expanded, swapped, outer, pair_delta = pl.pallas_call(
        functools.partial(outer_kernel, offsets),
        out_shape=(
            shape((owners * seqs, packed), BF16),
            shape((owners, seqs, tokens * LANES), BF16),
            shape((tokens * seqs, columns), BF16),
            shape((prow_n, groups * pairs, flat), BF16),
            shape(upstream_sensitivity.shape, BF16),
        ),
        in_specs=[smem] + [vmem] * 6,
        out_specs=(vmem,) * 5,
        scratch_shapes=[
            pltpu.VMEM((prow_n, groups, length, LANES), BF16),
            pltpu.VMEM((prow_n, groups, length, LANES), BF16),
            pltpu.VMEM((columns, tokens * seqs), BF16),
        ],
        compiler_params=params,
        cost_estimate=pl.CostEstimate(
            flops=2 * prow_n * groups * pairs * tokens * seqs * flat,
            bytes_accessed=2 * prow_n * groups * pairs * flat,
            transcendentals=0,
        ),
        name="outer_products",
    )(place, rows, theirs, mapping, left_wide, right_one, offset)
    grads, message = pl.pallas_call(
        back_kernel,
        out_shape=(
            shape((2, seqs, LANES), BF16),
            shape((flat + 2 * proj + seqs, LANES), BF16),
        ),
        in_specs=[smem] + [vmem] * 6,
        out_specs=(vmem,) * 2,
        scratch_shapes=[
            pltpu.VMEM((owners, seqs, LANES), BF16),
            pltpu.VMEM((groups * prow_n, seqs, LANES), BF16),
            pltpu.VMEM((columns, tokens * seqs), F32),
            pltpu.VMEM((pair_width, flat), F32),
        ],
        compiler_params=params,
        name="pull_further",
    )(place, rows_all, expanded, swapped, outer, cot, pulled)

    theirs = lax.ppermute(message, "pc", [(0, 1), (1, 0)])
    output_weight_gradient, left_weight_gradient, right_weight_gradient, alignment = pl.pallas_call(
        close_kernel,
        out_shape=(
            shape((flat, pair_width), F32),
            shape((proj, features), F32),
            shape((proj, features), F32),
            shape((seqs, tokens, features), BF16),
        ),
        in_specs=[vmem] * 7,
        out_specs=(vmem,) * 4,
        compiler_params=params,
        name="close",
    )(grads, message, theirs, normed, inverse, left_one, right_one)
    return (
        pair_delta,
        alignment,
        left_weight_gradient.T,
        right_weight_gradient.T,
        output_weight_gradient,
    )


def shapes_allow_gathering(
    mesh_shape, features, positions, first_side, second_side, mapping, offset, cot
):
    rows_n, cols_n = mesh_shape["prow"], mesh_shape["pcol"]
    parts = mesh_shape["rep"]
    tokens = features.shape[1] // (rows_n * cols_n)
    block_rows, block_cols = cot.shape[0] // (parts * rows_n), cot.shape[1] // cols_n
    proj, width = first_side.shape[1], cot.shape[2]
    return (
        cols_n % 2 == 0
        and cot.shape[1] * cot.shape[1] <= GATHERED_PAIRS
        and tokens * proj == LANES
        and tokens == 4
        and block_rows % tokens == 0
        and block_cols == rows_n * tokens == 16
        and rows_n & (rows_n - 1) == 0
        and cols_n & (cols_n - 1) == 0
        and width == LANES
        and features.shape[2] >= 2 * proj
        and positions.shape[0] // parts % 16 == 0
        and features.shape[2] * tokens % LANES == 0
    )


def solution(mesh):
    def run(local, over, columns, *args):
        tokens_split = P("rep", columns + ("prow",), None)
        pairs_split = P(("rep", "prow"), columns, None)
        return jax.shard_map(
            local,
            mesh=over,
            in_specs=(tokens_split, P("rep"), P(), P(), P(), P(), pairs_split),
            out_specs=(pairs_split, tokens_split, P("rep", None), P("rep", None), P("rep", None)),
            check_vma=False,
        )(*args)

    def program(*args):
        if not shapes_allow_gathering(mesh.shape, *args):
            return run(local_phased, mesh, ("pcol",), *args)
        reps, rows_n, cols_n = (mesh.shape[name] for name in ("rep", "prow", "pcol"))
        chips = Mesh(
            mesh.devices.reshape(reps, rows_n, cols_n // 2, 2), ("rep", "prow", "px", "pc")
        )
        return run(local_gathered, chips, ("px", "pc"), *args)

    return program
```

```python
import functools

import jax
import jax.numpy as jnp
from jax import lax
from jax.experimental import pallas as pl
from jax.experimental.pallas import tpu as pltpu
from jax.sharding import Mesh
from jax.sharding import PartitionSpec as P

BF16, F32 = jnp.bfloat16, jnp.float32
LANES = 128
GATHERED_PAIRS = 4096

PAIRS_AT_ONCE = 1024


def normalize(values):
    values = values.astype(jnp.float32)
    mean_factor = jnp.mean(values, axis=-1, keepdims=True)
    centered = values - mean_factor
    variance = jnp.mean(centered * centered, axis=-1, keepdims=True)
    inverse_spread = lax.rsqrt(variance + 1e-05)
    return (centered * inverse_spread, inverse_spread)


def transposed(rows_n, cols_n):
    return [
        (r * cols_n + c, c * rows_n + r) for r in range(rows_n) for c in range(cols_n)
    ]


def spread(values, axes, count):
    return lax.all_to_all(jnp.broadcast_to(values[None], (count,) + values.shape), axes, 0, 0)


def local_phased(
    homolog_features,
    subset_homolog_positions,
    first_side_matrix,
    second_side_matrix,
    final_mapping_matrix,
    final_offset_vector,
    upstream_sensitivity,
):
    axes = ("prow", "pcol")
    rows_n, cols_n = lax.axis_size("prow"), lax.axis_size("pcol")
    devices = rows_n * cols_n
    seq_count = subset_homolog_positions.shape[0]
    tokens, features = homolog_features.shape[1:]
    row_count, col_count, pair_width = upstream_sensitivity.shape
    proj = first_side_matrix.shape[1]
    flat = proj * proj
    to_rows = transposed(rows_n, cols_n)
    to_tokens = [(target, source) for source, target in to_rows]

    picked = jnp.take(homolog_features, subset_homolog_positions, axis=0)
    packed = picked.reshape(seq_count, tokens * features)
    row_own = lax.ppermute(packed, axes, to_rows)
    col_all = spread(packed, "prow", rows_n)
    row_all = spread(row_own, "pcol", cols_n)

    def side_of(chunks, count, matrix):
        chunks = chunks.reshape(count // tokens, seq_count, tokens, features)
        chunks = chunks.transpose(1, 0, 2, 3).reshape(seq_count, count, features)
        normed_low = normalize(chunks)[0].astype(jnp.bfloat16)
        side = jnp.einsum("stc,cp->stp", normed_low, matrix, preferred_element_type=jnp.float32)
        return normed_low, side.astype(jnp.bfloat16)

    row_normed, left = side_of(row_all, row_count, first_side_matrix)
    col_normed, right = side_of(col_all, col_count, second_side_matrix)

    def block_step(left_blk, cot_blk):
        rows = left_blk.shape[1]
        outer = jnp.einsum("sip,sjq->ijpq", left_blk, right, preferred_element_type=jnp.float32)
        outer = (outer / seq_count).astype(jnp.bfloat16).reshape(rows * col_count, flat)
        update = jnp.dot(outer, final_mapping_matrix, preferred_element_type=jnp.float32)
        update = (update + final_offset_vector).astype(jnp.bfloat16)
        cot_flat = cot_blk.reshape(rows * col_count, pair_width)
        grad_out = jnp.dot(outer.T, cot_flat, preferred_element_type=jnp.float32)
        grad_outer = jnp.dot(cot_flat, final_mapping_matrix.T, preferred_element_type=jnp.float32)
        grad_outer = grad_outer.astype(jnp.bfloat16).reshape(rows, col_count, proj, proj)
        grad_left = jnp.einsum(
            "ijpq,sjq->sip", grad_outer, right, preferred_element_type=jnp.float32
        )
        grad_right = jnp.einsum(
            "ijpq,sip->sjq", grad_outer, left_blk, preferred_element_type=jnp.float32
        )
        return update.reshape(rows, col_count, pair_width), grad_out, grad_left, grad_right

    block = max(1, min(row_count, PAIRS_AT_ONCE // col_count))
    blocks = row_count // block
    if blocks == 1:
        update, grad_out, grad_left, grad_right = block_step(left, upstream_sensitivity)
    else:
        def step(totals, inputs):
            update, grad_out, grad_left, grad_right = block_step(*inputs)
            return (totals[0] + grad_out, totals[1] + grad_right), (update, grad_left)

        (grad_out, grad_right), (update, grad_left) = lax.scan(
            step,
            (
                jnp.zeros((flat, pair_width), jnp.float32),
                jnp.zeros((seq_count, col_count, proj), jnp.float32),
            ),
            (
                left.reshape(seq_count, blocks, block, proj).transpose(1, 0, 2, 3),
                upstream_sensitivity.reshape(blocks, block, col_count, pair_width),
            ),
        )
        grad_left = grad_left.transpose(1, 0, 2, 3).reshape(seq_count, row_count, proj)
    pair_delta = update.reshape(row_count, col_count, pair_width)

    grad_left = (grad_left / seq_count).astype(jnp.bfloat16)
    grad_right = (grad_right / seq_count).astype(jnp.bfloat16)

    def weight_part(normed, grads):
        return jnp.einsum("stc,stp->cp", normed, grads, preferred_element_type=jnp.float32)

    side_part = jnp.concatenate(
        [weight_part(row_normed, grad_left), weight_part(col_normed, grad_right)], axis=1
    )
    share_rows = flat // devices
    side_rows = -(-features * 2 * proj // (pair_width * devices))
    side_flat = side_part.reshape(-1, pair_width)
    side_flat = jnp.pad(side_flat, ((0, side_rows * devices - side_flat.shape[0]), (0, 0)))
    shares = jnp.concatenate(
        [
            grad_out.reshape(devices, share_rows, pair_width),
            side_flat.reshape(devices, side_rows, pair_width),
        ],
        axis=1,
    ).astype(jnp.bfloat16)
    shares = lax.all_to_all(shares, axes, 0, 0)

    def chunks_of(grads, count):
        grads = grads.reshape(seq_count, count // tokens, tokens * proj)
        return grads.transpose(1, 0, 2)

    left_back = lax.all_to_all(chunks_of(grad_left, row_count), "pcol", 0, 0)
    right_back = lax.all_to_all(chunks_of(grad_right, col_count), "prow", 0, 0)
    left_back = jnp.sum(left_back.astype(jnp.float32), axis=0).astype(jnp.bfloat16)
    right_back = jnp.sum(right_back.astype(jnp.float32), axis=0).astype(jnp.bfloat16)
    left_back = lax.ppermute(left_back, axes, to_tokens)

    share = jnp.sum(shares.astype(jnp.float32), axis=0).astype(jnp.bfloat16)
    message = spread(share, axes, devices)
    output_weight_gradient = (
        message[:, :share_rows].reshape(flat, pair_width).astype(jnp.float32)
    )
    side = message[:, share_rows:].reshape(-1, pair_width).astype(jnp.float32)
    side = side[: features * 2 * proj // pair_width].reshape(features, 2 * proj)
    left_weight_gradient, right_weight_gradient = side[:, :proj], side[:, proj:]

    normed, inverse_spread = normalize(picked)
    both = jnp.concatenate(
        [
            left_back.reshape(seq_count, tokens, proj),
            right_back.reshape(seq_count, tokens, proj),
        ],
        axis=-1,
    )
    sides = jnp.concatenate([first_side_matrix, second_side_matrix], axis=1)
    grad_normed = jnp.einsum("stp,cp->stc", both, sides, preferred_element_type=jnp.float32)
    mean_factor = jnp.mean(grad_normed, axis=-1, keepdims=True)
    projected = jnp.mean(grad_normed * normed, axis=-1, keepdims=True)
    alignment_gradient = (
        inverse_spread * (grad_normed - mean_factor - normed * projected)
    ).astype(jnp.bfloat16)
    return (
        pair_delta,
        alignment_gradient,
        left_weight_gradient,
        right_weight_gradient,
        output_weight_gradient,
    )


def dot(x, y, contract=(1, 0), precision=None):
    return lax.dot_general(
        x, y, (((contract[0],), (contract[1],)), ((), ())),
        precision=precision, preferred_element_type=F32,
    )


def lane_ids(shape):
    return lax.broadcasted_iota(jnp.int32, shape, len(shape) - 1)


def fold_tokens(parts):
    quarter = LANES // 4
    chunk = lane_ids(parts[0].shape) // quarter
    first, even = chunk < 2, chunk % 2 == 0
    halves = [
        jnp.where(first, parts[t], parts[t + 2])
        + pltpu.roll(jnp.where(first, parts[t + 2], parts[t]), 2 * quarter, 1)
        for t in range(2)
    ]
    other = jnp.where(even, halves[1], halves[0])
    moved = jnp.where(even, pltpu.roll(other, 3 * quarter, 1), pltpu.roll(other, quarter, 1))
    return jnp.where(even, halves[0], halves[1]) + moved


def group_mean(x, group, precision):
    lanes = x.shape[1]
    rows_id = lax.broadcasted_iota(jnp.int32, (lanes, lanes), 0) // group
    cols_id = lax.broadcasted_iota(jnp.int32, (lanes, lanes), 1) // group
    block = jnp.where(rows_id == cols_id, 1.0 / group, 0.0).astype(x.dtype)
    return dot(x, block, precision=precision)


def pick_kernel(
    positions_ref,
    features_ref,
    cot_ref,
    normed_ref,
    inverse_ref,
    message_ref,
    positions,
    features,
    in_sems,
):
    pairs = cot_ref.shape[0]
    inputs = [
        pltpu.make_async_copy(source, target, in_sems.at[n])
        for n, (source, target) in enumerate(
            [
                (positions_ref, positions),
                (features_ref, features),
                (cot_ref, message_ref.at[pl.ds(0, pairs)]),
            ]
        )
    ]
    for copy in inputs:
        copy.start()
    heads = features_ref.shape[1]
    seqs, packed = normed_ref.shape
    channels = packed // 4
    for copy in inputs:
        copy.wait()
    wanted = positions[...] == lax.broadcasted_iota(jnp.int32, (heads, seqs), 0)
    chosen = dot(wanted.astype(BF16), features[...], contract=(0, 1))
    mean_factor = group_mean(chosen.astype(BF16), channels, None)
    centered = chosen - mean_factor
    variance = group_mean(centered * centered, channels, lax.Precision.HIGHEST)
    inverse = lax.rsqrt(variance + 1e-05)
    normed = centered * inverse
    for n in range(packed // LANES):
        message_ref[pairs + n * seqs : pairs + (n + 1) * seqs] = normed[
            :, n * LANES : (n + 1) * LANES
        ].astype(BF16)
    normed_ref[...] = normed
    inverse_ref[...] = inverse


def setup_kernel(
    first_ref,
    own_ref,
    mapping_ref,
    turned_mapping_ref,
    left_ref,
    right_ref,
    offset_ref,
    first_out_ref,
    own_out_ref,
    left_wide_ref,
    left_one_ref,
    right_one_ref,
    offset_out_ref,
):
    del mapping_ref, turned_mapping_ref
    first_out_ref[...] = first_ref[...]
    own_out_ref[...] = own_ref[...]
    offset_out_ref[...] = offset_ref[...]
    proj, channels = left_ref.shape
    tokens = left_one_ref.shape[0] // channels
    repeat = lane_ids((proj, LANES)) % proj
    repeat = (repeat == lax.broadcasted_iota(jnp.int32, (proj, LANES), 0)).astype(BF16)
    left_row = dot(left_ref[...], repeat, contract=(0, 0))
    right_row = dot(right_ref[...], repeat, contract=(0, 0))
    slot = lane_ids(left_row.shape) // proj
    nothing = jnp.zeros(left_row.shape, BF16)
    for t in range(tokens):
        here = slice(t * channels, (t + 1) * channels)
        left_one_ref[here] = jnp.where(slot == t, left_row, 0.0).astype(BF16)
        right_one_ref[here] = jnp.where(slot == t, right_row, 0.0).astype(BF16)
        for other in range(tokens):
            left_wide_ref[here, other * LANES : (other + 1) * LANES] = (
                left_row.astype(BF16) if other == t else nothing
            )


def place_blocks(place_ref, offsets, blocks, out_ref):
    for (down, across), block in zip(offsets, blocks, strict=True):
        out_ref[place_ref[0] ^ down, place_ref[1] ^ across] = block


def pull_blocks(cot_of, mapping_ref, pulled_ref, rows, at):
    block_rows = pulled_ref.shape[2] // LANES
    highs = mapping_ref.shape[1] // LANES

    def step(r, carry):
        cot = cot_of(r)
        block_cols = cot.shape[0] // block_rows
        for h in range(0, highs, 2):
            grad = dot(cot, mapping_ref[:, h * LANES : (h + 2) * LANES])
            for t in range(block_rows):
                for k in range(2):
                    pulled_ref[
                        r,
                        pl.ds(pl.multiple_of(at + (h + k) * block_cols, block_cols), block_cols),
                        t * LANES : (t + 1) * LANES,
                    ] = grad[
                        t * block_cols : (t + 1) * block_cols, k * LANES : (k + 1) * LANES
                    ].astype(BF16)
        return carry

    lax.fori_loop(0, rows, step, 0)


def pull_own_kernel(downs, place_ref, mapping_ref, *refs):
    *message_refs, pulled_ref, rows_ref, cot_ref = refs
    rows, pairs = cot_ref.shape[:2]
    for n, (down, ref) in enumerate(zip(downs, message_refs, strict=True)):
        cot_ref[place_ref[0] ^ down] = ref[:pairs]
        rows_ref[n] = ref[pairs:]
    pull_blocks(lambda r: cot_ref[r], mapping_ref, pulled_ref, rows, 0)


def pull_kernel(offsets, place_ref, mapping_ref, own_ref, *refs):
    *message_refs, cot_ref, pulled_ref = refs
    rows, groups, pairs, _ = cot_ref.shape
    place_blocks(place_ref, offsets, [ref[:pairs] for ref in message_refs], cot_ref)
    share = own_ref.shape[1]
    for across in range(1, groups):
        group = place_ref[1] ^ across
        pull_blocks(lambda r: cot_ref[r, group], mapping_ref, pulled_ref, rows, group * share)

    def keep(r, carry):
        at = pl.multiple_of(place_ref[1] * share, share)
        pulled_ref[r, pl.ds(at, share)] = own_ref[r]
        return carry

    lax.fori_loop(0, rows, keep, 0)


def outer_kernel(
    offsets,
    place_ref,
    mine_from_ref,
    theirs_from_ref,
    mapping_ref,
    left_ref,
    right_ref,
    offset_ref,
    rows_ref,
    expanded,
    swapped,
    outer_ref,
    pair_ref,
    mine_ref,
    theirs_ref,
    turned,
):
    for source, target in ((mine_from_ref, mine_ref), (theirs_from_ref, theirs_ref)):
        place_blocks(place_ref, offsets, [source[n] for n in range(source.shape[0])], target)
    prow_n, groups = mine_ref.shape[:2]
    block_rows, block_cols, pair_width = pair_ref.shape
    owners, seqs = expanded.shape[:2]
    packed = left_ref.shape[0]
    tokens = left_ref.shape[1] // LANES
    proj = LANES // tokens
    highs = proj // tokens
    span = highs * block_cols
    own_row, own_group, core = place_ref[0], place_ref[1], place_ref[2]

    def rows_of(ref, g, r):
        return jnp.concatenate(
            [ref[r, g, n * seqs : (n + 1) * seqs] for n in range(packed // LANES)], axis=1
        )

    places = [(g, r) for g in range(groups) for r in range(prow_n)]
    rows_mine = [rows_of(mine_ref, g, r) for g, r in places]
    rows_all = jnp.concatenate(
        rows_mine + [rows_of(theirs_ref, g, r) for g, r in places], axis=0
    )
    rows_ref[...] = rows_all
    wide_left = dot(rows_all, left_ref[...]).astype(BF16)
    for n, owner in enumerate(owner_order(places, prow_n, core)):
        expanded[owner] = wide_left[n * seqs : (n + 1) * seqs]

    side_rows = []
    for g in range(groups):
        chunks = rows_mine[g * prow_n : (g + 1) * prow_n]
        side_rows.append(
            jnp.concatenate([dot(x, right_ref[...]).astype(BF16) for x in chunks], axis=1)
        )
    right = dot(jnp.concatenate(side_rows, axis=0), shuffle_matrix(block_cols, proj, tokens))
    for g in range(groups):
        for l in range(tokens):
            swapped[l * seqs : (l + 1) * seqs, g * span : (g + 1) * span] = (
                right[g * seqs : (g + 1) * seqs, l * span : (l + 1) * span] * (1.0 / seqs)
            ).astype(BF16)
    turned[...] = swapped[...].astype(F32).T.astype(BF16)

    def step(row, carry):
        block = left_block(expanded, row, owners // prow_n, tokens)
        for t in range(block_rows):
            if t % 2 == 0:
                made = dot(turned[...], block[:, t * LANES : (t + 2) * LANES])
            lanes = slice(t % 2 * LANES, (t % 2 + 1) * LANES)
            for g in range(groups):
                start = (g * block_rows + t) * block_cols
                for h in range(highs):
                    there = slice((g * highs + h) * block_cols, (g * highs + h + 1) * block_cols)
                    outer_ref[row, start : start + block_cols, h * LANES : (h + 1) * LANES] = made[
                        there, lanes
                    ].astype(BF16)
        return carry

    lax.fori_loop(0, prow_n, step, 0)
    share = block_rows * block_cols
    mine = outer_ref[own_row, pl.ds(pl.multiple_of(own_group * share, share), share)]
    update = dot(mine, mapping_ref[...]) + offset_ref[...]
    pair_ref[...] = update.astype(BF16).reshape(pair_ref.shape)


def owner_order(places, prow_n, core):
    mine = [(2 * g + core) * prow_n + r for g, r in places]
    return mine + [(2 * g + 1 - core) * prow_n + r for g, r in places]


def shuffle_matrix(block_cols, proj, tokens):
    wide, highs = block_cols * proj, proj // tokens
    source = lax.broadcasted_iota(jnp.int32, (wide, wide), 0)
    target = lax.broadcasted_iota(jnp.int32, (wide, wide), 1)
    jj, qh = target % block_cols, target // block_cols % highs
    ql = target // (highs * block_cols)
    return (source == jj * proj + qh * tokens + ql).astype(BF16)


def left_block(expanded, row, step_owners, tokens):
    ahead = jnp.concatenate([expanded[row * step_owners + o] for o in range(step_owners)], axis=1)
    low = lane_ids(ahead.shape) % LANES // (LANES // tokens)
    return jnp.concatenate(
        [jnp.where(low == l, ahead, jnp.zeros_like(ahead)) for l in range(tokens)], axis=0
    )


def back_kernel(
    place_ref,
    rows_ref,
    expanded,
    swapped,
    outer_ref,
    cot_ref,
    pulled_ref,
    grads_ref,
    message_ref,
    left_back,
    right_back,
    sums,
    weights,
):
    prow_n, groups, pairs, pair_width = cot_ref.shape
    owners, seqs = left_back.shape[:2]
    tokens = swapped.shape[0] // seqs
    proj = LANES // tokens
    highs = proj // tokens
    span = swapped.shape[1] // groups
    block_cols = span // highs
    step_owners = owners // prow_n
    own_row, own_group, core = place_ref[0], place_ref[1], place_ref[2]
    places = [(g, r) for g in range(groups) for r in range(prow_n)]
    order = owner_order(places, prow_n, core)

    sums[...] = jnp.zeros_like(sums)
    weights[...] = jnp.zeros_like(weights)

    def step(row, carry):
        block = left_block(expanded, row, step_owners, tokens)
        cot = cot_ref[row].reshape(groups * pairs, pair_width)
        turned_cot = cot.astype(F32).T.astype(BF16)
        for at in range(0, weights.shape[1], 2 * LANES):
            chunk = slice(at, at + 2 * LANES)
            weights[:, chunk] += dot(turned_cot, outer_ref[row, :, chunk])
        for o in range(step_owners):
            chunk = slice(o * tokens * LANES, (o + 1) * tokens * LANES)
            back = dot(swapped[...], pulled_ref[row, :, chunk])
            low = lane_ids((seqs, back.shape[1])) % LANES // proj
            back = functools.reduce(
                jnp.add,
                [
                    jnp.where(low == l, back[l * seqs : (l + 1) * seqs], 0.0)
                    for l in range(tokens)
                ],
            )
            parts = [back[:, t * LANES : (t + 1) * LANES] for t in range(tokens)]
            left_back[row * step_owners + o] = fold_tokens(parts).astype(BF16)
        sums[...] += dot(pulled_ref[row], block, contract=(1, 1))
        return carry

    lax.fori_loop(0, prow_n, step, 0)

    back = (sums[...].T * (1.0 / seqs)).astype(BF16)
    back = jnp.concatenate(
        [
            jnp.concatenate(
                [
                    back[l * seqs : (l + 1) * seqs, g * span : (g + 1) * span]
                    for l in range(tokens)
                ],
                axis=1,
            )
            for g in range(groups)
        ],
        axis=0,
    )
    shuffle = shuffle_matrix(block_cols, proj, tokens)
    back = dot(back, shuffle, contract=(1, 1)).astype(BF16)
    for g, r in places:
        right_back[g * prow_n + r] = back[g * seqs : (g + 1) * seqs, r * LANES : (r + 1) * LANES]

    def side(grads, rows):
        total = dot(grads, rows, contract=(0, 0))
        features = rows.shape[1] // tokens
        return functools.reduce(
            jnp.add,
            [
                total[t * proj : (t + 1) * proj, t * features : (t + 1) * features]
                for t in range(tokens)
            ],
        )

    left_side = side(
        jnp.concatenate([left_back[owner] for owner in order], axis=0), rows_ref[...]
    )
    columns = groups * prow_n * seqs
    right_side = side(right_back[...].reshape(columns, LANES), rows_ref[:columns])
    both = jnp.concatenate([left_side, right_side], axis=0).astype(BF16)
    both = jnp.concatenate([both, jnp.zeros_like(both)], axis=1)

    flat = weights.shape[1]
    outer_f = weights[...].T
    weight_rows = outer_f.reshape(proj, proj, pair_width).swapaxes(0, 1).reshape(flat, pair_width)

    message_ref[:flat] = weight_rows.astype(BF16)
    message_ref[flat : flat + 2 * proj] = both
    message_ref[flat + 2 * proj :] = left_back[(2 * own_group + 1 - core) * prow_n + own_row]
    grads_ref[0] = left_back[(2 * own_group + core) * prow_n + own_row]
    grads_ref[1] = right_back[own_group * prow_n + own_row]


def close_kernel(
    grads_ref,
    own_ref,
    message_ref,
    normed_ref,
    inverse_ref,
    left_ref,
    right_ref,
    out_ref,
    left_out_ref,
    right_out_ref,
    rows_out_ref,
):
    flat = out_ref.shape[0]
    proj, features = left_out_ref.shape
    out_ref[...] = own_ref[:flat].astype(F32) + message_ref[:flat].astype(F32)
    sides = slice(flat, flat + 2 * proj)
    both = own_ref[sides, :features].astype(F32) + message_ref[sides, :features].astype(F32)
    left_out_ref[...] = both[:proj]
    right_out_ref[...] = both[proj:]
    left_back = grads_ref[0].astype(F32) + message_ref[flat + 2 * proj :].astype(F32)
    grad_normed = dot(left_back.astype(BF16), left_ref[...], contract=(1, 1))
    grad_normed = grad_normed + dot(grads_ref[1], right_ref[...], contract=(1, 1))
    normed = normed_ref[...]
    mean_factor = group_mean(grad_normed, features, lax.Precision.HIGHEST)
    projected = group_mean(grad_normed * normed, features, lax.Precision.HIGHEST)
    result = inverse_ref[...] * (grad_normed - mean_factor - normed * projected)
    rows_out_ref[...] = jnp.stack(
        [result[:, t * features : (t + 1) * features] for t in range(rows_out_ref.shape[1])],
        axis=1,
    ).astype(BF16)


def local_gathered(
    homolog_features,
    subset_homolog_positions,
    first_side_matrix,
    second_side_matrix,
    final_mapping_matrix,
    final_offset_vector,
    upstream_sensitivity,
):
    prow_n, groups = lax.axis_size("prow"), lax.axis_size("px")
    owners = prow_n * groups * 2
    heads, tokens, features = homolog_features.shape
    seqs = subset_homolog_positions.shape[0]
    block_rows, block_cols, pair_width = upstream_sensitivity.shape
    proj = first_side_matrix.shape[1]
    flat = proj * proj
    packed = tokens * features
    shape = jax.ShapeDtypeStruct
    vmem = pl.BlockSpec(memory_space=pltpu.VMEM)
    smem = pl.BlockSpec(memory_space=pltpu.SMEM)
    params = pltpu.CompilerParams(vmem_limit_bytes=36 * 1024 * 1024)

    pairs = block_rows * block_cols
    length = seqs * packed // LANES
    hbm = pl.BlockSpec(memory_space=pltpu.HBM)
    normed, inverse, sent = pl.pallas_call(
        pick_kernel,
        out_shape=(
            shape((seqs, packed), F32),
            shape((seqs, packed), F32),
            shape((pairs + length, LANES), BF16),
        ),
        in_specs=[hbm] * 3,
        out_specs=(vmem,) * 3,
        scratch_shapes=[
            pltpu.VMEM((1, seqs), jnp.int32),
            pltpu.VMEM((packed, heads), BF16),
            pltpu.SemaphoreType.DMA((3,)),
        ],
        compiler_params=pltpu.CompilerParams(vmem_limit_bytes=60 * 1024 * 1024),
        name="pick_rows",
    )(
        subset_homolog_positions.reshape(1, seqs),
        homolog_features.transpose(1, 2, 0).reshape(packed, heads),
        upstream_sensitivity.reshape(pairs, pair_width),
    )

    mapping = final_mapping_matrix.reshape(proj, proj, pair_width)
    mapping = mapping.swapaxes(0, 1).reshape(flat, pair_width)
    turned_mapping = mapping.T

    def swapped_with(values, axis, size, mask):
        return lax.ppermute(values, axis, [(n, n ^ mask) for n in range(size)])

    messages = [sent] + [
        swapped_with(sent, "prow", prow_n, down) for down in range(1, prow_n)
    ]
    messages[1], own, left_wide, left_one, right_one, offset = pl.pallas_call(
        setup_kernel,
        out_shape=(
            shape(sent.shape, BF16),
            shape(sent.shape, BF16),
            shape((packed, tokens * LANES), BF16),
            shape((packed, LANES), BF16),
            shape((packed, LANES), BF16),
            shape((1, pair_width), F32),
        ),
        in_specs=[vmem] * 7,
        out_specs=(vmem,) * 6,
        compiler_params=params,
        name="setup",
    )(
        messages[1],
        sent,
        mapping,
        turned_mapping,
        first_side_matrix.T,
        second_side_matrix.T,
        final_offset_vector.reshape(1, pair_width),
    )
    messages += [
        swapped_with(one, "px", groups, across) for across in range(1, groups) for one in messages
    ]
    messages[0] = own
    offsets = [(down, across) for across in range(groups) for down in range(prow_n)]
    place = jnp.stack([lax.axis_index("prow"), lax.axis_index("px"), lax.axis_index("pc")])

    columns = groups * proj // tokens * block_cols
    pull_cost = pl.CostEstimate(
        flops=prow_n * groups * pairs * pair_width * flat,
        bytes_accessed=prow_n * groups * pairs * (2 * pair_width + flat),
        transcendentals=0,
    )
    pulled_own, rows_own = pl.pallas_call(
        functools.partial(pull_own_kernel, [down for down, _ in offsets[:prow_n]]),
        out_shape=(
            shape((prow_n, columns // groups, block_rows * LANES), BF16),
            shape((prow_n, length, LANES), BF16),
        ),
        in_specs=[smem] + [vmem] * (1 + prow_n),
        out_specs=(vmem,) * 2,
        scratch_shapes=[pltpu.VMEM((prow_n, pairs, pair_width), BF16)],
        compiler_params=params,
        cost_estimate=pull_cost,
        name="pull_own",
    )(place, turned_mapping, *messages[:prow_n])
    rows = jnp.concatenate(
        [rows_own] + [one[None, pairs:] for one in messages[prow_n:]], axis=0
    )
    theirs = lax.ppermute(rows, "pc", [(0, 1), (1, 0)])
    cot, pulled = pl.pallas_call(
        functools.partial(pull_kernel, offsets),
        out_shape=(
            shape((prow_n, groups, pairs, pair_width), BF16),
            shape((prow_n, columns, block_rows * LANES), BF16),
        ),
        in_specs=[smem] + [vmem] * (2 + len(messages)),
        out_specs=(vmem,) * 2,
        compiler_params=params,
        cost_estimate=pull_cost,
        name="pull_back",
    )(place, turned_mapping, pulled_own, *messages)

    rows_all, expanded, swapped, outer, pair_delta = pl.pallas_call(
        functools.partial(outer_kernel, offsets),
        out_shape=(
            shape((owners * seqs, packed), BF16),
            shape((owners, seqs, tokens * LANES), BF16),
            shape((tokens * seqs, columns), BF16),
            shape((prow_n, groups * pairs, flat), BF16),
            shape(upstream_sensitivity.shape, BF16),
        ),
        in_specs=[smem] + [vmem] * 6,
        out_specs=(vmem,) * 5,
        scratch_shapes=[
            pltpu.VMEM((prow_n, groups, length, LANES), BF16),
            pltpu.VMEM((prow_n, groups, length, LANES), BF16),
            pltpu.VMEM((columns, tokens * seqs), BF16),
        ],
        compiler_params=params,
        cost_estimate=pl.CostEstimate(
            flops=2 * prow_n * groups * pairs * tokens * seqs * flat,
            bytes_accessed=2 * prow_n * groups * pairs * flat,
            transcendentals=0,
        ),
        name="outer_products",
    )(place, rows, theirs, mapping, left_wide, right_one, offset)
    grads, message = pl.pallas_call(
        back_kernel,
        out_shape=(
            shape((2, seqs, LANES), BF16),
            shape((flat + 2 * proj + seqs, LANES), BF16),
        ),
        in_specs=[smem] + [vmem] * 6,
        out_specs=(vmem,) * 2,
        scratch_shapes=[
            pltpu.VMEM((owners, seqs, LANES), BF16),
            pltpu.VMEM((groups * prow_n, seqs, LANES), BF16),
            pltpu.VMEM((columns, tokens * seqs), F32),
            pltpu.VMEM((pair_width, flat), F32),
        ],
        compiler_params=params,
        name="pull_further",
    )(place, rows_all, expanded, swapped, outer, cot, pulled)

    theirs = lax.ppermute(message, "pc", [(0, 1), (1, 0)])
    output_weight_gradient, left_weight_gradient, right_weight_gradient, alignment = pl.pallas_call(
        close_kernel,
        out_shape=(
            shape((flat, pair_width), F32),
            shape((proj, features), F32),
            shape((proj, features), F32),
            shape((seqs, tokens, features), BF16),
        ),
        in_specs=[vmem] * 7,
        out_specs=(vmem,) * 4,
        compiler_params=params,
        name="close",
    )(grads, message, theirs, normed, inverse, left_one, right_one)
    return (
        pair_delta,
        alignment,
        left_weight_gradient.T,
        right_weight_gradient.T,
        output_weight_gradient,
    )


def shapes_allow_gathering(
    mesh_shape, features, positions, first_side, second_side, mapping, offset, cot
):
    rows_n, cols_n = mesh_shape["prow"], mesh_shape["pcol"]
    parts = mesh_shape["rep"]
    tokens = features.shape[1] // (rows_n * cols_n)
    block_rows, block_cols = cot.shape[0] // (parts * rows_n), cot.shape[1] // cols_n
    proj, width = first_side.shape[1], cot.shape[2]
    return (
        cols_n % 2 == 0
        and cot.shape[1] * cot.shape[1] <= GATHERED_PAIRS
        and tokens * proj == LANES
        and tokens == 4
        and block_rows % tokens == 0
        and block_cols == rows_n * tokens == 16
        and rows_n & (rows_n - 1) == 0
        and cols_n & (cols_n - 1) == 0
        and width == LANES
        and features.shape[2] >= 2 * proj
        and positions.shape[0] // parts % 16 == 0
        and features.shape[2] * tokens % LANES == 0
    )


def solution(mesh):
    def run(local, over, columns, *args):
        tokens_split = P("rep", columns + ("prow",), None)
        pairs_split = P(("rep", "prow"), columns, None)
        return jax.shard_map(
            local,
            mesh=over,
            in_specs=(tokens_split, P("rep"), P(), P(), P(), P(), pairs_split),
            out_specs=(pairs_split, tokens_split, P("rep", None), P("rep", None), P("rep", None)),
            check_vma=False,
        )(*args)

    def program(*args):
        if not shapes_allow_gathering(mesh.shape, *args):
            return run(local_phased, mesh, ("pcol",), *args)
        reps, rows_n, cols_n = (mesh.shape[name] for name in ("rep", "prow", "pcol"))
        chips = Mesh(
            mesh.devices.reshape(reps, rows_n, cols_n // 2, 2), ("rep", "prow", "px", "pc")
        )
        return run(local_gathered, chips, ("px", "pc"), *args)

    return program
```

```python
import functools

import jax
import jax.numpy as jnp
from jax import lax
from jax.experimental import pallas as pl
from jax.experimental.pallas import tpu as pltpu
from jax.sharding import Mesh
from jax.sharding import PartitionSpec as P

BF16, F32 = jnp.bfloat16, jnp.float32
LANES = 128
GATHERED_PAIRS = 4096

PAIRS_AT_ONCE = 1024


def normalize(values):
    values = values.astype(jnp.float32)
    mean_factor = jnp.mean(values, axis=-1, keepdims=True)
    centered = values - mean_factor
    variance = jnp.mean(centered * centered, axis=-1, keepdims=True)
    inverse_spread = lax.rsqrt(variance + 1e-05)
    return (centered * inverse_spread, inverse_spread)


def transposed(rows_n, cols_n):
    return [
        (r * cols_n + c, c * rows_n + r) for r in range(rows_n) for c in range(cols_n)
    ]


def spread(values, axes, count):
    return lax.all_to_all(jnp.broadcast_to(values[None], (count,) + values.shape), axes, 0, 0)


def local_phased(
    homolog_features,
    subset_homolog_positions,
    first_side_matrix,
    second_side_matrix,
    final_mapping_matrix,
    final_offset_vector,
    upstream_sensitivity,
):
    axes = ("prow", "pcol")
    rows_n, cols_n = lax.axis_size("prow"), lax.axis_size("pcol")
    devices = rows_n * cols_n
    seq_count = subset_homolog_positions.shape[0]
    tokens, features = homolog_features.shape[1:]
    row_count, col_count, pair_width = upstream_sensitivity.shape
    proj = first_side_matrix.shape[1]
    flat = proj * proj
    to_rows = transposed(rows_n, cols_n)
    to_tokens = [(target, source) for source, target in to_rows]

    picked = jnp.take(homolog_features, subset_homolog_positions, axis=0)
    packed = picked.reshape(seq_count, tokens * features)
    row_own = lax.ppermute(packed, axes, to_rows)
    col_all = spread(packed, "prow", rows_n)
    row_all = spread(row_own, "pcol", cols_n)

    def side_of(chunks, count, matrix):
        chunks = chunks.reshape(count // tokens, seq_count, tokens, features)
        chunks = chunks.transpose(1, 0, 2, 3).reshape(seq_count, count, features)
        normed_low = normalize(chunks)[0].astype(jnp.bfloat16)
        side = jnp.einsum("stc,cp->stp", normed_low, matrix, preferred_element_type=jnp.float32)
        return normed_low, side.astype(jnp.bfloat16)

    row_normed, left = side_of(row_all, row_count, first_side_matrix)
    col_normed, right = side_of(col_all, col_count, second_side_matrix)

    def block_step(left_blk, cot_blk):
        rows = left_blk.shape[1]
        outer = jnp.einsum("sip,sjq->ijpq", left_blk, right, preferred_element_type=jnp.float32)
        outer = (outer / seq_count).astype(jnp.bfloat16).reshape(rows * col_count, flat)
        update = jnp.dot(outer, final_mapping_matrix, preferred_element_type=jnp.float32)
        update = (update + final_offset_vector).astype(jnp.bfloat16)
        cot_flat = cot_blk.reshape(rows * col_count, pair_width)
        grad_out = jnp.dot(outer.T, cot_flat, preferred_element_type=jnp.float32)
        grad_outer = jnp.dot(cot_flat, final_mapping_matrix.T, preferred_element_type=jnp.float32)
        grad_outer = grad_outer.astype(jnp.bfloat16).reshape(rows, col_count, proj, proj)
        grad_left = jnp.einsum(
            "ijpq,sjq->sip", grad_outer, right, preferred_element_type=jnp.float32
        )
        grad_right = jnp.einsum(
            "ijpq,sip->sjq", grad_outer, left_blk, preferred_element_type=jnp.float32
        )
        return update.reshape(rows, col_count, pair_width), grad_out, grad_left, grad_right

    block = max(1, min(row_count, PAIRS_AT_ONCE // col_count))
    blocks = row_count // block
    if blocks == 1:
        update, grad_out, grad_left, grad_right = block_step(left, upstream_sensitivity)
    else:
        def step(totals, inputs):
            update, grad_out, grad_left, grad_right = block_step(*inputs)
            return (totals[0] + grad_out, totals[1] + grad_right), (update, grad_left)

        (grad_out, grad_right), (update, grad_left) = lax.scan(
            step,
            (
                jnp.zeros((flat, pair_width), jnp.float32),
                jnp.zeros((seq_count, col_count, proj), jnp.float32),
            ),
            (
                left.reshape(seq_count, blocks, block, proj).transpose(1, 0, 2, 3),
                upstream_sensitivity.reshape(blocks, block, col_count, pair_width),
            ),
        )
        grad_left = grad_left.transpose(1, 0, 2, 3).reshape(seq_count, row_count, proj)
    pair_delta = update.reshape(row_count, col_count, pair_width)

    grad_left = (grad_left / seq_count).astype(jnp.bfloat16)
    grad_right = (grad_right / seq_count).astype(jnp.bfloat16)

    def weight_part(normed, grads):
        return jnp.einsum("stc,stp->cp", normed, grads, preferred_element_type=jnp.float32)

    side_part = jnp.concatenate(
        [weight_part(row_normed, grad_left), weight_part(col_normed, grad_right)], axis=1
    )
    share_rows = flat // devices
    side_rows = -(-features * 2 * proj // (pair_width * devices))
    side_flat = side_part.reshape(-1, pair_width)
    side_flat = jnp.pad(side_flat, ((0, side_rows * devices - side_flat.shape[0]), (0, 0)))
    shares = jnp.concatenate(
        [
            grad_out.reshape(devices, share_rows, pair_width),
            side_flat.reshape(devices, side_rows, pair_width),
        ],
        axis=1,
    ).astype(jnp.bfloat16)
    shares = lax.all_to_all(shares, axes, 0, 0)

    def chunks_of(grads, count):
        grads = grads.reshape(seq_count, count // tokens, tokens * proj)
        return grads.transpose(1, 0, 2)

    left_back = lax.all_to_all(chunks_of(grad_left, row_count), "pcol", 0, 0)
    right_back = lax.all_to_all(chunks_of(grad_right, col_count), "prow", 0, 0)
    left_back = jnp.sum(left_back.astype(jnp.float32), axis=0).astype(jnp.bfloat16)
    right_back = jnp.sum(right_back.astype(jnp.float32), axis=0).astype(jnp.bfloat16)
    left_back = lax.ppermute(left_back, axes, to_tokens)

    share = jnp.sum(shares.astype(jnp.float32), axis=0).astype(jnp.bfloat16)
    message = spread(share, axes, devices)
    output_weight_gradient = (
        message[:, :share_rows].reshape(flat, pair_width).astype(jnp.float32)
    )
    side = message[:, share_rows:].reshape(-1, pair_width).astype(jnp.float32)
    side = side[: features * 2 * proj // pair_width].reshape(features, 2 * proj)
    left_weight_gradient, right_weight_gradient = side[:, :proj], side[:, proj:]

    normed, inverse_spread = normalize(picked)
    both = jnp.concatenate(
        [
            left_back.reshape(seq_count, tokens, proj),
            right_back.reshape(seq_count, tokens, proj),
        ],
        axis=-1,
    )
    sides = jnp.concatenate([first_side_matrix, second_side_matrix], axis=1)
    grad_normed = jnp.einsum("stp,cp->stc", both, sides, preferred_element_type=jnp.float32)
    mean_factor = jnp.mean(grad_normed, axis=-1, keepdims=True)
    projected = jnp.mean(grad_normed * normed, axis=-1, keepdims=True)
    alignment_gradient = (
        inverse_spread * (grad_normed - mean_factor - normed * projected)
    ).astype(jnp.bfloat16)
    return (
        pair_delta,
        alignment_gradient,
        left_weight_gradient,
        right_weight_gradient,
        output_weight_gradient,
    )


def dot(x, y, contract=(1, 0), precision=None):
    return lax.dot_general(
        x, y, (((contract[0],), (contract[1],)), ((), ())),
        precision=precision, preferred_element_type=F32,
    )


def lane_ids(shape):
    return lax.broadcasted_iota(jnp.int32, shape, len(shape) - 1)


def fold_tokens(parts):
    quarter = LANES // 4
    chunk = lane_ids(parts[0].shape) // quarter
    first, even = chunk < 2, chunk % 2 == 0
    halves = [
        jnp.where(first, parts[t], parts[t + 2])
        + pltpu.roll(jnp.where(first, parts[t + 2], parts[t]), 2 * quarter, 1)
        for t in range(2)
    ]
    other = jnp.where(even, halves[1], halves[0])
    moved = jnp.where(even, pltpu.roll(other, 3 * quarter, 1), pltpu.roll(other, quarter, 1))
    return jnp.where(even, halves[0], halves[1]) + moved


def group_mean(x, group, precision):
    lanes = x.shape[1]
    rows_id = lax.broadcasted_iota(jnp.int32, (lanes, lanes), 0) // group
    cols_id = lax.broadcasted_iota(jnp.int32, (lanes, lanes), 1) // group
    block = jnp.where(rows_id == cols_id, 1.0 / group, 0.0).astype(x.dtype)
    return dot(x, block, precision=precision)


def pick_kernel(
    positions_ref,
    features_ref,
    cot_ref,
    normed_ref,
    inverse_ref,
    message_ref,
    positions,
    features,
    in_sems,
):
    pairs = cot_ref.shape[0]
    inputs = [
        pltpu.make_async_copy(source, target, in_sems.at[n])
        for n, (source, target) in enumerate(
            [
                (positions_ref, positions),
                (features_ref, features),
                (cot_ref, message_ref.at[pl.ds(0, pairs)]),
            ]
        )
    ]
    for copy in inputs:
        copy.start()
    heads = features_ref.shape[1]
    seqs, packed = normed_ref.shape
    channels = packed // 4
    for copy in inputs:
        copy.wait()
    wanted = positions[...] == lax.broadcasted_iota(jnp.int32, (heads, seqs), 0)
    chosen = dot(wanted.astype(BF16), features[...], contract=(0, 1))
    mean_factor = group_mean(chosen.astype(BF16), channels, None)
    centered = chosen - mean_factor
    variance = group_mean(centered * centered, channels, lax.Precision.HIGHEST)
    inverse = lax.rsqrt(variance + 1e-05)
    normed = centered * inverse
    for n in range(packed // LANES):
        message_ref[pairs + n * seqs : pairs + (n + 1) * seqs] = normed[
            :, n * LANES : (n + 1) * LANES
        ].astype(BF16)
    normed_ref[...] = normed
    inverse_ref[...] = inverse


def setup_kernel(
    first_ref,
    own_ref,
    mapping_ref,
    turned_mapping_ref,
    left_ref,
    right_ref,
    offset_ref,
    first_out_ref,
    own_out_ref,
    left_wide_ref,
    left_one_ref,
    right_one_ref,
    offset_out_ref,
):
    del mapping_ref, turned_mapping_ref
    first_out_ref[...] = first_ref[...]
    own_out_ref[...] = own_ref[...]
    offset_out_ref[...] = offset_ref[...]
    proj, channels = left_ref.shape
    tokens = left_one_ref.shape[0] // channels
    repeat = lane_ids((proj, LANES)) % proj
    repeat = (repeat == lax.broadcasted_iota(jnp.int32, (proj, LANES), 0)).astype(BF16)
    left_row = dot(left_ref[...], repeat, contract=(0, 0))
    right_row = dot(right_ref[...], repeat, contract=(0, 0))
    slot = lane_ids(left_row.shape) // proj
    nothing = jnp.zeros(left_row.shape, BF16)
    for t in range(tokens):
        here = slice(t * channels, (t + 1) * channels)
        left_one_ref[here] = jnp.where(slot == t, left_row, 0.0).astype(BF16)
        right_one_ref[here] = jnp.where(slot == t, right_row, 0.0).astype(BF16)
        for other in range(tokens):
            left_wide_ref[here, other * LANES : (other + 1) * LANES] = (
                left_row.astype(BF16) if other == t else nothing
            )


def place_blocks(place_ref, offsets, blocks, out_ref):
    for (down, across), block in zip(offsets, blocks, strict=True):
        out_ref[place_ref[0] ^ down, place_ref[1] ^ across] = block


def pull_kernel(offsets, place_ref, mapping_ref, *refs):
    *message_refs, cot_ref, pulled_ref = refs
    prow_n, groups, pairs, pair_width = cot_ref.shape
    highs = mapping_ref.shape[1] // LANES
    block_rows = pulled_ref.shape[2] // LANES
    block_cols = pairs // block_rows
    place_blocks(place_ref, offsets, [ref[:pairs] for ref in message_refs], cot_ref)

    def step(r, carry):
        grad = dot(cot_ref[r].reshape(groups * pairs, pair_width), mapping_ref[...])
        for g in range(groups):
            for t in range(block_rows):
                start = (g * block_rows + t) * block_cols
                lanes = slice(t * LANES, (t + 1) * LANES)
                for h in range(highs):
                    there = slice((g * highs + h) * block_cols, (g * highs + h + 1) * block_cols)
                    pulled_ref[r, there, lanes] = grad[
                        start : start + block_cols, h * LANES : (h + 1) * LANES
                    ].astype(BF16)
        return carry

    lax.fori_loop(0, prow_n, step, 0, unroll=True)


def outer_kernel(
    offsets,
    place_ref,
    mine_from_ref,
    theirs_from_ref,
    mapping_ref,
    left_ref,
    right_ref,
    offset_ref,
    rows_ref,
    expanded,
    swapped,
    outer_ref,
    pair_ref,
    mine_ref,
    theirs_ref,
    turned,
):
    for source, target in ((mine_from_ref, mine_ref), (theirs_from_ref, theirs_ref)):
        place_blocks(place_ref, offsets, [source[n] for n in range(source.shape[0])], target)
    prow_n, groups = mine_ref.shape[:2]
    block_rows, block_cols, pair_width = pair_ref.shape
    owners, seqs = expanded.shape[:2]
    packed = left_ref.shape[0]
    tokens = left_ref.shape[1] // LANES
    proj = LANES // tokens
    highs = proj // tokens
    span = highs * block_cols
    own_row, own_group, core = place_ref[0], place_ref[1], place_ref[2]

    def rows_of(ref, g, r):
        return jnp.concatenate(
            [ref[r, g, n * seqs : (n + 1) * seqs] for n in range(packed // LANES)], axis=1
        )

    places = [(g, r) for g in range(groups) for r in range(prow_n)]
    rows_mine = [rows_of(mine_ref, g, r) for g, r in places]
    rows_all = jnp.concatenate(
        rows_mine + [rows_of(theirs_ref, g, r) for g, r in places], axis=0
    )
    rows_ref[...] = rows_all
    wide_left = dot(rows_all, left_ref[...]).astype(BF16)
    for n, owner in enumerate(owner_order(places, prow_n, core)):
        expanded[owner] = wide_left[n * seqs : (n + 1) * seqs]

    side_rows = []
    for g in range(groups):
        chunks = rows_mine[g * prow_n : (g + 1) * prow_n]
        side_rows.append(
            jnp.concatenate([dot(x, right_ref[...]).astype(BF16) for x in chunks], axis=1)
        )
    right = dot(jnp.concatenate(side_rows, axis=0), shuffle_matrix(block_cols, proj, tokens))
    for g in range(groups):
        for l in range(tokens):
            swapped[l * seqs : (l + 1) * seqs, g * span : (g + 1) * span] = (
                right[g * seqs : (g + 1) * seqs, l * span : (l + 1) * span] * (1.0 / seqs)
            ).astype(BF16)
    turned[...] = swapped[...].astype(F32).T.astype(BF16)

    def step(row, carry):
        made = dot(turned[...], left_block(expanded, row, owners // prow_n, tokens))
        for g in range(groups):
            for t in range(block_rows):
                start = (g * block_rows + t) * block_cols
                lanes = slice(t * LANES, (t + 1) * LANES)
                for h in range(highs):
                    there = slice((g * highs + h) * block_cols, (g * highs + h + 1) * block_cols)
                    outer_ref[row, start : start + block_cols, h * LANES : (h + 1) * LANES] = made[
                        there, lanes
                    ].astype(BF16)
        return carry

    lax.fori_loop(0, prow_n, step, 0, unroll=True)
    share = block_rows * block_cols
    mine = outer_ref[own_row, pl.ds(pl.multiple_of(own_group * share, share), share)]
    update = dot(mine, mapping_ref[...]) + offset_ref[...]
    pair_ref[...] = update.astype(BF16).reshape(pair_ref.shape)


def owner_order(places, prow_n, core):
    mine = [(2 * g + core) * prow_n + r for g, r in places]
    return mine + [(2 * g + 1 - core) * prow_n + r for g, r in places]


def shuffle_matrix(block_cols, proj, tokens):
    wide, highs = block_cols * proj, proj // tokens
    source = lax.broadcasted_iota(jnp.int32, (wide, wide), 0)
    target = lax.broadcasted_iota(jnp.int32, (wide, wide), 1)
    jj, qh = target % block_cols, target // block_cols % highs
    ql = target // (highs * block_cols)
    return (source == jj * proj + qh * tokens + ql).astype(BF16)


def left_block(expanded, row, step_owners, tokens):
    ahead = jnp.concatenate([expanded[row * step_owners + o] for o in range(step_owners)], axis=1)
    low = lane_ids(ahead.shape) % LANES // (LANES // tokens)
    return jnp.concatenate(
        [jnp.where(low == l, ahead, jnp.zeros_like(ahead)) for l in range(tokens)], axis=0
    )


def back_kernel(
    place_ref,
    rows_ref,
    expanded,
    swapped,
    outer_ref,
    cot_ref,
    pulled_ref,
    grads_ref,
    message_ref,
    left_back,
    right_back,
    sums,
    weights,
):
    prow_n, groups, pairs, pair_width = cot_ref.shape
    owners, seqs = left_back.shape[:2]
    tokens = swapped.shape[0] // seqs
    proj = LANES // tokens
    highs = proj // tokens
    span = swapped.shape[1] // groups
    block_cols = span // highs
    step_owners = owners // prow_n
    own_row, own_group, core = place_ref[0], place_ref[1], place_ref[2]
    places = [(g, r) for g in range(groups) for r in range(prow_n)]
    order = owner_order(places, prow_n, core)

    sums[...] = jnp.zeros_like(sums)
    weights[...] = jnp.zeros_like(weights)

    def step(row, carry):
        block = left_block(expanded, row, step_owners, tokens)
        cot = cot_ref[row].reshape(groups * pairs, pair_width)
        weights[...] += dot(cot, outer_ref[row], contract=(0, 0))
        pulled = pulled_ref[row]
        back = dot(swapped[...], pulled)
        low = lane_ids((seqs, back.shape[1])) % LANES // proj
        back = functools.reduce(
            jnp.add,
            [
                jnp.where(low == l, back[l * seqs : (l + 1) * seqs], 0.0)
                for l in range(tokens)
            ],
        )
        for o in range(step_owners):
            parts = [
                back[:, (o * tokens + t) * LANES : (o * tokens + t + 1) * LANES]
                for t in range(tokens)
            ]
            left_back[row * step_owners + o] = fold_tokens(parts).astype(BF16)
        sums[...] += dot(pulled, block, contract=(1, 1))
        return carry

    lax.fori_loop(0, prow_n, step, 0, unroll=True)

    back = (sums[...].T * (1.0 / seqs)).astype(BF16)
    back = jnp.concatenate(
        [
            jnp.concatenate(
                [
                    back[l * seqs : (l + 1) * seqs, g * span : (g + 1) * span]
                    for l in range(tokens)
                ],
                axis=1,
            )
            for g in range(groups)
        ],
        axis=0,
    )
    shuffle = shuffle_matrix(block_cols, proj, tokens)
    back = dot(back, shuffle, contract=(1, 1)).astype(BF16)
    for g, r in places:
        right_back[g * prow_n + r] = back[g * seqs : (g + 1) * seqs, r * LANES : (r + 1) * LANES]

    def side(grads, rows):
        total = dot(grads, rows, contract=(0, 0))
        features = rows.shape[1] // tokens
        return functools.reduce(
            jnp.add,
            [
                total[t * proj : (t + 1) * proj, t * features : (t + 1) * features]
                for t in range(tokens)
            ],
        )

    left_side = side(
        jnp.concatenate([left_back[owner] for owner in order], axis=0), rows_ref[...]
    )
    columns = groups * prow_n * seqs
    right_side = side(right_back[...].reshape(columns, LANES), rows_ref[:columns])
    both = jnp.concatenate([left_side, right_side], axis=0).astype(BF16)
    both = jnp.concatenate([both, jnp.zeros_like(both)], axis=1)

    flat = weights.shape[1]
    outer_f = weights[...].T
    weight_rows = outer_f.reshape(proj, proj, pair_width).swapaxes(0, 1).reshape(flat, pair_width)

    message_ref[:flat] = weight_rows.astype(BF16)
    message_ref[flat : flat + 2 * proj] = both
    message_ref[flat + 2 * proj :] = left_back[(2 * own_group + 1 - core) * prow_n + own_row]
    grads_ref[0] = left_back[(2 * own_group + core) * prow_n + own_row]
    grads_ref[1] = right_back[own_group * prow_n + own_row]


def close_kernel(
    grads_ref,
    own_ref,
    message_ref,
    normed_ref,
    inverse_ref,
    left_ref,
    right_ref,
    out_ref,
    left_out_ref,
    right_out_ref,
    rows_out_ref,
    total,
    out_sems,
):
    flat = out_ref.shape[0]
    proj, features = left_out_ref.shape
    copies = []
    for n in range(out_sems.shape[0]):
        share = flat // out_sems.shape[0]
        here = pl.ds(n * share, share)
        total[here] = own_ref[here].astype(F32) + message_ref[here].astype(F32)
        copies.append(pltpu.make_async_copy(total.at[here], out_ref.at[here], out_sems.at[n]))
        copies[-1].start()
    sides = slice(flat, flat + 2 * proj)
    both = own_ref[sides, :features].astype(F32) + message_ref[sides, :features].astype(F32)
    left_out_ref[...] = both[:proj]
    right_out_ref[...] = both[proj:]
    left_back = grads_ref[0].astype(F32) + message_ref[flat + 2 * proj :].astype(F32)
    grad_normed = dot(left_back.astype(BF16), left_ref[...], contract=(1, 1))
    grad_normed = grad_normed + dot(grads_ref[1], right_ref[...], contract=(1, 1))
    normed = normed_ref[...]
    mean_factor = group_mean(grad_normed, features, lax.Precision.HIGHEST)
    projected = group_mean(grad_normed * normed, features, lax.Precision.HIGHEST)
    result = inverse_ref[...] * (grad_normed - mean_factor - normed * projected)
    rows_out_ref[...] = jnp.stack(
        [result[:, t * features : (t + 1) * features] for t in range(rows_out_ref.shape[1])],
        axis=1,
    ).astype(BF16)
    for copy in copies:
        copy.wait()


def local_gathered(
    homolog_features,
    subset_homolog_positions,
    first_side_matrix,
    second_side_matrix,
    final_mapping_matrix,
    final_offset_vector,
    upstream_sensitivity,
):
    prow_n, groups = lax.axis_size("prow"), lax.axis_size("px")
    owners = prow_n * groups * 2
    heads, tokens, features = homolog_features.shape
    seqs = subset_homolog_positions.shape[0]
    block_rows, block_cols, pair_width = upstream_sensitivity.shape
    proj = first_side_matrix.shape[1]
    flat = proj * proj
    packed = tokens * features
    shape = jax.ShapeDtypeStruct
    vmem = pl.BlockSpec(memory_space=pltpu.VMEM)
    smem = pl.BlockSpec(memory_space=pltpu.SMEM)
    params = pltpu.CompilerParams(vmem_limit_bytes=36 * 1024 * 1024)

    pairs = block_rows * block_cols
    length = seqs * packed // LANES
    hbm = pl.BlockSpec(memory_space=pltpu.HBM)
    normed, inverse, sent = pl.pallas_call(
        pick_kernel,
        out_shape=(
            shape((seqs, packed), F32),
            shape((seqs, packed), F32),
            shape((pairs + length, LANES), BF16),
        ),
        in_specs=[hbm] * 3,
        out_specs=(vmem,) * 3,
        scratch_shapes=[
            pltpu.VMEM((1, seqs), jnp.int32),
            pltpu.VMEM((packed, heads), BF16),
            pltpu.SemaphoreType.DMA((3,)),
        ],
        compiler_params=pltpu.CompilerParams(vmem_limit_bytes=60 * 1024 * 1024),
        name="pick_rows",
    )(
        subset_homolog_positions.reshape(1, seqs),
        homolog_features.transpose(1, 2, 0).reshape(packed, heads),
        upstream_sensitivity.reshape(pairs, pair_width),
    )

    mapping = final_mapping_matrix.reshape(proj, proj, pair_width)
    mapping = mapping.swapaxes(0, 1).reshape(flat, pair_width)
    turned_mapping = mapping.T

    def swapped_with(values, axis, size, mask):
        return lax.ppermute(values, axis, [(n, n ^ mask) for n in range(size)])

    messages = [sent] + [
        swapped_with(sent, "prow", prow_n, down) for down in range(1, prow_n)
    ]
    messages[1], own, left_wide, left_one, right_one, offset = pl.pallas_call(
        setup_kernel,
        out_shape=(
            shape(sent.shape, BF16),
            shape(sent.shape, BF16),
            shape((packed, tokens * LANES), BF16),
            shape((packed, LANES), BF16),
            shape((packed, LANES), BF16),
            shape((1, pair_width), F32),
        ),
        in_specs=[vmem] * 7,
        out_specs=(vmem,) * 6,
        compiler_params=params,
        name="setup",
    )(
        messages[1],
        sent,
        mapping,
        turned_mapping,
        first_side_matrix.T,
        second_side_matrix.T,
        final_offset_vector.reshape(1, pair_width),
    )
    messages += [
        swapped_with(one, "px", groups, across) for across in range(1, groups) for one in messages
    ]
    messages[0] = own
    offsets = [(down, across) for across in range(groups) for down in range(prow_n)]
    rows = jnp.stack([one[pairs:] for one in messages])
    theirs = lax.ppermute(rows, "pc", [(0, 1), (1, 0)])

    place = jnp.stack([lax.axis_index("prow"), lax.axis_index("px"), lax.axis_index("pc")])

    columns = groups * proj // tokens * block_cols
    cot, pulled = pl.pallas_call(
        functools.partial(pull_kernel, offsets),
        out_shape=(
            shape((prow_n, groups, pairs, pair_width), BF16),
            shape((prow_n, columns, block_rows * LANES), BF16),
        ),
        in_specs=[smem] + [vmem] * (1 + len(messages)),
        out_specs=(vmem,) * 2,
        compiler_params=params,
        cost_estimate=pl.CostEstimate(
            flops=2 * prow_n * groups * pairs * pair_width * flat,
            bytes_accessed=2 * prow_n * groups * pairs * (2 * pair_width + flat),
            transcendentals=0,
        ),
        name="pull_back",
    )(place, turned_mapping, *messages)

    rows_all, expanded, swapped, outer, pair_delta = pl.pallas_call(
        functools.partial(outer_kernel, offsets),
        out_shape=(
            shape((owners * seqs, packed), BF16),
            shape((owners, seqs, tokens * LANES), BF16),
            shape((tokens * seqs, columns), BF16),
            shape((prow_n, groups * pairs, flat), BF16),
            shape(upstream_sensitivity.shape, BF16),
        ),
        in_specs=[smem] + [vmem] * 6,
        out_specs=(vmem,) * 5,
        scratch_shapes=[
            pltpu.VMEM((prow_n, groups, length, LANES), BF16),
            pltpu.VMEM((prow_n, groups, length, LANES), BF16),
            pltpu.VMEM((columns, tokens * seqs), BF16),
        ],
        compiler_params=params,
        cost_estimate=pl.CostEstimate(
            flops=2 * prow_n * groups * pairs * tokens * seqs * flat,
            bytes_accessed=2 * prow_n * groups * pairs * flat,
            transcendentals=0,
        ),
        name="outer_products",
    )(place, rows, theirs, mapping, left_wide, right_one, offset)
    grads, message = pl.pallas_call(
        back_kernel,
        out_shape=(
            shape((2, seqs, LANES), BF16),
            shape((flat + 2 * proj + seqs, LANES), BF16),
        ),
        in_specs=[smem] + [vmem] * 6,
        out_specs=(vmem,) * 2,
        scratch_shapes=[
            pltpu.VMEM((owners, seqs, LANES), BF16),
            pltpu.VMEM((groups * prow_n, seqs, LANES), BF16),
            pltpu.VMEM((columns, tokens * seqs), F32),
            pltpu.VMEM((pair_width, flat), F32),
        ],
        compiler_params=params,
        name="pull_further",
    )(place, rows_all, expanded, swapped, outer, cot, pulled)

    theirs = lax.ppermute(message, "pc", [(0, 1), (1, 0)])
    output_weight_gradient, left_weight_gradient, right_weight_gradient, alignment = pl.pallas_call(
        close_kernel,
        out_shape=(
            shape((flat, pair_width), F32),
            shape((proj, features), F32),
            shape((proj, features), F32),
            shape((seqs, tokens, features), BF16),
        ),
        in_specs=[vmem] * 7,
        out_specs=(hbm,) + (vmem,) * 3,
        scratch_shapes=[
            pltpu.VMEM((flat, pair_width), F32),
            pltpu.SemaphoreType.DMA((2,)),
        ],
        compiler_params=params,
        name="close",
    )(grads, message, theirs, normed, inverse, left_one, right_one)
    return (
        pair_delta,
        alignment,
        left_weight_gradient.T,
        right_weight_gradient.T,
        output_weight_gradient,
    )


def shapes_allow_gathering(
    mesh_shape, features, positions, first_side, second_side, mapping, offset, cot
):
    rows_n, cols_n = mesh_shape["prow"], mesh_shape["pcol"]
    parts = mesh_shape["rep"]
    tokens = features.shape[1] // (rows_n * cols_n)
    block_rows, block_cols = cot.shape[0] // (parts * rows_n), cot.shape[1] // cols_n
    proj, width = first_side.shape[1], cot.shape[2]
    return (
        cols_n % 2 == 0
        and cot.shape[1] * cot.shape[1] <= GATHERED_PAIRS
        and tokens * proj == LANES
        and tokens == 4
        and block_rows % tokens == 0
        and block_cols == rows_n * tokens == 16
        and rows_n & (rows_n - 1) == 0
        and cols_n & (cols_n - 1) == 0
        and width == LANES
        and features.shape[2] >= 2 * proj
        and positions.shape[0] // parts % 16 == 0
        and features.shape[2] * tokens % LANES == 0
    )


def solution(mesh):
    def run(local, over, columns, *args):
        tokens_split = P("rep", columns + ("prow",), None)
        pairs_split = P(("rep", "prow"), columns, None)
        return jax.shard_map(
            local,
            mesh=over,
            in_specs=(tokens_split, P("rep"), P(), P(), P(), P(), pairs_split),
            out_specs=(pairs_split, tokens_split, P("rep", None), P("rep", None), P("rep", None)),
            check_vma=False,
        )(*args)

    def program(*args):
        if not shapes_allow_gathering(mesh.shape, *args):
            return run(local_phased, mesh, ("pcol",), *args)
        reps, rows_n, cols_n = (mesh.shape[name] for name in ("rep", "prow", "pcol"))
        chips = Mesh(
            mesh.devices.reshape(reps, rows_n, cols_n // 2, 2), ("rep", "prow", "px", "pc")
        )
        return run(local_gathered, chips, ("px", "pc"), *args)

    return program
```

```python
import functools

import jax
import jax.numpy as jnp
from jax import lax
from jax.experimental import pallas as pl
from jax.experimental.pallas import tpu as pltpu
from jax.sharding import Mesh
from jax.sharding import PartitionSpec as P

BF16, F32 = jnp.bfloat16, jnp.float32
LANES = 128
GATHERED_PAIRS = 4096

PAIRS_AT_ONCE = 1024


def normalize(values):
    values = values.astype(jnp.float32)
    mean_factor = jnp.mean(values, axis=-1, keepdims=True)
    centered = values - mean_factor
    variance = jnp.mean(centered * centered, axis=-1, keepdims=True)
    inverse_spread = lax.rsqrt(variance + 1e-05)
    return (centered * inverse_spread, inverse_spread)


def transposed(rows_n, cols_n):
    return [
        (r * cols_n + c, c * rows_n + r) for r in range(rows_n) for c in range(cols_n)
    ]


def spread(values, axes, count):
    return lax.all_to_all(jnp.broadcast_to(values[None], (count,) + values.shape), axes, 0, 0)


def local_phased(
    homolog_features,
    subset_homolog_positions,
    first_side_matrix,
    second_side_matrix,
    final_mapping_matrix,
    final_offset_vector,
    upstream_sensitivity,
):
    axes = ("prow", "pcol")
    rows_n, cols_n = lax.axis_size("prow"), lax.axis_size("pcol")
    devices = rows_n * cols_n
    seq_count = subset_homolog_positions.shape[0]
    tokens, features = homolog_features.shape[1:]
    row_count, col_count, pair_width = upstream_sensitivity.shape
    proj = first_side_matrix.shape[1]
    flat = proj * proj
    to_rows = transposed(rows_n, cols_n)
    to_tokens = [(target, source) for source, target in to_rows]

    picked = jnp.take(homolog_features, subset_homolog_positions, axis=0)
    packed = picked.reshape(seq_count, tokens * features)
    row_own = lax.ppermute(packed, axes, to_rows)
    col_all = spread(packed, "prow", rows_n)
    row_all = spread(row_own, "pcol", cols_n)

    def side_of(chunks, count, matrix):
        chunks = chunks.reshape(count // tokens, seq_count, tokens, features)
        chunks = chunks.transpose(1, 0, 2, 3).reshape(seq_count, count, features)
        normed_low = normalize(chunks)[0].astype(jnp.bfloat16)
        side = jnp.einsum("stc,cp->stp", normed_low, matrix, preferred_element_type=jnp.float32)
        return normed_low, side.astype(jnp.bfloat16)

    row_normed, left = side_of(row_all, row_count, first_side_matrix)
    col_normed, right = side_of(col_all, col_count, second_side_matrix)

    def block_step(left_blk, cot_blk):
        rows = left_blk.shape[1]
        outer = jnp.einsum("sip,sjq->ijpq", left_blk, right, preferred_element_type=jnp.float32)
        outer = (outer / seq_count).astype(jnp.bfloat16).reshape(rows * col_count, flat)
        update = jnp.dot(outer, final_mapping_matrix, preferred_element_type=jnp.float32)
        update = (update + final_offset_vector).astype(jnp.bfloat16)
        cot_flat = cot_blk.reshape(rows * col_count, pair_width)
        grad_out = jnp.dot(outer.T, cot_flat, preferred_element_type=jnp.float32)
        grad_outer = jnp.dot(cot_flat, final_mapping_matrix.T, preferred_element_type=jnp.float32)
        grad_outer = grad_outer.astype(jnp.bfloat16).reshape(rows, col_count, proj, proj)
        grad_left = jnp.einsum(
            "ijpq,sjq->sip", grad_outer, right, preferred_element_type=jnp.float32
        )
        grad_right = jnp.einsum(
            "ijpq,sip->sjq", grad_outer, left_blk, preferred_element_type=jnp.float32
        )
        return update.reshape(rows, col_count, pair_width), grad_out, grad_left, grad_right

    block = max(1, min(row_count, PAIRS_AT_ONCE // col_count))
    blocks = row_count // block
    if blocks == 1:
        update, grad_out, grad_left, grad_right = block_step(left, upstream_sensitivity)
    else:
        def step(totals, inputs):
            update, grad_out, grad_left, grad_right = block_step(*inputs)
            return (totals[0] + grad_out, totals[1] + grad_right), (update, grad_left)

        (grad_out, grad_right), (update, grad_left) = lax.scan(
            step,
            (
                jnp.zeros((flat, pair_width), jnp.float32),
                jnp.zeros((seq_count, col_count, proj), jnp.float32),
            ),
            (
                left.reshape(seq_count, blocks, block, proj).transpose(1, 0, 2, 3),
                upstream_sensitivity.reshape(blocks, block, col_count, pair_width),
            ),
        )
        grad_left = grad_left.transpose(1, 0, 2, 3).reshape(seq_count, row_count, proj)
    pair_delta = update.reshape(row_count, col_count, pair_width)

    grad_left = (grad_left / seq_count).astype(jnp.bfloat16)
    grad_right = (grad_right / seq_count).astype(jnp.bfloat16)

    def weight_part(normed, grads):
        return jnp.einsum("stc,stp->cp", normed, grads, preferred_element_type=jnp.float32)

    side_part = jnp.concatenate(
        [weight_part(row_normed, grad_left), weight_part(col_normed, grad_right)], axis=1
    )
    share_rows = flat // devices
    side_rows = -(-features * 2 * proj // (pair_width * devices))
    side_flat = side_part.reshape(-1, pair_width)
    side_flat = jnp.pad(side_flat, ((0, side_rows * devices - side_flat.shape[0]), (0, 0)))
    shares = jnp.concatenate(
        [
            grad_out.reshape(devices, share_rows, pair_width),
            side_flat.reshape(devices, side_rows, pair_width),
        ],
        axis=1,
    ).astype(jnp.bfloat16)
    shares = lax.all_to_all(shares, axes, 0, 0)

    def chunks_of(grads, count):
        grads = grads.reshape(seq_count, count // tokens, tokens * proj)
        return grads.transpose(1, 0, 2)

    left_back = lax.all_to_all(chunks_of(grad_left, row_count), "pcol", 0, 0)
    right_back = lax.all_to_all(chunks_of(grad_right, col_count), "prow", 0, 0)
    left_back = jnp.sum(left_back.astype(jnp.float32), axis=0).astype(jnp.bfloat16)
    right_back = jnp.sum(right_back.astype(jnp.float32), axis=0).astype(jnp.bfloat16)
    left_back = lax.ppermute(left_back, axes, to_tokens)

    share = jnp.sum(shares.astype(jnp.float32), axis=0).astype(jnp.bfloat16)
    message = spread(share, axes, devices)
    output_weight_gradient = (
        message[:, :share_rows].reshape(flat, pair_width).astype(jnp.float32)
    )
    side = message[:, share_rows:].reshape(-1, pair_width).astype(jnp.float32)
    side = side[: features * 2 * proj // pair_width].reshape(features, 2 * proj)
    left_weight_gradient, right_weight_gradient = side[:, :proj], side[:, proj:]

    normed, inverse_spread = normalize(picked)
    both = jnp.concatenate(
        [
            left_back.reshape(seq_count, tokens, proj),
            right_back.reshape(seq_count, tokens, proj),
        ],
        axis=-1,
    )
    sides = jnp.concatenate([first_side_matrix, second_side_matrix], axis=1)
    grad_normed = jnp.einsum("stp,cp->stc", both, sides, preferred_element_type=jnp.float32)
    mean_factor = jnp.mean(grad_normed, axis=-1, keepdims=True)
    projected = jnp.mean(grad_normed * normed, axis=-1, keepdims=True)
    alignment_gradient = (
        inverse_spread * (grad_normed - mean_factor - normed * projected)
    ).astype(jnp.bfloat16)
    return (
        pair_delta,
        alignment_gradient,
        left_weight_gradient,
        right_weight_gradient,
        output_weight_gradient,
    )


def dot(x, y, contract=(1, 0), precision=None):
    return lax.dot_general(
        x, y, (((contract[0],), (contract[1],)), ((), ())),
        precision=precision, preferred_element_type=F32,
    )


def lane_ids(shape):
    return lax.broadcasted_iota(jnp.int32, shape, len(shape) - 1)


def fold_tokens(parts):
    quarter = LANES // 4
    chunk = lane_ids(parts[0].shape) // quarter
    first, even = chunk < 2, chunk % 2 == 0
    halves = [
        jnp.where(first, parts[t], parts[t + 2])
        + pltpu.roll(jnp.where(first, parts[t + 2], parts[t]), 2 * quarter, 1)
        for t in range(2)
    ]
    other = jnp.where(even, halves[1], halves[0])
    moved = jnp.where(even, pltpu.roll(other, 3 * quarter, 1), pltpu.roll(other, quarter, 1))
    return jnp.where(even, halves[0], halves[1]) + moved


def group_mean(x, group, precision):
    lanes = x.shape[1]
    rows_id = lax.broadcasted_iota(jnp.int32, (lanes, lanes), 0) // group
    cols_id = lax.broadcasted_iota(jnp.int32, (lanes, lanes), 1) // group
    block = jnp.where(rows_id == cols_id, 1.0 / group, 0.0).astype(x.dtype)
    return dot(x, block, precision=precision)


def pick_kernel(
    positions_ref,
    features_ref,
    cot_ref,
    normed_ref,
    inverse_ref,
    message_ref,
    positions,
    features,
    in_sems,
):
    pairs = cot_ref.shape[0]
    inputs = [
        pltpu.make_async_copy(source, target, in_sems.at[n])
        for n, (source, target) in enumerate(
            [
                (positions_ref, positions),
                (features_ref, features),
                (cot_ref, message_ref.at[pl.ds(0, pairs)]),
            ]
        )
    ]
    for copy in inputs:
        copy.start()
    heads = features_ref.shape[1]
    seqs, packed = normed_ref.shape
    channels = packed // 4
    for copy in inputs:
        copy.wait()
    wanted = positions[...] == lax.broadcasted_iota(jnp.int32, (heads, seqs), 0)
    chosen = dot(wanted.astype(BF16), features[...], contract=(0, 1))
    mean_factor = group_mean(chosen.astype(BF16), channels, None)
    centered = chosen - mean_factor
    variance = group_mean(centered * centered, channels, lax.Precision.HIGHEST)
    inverse = lax.rsqrt(variance + 1e-05)
    normed = centered * inverse
    for n in range(packed // LANES):
        message_ref[pairs + n * seqs : pairs + (n + 1) * seqs] = normed[
            :, n * LANES : (n + 1) * LANES
        ].astype(BF16)
    normed_ref[...] = normed
    inverse_ref[...] = inverse


def setup_kernel(
    first_ref,
    own_ref,
    mapping_ref,
    turned_mapping_ref,
    left_ref,
    right_ref,
    offset_ref,
    first_out_ref,
    own_out_ref,
    left_wide_ref,
    left_one_ref,
    right_one_ref,
    offset_out_ref,
):
    del mapping_ref, turned_mapping_ref
    first_out_ref[...] = first_ref[...]
    own_out_ref[...] = own_ref[...]
    offset_out_ref[...] = offset_ref[...]
    proj, channels = left_ref.shape
    tokens = left_one_ref.shape[0] // channels
    repeat = lane_ids((proj, LANES)) % proj
    repeat = (repeat == lax.broadcasted_iota(jnp.int32, (proj, LANES), 0)).astype(BF16)
    left_row = dot(left_ref[...], repeat, contract=(0, 0))
    right_row = dot(right_ref[...], repeat, contract=(0, 0))
    slot = lane_ids(left_row.shape) // proj
    nothing = jnp.zeros(left_row.shape, BF16)
    for t in range(tokens):
        here = slice(t * channels, (t + 1) * channels)
        left_one_ref[here] = jnp.where(slot == t, left_row, 0.0).astype(BF16)
        right_one_ref[here] = jnp.where(slot == t, right_row, 0.0).astype(BF16)
        for other in range(tokens):
            left_wide_ref[here, other * LANES : (other + 1) * LANES] = (
                left_row.astype(BF16) if other == t else nothing
            )


def place_blocks(place_ref, offsets, blocks, out_ref):
    for (down, across), block in zip(offsets, blocks, strict=True):
        out_ref[place_ref[0] ^ down, place_ref[1] ^ across] = block


def pull_kernel(offsets, place_ref, mapping_ref, *refs):
    *message_refs, cot_ref, pulled_ref = refs
    prow_n, groups, pairs, pair_width = cot_ref.shape
    highs = mapping_ref.shape[1] // LANES
    block_rows = pulled_ref.shape[2] // LANES
    block_cols = pairs // block_rows
    place_blocks(place_ref, offsets, [ref[:pairs] for ref in message_refs], cot_ref)

    def step(r, carry):
        grad = dot(cot_ref[r].reshape(groups * pairs, pair_width), mapping_ref[...])
        for g in range(groups):
            for t in range(block_rows):
                start = (g * block_rows + t) * block_cols
                lanes = slice(t * LANES, (t + 1) * LANES)
                for h in range(highs):
                    there = slice((g * highs + h) * block_cols, (g * highs + h + 1) * block_cols)
                    pulled_ref[r, there, lanes] = grad[
                        start : start + block_cols, h * LANES : (h + 1) * LANES
                    ].astype(BF16)
        return carry

    lax.fori_loop(0, prow_n, step, 0, unroll=True)


def owner_order(places, prow_n, core):
    mine = [(2 * g + core) * prow_n + r for g, r in places]
    return mine + [(2 * g + 1 - core) * prow_n + r for g, r in places]


def shuffle_matrix(block_cols, proj, tokens):
    wide, highs = block_cols * proj, proj // tokens
    source = lax.broadcasted_iota(jnp.int32, (wide, wide), 0)
    target = lax.broadcasted_iota(jnp.int32, (wide, wide), 1)
    jj, qh = target % block_cols, target // block_cols % highs
    ql = target // (highs * block_cols)
    return (source == jj * proj + qh * tokens + ql).astype(BF16)


def left_block(expanded, row, step_owners, tokens):
    ahead = jnp.concatenate([expanded[row * step_owners + o] for o in range(step_owners)], axis=1)
    low = lane_ids(ahead.shape) % LANES // (LANES // tokens)
    return jnp.concatenate(
        [jnp.where(low == l, ahead, jnp.zeros_like(ahead)) for l in range(tokens)], axis=0
    )


def pair_kernel(
    offsets,
    place_ref,
    mine_from_ref,
    theirs_from_ref,
    mapping_ref,
    left_ref,
    right_ref,
    offset_ref,
    cot_ref,
    pulled_ref,
    pair_ref,
    grads_ref,
    message_ref,
    rows_ref,
    expanded,
    swapped,
    outer_ref,
    mine_ref,
    theirs_ref,
    turned,
    left_back,
    right_back,
    sums,
    weights,
):
    for source, target in ((mine_from_ref, mine_ref), (theirs_from_ref, theirs_ref)):
        place_blocks(place_ref, offsets, [source[n] for n in range(source.shape[0])], target)
    prow_n, groups = mine_ref.shape[:2]
    block_rows, block_cols, pair_width = pair_ref.shape
    owners, seqs = expanded.shape[:2]
    packed = left_ref.shape[0]
    tokens = left_ref.shape[1] // LANES
    proj = LANES // tokens
    highs = proj // tokens
    span = highs * block_cols
    own_row, own_group, core = place_ref[0], place_ref[1], place_ref[2]

    def rows_of(ref, g, r):
        return jnp.concatenate(
            [ref[r, g, n * seqs : (n + 1) * seqs] for n in range(packed // LANES)], axis=1
        )

    places = [(g, r) for g in range(groups) for r in range(prow_n)]
    rows_mine = [rows_of(mine_ref, g, r) for g, r in places]
    rows_all = jnp.concatenate(
        rows_mine + [rows_of(theirs_ref, g, r) for g, r in places], axis=0
    )
    rows_ref[...] = rows_all
    wide_left = dot(rows_all, left_ref[...]).astype(BF16)
    for n, owner in enumerate(owner_order(places, prow_n, core)):
        expanded[owner] = wide_left[n * seqs : (n + 1) * seqs]

    side_rows = []
    for g in range(groups):
        chunks = rows_mine[g * prow_n : (g + 1) * prow_n]
        side_rows.append(
            jnp.concatenate([dot(x, right_ref[...]).astype(BF16) for x in chunks], axis=1)
        )
    right = dot(jnp.concatenate(side_rows, axis=0), shuffle_matrix(block_cols, proj, tokens))
    for g in range(groups):
        for l in range(tokens):
            swapped[l * seqs : (l + 1) * seqs, g * span : (g + 1) * span] = (
                right[g * seqs : (g + 1) * seqs, l * span : (l + 1) * span] * (1.0 / seqs)
            ).astype(BF16)
    turned[...] = swapped[...].astype(F32).T.astype(BF16)

    order = owner_order(places, prow_n, core)
    pairs = block_rows * block_cols
    step_owners = owners // prow_n
    for row in range(prow_n):
        block = left_block(expanded, row, step_owners, tokens)
        made = dot(turned[...], block)
        for g in range(groups):
            for t in range(block_rows):
                start = (g * block_rows + t) * block_cols
                lanes = slice(t * LANES, (t + 1) * LANES)
                for h in range(highs):
                    there = slice((g * highs + h) * block_cols, (g * highs + h + 1) * block_cols)
                    outer_ref[row, start : start + block_cols, h * LANES : (h + 1) * LANES] = made[
                        there, lanes
                    ].astype(BF16)
        cot = cot_ref[row].reshape(groups * pairs, pair_width)
        weight_part = dot(cot, outer_ref[row], contract=(0, 0))
        weights[...] = weight_part if row == 0 else weights[...] + weight_part
        pulled = pulled_ref[row]
        back = dot(swapped[...], pulled)
        low = lane_ids((seqs, back.shape[1])) % LANES // proj
        back = functools.reduce(
            jnp.add,
            [
                jnp.where(low == l, back[l * seqs : (l + 1) * seqs], 0.0)
                for l in range(tokens)
            ],
        )
        for o in range(step_owners):
            parts = [
                back[:, (o * tokens + t) * LANES : (o * tokens + t + 1) * LANES]
                for t in range(tokens)
            ]
            left_back[row * step_owners + o] = fold_tokens(parts).astype(BF16)
        sum_part = dot(pulled, block, contract=(1, 1))
        sums[...] = sum_part if row == 0 else sums[...] + sum_part

    share = block_rows * block_cols
    mine = outer_ref[own_row, pl.ds(pl.multiple_of(own_group * share, share), share)]
    update = dot(mine, mapping_ref[...]) + offset_ref[...]
    pair_ref[...] = update.astype(BF16).reshape(pair_ref.shape)

    back = (sums[...].T * (1.0 / seqs)).astype(BF16)
    back = jnp.concatenate(
        [
            jnp.concatenate(
                [
                    back[l * seqs : (l + 1) * seqs, g * span : (g + 1) * span]
                    for l in range(tokens)
                ],
                axis=1,
            )
            for g in range(groups)
        ],
        axis=0,
    )
    shuffle = shuffle_matrix(block_cols, proj, tokens)
    back = dot(back, shuffle, contract=(1, 1)).astype(BF16)
    for g, r in places:
        right_back[g * prow_n + r] = back[g * seqs : (g + 1) * seqs, r * LANES : (r + 1) * LANES]

    def side(grads, rows):
        total = dot(grads, rows, contract=(0, 0))
        features = rows.shape[1] // tokens
        return functools.reduce(
            jnp.add,
            [
                total[t * proj : (t + 1) * proj, t * features : (t + 1) * features]
                for t in range(tokens)
            ],
        )

    left_side = side(
        jnp.concatenate([left_back[owner] for owner in order], axis=0), rows_ref[...]
    )
    columns = groups * prow_n * seqs
    right_side = side(right_back[...].reshape(columns, LANES), rows_ref[:columns])
    both = jnp.concatenate([left_side, right_side], axis=0).astype(BF16)
    both = jnp.concatenate([both, jnp.zeros_like(both)], axis=1)

    flat = weights.shape[1]
    outer_f = weights[...].T
    weight_rows = outer_f.reshape(proj, proj, pair_width).swapaxes(0, 1).reshape(flat, pair_width)

    message_ref[:flat] = weight_rows.astype(BF16)
    message_ref[flat : flat + 2 * proj] = both
    message_ref[flat + 2 * proj :] = left_back[(2 * own_group + 1 - core) * prow_n + own_row]
    grads_ref[0] = left_back[(2 * own_group + core) * prow_n + own_row]
    grads_ref[1] = right_back[own_group * prow_n + own_row]


def close_kernel(
    grads_ref,
    own_ref,
    message_ref,
    normed_ref,
    inverse_ref,
    left_ref,
    right_ref,
    out_ref,
    left_out_ref,
    right_out_ref,
    rows_out_ref,
):
    flat = out_ref.shape[0]
    proj, features = left_out_ref.shape
    out_ref[...] = own_ref[:flat].astype(F32) + message_ref[:flat].astype(F32)
    sides = slice(flat, flat + 2 * proj)
    both = own_ref[sides, :features].astype(F32) + message_ref[sides, :features].astype(F32)
    left_out_ref[...] = both[:proj]
    right_out_ref[...] = both[proj:]
    left_back = grads_ref[0].astype(F32) + message_ref[flat + 2 * proj :].astype(F32)
    grad_normed = dot(left_back.astype(BF16), left_ref[...], contract=(1, 1))
    grad_normed = grad_normed + dot(grads_ref[1], right_ref[...], contract=(1, 1))
    normed = normed_ref[...]
    mean_factor = group_mean(grad_normed, features, lax.Precision.HIGHEST)
    projected = group_mean(grad_normed * normed, features, lax.Precision.HIGHEST)
    result = inverse_ref[...] * (grad_normed - mean_factor - normed * projected)
    rows_out_ref[...] = jnp.stack(
        [result[:, t * features : (t + 1) * features] for t in range(rows_out_ref.shape[1])],
        axis=1,
    ).astype(BF16)


def local_gathered(
    homolog_features,
    subset_homolog_positions,
    first_side_matrix,
    second_side_matrix,
    final_mapping_matrix,
    final_offset_vector,
    upstream_sensitivity,
):
    prow_n, groups = lax.axis_size("prow"), lax.axis_size("px")
    owners = prow_n * groups * 2
    heads, tokens, features = homolog_features.shape
    seqs = subset_homolog_positions.shape[0]
    block_rows, block_cols, pair_width = upstream_sensitivity.shape
    proj = first_side_matrix.shape[1]
    flat = proj * proj
    packed = tokens * features
    shape = jax.ShapeDtypeStruct
    vmem = pl.BlockSpec(memory_space=pltpu.VMEM)
    smem = pl.BlockSpec(memory_space=pltpu.SMEM)
    params = pltpu.CompilerParams(vmem_limit_bytes=36 * 1024 * 1024)

    pairs = block_rows * block_cols
    length = seqs * packed // LANES
    hbm = pl.BlockSpec(memory_space=pltpu.HBM)
    normed, inverse, sent = pl.pallas_call(
        pick_kernel,
        out_shape=(
            shape((seqs, packed), F32),
            shape((seqs, packed), F32),
            shape((pairs + length, LANES), BF16),
        ),
        in_specs=[hbm] * 3,
        out_specs=(vmem,) * 3,
        scratch_shapes=[
            pltpu.VMEM((1, seqs), jnp.int32),
            pltpu.VMEM((packed, heads), BF16),
            pltpu.SemaphoreType.DMA((3,)),
        ],
        compiler_params=pltpu.CompilerParams(vmem_limit_bytes=60 * 1024 * 1024),
        name="pick_rows",
    )(
        subset_homolog_positions.reshape(1, seqs),
        homolog_features.transpose(1, 2, 0).reshape(packed, heads),
        upstream_sensitivity.reshape(pairs, pair_width),
    )

    mapping = final_mapping_matrix.reshape(proj, proj, pair_width)
    mapping = mapping.swapaxes(0, 1).reshape(flat, pair_width)
    turned_mapping = mapping.T

    def swapped_with(values, axis, size, mask):
        return lax.ppermute(values, axis, [(n, n ^ mask) for n in range(size)])

    messages = [sent] + [
        swapped_with(sent, "prow", prow_n, down) for down in range(1, prow_n)
    ]
    messages[1], own, left_wide, left_one, right_one, offset = pl.pallas_call(
        setup_kernel,
        out_shape=(
            shape(sent.shape, BF16),
            shape(sent.shape, BF16),
            shape((packed, tokens * LANES), BF16),
            shape((packed, LANES), BF16),
            shape((packed, LANES), BF16),
            shape((1, pair_width), F32),
        ),
        in_specs=[vmem] * 7,
        out_specs=(vmem,) * 6,
        compiler_params=params,
        name="setup",
    )(
        messages[1],
        sent,
        mapping,
        turned_mapping,
        first_side_matrix.T,
        second_side_matrix.T,
        final_offset_vector.reshape(1, pair_width),
    )
    messages += [
        swapped_with(one, "px", groups, across) for across in range(1, groups) for one in messages
    ]
    messages[0] = own
    offsets = [(down, across) for across in range(groups) for down in range(prow_n)]
    rows = jnp.stack([one[pairs:] for one in messages])
    theirs = lax.ppermute(rows, "pc", [(0, 1), (1, 0)])

    place = jnp.stack([lax.axis_index("prow"), lax.axis_index("px"), lax.axis_index("pc")])

    columns = groups * proj // tokens * block_cols
    cot, pulled = pl.pallas_call(
        functools.partial(pull_kernel, offsets),
        out_shape=(
            shape((prow_n, groups, pairs, pair_width), BF16),
            shape((prow_n, columns, block_rows * LANES), BF16),
        ),
        in_specs=[smem] + [vmem] * (1 + len(messages)),
        out_specs=(vmem,) * 2,
        compiler_params=params,
        cost_estimate=pl.CostEstimate(
            flops=2 * prow_n * groups * pairs * pair_width * flat,
            bytes_accessed=2 * prow_n * groups * pairs * (2 * pair_width + flat),
            transcendentals=0,
        ),
        name="pull_back",
    )(place, turned_mapping, *messages)

    pair_delta, grads, message = pl.pallas_call(
        functools.partial(pair_kernel, offsets),
        out_shape=(
            shape(upstream_sensitivity.shape, BF16),
            shape((2, seqs, LANES), BF16),
            shape((flat + 2 * proj + seqs, LANES), BF16),
        ),
        in_specs=[smem] + [vmem] * 8,
        out_specs=(vmem,) * 3,
        scratch_shapes=[
            pltpu.VMEM((owners * seqs, packed), BF16),
            pltpu.VMEM((owners, seqs, tokens * LANES), BF16),
            pltpu.VMEM((tokens * seqs, columns), BF16),
            pltpu.VMEM((prow_n, groups * pairs, flat), BF16),
            pltpu.VMEM((prow_n, groups, length, LANES), BF16),
            pltpu.VMEM((prow_n, groups, length, LANES), BF16),
            pltpu.VMEM((columns, tokens * seqs), BF16),
            pltpu.VMEM((owners, seqs, LANES), BF16),
            pltpu.VMEM((groups * prow_n, seqs, LANES), BF16),
            pltpu.VMEM((columns, tokens * seqs), F32),
            pltpu.VMEM((pair_width, flat), F32),
        ],
        compiler_params=params,
        name="pair_work",
    )(place, rows, theirs, mapping, left_wide, right_one, offset, cot, pulled)

    theirs = lax.ppermute(message, "pc", [(0, 1), (1, 0)])
    output_weight_gradient, left_weight_gradient, right_weight_gradient, alignment = pl.pallas_call(
        close_kernel,
        out_shape=(
            shape((flat, pair_width), F32),
            shape((proj, features), F32),
            shape((proj, features), F32),
            shape((seqs, tokens, features), BF16),
        ),
        in_specs=[vmem] * 7,
        out_specs=(vmem,) * 4,
        compiler_params=params,
        name="close",
    )(grads, message, theirs, normed, inverse, left_one, right_one)
    return (
        pair_delta,
        alignment,
        left_weight_gradient.T,
        right_weight_gradient.T,
        output_weight_gradient,
    )


def shapes_allow_gathering(
    mesh_shape, features, positions, first_side, second_side, mapping, offset, cot
):
    rows_n, cols_n = mesh_shape["prow"], mesh_shape["pcol"]
    parts = mesh_shape["rep"]
    tokens = features.shape[1] // (rows_n * cols_n)
    block_rows, block_cols = cot.shape[0] // (parts * rows_n), cot.shape[1] // cols_n
    proj, width = first_side.shape[1], cot.shape[2]
    return (
        cols_n % 2 == 0
        and cot.shape[1] * cot.shape[1] <= GATHERED_PAIRS
        and tokens * proj == LANES
        and tokens == 4
        and block_rows % tokens == 0
        and block_cols == rows_n * tokens == 16
        and rows_n & (rows_n - 1) == 0
        and cols_n & (cols_n - 1) == 0
        and width == LANES
        and features.shape[2] >= 2 * proj
        and positions.shape[0] // parts % 16 == 0
        and features.shape[2] * tokens % LANES == 0
    )


def solution(mesh):
    def run(local, over, columns, *args):
        tokens_split = P("rep", columns + ("prow",), None)
        pairs_split = P(("rep", "prow"), columns, None)
        return jax.shard_map(
            local,
            mesh=over,
            in_specs=(tokens_split, P("rep"), P(), P(), P(), P(), pairs_split),
            out_specs=(pairs_split, tokens_split, P("rep", None), P("rep", None), P("rep", None)),
            check_vma=False,
        )(*args)

    def program(*args):
        if not shapes_allow_gathering(mesh.shape, *args):
            return run(local_phased, mesh, ("pcol",), *args)
        reps, rows_n, cols_n = (mesh.shape[name] for name in ("rep", "prow", "pcol"))
        chips = Mesh(
            mesh.devices.reshape(reps, rows_n, cols_n // 2, 2), ("rep", "prow", "px", "pc")
        )
        return run(local_gathered, chips, ("px", "pc"), *args)

    return program
```

```python
import functools

import jax
import jax.numpy as jnp
from jax import lax
from jax.experimental import pallas as pl
from jax.experimental.pallas import tpu as pltpu
from jax.sharding import Mesh
from jax.sharding import PartitionSpec as P

BF16, F32 = jnp.bfloat16, jnp.float32
LANES = 128
GATHERED_PAIRS = 4096

PAIRS_AT_ONCE = 1024


def normalize(values):
    values = values.astype(jnp.float32)
    mean_factor = jnp.mean(values, axis=-1, keepdims=True)
    centered = values - mean_factor
    variance = jnp.mean(centered * centered, axis=-1, keepdims=True)
    inverse_spread = lax.rsqrt(variance + 1e-05)
    return (centered * inverse_spread, inverse_spread)


def transposed(rows_n, cols_n):
    return [
        (r * cols_n + c, c * rows_n + r) for r in range(rows_n) for c in range(cols_n)
    ]


def spread(values, axes, count):
    return lax.all_to_all(jnp.broadcast_to(values[None], (count,) + values.shape), axes, 0, 0)


def local_phased(
    homolog_features,
    subset_homolog_positions,
    first_side_matrix,
    second_side_matrix,
    final_mapping_matrix,
    final_offset_vector,
    upstream_sensitivity,
):
    axes = ("prow", "pcol")
    rows_n, cols_n = lax.axis_size("prow"), lax.axis_size("pcol")
    devices = rows_n * cols_n
    seq_count = subset_homolog_positions.shape[0]
    tokens, features = homolog_features.shape[1:]
    row_count, col_count, pair_width = upstream_sensitivity.shape
    proj = first_side_matrix.shape[1]
    flat = proj * proj
    to_rows = transposed(rows_n, cols_n)
    to_tokens = [(target, source) for source, target in to_rows]

    picked = jnp.take(homolog_features, subset_homolog_positions, axis=0)
    packed = picked.reshape(seq_count, tokens * features)
    row_own = lax.ppermute(packed, axes, to_rows)
    col_all = spread(packed, "prow", rows_n)
    row_all = spread(row_own, "pcol", cols_n)

    def side_of(chunks, count, matrix):
        chunks = chunks.reshape(count // tokens, seq_count, tokens, features)
        chunks = chunks.transpose(1, 0, 2, 3).reshape(seq_count, count, features)
        normed_low = normalize(chunks)[0].astype(jnp.bfloat16)
        side = jnp.einsum("stc,cp->stp", normed_low, matrix, preferred_element_type=jnp.float32)
        return normed_low, side.astype(jnp.bfloat16)

    row_normed, left = side_of(row_all, row_count, first_side_matrix)
    col_normed, right = side_of(col_all, col_count, second_side_matrix)

    def block_step(left_blk, cot_blk):
        rows = left_blk.shape[1]
        outer = jnp.einsum("sip,sjq->ijpq", left_blk, right, preferred_element_type=jnp.float32)
        outer = (outer / seq_count).astype(jnp.bfloat16).reshape(rows * col_count, flat)
        update = jnp.dot(outer, final_mapping_matrix, preferred_element_type=jnp.float32)
        update = (update + final_offset_vector).astype(jnp.bfloat16)
        cot_flat = cot_blk.reshape(rows * col_count, pair_width)
        grad_out = jnp.dot(outer.T, cot_flat, preferred_element_type=jnp.float32)
        grad_outer = jnp.dot(cot_flat, final_mapping_matrix.T, preferred_element_type=jnp.float32)
        grad_outer = grad_outer.astype(jnp.bfloat16).reshape(rows, col_count, proj, proj)
        grad_left = jnp.einsum(
            "ijpq,sjq->sip", grad_outer, right, preferred_element_type=jnp.float32
        )
        grad_right = jnp.einsum(
            "ijpq,sip->sjq", grad_outer, left_blk, preferred_element_type=jnp.float32
        )
        return update.reshape(rows, col_count, pair_width), grad_out, grad_left, grad_right

    block = max(1, min(row_count, PAIRS_AT_ONCE // col_count))
    blocks = row_count // block
    if blocks == 1:
        update, grad_out, grad_left, grad_right = block_step(left, upstream_sensitivity)
    else:
        def step(totals, inputs):
            update, grad_out, grad_left, grad_right = block_step(*inputs)
            return (totals[0] + grad_out, totals[1] + grad_right), (update, grad_left)

        (grad_out, grad_right), (update, grad_left) = lax.scan(
            step,
            (
                jnp.zeros((flat, pair_width), jnp.float32),
                jnp.zeros((seq_count, col_count, proj), jnp.float32),
            ),
            (
                left.reshape(seq_count, blocks, block, proj).transpose(1, 0, 2, 3),
                upstream_sensitivity.reshape(blocks, block, col_count, pair_width),
            ),
        )
        grad_left = grad_left.transpose(1, 0, 2, 3).reshape(seq_count, row_count, proj)
    pair_delta = update.reshape(row_count, col_count, pair_width)

    grad_left = (grad_left / seq_count).astype(jnp.bfloat16)
    grad_right = (grad_right / seq_count).astype(jnp.bfloat16)

    def weight_part(normed, grads):
        return jnp.einsum("stc,stp->cp", normed, grads, preferred_element_type=jnp.float32)

    side_part = jnp.concatenate(
        [weight_part(row_normed, grad_left), weight_part(col_normed, grad_right)], axis=1
    )
    share_rows = flat // devices
    side_rows = -(-features * 2 * proj // (pair_width * devices))
    side_flat = side_part.reshape(-1, pair_width)
    side_flat = jnp.pad(side_flat, ((0, side_rows * devices - side_flat.shape[0]), (0, 0)))
    shares = jnp.concatenate(
        [
            grad_out.reshape(devices, share_rows, pair_width),
            side_flat.reshape(devices, side_rows, pair_width),
        ],
        axis=1,
    ).astype(jnp.bfloat16)
    shares = lax.all_to_all(shares, axes, 0, 0)

    def chunks_of(grads, count):
        grads = grads.reshape(seq_count, count // tokens, tokens * proj)
        return grads.transpose(1, 0, 2)

    left_back = lax.all_to_all(chunks_of(grad_left, row_count), "pcol", 0, 0)
    right_back = lax.all_to_all(chunks_of(grad_right, col_count), "prow", 0, 0)
    left_back = jnp.sum(left_back.astype(jnp.float32), axis=0).astype(jnp.bfloat16)
    right_back = jnp.sum(right_back.astype(jnp.float32), axis=0).astype(jnp.bfloat16)
    left_back = lax.ppermute(left_back, axes, to_tokens)

    share = jnp.sum(shares.astype(jnp.float32), axis=0).astype(jnp.bfloat16)
    message = spread(share, axes, devices)
    output_weight_gradient = (
        message[:, :share_rows].reshape(flat, pair_width).astype(jnp.float32)
    )
    side = message[:, share_rows:].reshape(-1, pair_width).astype(jnp.float32)
    side = side[: features * 2 * proj // pair_width].reshape(features, 2 * proj)
    left_weight_gradient, right_weight_gradient = side[:, :proj], side[:, proj:]

    normed, inverse_spread = normalize(picked)
    both = jnp.concatenate(
        [
            left_back.reshape(seq_count, tokens, proj),
            right_back.reshape(seq_count, tokens, proj),
        ],
        axis=-1,
    )
    sides = jnp.concatenate([first_side_matrix, second_side_matrix], axis=1)
    grad_normed = jnp.einsum("stp,cp->stc", both, sides, preferred_element_type=jnp.float32)
    mean_factor = jnp.mean(grad_normed, axis=-1, keepdims=True)
    projected = jnp.mean(grad_normed * normed, axis=-1, keepdims=True)
    alignment_gradient = (
        inverse_spread * (grad_normed - mean_factor - normed * projected)
    ).astype(jnp.bfloat16)
    return (
        pair_delta,
        alignment_gradient,
        left_weight_gradient,
        right_weight_gradient,
        output_weight_gradient,
    )


def dot(x, y, contract=(1, 0), precision=None):
    return lax.dot_general(
        x, y, (((contract[0],), (contract[1],)), ((), ())),
        precision=precision, preferred_element_type=F32,
    )


def lane_ids(shape):
    return lax.broadcasted_iota(jnp.int32, shape, len(shape) - 1)


def fold_tokens(parts):
    quarter = LANES // 4
    chunk = lane_ids(parts[0].shape) // quarter
    first, even = chunk < 2, chunk % 2 == 0
    halves = [
        jnp.where(first, parts[t], parts[t + 2])
        + pltpu.roll(jnp.where(first, parts[t + 2], parts[t]), 2 * quarter, 1)
        for t in range(2)
    ]
    other = jnp.where(even, halves[1], halves[0])
    moved = jnp.where(even, pltpu.roll(other, 3 * quarter, 1), pltpu.roll(other, quarter, 1))
    return jnp.where(even, halves[0], halves[1]) + moved


def group_mean(x, group, precision):
    lanes = x.shape[1]
    rows_id = lax.broadcasted_iota(jnp.int32, (lanes, lanes), 0) // group
    cols_id = lax.broadcasted_iota(jnp.int32, (lanes, lanes), 1) // group
    block = jnp.where(rows_id == cols_id, 1.0 / group, 0.0).astype(x.dtype)
    return dot(x, block, precision=precision)


def pick_kernel(
    positions_ref,
    features_ref,
    cot_ref,
    normed_ref,
    inverse_ref,
    message_ref,
    positions,
    features,
    in_sems,
):
    pairs = cot_ref.shape[0]
    inputs = [
        pltpu.make_async_copy(source, target, in_sems.at[n])
        for n, (source, target) in enumerate(
            [
                (positions_ref, positions),
                (features_ref, features),
                (cot_ref, message_ref.at[pl.ds(0, pairs)]),
            ]
        )
    ]
    for copy in inputs:
        copy.start()
    heads = features_ref.shape[1]
    seqs, packed = normed_ref.shape
    channels = packed // 4
    for copy in inputs:
        copy.wait()
    wanted = positions[...] == lax.broadcasted_iota(jnp.int32, (heads, seqs), 0)
    chosen = dot(wanted.astype(BF16), features[...], contract=(0, 1))
    mean_factor = group_mean(chosen.astype(BF16), channels, None)
    centered = chosen - mean_factor
    variance = group_mean(centered * centered, channels, lax.Precision.HIGHEST)
    inverse = lax.rsqrt(variance + 1e-05)
    normed = centered * inverse
    for n in range(packed // LANES):
        message_ref[pairs + n * seqs : pairs + (n + 1) * seqs] = normed[
            :, n * LANES : (n + 1) * LANES
        ].astype(BF16)
    normed_ref[...] = normed
    inverse_ref[...] = inverse


def setup_kernel(
    first_ref,
    own_ref,
    mapping_ref,
    turned_mapping_ref,
    left_ref,
    right_ref,
    offset_ref,
    first_out_ref,
    own_out_ref,
    left_wide_ref,
    left_one_ref,
    right_one_ref,
    offset_out_ref,
):
    del mapping_ref, turned_mapping_ref
    first_out_ref[...] = first_ref[...]
    own_out_ref[...] = own_ref[...]
    offset_out_ref[...] = offset_ref[...]
    proj, channels = left_ref.shape
    tokens = left_one_ref.shape[0] // channels
    repeat = lane_ids((proj, LANES)) % proj
    repeat = (repeat == lax.broadcasted_iota(jnp.int32, (proj, LANES), 0)).astype(BF16)
    left_row = dot(left_ref[...], repeat, contract=(0, 0))
    right_row = dot(right_ref[...], repeat, contract=(0, 0))
    slot = lane_ids(left_row.shape) // proj
    nothing = jnp.zeros(left_row.shape, BF16)
    for t in range(tokens):
        here = slice(t * channels, (t + 1) * channels)
        left_one_ref[here] = jnp.where(slot == t, left_row, 0.0).astype(BF16)
        right_one_ref[here] = jnp.where(slot == t, right_row, 0.0).astype(BF16)
        for other in range(tokens):
            left_wide_ref[here, other * LANES : (other + 1) * LANES] = (
                left_row.astype(BF16) if other == t else nothing
            )


def place_blocks(place_ref, offsets, blocks, out_ref):
    for (down, across), block in zip(offsets, blocks, strict=True):
        out_ref[place_ref[0] ^ down, place_ref[1] ^ across] = block


def pull_kernel(offsets, place_ref, mapping_ref, *refs):
    *message_refs, cot_ref, pulled_ref = refs
    prow_n, groups, pairs, pair_width = cot_ref.shape
    highs = mapping_ref.shape[1] // LANES
    block_rows = pulled_ref.shape[2] // LANES
    block_cols = pairs // block_rows
    place_blocks(place_ref, offsets, [ref[:pairs] for ref in message_refs], cot_ref)

    def step(r, carry):
        grad = dot(cot_ref[r].reshape(groups * pairs, pair_width), mapping_ref[...])
        for g in range(groups):
            for t in range(block_rows):
                start = (g * block_rows + t) * block_cols
                lanes = slice(t * LANES, (t + 1) * LANES)
                for h in range(highs):
                    there = slice((g * highs + h) * block_cols, (g * highs + h + 1) * block_cols)
                    pulled_ref[r, there, lanes] = grad[
                        start : start + block_cols, h * LANES : (h + 1) * LANES
                    ].astype(BF16)
        return carry

    lax.fori_loop(0, prow_n, step, 0, unroll=True)


def owner_order(places, prow_n, core):
    mine = [(2 * g + core) * prow_n + r for g, r in places]
    return mine + [(2 * g + 1 - core) * prow_n + r for g, r in places]


def shuffle_matrix(block_cols, proj, tokens):
    wide, highs = block_cols * proj, proj // tokens
    source = lax.broadcasted_iota(jnp.int32, (wide, wide), 0)
    target = lax.broadcasted_iota(jnp.int32, (wide, wide), 1)
    jj, qh = target % block_cols, target // block_cols % highs
    ql = target // (highs * block_cols)
    return (source == jj * proj + qh * tokens + ql).astype(BF16)


def left_block(expanded, row, step_owners, tokens):
    ahead = jnp.concatenate([expanded[row * step_owners + o] for o in range(step_owners)], axis=1)
    low = lane_ids(ahead.shape) % LANES // (LANES // tokens)
    return jnp.concatenate(
        [jnp.where(low == l, ahead, jnp.zeros_like(ahead)) for l in range(tokens)], axis=0
    )


def pair_kernel(
    offsets,
    place_ref,
    mine_from_ref,
    theirs_from_ref,
    mapping_ref,
    left_ref,
    right_ref,
    offset_ref,
    cot_ref,
    pulled_ref,
    pair_ref,
    grads_ref,
    message_ref,
    rows_ref,
    expanded,
    swapped,
    outer_ref,
    mine_ref,
    theirs_ref,
    turned,
    left_back,
    right_back,
    sums,
    weights,
):
    for source, target in ((mine_from_ref, mine_ref), (theirs_from_ref, theirs_ref)):
        place_blocks(place_ref, offsets, [source[n] for n in range(source.shape[0])], target)
    prow_n, groups = mine_ref.shape[:2]
    block_rows, block_cols, pair_width = pair_ref.shape
    owners, seqs = expanded.shape[:2]
    packed = left_ref.shape[0]
    tokens = left_ref.shape[1] // LANES
    proj = LANES // tokens
    highs = proj // tokens
    span = highs * block_cols
    own_row, own_group, core = place_ref[0], place_ref[1], place_ref[2]

    def rows_of(ref, g, r):
        return jnp.concatenate(
            [ref[r, g, n * seqs : (n + 1) * seqs] for n in range(packed // LANES)], axis=1
        )

    places = [(g, r) for g in range(groups) for r in range(prow_n)]
    rows_mine = [rows_of(mine_ref, g, r) for g, r in places]
    rows_all = jnp.concatenate(
        rows_mine + [rows_of(theirs_ref, g, r) for g, r in places], axis=0
    )
    rows_ref[...] = rows_all
    wide_left = dot(rows_all, left_ref[...]).astype(BF16)
    for n, owner in enumerate(owner_order(places, prow_n, core)):
        expanded[owner] = wide_left[n * seqs : (n + 1) * seqs]

    side_rows = []
    for g in range(groups):
        chunks = rows_mine[g * prow_n : (g + 1) * prow_n]
        side_rows.append(
            jnp.concatenate([dot(x, right_ref[...]).astype(BF16) for x in chunks], axis=1)
        )
    right = dot(jnp.concatenate(side_rows, axis=0), shuffle_matrix(block_cols, proj, tokens))
    for g in range(groups):
        for l in range(tokens):
            swapped[l * seqs : (l + 1) * seqs, g * span : (g + 1) * span] = (
                right[g * seqs : (g + 1) * seqs, l * span : (l + 1) * span] * (1.0 / seqs)
            ).astype(BF16)
    turned[...] = swapped[...].astype(F32).T.astype(BF16)

    order = owner_order(places, prow_n, core)
    pairs = block_rows * block_cols
    step_owners = owners // prow_n
    for row in range(prow_n):
        block = left_block(expanded, row, step_owners, tokens)
        made = dot(turned[...], block)
        for g in range(groups):
            for t in range(block_rows):
                start = (g * block_rows + t) * block_cols
                lanes = slice(t * LANES, (t + 1) * LANES)
                for h in range(highs):
                    there = slice((g * highs + h) * block_cols, (g * highs + h + 1) * block_cols)
                    outer_ref[row, start : start + block_cols, h * LANES : (h + 1) * LANES] = made[
                        there, lanes
                    ].astype(BF16)
        cot = cot_ref[row].reshape(groups * pairs, pair_width)
        weight_part = dot(cot, outer_ref[row], contract=(0, 0))
        weights[...] = weight_part if row == 0 else weights[...] + weight_part
        if row == prow_n - 1:
            share = block_rows * block_cols
            mine = outer_ref[own_row, pl.ds(pl.multiple_of(own_group * share, share), share)]
            update = dot(mine, mapping_ref[...]) + offset_ref[...]
            pair_ref[...] = update.astype(BF16).reshape(pair_ref.shape)
            flat = weights.shape[1]
            outer_f = weights[...].T
            weight_rows = outer_f.reshape(proj, proj, pair_width).swapaxes(0, 1).reshape(flat, pair_width)

            message_ref[:flat] = weight_rows.astype(BF16)
        pulled = pulled_ref[row]
        back = dot(swapped[...], pulled)
        low = lane_ids((seqs, back.shape[1])) % LANES // proj
        back = functools.reduce(
            jnp.add,
            [
                jnp.where(low == l, back[l * seqs : (l + 1) * seqs], 0.0)
                for l in range(tokens)
            ],
        )
        for o in range(step_owners):
            parts = [
                back[:, (o * tokens + t) * LANES : (o * tokens + t + 1) * LANES]
                for t in range(tokens)
            ]
            left_back[row * step_owners + o] = fold_tokens(parts).astype(BF16)
        sum_part = dot(pulled, block, contract=(1, 1))
        sums[...] = sum_part if row == 0 else sums[...] + sum_part

    back = (sums[...].T * (1.0 / seqs)).astype(BF16)
    back = jnp.concatenate(
        [
            jnp.concatenate(
                [
                    back[l * seqs : (l + 1) * seqs, g * span : (g + 1) * span]
                    for l in range(tokens)
                ],
                axis=1,
            )
            for g in range(groups)
        ],
        axis=0,
    )
    shuffle = shuffle_matrix(block_cols, proj, tokens)
    back = dot(back, shuffle, contract=(1, 1)).astype(BF16)
    for g, r in places:
        right_back[g * prow_n + r] = back[g * seqs : (g + 1) * seqs, r * LANES : (r + 1) * LANES]

    def side(grads, rows):
        total = dot(grads, rows, contract=(0, 0))
        features = rows.shape[1] // tokens
        return functools.reduce(
            jnp.add,
            [
                total[t * proj : (t + 1) * proj, t * features : (t + 1) * features]
                for t in range(tokens)
            ],
        )

    left_side = side(
        jnp.concatenate([left_back[owner] for owner in order], axis=0), rows_ref[...]
    )
    columns = groups * prow_n * seqs
    right_side = side(right_back[...].reshape(columns, LANES), rows_ref[:columns])
    both = jnp.concatenate([left_side, right_side], axis=0).astype(BF16)
    both = jnp.concatenate([both, jnp.zeros_like(both)], axis=1)

    message_ref[flat : flat + 2 * proj] = both
    message_ref[flat + 2 * proj :] = left_back[(2 * own_group + 1 - core) * prow_n + own_row]
    grads_ref[0] = left_back[(2 * own_group + core) * prow_n + own_row]
    grads_ref[1] = right_back[own_group * prow_n + own_row]


def close_kernel(
    grads_ref,
    own_ref,
    message_ref,
    normed_ref,
    inverse_ref,
    left_ref,
    right_ref,
    out_ref,
    left_out_ref,
    right_out_ref,
    rows_out_ref,
):
    flat = out_ref.shape[0]
    proj, features = left_out_ref.shape
    out_ref[...] = own_ref[:flat].astype(F32) + message_ref[:flat].astype(F32)
    sides = slice(flat, flat + 2 * proj)
    both = own_ref[sides, :features].astype(F32) + message_ref[sides, :features].astype(F32)
    left_out_ref[...] = both[:proj]
    right_out_ref[...] = both[proj:]
    left_back = grads_ref[0].astype(F32) + message_ref[flat + 2 * proj :].astype(F32)
    grad_normed = dot(left_back.astype(BF16), left_ref[...], contract=(1, 1))
    grad_normed = grad_normed + dot(grads_ref[1], right_ref[...], contract=(1, 1))
    normed = normed_ref[...]
    means = jnp.concatenate([grad_normed, grad_normed * normed], axis=0)
    means = group_mean(means, features, lax.Precision.HIGHEST)
    mean_factor, projected = means[: normed.shape[0]], means[normed.shape[0] :]
    result = inverse_ref[...] * (grad_normed - mean_factor - normed * projected)
    rows_out_ref[...] = jnp.stack(
        [result[:, t * features : (t + 1) * features] for t in range(rows_out_ref.shape[1])],
        axis=1,
    ).astype(BF16)


def local_gathered(
    homolog_features,
    subset_homolog_positions,
    first_side_matrix,
    second_side_matrix,
    final_mapping_matrix,
    final_offset_vector,
    upstream_sensitivity,
):
    prow_n, groups = lax.axis_size("prow"), lax.axis_size("px")
    owners = prow_n * groups * 2
    heads, tokens, features = homolog_features.shape
    seqs = subset_homolog_positions.shape[0]
    block_rows, block_cols, pair_width = upstream_sensitivity.shape
    proj = first_side_matrix.shape[1]
    flat = proj * proj
    packed = tokens * features
    shape = jax.ShapeDtypeStruct
    vmem = pl.BlockSpec(memory_space=pltpu.VMEM)
    smem = pl.BlockSpec(memory_space=pltpu.SMEM)
    params = pltpu.CompilerParams(vmem_limit_bytes=36 * 1024 * 1024)

    pairs = block_rows * block_cols
    length = seqs * packed // LANES
    hbm = pl.BlockSpec(memory_space=pltpu.HBM)
    normed, inverse, sent = pl.pallas_call(
        pick_kernel,
        out_shape=(
            shape((seqs, packed), F32),
            shape((seqs, packed), F32),
            shape((pairs + length, LANES), BF16),
        ),
        in_specs=[hbm] * 3,
        out_specs=(vmem,) * 3,
        scratch_shapes=[
            pltpu.VMEM((1, seqs), jnp.int32),
            pltpu.VMEM((packed, heads), BF16),
            pltpu.SemaphoreType.DMA((3,)),
        ],
        compiler_params=pltpu.CompilerParams(vmem_limit_bytes=60 * 1024 * 1024),
        name="pick_rows",
    )(
        subset_homolog_positions.reshape(1, seqs),
        homolog_features.transpose(1, 2, 0).reshape(packed, heads),
        upstream_sensitivity.reshape(pairs, pair_width),
    )

    mapping = final_mapping_matrix.reshape(proj, proj, pair_width)
    mapping = mapping.swapaxes(0, 1).reshape(flat, pair_width)
    turned_mapping = mapping.T

    def swapped_with(values, axis, size, mask):
        return lax.ppermute(values, axis, [(n, n ^ mask) for n in range(size)])

    messages = [sent] + [
        swapped_with(sent, "prow", prow_n, down) for down in range(1, prow_n)
    ]
    messages[1], own, left_wide, left_one, right_one, offset = pl.pallas_call(
        setup_kernel,
        out_shape=(
            shape(sent.shape, BF16),
            shape(sent.shape, BF16),
            shape((packed, tokens * LANES), BF16),
            shape((packed, LANES), BF16),
            shape((packed, LANES), BF16),
            shape((1, pair_width), F32),
        ),
        in_specs=[vmem] * 7,
        out_specs=(vmem,) * 6,
        compiler_params=params,
        name="setup",
    )(
        messages[1],
        sent,
        mapping,
        turned_mapping,
        first_side_matrix.T,
        second_side_matrix.T,
        final_offset_vector.reshape(1, pair_width),
    )
    messages += [
        swapped_with(one, "px", groups, across) for across in range(1, groups) for one in messages
    ]
    messages[0] = own
    offsets = [(down, across) for across in range(groups) for down in range(prow_n)]
    rows = jnp.stack([one[pairs:] for one in messages])
    theirs = lax.ppermute(rows, "pc", [(0, 1), (1, 0)])

    place = jnp.stack([lax.axis_index("prow"), lax.axis_index("px"), lax.axis_index("pc")])

    columns = groups * proj // tokens * block_cols
    cot, pulled = pl.pallas_call(
        functools.partial(pull_kernel, offsets),
        out_shape=(
            shape((prow_n, groups, pairs, pair_width), BF16),
            shape((prow_n, columns, block_rows * LANES), BF16),
        ),
        in_specs=[smem] + [vmem] * (1 + len(messages)),
        out_specs=(vmem,) * 2,
        compiler_params=params,
        cost_estimate=pl.CostEstimate(
            flops=2 * prow_n * groups * pairs * pair_width * flat,
            bytes_accessed=2 * prow_n * groups * pairs * (2 * pair_width + flat),
            transcendentals=0,
        ),
        name="pull_back",
    )(place, turned_mapping, *messages)

    pair_delta, grads, message = pl.pallas_call(
        functools.partial(pair_kernel, offsets),
        out_shape=(
            shape(upstream_sensitivity.shape, BF16),
            shape((2, seqs, LANES), BF16),
            shape((flat + 2 * proj + seqs, LANES), BF16),
        ),
        in_specs=[smem] + [vmem] * 8,
        out_specs=(vmem,) * 3,
        scratch_shapes=[
            pltpu.VMEM((owners * seqs, packed), BF16),
            pltpu.VMEM((owners, seqs, tokens * LANES), BF16),
            pltpu.VMEM((tokens * seqs, columns), BF16),
            pltpu.VMEM((prow_n, groups * pairs, flat), BF16),
            pltpu.VMEM((prow_n, groups, length, LANES), BF16),
            pltpu.VMEM((prow_n, groups, length, LANES), BF16),
            pltpu.VMEM((columns, tokens * seqs), BF16),
            pltpu.VMEM((owners, seqs, LANES), BF16),
            pltpu.VMEM((groups * prow_n, seqs, LANES), BF16),
            pltpu.VMEM((columns, tokens * seqs), F32),
            pltpu.VMEM((pair_width, flat), F32),
        ],
        compiler_params=params,
        name="pair_work",
    )(place, rows, theirs, mapping, left_wide, right_one, offset, cot, pulled)

    theirs = lax.ppermute(message, "pc", [(0, 1), (1, 0)])
    output_weight_gradient, left_weight_gradient, right_weight_gradient, alignment = pl.pallas_call(
        close_kernel,
        out_shape=(
            shape((flat, pair_width), F32),
            shape((proj, features), F32),
            shape((proj, features), F32),
            shape((seqs, tokens, features), BF16),
        ),
        in_specs=[vmem] * 7,
        out_specs=(vmem,) * 4,
        compiler_params=params,
        name="close",
    )(grads, message, theirs, normed, inverse, left_one, right_one)
    return (
        pair_delta,
        alignment,
        left_weight_gradient.T,
        right_weight_gradient.T,
        output_weight_gradient,
    )


def shapes_allow_gathering(
    mesh_shape, features, positions, first_side, second_side, mapping, offset, cot
):
    rows_n, cols_n = mesh_shape["prow"], mesh_shape["pcol"]
    parts = mesh_shape["rep"]
    tokens = features.shape[1] // (rows_n * cols_n)
    block_rows, block_cols = cot.shape[0] // (parts * rows_n), cot.shape[1] // cols_n
    proj, width = first_side.shape[1], cot.shape[2]
    return (
        cols_n % 2 == 0
        and cot.shape[1] * cot.shape[1] <= GATHERED_PAIRS
        and tokens * proj == LANES
        and tokens == 4
        and block_rows % tokens == 0
        and block_cols == rows_n * tokens == 16
        and rows_n & (rows_n - 1) == 0
        and cols_n & (cols_n - 1) == 0
        and width == LANES
        and features.shape[2] >= 2 * proj
        and positions.shape[0] // parts % 16 == 0
        and features.shape[2] * tokens % LANES == 0
    )


def solution(mesh):
    def run(local, over, columns, *args):
        tokens_split = P("rep", columns + ("prow",), None)
        pairs_split = P(("rep", "prow"), columns, None)
        return jax.shard_map(
            local,
            mesh=over,
            in_specs=(tokens_split, P("rep"), P(), P(), P(), P(), pairs_split),
            out_specs=(pairs_split, tokens_split, P("rep", None), P("rep", None), P("rep", None)),
            check_vma=False,
        )(*args)

    def program(*args):
        if not shapes_allow_gathering(mesh.shape, *args):
            return run(local_phased, mesh, ("pcol",), *args)
        reps, rows_n, cols_n = (mesh.shape[name] for name in ("rep", "prow", "pcol"))
        chips = Mesh(
            mesh.devices.reshape(reps, rows_n, cols_n // 2, 2), ("rep", "prow", "px", "pc")
        )
        return run(local_gathered, chips, ("px", "pc"), *args)

    return program
```

```python
import functools

import jax
import jax.numpy as jnp
from jax import lax
from jax.experimental import pallas as pl
from jax.experimental.pallas import tpu as pltpu
from jax.sharding import Mesh
from jax.sharding import PartitionSpec as P

BF16, F32 = jnp.bfloat16, jnp.float32
LANES = 128
GATHERED_PAIRS = 4096

PAIRS_AT_ONCE = 1024


def normalize(values):
    values = values.astype(jnp.float32)
    mean_factor = jnp.mean(values, axis=-1, keepdims=True)
    centered = values - mean_factor
    variance = jnp.mean(centered * centered, axis=-1, keepdims=True)
    inverse_spread = lax.rsqrt(variance + 1e-05)
    return (centered * inverse_spread, inverse_spread)


def transposed(rows_n, cols_n):
    return [
        (r * cols_n + c, c * rows_n + r) for r in range(rows_n) for c in range(cols_n)
    ]


def spread(values, axes, count):
    return lax.all_to_all(jnp.broadcast_to(values[None], (count,) + values.shape), axes, 0, 0)


def local_phased(
    homolog_features,
    subset_homolog_positions,
    first_side_matrix,
    second_side_matrix,
    final_mapping_matrix,
    final_offset_vector,
    upstream_sensitivity,
):
    axes = ("prow", "pcol")
    rows_n, cols_n = lax.axis_size("prow"), lax.axis_size("pcol")
    devices = rows_n * cols_n
    seq_count = subset_homolog_positions.shape[0]
    tokens, features = homolog_features.shape[1:]
    row_count, col_count, pair_width = upstream_sensitivity.shape
    proj = first_side_matrix.shape[1]
    flat = proj * proj
    to_rows = transposed(rows_n, cols_n)
    to_tokens = [(target, source) for source, target in to_rows]

    picked = jnp.take(homolog_features, subset_homolog_positions, axis=0)
    packed = picked.reshape(seq_count, tokens * features)
    row_own = lax.ppermute(packed, axes, to_rows)
    col_all = spread(packed, "prow", rows_n)
    row_all = spread(row_own, "pcol", cols_n)

    def side_of(chunks, count, matrix):
        chunks = chunks.reshape(count // tokens, seq_count, tokens, features)
        chunks = chunks.transpose(1, 0, 2, 3).reshape(seq_count, count, features)
        normed_low = normalize(chunks)[0].astype(jnp.bfloat16)
        side = jnp.einsum("stc,cp->stp", normed_low, matrix, preferred_element_type=jnp.float32)
        return normed_low, side.astype(jnp.bfloat16)

    row_normed, left = side_of(row_all, row_count, first_side_matrix)
    col_normed, right = side_of(col_all, col_count, second_side_matrix)

    def block_step(left_blk, cot_blk):
        rows = left_blk.shape[1]
        outer = jnp.einsum("sip,sjq->ijpq", left_blk, right, preferred_element_type=jnp.float32)
        outer = (outer / seq_count).astype(jnp.bfloat16).reshape(rows * col_count, flat)
        update = jnp.dot(outer, final_mapping_matrix, preferred_element_type=jnp.float32)
        update = (update + final_offset_vector).astype(jnp.bfloat16)
        cot_flat = cot_blk.reshape(rows * col_count, pair_width)
        grad_out = jnp.dot(outer.T, cot_flat, preferred_element_type=jnp.float32)
        grad_outer = jnp.dot(cot_flat, final_mapping_matrix.T, preferred_element_type=jnp.float32)
        grad_outer = grad_outer.astype(jnp.bfloat16).reshape(rows, col_count, proj, proj)
        grad_left = jnp.einsum(
            "ijpq,sjq->sip", grad_outer, right, preferred_element_type=jnp.float32
        )
        grad_right = jnp.einsum(
            "ijpq,sip->sjq", grad_outer, left_blk, preferred_element_type=jnp.float32
        )
        return update.reshape(rows, col_count, pair_width), grad_out, grad_left, grad_right

    block = max(1, min(row_count, PAIRS_AT_ONCE // col_count))
    blocks = row_count // block
    if blocks == 1:
        update, grad_out, grad_left, grad_right = block_step(left, upstream_sensitivity)
    else:
        def step(totals, inputs):
            update, grad_out, grad_left, grad_right = block_step(*inputs)
            return (totals[0] + grad_out, totals[1] + grad_right), (update, grad_left)

        (grad_out, grad_right), (update, grad_left) = lax.scan(
            step,
            (
                jnp.zeros((flat, pair_width), jnp.float32),
                jnp.zeros((seq_count, col_count, proj), jnp.float32),
            ),
            (
                left.reshape(seq_count, blocks, block, proj).transpose(1, 0, 2, 3),
                upstream_sensitivity.reshape(blocks, block, col_count, pair_width),
            ),
        )
        grad_left = grad_left.transpose(1, 0, 2, 3).reshape(seq_count, row_count, proj)
    pair_delta = update.reshape(row_count, col_count, pair_width)

    grad_left = (grad_left / seq_count).astype(jnp.bfloat16)
    grad_right = (grad_right / seq_count).astype(jnp.bfloat16)

    def weight_part(normed, grads):
        return jnp.einsum("stc,stp->cp", normed, grads, preferred_element_type=jnp.float32)

    side_part = jnp.concatenate(
        [weight_part(row_normed, grad_left), weight_part(col_normed, grad_right)], axis=1
    )
    share_rows = flat // devices
    side_rows = -(-features * 2 * proj // (pair_width * devices))
    side_flat = side_part.reshape(-1, pair_width)
    side_flat = jnp.pad(side_flat, ((0, side_rows * devices - side_flat.shape[0]), (0, 0)))
    shares = jnp.concatenate(
        [
            grad_out.reshape(devices, share_rows, pair_width),
            side_flat.reshape(devices, side_rows, pair_width),
        ],
        axis=1,
    ).astype(jnp.bfloat16)
    shares = lax.all_to_all(shares, axes, 0, 0)

    def chunks_of(grads, count):
        grads = grads.reshape(seq_count, count // tokens, tokens * proj)
        return grads.transpose(1, 0, 2)

    left_back = lax.all_to_all(chunks_of(grad_left, row_count), "pcol", 0, 0)
    right_back = lax.all_to_all(chunks_of(grad_right, col_count), "prow", 0, 0)
    left_back = jnp.sum(left_back.astype(jnp.float32), axis=0).astype(jnp.bfloat16)
    right_back = jnp.sum(right_back.astype(jnp.float32), axis=0).astype(jnp.bfloat16)
    left_back = lax.ppermute(left_back, axes, to_tokens)

    share = jnp.sum(shares.astype(jnp.float32), axis=0).astype(jnp.bfloat16)
    message = spread(share, axes, devices)
    output_weight_gradient = (
        message[:, :share_rows].reshape(flat, pair_width).astype(jnp.float32)
    )
    side = message[:, share_rows:].reshape(-1, pair_width).astype(jnp.float32)
    side = side[: features * 2 * proj // pair_width].reshape(features, 2 * proj)
    left_weight_gradient, right_weight_gradient = side[:, :proj], side[:, proj:]

    normed, inverse_spread = normalize(picked)
    both = jnp.concatenate(
        [
            left_back.reshape(seq_count, tokens, proj),
            right_back.reshape(seq_count, tokens, proj),
        ],
        axis=-1,
    )
    sides = jnp.concatenate([first_side_matrix, second_side_matrix], axis=1)
    grad_normed = jnp.einsum("stp,cp->stc", both, sides, preferred_element_type=jnp.float32)
    mean_factor = jnp.mean(grad_normed, axis=-1, keepdims=True)
    projected = jnp.mean(grad_normed * normed, axis=-1, keepdims=True)
    alignment_gradient = (
        inverse_spread * (grad_normed - mean_factor - normed * projected)
    ).astype(jnp.bfloat16)
    return (
        pair_delta,
        alignment_gradient,
        left_weight_gradient,
        right_weight_gradient,
        output_weight_gradient,
    )


def dot(x, y, contract=(1, 0), precision=None):
    return lax.dot_general(
        x, y, (((contract[0],), (contract[1],)), ((), ())),
        precision=precision, preferred_element_type=F32,
    )


def lane_ids(shape):
    return lax.broadcasted_iota(jnp.int32, shape, len(shape) - 1)


def fold_tokens(parts):
    quarter = LANES // 4
    chunk = lane_ids(parts[0].shape) // quarter
    first, even = chunk < 2, chunk % 2 == 0
    halves = [
        jnp.where(first, parts[t], parts[t + 2])
        + pltpu.roll(jnp.where(first, parts[t + 2], parts[t]), 2 * quarter, 1)
        for t in range(2)
    ]
    other = jnp.where(even, halves[1], halves[0])
    moved = jnp.where(even, pltpu.roll(other, 3 * quarter, 1), pltpu.roll(other, quarter, 1))
    return jnp.where(even, halves[0], halves[1]) + moved


def group_mean(x, group):
    rows, lanes = x.shape
    rows_id = lax.broadcasted_iota(jnp.int32, (lanes, lanes), 0) // group
    cols_id = lax.broadcasted_iota(jnp.int32, (lanes, lanes), 1) // group
    block = (rows_id == cols_id).astype(BF16)
    pieces = [x.astype(BF16)]
    if x.dtype == F32:
        for _ in range(2):
            x = x - pieces[-1].astype(F32)
            pieces.append(x.astype(BF16))
    total = dot(jnp.concatenate(pieces, axis=0), block)
    total = functools.reduce(
        jnp.add, [total[n * rows : (n + 1) * rows] for n in reversed(range(len(pieces)))]
    )
    return total * (1.0 / group)


def pick_kernel(
    positions_ref,
    features_ref,
    cot_ref,
    normed_ref,
    inverse_ref,
    message_ref,
    positions,
    features,
    in_sems,
):
    pairs = cot_ref.shape[0]
    inputs = [
        pltpu.make_async_copy(source, target, in_sems.at[n])
        for n, (source, target) in enumerate(
            [
                (positions_ref, positions),
                (features_ref, features),
                (cot_ref, message_ref.at[pl.ds(0, pairs)]),
            ]
        )
    ]
    for copy in inputs:
        copy.start()
    heads = features_ref.shape[1]
    seqs, packed = normed_ref.shape
    channels = packed // 4
    for copy in inputs:
        copy.wait()
    wanted = positions[...] == lax.broadcasted_iota(jnp.int32, (heads, seqs), 0)
    chosen = dot(wanted.astype(BF16), features[...], contract=(0, 1))
    mean_factor = group_mean(chosen.astype(BF16), channels)
    centered = chosen - mean_factor
    variance = group_mean(centered * centered, channels)
    inverse = lax.rsqrt(variance + 1e-05)
    normed = centered * inverse
    for n in range(packed // LANES):
        message_ref[pairs + n * seqs : pairs + (n + 1) * seqs] = normed[
            :, n * LANES : (n + 1) * LANES
        ].astype(BF16)
    normed_ref[...] = normed
    inverse_ref[...] = inverse


def setup_kernel(
    first_ref,
    own_ref,
    mapping_ref,
    turned_mapping_ref,
    left_ref,
    right_ref,
    offset_ref,
    first_out_ref,
    own_out_ref,
    left_wide_ref,
    left_one_ref,
    right_one_ref,
    offset_out_ref,
):
    del mapping_ref, turned_mapping_ref
    first_out_ref[...] = first_ref[...]
    own_out_ref[...] = own_ref[...]
    offset_out_ref[...] = offset_ref[...]
    proj, channels = left_ref.shape
    tokens = left_one_ref.shape[0] // channels
    repeat = lane_ids((proj, LANES)) % proj
    repeat = (repeat == lax.broadcasted_iota(jnp.int32, (proj, LANES), 0)).astype(BF16)
    left_row = dot(left_ref[...], repeat, contract=(0, 0))
    right_row = dot(right_ref[...], repeat, contract=(0, 0))
    slot = lane_ids(left_row.shape) // proj
    nothing = jnp.zeros(left_row.shape, BF16)
    for t in range(tokens):
        here = slice(t * channels, (t + 1) * channels)
        left_one_ref[here] = jnp.where(slot == t, left_row, 0.0).astype(BF16)
        right_one_ref[here] = jnp.where(slot == t, right_row, 0.0).astype(BF16)
        for other in range(tokens):
            left_wide_ref[here, other * LANES : (other + 1) * LANES] = (
                left_row.astype(BF16) if other == t else nothing
            )


def place_blocks(place_ref, offsets, blocks, out_ref):
    for (down, across), block in zip(offsets, blocks, strict=True):
        out_ref[place_ref[0] ^ down, place_ref[1] ^ across] = block


def pull_kernel(offsets, place_ref, mapping_ref, *refs):
    *message_refs, cot_ref, pulled_ref = refs
    prow_n, groups, pairs, pair_width = cot_ref.shape
    highs = mapping_ref.shape[1] // LANES
    block_rows = pulled_ref.shape[2] // LANES
    block_cols = pairs // block_rows
    place_blocks(place_ref, offsets, [ref[:pairs] for ref in message_refs], cot_ref)

    def step(r, carry):
        grad = dot(cot_ref[r].reshape(groups * pairs, pair_width), mapping_ref[...])
        for g in range(groups):
            for t in range(block_rows):
                start = (g * block_rows + t) * block_cols
                lanes = slice(t * LANES, (t + 1) * LANES)
                for h in range(highs):
                    there = slice((g * highs + h) * block_cols, (g * highs + h + 1) * block_cols)
                    pulled_ref[r, there, lanes] = grad[
                        start : start + block_cols, h * LANES : (h + 1) * LANES
                    ].astype(BF16)
        return carry

    lax.fori_loop(0, prow_n, step, 0, unroll=True)


def owner_order(places, prow_n, core):
    mine = [(2 * g + core) * prow_n + r for g, r in places]
    return mine + [(2 * g + 1 - core) * prow_n + r for g, r in places]


def shuffle_matrix(block_cols, proj, tokens):
    wide, highs = block_cols * proj, proj // tokens
    source = lax.broadcasted_iota(jnp.int32, (wide, wide), 0)
    target = lax.broadcasted_iota(jnp.int32, (wide, wide), 1)
    jj, qh = target % block_cols, target // block_cols % highs
    ql = target // (highs * block_cols)
    return (source == jj * proj + qh * tokens + ql).astype(BF16)


def left_block(expanded, row, step_owners, tokens):
    ahead = jnp.concatenate([expanded[row * step_owners + o] for o in range(step_owners)], axis=1)
    low = lane_ids(ahead.shape) % LANES // (LANES // tokens)
    return jnp.concatenate(
        [jnp.where(low == l, ahead, jnp.zeros_like(ahead)) for l in range(tokens)], axis=0
    )


def pair_kernel(
    offsets,
    place_ref,
    mine_from_ref,
    theirs_from_ref,
    mapping_ref,
    left_ref,
    right_ref,
    offset_ref,
    cot_ref,
    pulled_ref,
    pair_ref,
    grads_ref,
    message_ref,
    rows_ref,
    expanded,
    swapped,
    outer_ref,
    mine_ref,
    theirs_ref,
    turned,
    left_back,
    right_back,
    sums,
    weights,
):
    for source, target in ((mine_from_ref, mine_ref), (theirs_from_ref, theirs_ref)):
        place_blocks(place_ref, offsets, [source[n] for n in range(source.shape[0])], target)
    prow_n, groups = mine_ref.shape[:2]
    block_rows, block_cols, pair_width = pair_ref.shape
    owners, seqs = expanded.shape[:2]
    packed = left_ref.shape[0]
    tokens = left_ref.shape[1] // LANES
    proj = LANES // tokens
    highs = proj // tokens
    span = highs * block_cols
    own_row, own_group, core = place_ref[0], place_ref[1], place_ref[2]

    def rows_of(ref, g, r):
        return jnp.concatenate(
            [ref[r, g, n * seqs : (n + 1) * seqs] for n in range(packed // LANES)], axis=1
        )

    places = [(g, r) for g in range(groups) for r in range(prow_n)]
    rows_mine = [rows_of(mine_ref, g, r) for g, r in places]
    rows_all = jnp.concatenate(
        rows_mine + [rows_of(theirs_ref, g, r) for g, r in places], axis=0
    )
    rows_ref[...] = rows_all
    wide_left = dot(rows_all, left_ref[...]).astype(BF16)
    for n, owner in enumerate(owner_order(places, prow_n, core)):
        expanded[owner] = wide_left[n * seqs : (n + 1) * seqs]

    side_rows = []
    for g in range(groups):
        chunks = rows_mine[g * prow_n : (g + 1) * prow_n]
        side_rows.append(
            jnp.concatenate([dot(x, right_ref[...]).astype(BF16) for x in chunks], axis=1)
        )
    right = dot(jnp.concatenate(side_rows, axis=0), shuffle_matrix(block_cols, proj, tokens))
    for g in range(groups):
        for l in range(tokens):
            swapped[l * seqs : (l + 1) * seqs, g * span : (g + 1) * span] = (
                right[g * seqs : (g + 1) * seqs, l * span : (l + 1) * span] * (1.0 / seqs)
            ).astype(BF16)
    turned[...] = swapped[...].astype(F32).T.astype(BF16)

    order = owner_order(places, prow_n, core)
    pairs = block_rows * block_cols
    step_owners = owners // prow_n
    for row in range(prow_n):
        block = left_block(expanded, row, step_owners, tokens)
        made = dot(turned[...], block)
        for g in range(groups):
            for t in range(block_rows):
                start = (g * block_rows + t) * block_cols
                lanes = slice(t * LANES, (t + 1) * LANES)
                for h in range(highs):
                    there = slice((g * highs + h) * block_cols, (g * highs + h + 1) * block_cols)
                    outer_ref[row, start : start + block_cols, h * LANES : (h + 1) * LANES] = made[
                        there, lanes
                    ].astype(BF16)
        cot = cot_ref[row].reshape(groups * pairs, pair_width)
        weight_part = dot(cot, outer_ref[row], contract=(0, 0))
        weights[...] = weight_part if row == 0 else weights[...] + weight_part
        if row == prow_n - 1:
            share = block_rows * block_cols
            mine = outer_ref[own_row, pl.ds(pl.multiple_of(own_group * share, share), share)]
            update = dot(mine, mapping_ref[...]) + offset_ref[...]
            pair_ref[...] = update.astype(BF16).reshape(pair_ref.shape)
            flat = weights.shape[1]
            outer_f = weights[...].T
            weight_rows = outer_f.reshape(proj, proj, pair_width).swapaxes(0, 1).reshape(flat, pair_width)

            message_ref[:flat] = weight_rows.astype(BF16)
        pulled = pulled_ref[row]
        back = dot(swapped[...], pulled)
        low = lane_ids((seqs, back.shape[1])) % LANES // proj
        back = functools.reduce(
            jnp.add,
            [
                jnp.where(low == l, back[l * seqs : (l + 1) * seqs], 0.0)
                for l in range(tokens)
            ],
        )
        for o in range(step_owners):
            parts = [
                back[:, (o * tokens + t) * LANES : (o * tokens + t + 1) * LANES]
                for t in range(tokens)
            ]
            left_back[row * step_owners + o] = fold_tokens(parts).astype(BF16)
        sum_part = dot(pulled, block, contract=(1, 1))
        sums[...] = sum_part if row == 0 else sums[...] + sum_part

    back = (sums[...].T * (1.0 / seqs)).astype(BF16)
    back = jnp.concatenate(
        [
            jnp.concatenate(
                [
                    back[l * seqs : (l + 1) * seqs, g * span : (g + 1) * span]
                    for l in range(tokens)
                ],
                axis=1,
            )
            for g in range(groups)
        ],
        axis=0,
    )
    shuffle = shuffle_matrix(block_cols, proj, tokens)
    back = dot(back, shuffle, contract=(1, 1)).astype(BF16)
    for g, r in places:
        right_back[g * prow_n + r] = back[g * seqs : (g + 1) * seqs, r * LANES : (r + 1) * LANES]

    def side(grads, rows):
        total = dot(grads, rows, contract=(0, 0))
        features = rows.shape[1] // tokens
        return functools.reduce(
            jnp.add,
            [
                total[t * proj : (t + 1) * proj, t * features : (t + 1) * features]
                for t in range(tokens)
            ],
        )

    left_side = side(
        jnp.concatenate([left_back[owner] for owner in order], axis=0), rows_ref[...]
    )
    columns = groups * prow_n * seqs
    right_side = side(right_back[...].reshape(columns, LANES), rows_ref[:columns])
    both = jnp.concatenate([left_side, right_side], axis=0).astype(BF16)
    both = jnp.concatenate([both, jnp.zeros_like(both)], axis=1)

    message_ref[flat : flat + 2 * proj] = both
    message_ref[flat + 2 * proj :] = left_back[(2 * own_group + 1 - core) * prow_n + own_row]
    grads_ref[0] = left_back[(2 * own_group + core) * prow_n + own_row]
    grads_ref[1] = right_back[own_group * prow_n + own_row]


def close_kernel(
    grads_ref,
    own_ref,
    message_ref,
    normed_ref,
    inverse_ref,
    left_ref,
    right_ref,
    out_ref,
    left_out_ref,
    right_out_ref,
    rows_out_ref,
):
    flat = out_ref.shape[0]
    proj, features = left_out_ref.shape
    out_ref[...] = own_ref[:flat].astype(F32) + message_ref[:flat].astype(F32)
    sides = slice(flat, flat + 2 * proj)
    both = own_ref[sides, :features].astype(F32) + message_ref[sides, :features].astype(F32)
    left_out_ref[...] = both[:proj]
    right_out_ref[...] = both[proj:]
    left_back = grads_ref[0].astype(F32) + message_ref[flat + 2 * proj :].astype(F32)
    grad_normed = dot(left_back.astype(BF16), left_ref[...], contract=(1, 1))
    grad_normed = grad_normed + dot(grads_ref[1], right_ref[...], contract=(1, 1))
    normed = normed_ref[...]
    means = jnp.concatenate([grad_normed, grad_normed * normed], axis=0)
    means = group_mean(means, features)
    mean_factor, projected = means[: normed.shape[0]], means[normed.shape[0] :]
    result = inverse_ref[...] * (grad_normed - mean_factor - normed * projected)
    rows_out_ref[...] = jnp.stack(
        [result[:, t * features : (t + 1) * features] for t in range(rows_out_ref.shape[1])],
        axis=1,
    ).astype(BF16)


def local_gathered(
    homolog_features,
    subset_homolog_positions,
    first_side_matrix,
    second_side_matrix,
    final_mapping_matrix,
    final_offset_vector,
    upstream_sensitivity,
):
    prow_n, groups = lax.axis_size("prow"), lax.axis_size("px")
    owners = prow_n * groups * 2
    heads, tokens, features = homolog_features.shape
    seqs = subset_homolog_positions.shape[0]
    block_rows, block_cols, pair_width = upstream_sensitivity.shape
    proj = first_side_matrix.shape[1]
    flat = proj * proj
    packed = tokens * features
    shape = jax.ShapeDtypeStruct
    vmem = pl.BlockSpec(memory_space=pltpu.VMEM)
    smem = pl.BlockSpec(memory_space=pltpu.SMEM)
    params = pltpu.CompilerParams(vmem_limit_bytes=36 * 1024 * 1024)

    pairs = block_rows * block_cols
    length = seqs * packed // LANES
    hbm = pl.BlockSpec(memory_space=pltpu.HBM)
    normed, inverse, sent = pl.pallas_call(
        pick_kernel,
        out_shape=(
            shape((seqs, packed), F32),
            shape((seqs, packed), F32),
            shape((pairs + length, LANES), BF16),
        ),
        in_specs=[hbm] * 3,
        out_specs=(vmem,) * 3,
        scratch_shapes=[
            pltpu.VMEM((1, seqs), jnp.int32),
            pltpu.VMEM((packed, heads), BF16),
            pltpu.SemaphoreType.DMA((3,)),
        ],
        compiler_params=pltpu.CompilerParams(vmem_limit_bytes=60 * 1024 * 1024),
        name="pick_rows",
    )(
        subset_homolog_positions.reshape(1, seqs),
        homolog_features.transpose(1, 2, 0).reshape(packed, heads),
        upstream_sensitivity.reshape(pairs, pair_width),
    )

    mapping = final_mapping_matrix.reshape(proj, proj, pair_width)
    mapping = mapping.swapaxes(0, 1).reshape(flat, pair_width)
    turned_mapping = mapping.T

    def swapped_with(values, axis, size, mask):
        return lax.ppermute(values, axis, [(n, n ^ mask) for n in range(size)])

    messages = [sent] + [
        swapped_with(sent, "prow", prow_n, down) for down in range(1, prow_n)
    ]
    messages[1], own, left_wide, left_one, right_one, offset = pl.pallas_call(
        setup_kernel,
        out_shape=(
            shape(sent.shape, BF16),
            shape(sent.shape, BF16),
            shape((packed, tokens * LANES), BF16),
            shape((packed, LANES), BF16),
            shape((packed, LANES), BF16),
            shape((1, pair_width), F32),
        ),
        in_specs=[vmem] * 7,
        out_specs=(vmem,) * 6,
        compiler_params=params,
        name="setup",
    )(
        messages[1],
        sent,
        mapping,
        turned_mapping,
        first_side_matrix.T,
        second_side_matrix.T,
        final_offset_vector.reshape(1, pair_width),
    )
    messages += [
        swapped_with(one, "px", groups, across) for across in range(1, groups) for one in messages
    ]
    messages[0] = own
    offsets = [(down, across) for across in range(groups) for down in range(prow_n)]
    rows = jnp.stack([one[pairs:] for one in messages])
    theirs = lax.ppermute(rows, "pc", [(0, 1), (1, 0)])

    place = jnp.stack([lax.axis_index("prow"), lax.axis_index("px"), lax.axis_index("pc")])

    columns = groups * proj // tokens * block_cols
    cot, pulled = pl.pallas_call(
        functools.partial(pull_kernel, offsets),
        out_shape=(
            shape((prow_n, groups, pairs, pair_width), BF16),
            shape((prow_n, columns, block_rows * LANES), BF16),
        ),
        in_specs=[smem] + [vmem] * (1 + len(messages)),
        out_specs=(vmem,) * 2,
        compiler_params=params,
        cost_estimate=pl.CostEstimate(
            flops=2 * prow_n * groups * pairs * pair_width * flat,
            bytes_accessed=2 * prow_n * groups * pairs * (2 * pair_width + flat),
            transcendentals=0,
        ),
        name="pull_back",
    )(place, turned_mapping, *messages)

    pair_delta, grads, message = pl.pallas_call(
        functools.partial(pair_kernel, offsets),
        out_shape=(
            shape(upstream_sensitivity.shape, BF16),
            shape((2, seqs, LANES), BF16),
            shape((flat + 2 * proj + seqs, LANES), BF16),
        ),
        in_specs=[smem] + [vmem] * 8,
        out_specs=(vmem,) * 3,
        scratch_shapes=[
            pltpu.VMEM((owners * seqs, packed), BF16),
            pltpu.VMEM((owners, seqs, tokens * LANES), BF16),
            pltpu.VMEM((tokens * seqs, columns), BF16),
            pltpu.VMEM((prow_n, groups * pairs, flat), BF16),
            pltpu.VMEM((prow_n, groups, length, LANES), BF16),
            pltpu.VMEM((prow_n, groups, length, LANES), BF16),
            pltpu.VMEM((columns, tokens * seqs), BF16),
            pltpu.VMEM((owners, seqs, LANES), BF16),
            pltpu.VMEM((groups * prow_n, seqs, LANES), BF16),
            pltpu.VMEM((columns, tokens * seqs), F32),
            pltpu.VMEM((pair_width, flat), F32),
        ],
        compiler_params=params,
        name="pair_work",
    )(place, rows, theirs, mapping, left_wide, right_one, offset, cot, pulled)

    theirs = lax.ppermute(message, "pc", [(0, 1), (1, 0)])
    output_weight_gradient, left_weight_gradient, right_weight_gradient, alignment = pl.pallas_call(
        close_kernel,
        out_shape=(
            shape((flat, pair_width), F32),
            shape((proj, features), F32),
            shape((proj, features), F32),
            shape((seqs, tokens, features), BF16),
        ),
        in_specs=[vmem] * 7,
        out_specs=(vmem,) * 4,
        compiler_params=params,
        name="close",
    )(grads, message, theirs, normed, inverse, left_one, right_one)
    return (
        pair_delta,
        alignment,
        left_weight_gradient.T,
        right_weight_gradient.T,
        output_weight_gradient,
    )


def shapes_allow_gathering(
    mesh_shape, features, positions, first_side, second_side, mapping, offset, cot
):
    rows_n, cols_n = mesh_shape["prow"], mesh_shape["pcol"]
    parts = mesh_shape["rep"]
    tokens = features.shape[1] // (rows_n * cols_n)
    block_rows, block_cols = cot.shape[0] // (parts * rows_n), cot.shape[1] // cols_n
    proj, width = first_side.shape[1], cot.shape[2]
    return (
        cols_n % 2 == 0
        and cot.shape[1] * cot.shape[1] <= GATHERED_PAIRS
        and tokens * proj == LANES
        and tokens == 4
        and block_rows % tokens == 0
        and block_cols == rows_n * tokens == 16
        and rows_n & (rows_n - 1) == 0
        and cols_n & (cols_n - 1) == 0
        and width == LANES
        and features.shape[2] >= 2 * proj
        and positions.shape[0] // parts % 16 == 0
        and features.shape[2] * tokens % LANES == 0
    )


def solution(mesh):
    def run(local, over, columns, *args):
        tokens_split = P("rep", columns + ("prow",), None)
        pairs_split = P(("rep", "prow"), columns, None)
        return jax.shard_map(
            local,
            mesh=over,
            in_specs=(tokens_split, P("rep"), P(), P(), P(), P(), pairs_split),
            out_specs=(pairs_split, tokens_split, P("rep", None), P("rep", None), P("rep", None)),
            check_vma=False,
        )(*args)

    def program(*args):
        if not shapes_allow_gathering(mesh.shape, *args):
            return run(local_phased, mesh, ("pcol",), *args)
        reps, rows_n, cols_n = (mesh.shape[name] for name in ("rep", "prow", "pcol"))
        chips = Mesh(
            mesh.devices.reshape(reps, rows_n, cols_n // 2, 2), ("rep", "prow", "px", "pc")
        )
        return run(local_gathered, chips, ("px", "pc"), *args)

    return program
```

```python
import functools

import jax
import jax.numpy as jnp
from jax import lax
from jax.experimental import pallas as pl
from jax.experimental.pallas import tpu as pltpu
from jax.sharding import Mesh
from jax.sharding import PartitionSpec as P

BF16, F32 = jnp.bfloat16, jnp.float32
LANES = 128
GATHERED_PAIRS = 4096

PAIRS_AT_ONCE = 1024


def normalize(values):
    values = values.astype(jnp.float32)
    mean_factor = jnp.mean(values, axis=-1, keepdims=True)
    centered = values - mean_factor
    variance = jnp.mean(centered * centered, axis=-1, keepdims=True)
    inverse_spread = lax.rsqrt(variance + 1e-05)
    return (centered * inverse_spread, inverse_spread)


def transposed(rows_n, cols_n):
    return [
        (r * cols_n + c, c * rows_n + r) for r in range(rows_n) for c in range(cols_n)
    ]


def spread(values, axes, count):
    return lax.all_to_all(jnp.broadcast_to(values[None], (count,) + values.shape), axes, 0, 0)


def local_phased(
    homolog_features,
    subset_homolog_positions,
    first_side_matrix,
    second_side_matrix,
    final_mapping_matrix,
    final_offset_vector,
    upstream_sensitivity,
):
    axes = ("prow", "pcol")
    rows_n, cols_n = lax.axis_size("prow"), lax.axis_size("pcol")
    devices = rows_n * cols_n
    seq_count = subset_homolog_positions.shape[0]
    tokens, features = homolog_features.shape[1:]
    row_count, col_count, pair_width = upstream_sensitivity.shape
    proj = first_side_matrix.shape[1]
    flat = proj * proj
    to_rows = transposed(rows_n, cols_n)
    to_tokens = [(target, source) for source, target in to_rows]

    picked = jnp.take(homolog_features, subset_homolog_positions, axis=0)
    packed = picked.reshape(seq_count, tokens * features)
    row_own = lax.ppermute(packed, axes, to_rows)
    col_all = spread(packed, "prow", rows_n)
    row_all = spread(row_own, "pcol", cols_n)

    def side_of(chunks, count, matrix):
        chunks = chunks.reshape(count // tokens, seq_count, tokens, features)
        chunks = chunks.transpose(1, 0, 2, 3).reshape(seq_count, count, features)
        normed_low = normalize(chunks)[0].astype(jnp.bfloat16)
        side = jnp.einsum("stc,cp->stp", normed_low, matrix, preferred_element_type=jnp.float32)
        return normed_low, side.astype(jnp.bfloat16)

    row_normed, left = side_of(row_all, row_count, first_side_matrix)
    col_normed, right = side_of(col_all, col_count, second_side_matrix)

    def block_step(left_blk, cot_blk):
        rows = left_blk.shape[1]
        outer = jnp.einsum("sip,sjq->ijpq", left_blk, right, preferred_element_type=jnp.float32)
        outer = (outer / seq_count).astype(jnp.bfloat16).reshape(rows * col_count, flat)
        update = jnp.dot(outer, final_mapping_matrix, preferred_element_type=jnp.float32)
        update = (update + final_offset_vector).astype(jnp.bfloat16)
        cot_flat = cot_blk.reshape(rows * col_count, pair_width)
        grad_out = jnp.dot(outer.T, cot_flat, preferred_element_type=jnp.float32)
        grad_outer = jnp.dot(cot_flat, final_mapping_matrix.T, preferred_element_type=jnp.float32)
        grad_outer = grad_outer.astype(jnp.bfloat16).reshape(rows, col_count, proj, proj)
        grad_left = jnp.einsum(
            "ijpq,sjq->sip", grad_outer, right, preferred_element_type=jnp.float32
        )
        grad_right = jnp.einsum(
            "ijpq,sip->sjq", grad_outer, left_blk, preferred_element_type=jnp.float32
        )
        return update.reshape(rows, col_count, pair_width), grad_out, grad_left, grad_right

    block = max(1, min(row_count, PAIRS_AT_ONCE // col_count))
    blocks = row_count // block
    if blocks == 1:
        update, grad_out, grad_left, grad_right = block_step(left, upstream_sensitivity)
    else:
        def step(totals, inputs):
            update, grad_out, grad_left, grad_right = block_step(*inputs)
            return (totals[0] + grad_out, totals[1] + grad_right), (update, grad_left)

        (grad_out, grad_right), (update, grad_left) = lax.scan(
            step,
            (
                jnp.zeros((flat, pair_width), jnp.float32),
                jnp.zeros((seq_count, col_count, proj), jnp.float32),
            ),
            (
                left.reshape(seq_count, blocks, block, proj).transpose(1, 0, 2, 3),
                upstream_sensitivity.reshape(blocks, block, col_count, pair_width),
            ),
        )
        grad_left = grad_left.transpose(1, 0, 2, 3).reshape(seq_count, row_count, proj)
    pair_delta = update.reshape(row_count, col_count, pair_width)

    grad_left = (grad_left / seq_count).astype(jnp.bfloat16)
    grad_right = (grad_right / seq_count).astype(jnp.bfloat16)

    def weight_part(normed, grads):
        return jnp.einsum("stc,stp->cp", normed, grads, preferred_element_type=jnp.float32)

    side_part = jnp.concatenate(
        [weight_part(row_normed, grad_left), weight_part(col_normed, grad_right)], axis=1
    )
    share_rows = flat // devices
    side_rows = -(-features * 2 * proj // (pair_width * devices))
    side_flat = side_part.reshape(-1, pair_width)
    side_flat = jnp.pad(side_flat, ((0, side_rows * devices - side_flat.shape[0]), (0, 0)))
    shares = jnp.concatenate(
        [
            grad_out.reshape(devices, share_rows, pair_width),
            side_flat.reshape(devices, side_rows, pair_width),
        ],
        axis=1,
    ).astype(jnp.bfloat16)
    shares = lax.all_to_all(shares, axes, 0, 0)

    def chunks_of(grads, count):
        grads = grads.reshape(seq_count, count // tokens, tokens * proj)
        return grads.transpose(1, 0, 2)

    left_back = lax.all_to_all(chunks_of(grad_left, row_count), "pcol", 0, 0)
    right_back = lax.all_to_all(chunks_of(grad_right, col_count), "prow", 0, 0)
    left_back = jnp.sum(left_back.astype(jnp.float32), axis=0).astype(jnp.bfloat16)
    right_back = jnp.sum(right_back.astype(jnp.float32), axis=0).astype(jnp.bfloat16)
    left_back = lax.ppermute(left_back, axes, to_tokens)

    share = jnp.sum(shares.astype(jnp.float32), axis=0).astype(jnp.bfloat16)
    message = spread(share, axes, devices)
    output_weight_gradient = (
        message[:, :share_rows].reshape(flat, pair_width).astype(jnp.float32)
    )
    side = message[:, share_rows:].reshape(-1, pair_width).astype(jnp.float32)
    side = side[: features * 2 * proj // pair_width].reshape(features, 2 * proj)
    left_weight_gradient, right_weight_gradient = side[:, :proj], side[:, proj:]

    normed, inverse_spread = normalize(picked)
    both = jnp.concatenate(
        [
            left_back.reshape(seq_count, tokens, proj),
            right_back.reshape(seq_count, tokens, proj),
        ],
        axis=-1,
    )
    sides = jnp.concatenate([first_side_matrix, second_side_matrix], axis=1)
    grad_normed = jnp.einsum("stp,cp->stc", both, sides, preferred_element_type=jnp.float32)
    mean_factor = jnp.mean(grad_normed, axis=-1, keepdims=True)
    projected = jnp.mean(grad_normed * normed, axis=-1, keepdims=True)
    alignment_gradient = (
        inverse_spread * (grad_normed - mean_factor - normed * projected)
    ).astype(jnp.bfloat16)
    return (
        pair_delta,
        alignment_gradient,
        left_weight_gradient,
        right_weight_gradient,
        output_weight_gradient,
    )


def dot(x, y, contract=(1, 0), precision=None):
    return lax.dot_general(
        x, y, (((contract[0],), (contract[1],)), ((), ())),
        precision=precision, preferred_element_type=F32,
    )


def lane_ids(shape):
    return lax.broadcasted_iota(jnp.int32, shape, len(shape) - 1)


def fold_tokens(parts):
    quarter = LANES // 4
    chunk = lane_ids(parts[0].shape) // quarter
    first, even = chunk < 2, chunk % 2 == 0
    halves = [
        jnp.where(first, parts[t], parts[t + 2])
        + pltpu.roll(jnp.where(first, parts[t + 2], parts[t]), 2 * quarter, 1)
        for t in range(2)
    ]
    other = jnp.where(even, halves[1], halves[0])
    moved = jnp.where(even, pltpu.roll(other, 3 * quarter, 1), pltpu.roll(other, quarter, 1))
    return jnp.where(even, halves[0], halves[1]) + moved


def group_mean(x, group):
    rows, lanes = x.shape
    rows_id = lax.broadcasted_iota(jnp.int32, (lanes, lanes), 0) // group
    cols_id = lax.broadcasted_iota(jnp.int32, (lanes, lanes), 1) // group
    block = (rows_id == cols_id).astype(BF16)
    pieces = [x.astype(BF16)]
    if x.dtype == F32:
        for _ in range(2):
            x = x - pieces[-1].astype(F32)
            pieces.append(x.astype(BF16))
    total = dot(jnp.concatenate(pieces, axis=0), block)
    total = functools.reduce(
        jnp.add, [total[n * rows : (n + 1) * rows] for n in reversed(range(len(pieces)))]
    )
    return total * (1.0 / group)


def pick_kernel(
    positions_ref,
    features_ref,
    cot_ref,
    normed_ref,
    inverse_ref,
    message_ref,
    positions,
    features,
    in_sems,
):
    pairs = cot_ref.shape[0]
    inputs = [
        pltpu.make_async_copy(source, target, in_sems.at[n])
        for n, (source, target) in enumerate(
            [
                (positions_ref, positions),
                (features_ref, features),
                (cot_ref, message_ref.at[pl.ds(0, pairs)]),
            ]
        )
    ]
    for copy in inputs:
        copy.start()
    heads = features_ref.shape[1]
    seqs, packed = normed_ref.shape
    channels = packed // 4
    for copy in inputs:
        copy.wait()
    wanted = positions[...] == lax.broadcasted_iota(jnp.int32, (heads, seqs), 0)
    chosen = dot(wanted.astype(BF16), features[...], contract=(0, 1))
    mean_factor = group_mean(chosen.astype(BF16), channels)
    centered = chosen - mean_factor
    variance = group_mean(centered * centered, channels)
    inverse = lax.rsqrt(variance + 1e-05)
    normed = centered * inverse
    for n in range(packed // LANES):
        message_ref[pairs + n * seqs : pairs + (n + 1) * seqs] = normed[
            :, n * LANES : (n + 1) * LANES
        ].astype(BF16)
    normed_ref[...] = normed
    inverse_ref[...] = inverse


def setup_kernel(
    first_ref,
    own_ref,
    mapping_ref,
    turned_mapping_ref,
    left_ref,
    right_ref,
    offset_ref,
    first_out_ref,
    own_out_ref,
    left_wide_ref,
    left_one_ref,
    right_one_ref,
    offset_out_ref,
):
    del mapping_ref, turned_mapping_ref
    first_out_ref[...] = first_ref[...]
    own_out_ref[...] = own_ref[...]
    offset_out_ref[...] = offset_ref[...]
    proj, channels = left_ref.shape
    tokens = left_one_ref.shape[0] // channels
    repeat = lane_ids((proj, LANES)) % proj
    repeat = (repeat == lax.broadcasted_iota(jnp.int32, (proj, LANES), 0)).astype(BF16)
    left_row = dot(left_ref[...], repeat, contract=(0, 0))
    right_row = dot(right_ref[...], repeat, contract=(0, 0))
    slot = lane_ids(left_row.shape) // proj
    nothing = jnp.zeros(left_row.shape, BF16)
    for t in range(tokens):
        here = slice(t * channels, (t + 1) * channels)
        left_one_ref[here] = jnp.where(slot == t, left_row, 0.0).astype(BF16)
        right_one_ref[here] = jnp.where(slot == t, right_row, 0.0).astype(BF16)
        for other in range(tokens):
            left_wide_ref[here, other * LANES : (other + 1) * LANES] = (
                left_row.astype(BF16) if other == t else nothing
            )


def place_blocks(place_ref, offsets, blocks, out_ref):
    for (down, across), block in zip(offsets, blocks, strict=True):
        out_ref[place_ref[0] ^ down, place_ref[1] ^ across] = block


def pull_blocks(cot, mapping_ref, pulled_ref, r, at):
    block_rows = pulled_ref.shape[2] // LANES
    block_cols = cot.shape[0] // block_rows
    grad = dot(cot, mapping_ref[...])
    for h in range(mapping_ref.shape[1] // LANES):
        there = pl.ds(pl.multiple_of(at + h * block_cols, block_cols), block_cols)
        for t in range(block_rows):
            pulled_ref[r, there, t * LANES : (t + 1) * LANES] = grad[
                t * block_cols : (t + 1) * block_cols, h * LANES : (h + 1) * LANES
            ].astype(BF16)


def pull_own_kernel(downs, place_ref, mapping_ref, *refs):
    *message_refs, pulled_ref, rows_ref = refs
    pairs = message_refs[0].shape[0] - rows_ref.shape[1]
    for n, (down, ref) in enumerate(zip(downs, message_refs, strict=True)):
        rows_ref[n] = ref[pairs:]
        pull_blocks(ref[:pairs], mapping_ref, pulled_ref, place_ref[0] ^ down, 0)


def pull_kernel(offsets, place_ref, mapping_ref, own_ref, *refs):
    *message_refs, cot_ref, pulled_ref = refs
    rows, groups, pairs, _ = cot_ref.shape
    place_blocks(place_ref, offsets, [ref[:pairs] for ref in message_refs], cot_ref)
    share = own_ref.shape[1]
    for r in range(rows):
        for across in range(1, groups):
            group = place_ref[1] ^ across
            pull_blocks(cot_ref[r, group], mapping_ref, pulled_ref, r, group * share)
        at = pl.multiple_of(place_ref[1] * share, share)
        pulled_ref[r, pl.ds(at, share)] = own_ref[r]


def owner_order(places, prow_n, core):
    mine = [(2 * g + core) * prow_n + r for g, r in places]
    return mine + [(2 * g + 1 - core) * prow_n + r for g, r in places]


def shuffle_matrix(block_cols, proj, tokens):
    wide, highs = block_cols * proj, proj // tokens
    source = lax.broadcasted_iota(jnp.int32, (wide, wide), 0)
    target = lax.broadcasted_iota(jnp.int32, (wide, wide), 1)
    jj, qh = target % block_cols, target // block_cols % highs
    ql = target // (highs * block_cols)
    return (source == jj * proj + qh * tokens + ql).astype(BF16)


def left_block(expanded, row, step_owners, tokens):
    ahead = jnp.concatenate([expanded[row * step_owners + o] for o in range(step_owners)], axis=1)
    low = lane_ids(ahead.shape) % LANES // (LANES // tokens)
    return jnp.concatenate(
        [jnp.where(low == l, ahead, jnp.zeros_like(ahead)) for l in range(tokens)], axis=0
    )


def pair_kernel(
    offsets,
    place_ref,
    mine_from_ref,
    theirs_from_ref,
    mapping_ref,
    left_ref,
    right_ref,
    offset_ref,
    cot_ref,
    pulled_ref,
    pair_ref,
    grads_ref,
    message_ref,
    rows_ref,
    expanded,
    swapped,
    outer_ref,
    mine_ref,
    theirs_ref,
    turned,
    left_back,
    right_back,
    sums,
    weights,
):
    for source, target in ((mine_from_ref, mine_ref), (theirs_from_ref, theirs_ref)):
        place_blocks(place_ref, offsets, [source[n] for n in range(source.shape[0])], target)
    prow_n, groups = mine_ref.shape[:2]
    block_rows, block_cols, pair_width = pair_ref.shape
    owners, seqs = expanded.shape[:2]
    packed = left_ref.shape[0]
    tokens = left_ref.shape[1] // LANES
    proj = LANES // tokens
    highs = proj // tokens
    span = highs * block_cols
    own_row, own_group, core = place_ref[0], place_ref[1], place_ref[2]

    def rows_of(ref, g, r):
        return jnp.concatenate(
            [ref[r, g, n * seqs : (n + 1) * seqs] for n in range(packed // LANES)], axis=1
        )

    places = [(g, r) for g in range(groups) for r in range(prow_n)]
    rows_mine = [rows_of(mine_ref, g, r) for g, r in places]
    rows_all = jnp.concatenate(
        rows_mine + [rows_of(theirs_ref, g, r) for g, r in places], axis=0
    )
    rows_ref[...] = rows_all
    wide_left = dot(rows_all, left_ref[...]).astype(BF16)
    for n, owner in enumerate(owner_order(places, prow_n, core)):
        expanded[owner] = wide_left[n * seqs : (n + 1) * seqs]

    side_rows = []
    for g in range(groups):
        chunks = rows_mine[g * prow_n : (g + 1) * prow_n]
        side_rows.append(
            jnp.concatenate([dot(x, right_ref[...]).astype(BF16) for x in chunks], axis=1)
        )
    right = dot(jnp.concatenate(side_rows, axis=0), shuffle_matrix(block_cols, proj, tokens))
    for g in range(groups):
        for l in range(tokens):
            swapped[l * seqs : (l + 1) * seqs, g * span : (g + 1) * span] = (
                right[g * seqs : (g + 1) * seqs, l * span : (l + 1) * span] * (1.0 / seqs)
            ).astype(BF16)
    turned[...] = swapped[...].astype(F32).T.astype(BF16)

    order = owner_order(places, prow_n, core)
    pairs = block_rows * block_cols
    step_owners = owners // prow_n
    for row in range(prow_n):
        block = left_block(expanded, row, step_owners, tokens)
        made = dot(turned[...], block)
        for g in range(groups):
            for t in range(block_rows):
                start = (g * block_rows + t) * block_cols
                lanes = slice(t * LANES, (t + 1) * LANES)
                for h in range(highs):
                    there = slice((g * highs + h) * block_cols, (g * highs + h + 1) * block_cols)
                    outer_ref[row, start : start + block_cols, h * LANES : (h + 1) * LANES] = made[
                        there, lanes
                    ].astype(BF16)
        cot = cot_ref[row].reshape(groups * pairs, pair_width)
        weight_part = dot(cot, outer_ref[row], contract=(0, 0))
        weights[...] = weight_part if row == 0 else weights[...] + weight_part
        if row == prow_n - 1:
            share = block_rows * block_cols
            mine = outer_ref[own_row, pl.ds(pl.multiple_of(own_group * share, share), share)]
            update = dot(mine, mapping_ref[...]) + offset_ref[...]
            pair_ref[...] = update.astype(BF16).reshape(pair_ref.shape)
            flat = weights.shape[1]
            outer_f = weights[...].T
            weight_rows = outer_f.reshape(proj, proj, pair_width).swapaxes(0, 1).reshape(flat, pair_width)

            message_ref[:flat] = weight_rows.astype(BF16)
        pulled = pulled_ref[row]
        back = dot(swapped[...], pulled)
        low = lane_ids((seqs, back.shape[1])) % LANES // proj
        back = functools.reduce(
            jnp.add,
            [
                jnp.where(low == l, back[l * seqs : (l + 1) * seqs], 0.0)
                for l in range(tokens)
            ],
        )
        for o in range(step_owners):
            parts = [
                back[:, (o * tokens + t) * LANES : (o * tokens + t + 1) * LANES]
                for t in range(tokens)
            ]
            left_back[row * step_owners + o] = fold_tokens(parts).astype(BF16)
        sum_part = dot(pulled, block, contract=(1, 1))
        sums[...] = sum_part if row == 0 else sums[...] + sum_part

    back = (sums[...].T * (1.0 / seqs)).astype(BF16)
    back = jnp.concatenate(
        [
            jnp.concatenate(
                [
                    back[l * seqs : (l + 1) * seqs, g * span : (g + 1) * span]
                    for l in range(tokens)
                ],
                axis=1,
            )
            for g in range(groups)
        ],
        axis=0,
    )
    shuffle = shuffle_matrix(block_cols, proj, tokens)
    back = dot(back, shuffle, contract=(1, 1)).astype(BF16)
    for g, r in places:
        right_back[g * prow_n + r] = back[g * seqs : (g + 1) * seqs, r * LANES : (r + 1) * LANES]

    def side(grads, rows):
        total = dot(grads, rows, contract=(0, 0))
        features = rows.shape[1] // tokens
        return functools.reduce(
            jnp.add,
            [
                total[t * proj : (t + 1) * proj, t * features : (t + 1) * features]
                for t in range(tokens)
            ],
        )

    left_side = side(
        jnp.concatenate([left_back[owner] for owner in order], axis=0), rows_ref[...]
    )
    columns = groups * prow_n * seqs
    right_side = side(right_back[...].reshape(columns, LANES), rows_ref[:columns])
    both = jnp.concatenate([left_side, right_side], axis=0).astype(BF16)
    both = jnp.concatenate([both, jnp.zeros_like(both)], axis=1)

    message_ref[flat : flat + 2 * proj] = both
    message_ref[flat + 2 * proj :] = left_back[(2 * own_group + 1 - core) * prow_n + own_row]
    grads_ref[0] = left_back[(2 * own_group + core) * prow_n + own_row]
    grads_ref[1] = right_back[own_group * prow_n + own_row]


def close_kernel(
    grads_ref,
    own_ref,
    message_ref,
    normed_ref,
    inverse_ref,
    left_ref,
    right_ref,
    out_ref,
    left_out_ref,
    right_out_ref,
    rows_out_ref,
):
    flat = out_ref.shape[0]
    proj, features = left_out_ref.shape
    out_ref[...] = own_ref[:flat].astype(F32) + message_ref[:flat].astype(F32)
    sides = slice(flat, flat + 2 * proj)
    both = own_ref[sides, :features].astype(F32) + message_ref[sides, :features].astype(F32)
    left_out_ref[...] = both[:proj]
    right_out_ref[...] = both[proj:]
    left_back = grads_ref[0].astype(F32) + message_ref[flat + 2 * proj :].astype(F32)
    grad_normed = dot(left_back.astype(BF16), left_ref[...], contract=(1, 1))
    grad_normed = grad_normed + dot(grads_ref[1], right_ref[...], contract=(1, 1))
    normed = normed_ref[...]
    means = jnp.concatenate([grad_normed, grad_normed * normed], axis=0)
    means = group_mean(means, features)
    mean_factor, projected = means[: normed.shape[0]], means[normed.shape[0] :]
    result = inverse_ref[...] * (grad_normed - mean_factor - normed * projected)
    rows_out_ref[...] = jnp.stack(
        [result[:, t * features : (t + 1) * features] for t in range(rows_out_ref.shape[1])],
        axis=1,
    ).astype(BF16)


def local_gathered(
    homolog_features,
    subset_homolog_positions,
    first_side_matrix,
    second_side_matrix,
    final_mapping_matrix,
    final_offset_vector,
    upstream_sensitivity,
):
    prow_n, groups = lax.axis_size("prow"), lax.axis_size("px")
    owners = prow_n * groups * 2
    heads, tokens, features = homolog_features.shape
    seqs = subset_homolog_positions.shape[0]
    block_rows, block_cols, pair_width = upstream_sensitivity.shape
    proj = first_side_matrix.shape[1]
    flat = proj * proj
    packed = tokens * features
    shape = jax.ShapeDtypeStruct
    vmem = pl.BlockSpec(memory_space=pltpu.VMEM)
    smem = pl.BlockSpec(memory_space=pltpu.SMEM)
    params = pltpu.CompilerParams(vmem_limit_bytes=36 * 1024 * 1024)

    pairs = block_rows * block_cols
    length = seqs * packed // LANES
    hbm = pl.BlockSpec(memory_space=pltpu.HBM)
    normed, inverse, sent = pl.pallas_call(
        pick_kernel,
        out_shape=(
            shape((seqs, packed), F32),
            shape((seqs, packed), F32),
            shape((pairs + length, LANES), BF16),
        ),
        in_specs=[hbm] * 3,
        out_specs=(vmem,) * 3,
        scratch_shapes=[
            pltpu.VMEM((1, seqs), jnp.int32),
            pltpu.VMEM((packed, heads), BF16),
            pltpu.SemaphoreType.DMA((3,)),
        ],
        compiler_params=pltpu.CompilerParams(vmem_limit_bytes=60 * 1024 * 1024),
        name="pick_rows",
    )(
        subset_homolog_positions.reshape(1, seqs),
        homolog_features.transpose(1, 2, 0).reshape(packed, heads),
        upstream_sensitivity.reshape(pairs, pair_width),
    )

    mapping = final_mapping_matrix.reshape(proj, proj, pair_width)
    mapping = mapping.swapaxes(0, 1).reshape(flat, pair_width)
    turned_mapping = mapping.T

    def swapped_with(values, axis, size, mask):
        return lax.ppermute(values, axis, [(n, n ^ mask) for n in range(size)])

    messages = [sent] + [
        swapped_with(sent, "prow", prow_n, down) for down in range(1, prow_n)
    ]
    messages[1], own, left_wide, left_one, right_one, offset = pl.pallas_call(
        setup_kernel,
        out_shape=(
            shape(sent.shape, BF16),
            shape(sent.shape, BF16),
            shape((packed, tokens * LANES), BF16),
            shape((packed, LANES), BF16),
            shape((packed, LANES), BF16),
            shape((1, pair_width), F32),
        ),
        in_specs=[vmem] * 7,
        out_specs=(vmem,) * 6,
        compiler_params=params,
        name="setup",
    )(
        messages[1],
        sent,
        mapping,
        turned_mapping,
        first_side_matrix.T,
        second_side_matrix.T,
        final_offset_vector.reshape(1, pair_width),
    )
    messages += [
        swapped_with(one, "px", groups, across) for across in range(1, groups) for one in messages
    ]
    messages[0] = own
    offsets = [(down, across) for across in range(groups) for down in range(prow_n)]
    place = jnp.stack([lax.axis_index("prow"), lax.axis_index("px"), lax.axis_index("pc")])

    columns = groups * proj // tokens * block_cols
    pull_cost = pl.CostEstimate(
        flops=prow_n * groups * pairs * pair_width * flat,
        bytes_accessed=prow_n * groups * pairs * (2 * pair_width + flat),
        transcendentals=0,
    )
    pulled_own, rows_own = pl.pallas_call(
        functools.partial(pull_own_kernel, [down for down, _ in offsets[:prow_n]]),
        out_shape=(
            shape((prow_n, columns // groups, block_rows * LANES), BF16),
            shape((prow_n, length, LANES), BF16),
        ),
        in_specs=[smem] + [vmem] * (1 + prow_n),
        out_specs=(vmem,) * 2,
        compiler_params=params,
        cost_estimate=pull_cost,
        name="pull_own",
    )(place, turned_mapping, *messages[:prow_n])
    rows = jnp.concatenate(
        [rows_own] + [one[None, pairs:] for one in messages[prow_n:]], axis=0
    )
    theirs = lax.ppermute(rows, "pc", [(0, 1), (1, 0)])
    cot, pulled = pl.pallas_call(
        functools.partial(pull_kernel, offsets),
        out_shape=(
            shape((prow_n, groups, pairs, pair_width), BF16),
            shape((prow_n, columns, block_rows * LANES), BF16),
        ),
        in_specs=[smem] + [vmem] * (2 + len(messages)),
        out_specs=(vmem,) * 2,
        compiler_params=params,
        cost_estimate=pull_cost,
        name="pull_back",
    )(place, turned_mapping, pulled_own, *messages)
    pair_delta, grads, message = pl.pallas_call(
        functools.partial(pair_kernel, offsets),
        out_shape=(
            shape(upstream_sensitivity.shape, BF16),
            shape((2, seqs, LANES), BF16),
            shape((flat + 2 * proj + seqs, LANES), BF16),
        ),
        in_specs=[smem] + [vmem] * 8,
        out_specs=(vmem,) * 3,
        scratch_shapes=[
            pltpu.VMEM((owners * seqs, packed), BF16),
            pltpu.VMEM((owners, seqs, tokens * LANES), BF16),
            pltpu.VMEM((tokens * seqs, columns), BF16),
            pltpu.VMEM((prow_n, groups * pairs, flat), BF16),
            pltpu.VMEM((prow_n, groups, length, LANES), BF16),
            pltpu.VMEM((prow_n, groups, length, LANES), BF16),
            pltpu.VMEM((columns, tokens * seqs), BF16),
            pltpu.VMEM((owners, seqs, LANES), BF16),
            pltpu.VMEM((groups * prow_n, seqs, LANES), BF16),
            pltpu.VMEM((columns, tokens * seqs), F32),
            pltpu.VMEM((pair_width, flat), F32),
        ],
        compiler_params=params,
        name="pair_work",
    )(place, rows, theirs, mapping, left_wide, right_one, offset, cot, pulled)

    theirs = lax.ppermute(message, "pc", [(0, 1), (1, 0)])
    output_weight_gradient, left_weight_gradient, right_weight_gradient, alignment = pl.pallas_call(
        close_kernel,
        out_shape=(
            shape((flat, pair_width), F32),
            shape((proj, features), F32),
            shape((proj, features), F32),
            shape((seqs, tokens, features), BF16),
        ),
        in_specs=[vmem] * 7,
        out_specs=(vmem,) * 4,
        compiler_params=params,
        name="close",
    )(grads, message, theirs, normed, inverse, left_one, right_one)
    return (
        pair_delta,
        alignment,
        left_weight_gradient.T,
        right_weight_gradient.T,
        output_weight_gradient,
    )


def shapes_allow_gathering(
    mesh_shape, features, positions, first_side, second_side, mapping, offset, cot
):
    rows_n, cols_n = mesh_shape["prow"], mesh_shape["pcol"]
    parts = mesh_shape["rep"]
    tokens = features.shape[1] // (rows_n * cols_n)
    block_rows, block_cols = cot.shape[0] // (parts * rows_n), cot.shape[1] // cols_n
    proj, width = first_side.shape[1], cot.shape[2]
    return (
        cols_n % 2 == 0
        and cot.shape[1] * cot.shape[1] <= GATHERED_PAIRS
        and tokens * proj == LANES
        and tokens == 4
        and block_rows % tokens == 0
        and block_cols == rows_n * tokens == 16
        and rows_n & (rows_n - 1) == 0
        and cols_n & (cols_n - 1) == 0
        and width == LANES
        and features.shape[2] >= 2 * proj
        and positions.shape[0] // parts % 16 == 0
        and features.shape[2] * tokens % LANES == 0
    )


def solution(mesh):
    def run(local, over, columns, *args):
        tokens_split = P("rep", columns + ("prow",), None)
        pairs_split = P(("rep", "prow"), columns, None)
        return jax.shard_map(
            local,
            mesh=over,
            in_specs=(tokens_split, P("rep"), P(), P(), P(), P(), pairs_split),
            out_specs=(pairs_split, tokens_split, P("rep", None), P("rep", None), P("rep", None)),
            check_vma=False,
        )(*args)

    def program(*args):
        if not shapes_allow_gathering(mesh.shape, *args):
            return run(local_phased, mesh, ("pcol",), *args)
        reps, rows_n, cols_n = (mesh.shape[name] for name in ("rep", "prow", "pcol"))
        chips = Mesh(
            mesh.devices.reshape(reps, rows_n, cols_n // 2, 2), ("rep", "prow", "px", "pc")
        )
        return run(local_gathered, chips, ("px", "pc"), *args)

    return program
```

```python
import functools

import jax
import jax.numpy as jnp
from jax import lax
from jax.experimental import pallas as pl
from jax.experimental.pallas import tpu as pltpu
from jax.sharding import Mesh
from jax.sharding import PartitionSpec as P

BF16, F32 = jnp.bfloat16, jnp.float32
LANES = 128
GATHERED_PAIRS = 4096

PAIRS_AT_ONCE = 1024


def normalize(values):
    values = values.astype(jnp.float32)
    mean_factor = jnp.mean(values, axis=-1, keepdims=True)
    centered = values - mean_factor
    variance = jnp.mean(centered * centered, axis=-1, keepdims=True)
    inverse_spread = lax.rsqrt(variance + 1e-05)
    return (centered * inverse_spread, inverse_spread)


def transposed(rows_n, cols_n):
    return [
        (r * cols_n + c, c * rows_n + r) for r in range(rows_n) for c in range(cols_n)
    ]


def spread(values, axes, count):
    return lax.all_to_all(jnp.broadcast_to(values[None], (count,) + values.shape), axes, 0, 0)


def local_phased(
    homolog_features,
    subset_homolog_positions,
    first_side_matrix,
    second_side_matrix,
    final_mapping_matrix,
    final_offset_vector,
    upstream_sensitivity,
):
    axes = ("prow", "pcol")
    rows_n, cols_n = lax.axis_size("prow"), lax.axis_size("pcol")
    devices = rows_n * cols_n
    seq_count = subset_homolog_positions.shape[0]
    tokens, features = homolog_features.shape[1:]
    row_count, col_count, pair_width = upstream_sensitivity.shape
    proj = first_side_matrix.shape[1]
    flat = proj * proj
    to_rows = transposed(rows_n, cols_n)
    to_tokens = [(target, source) for source, target in to_rows]

    picked = jnp.take(homolog_features, subset_homolog_positions, axis=0)
    packed = picked.reshape(seq_count, tokens * features)
    row_own = lax.ppermute(packed, axes, to_rows)
    col_all = spread(packed, "prow", rows_n)
    row_all = spread(row_own, "pcol", cols_n)

    def side_of(chunks, count, matrix):
        chunks = chunks.reshape(count // tokens, seq_count, tokens, features)
        chunks = chunks.transpose(1, 0, 2, 3).reshape(seq_count, count, features)
        normed_low = normalize(chunks)[0].astype(jnp.bfloat16)
        side = jnp.einsum("stc,cp->stp", normed_low, matrix, preferred_element_type=jnp.float32)
        return normed_low, side.astype(jnp.bfloat16)

    row_normed, left = side_of(row_all, row_count, first_side_matrix)
    col_normed, right = side_of(col_all, col_count, second_side_matrix)

    def block_step(left_blk, cot_blk):
        rows = left_blk.shape[1]
        outer = jnp.einsum("sip,sjq->ijpq", left_blk, right, preferred_element_type=jnp.float32)
        outer = (outer / seq_count).astype(jnp.bfloat16).reshape(rows * col_count, flat)
        update = jnp.dot(outer, final_mapping_matrix, preferred_element_type=jnp.float32)
        update = (update + final_offset_vector).astype(jnp.bfloat16)
        cot_flat = cot_blk.reshape(rows * col_count, pair_width)
        grad_out = jnp.dot(outer.T, cot_flat, preferred_element_type=jnp.float32)
        grad_outer = jnp.dot(cot_flat, final_mapping_matrix.T, preferred_element_type=jnp.float32)
        grad_outer = grad_outer.astype(jnp.bfloat16).reshape(rows, col_count, proj, proj)
        grad_left = jnp.einsum(
            "ijpq,sjq->sip", grad_outer, right, preferred_element_type=jnp.float32
        )
        grad_right = jnp.einsum(
            "ijpq,sip->sjq", grad_outer, left_blk, preferred_element_type=jnp.float32
        )
        return update.reshape(rows, col_count, pair_width), grad_out, grad_left, grad_right

    block = max(1, min(row_count, PAIRS_AT_ONCE // col_count))
    blocks = row_count // block
    if blocks == 1:
        update, grad_out, grad_left, grad_right = block_step(left, upstream_sensitivity)
    else:
        def step(totals, inputs):
            update, grad_out, grad_left, grad_right = block_step(*inputs)
            return (totals[0] + grad_out, totals[1] + grad_right), (update, grad_left)

        (grad_out, grad_right), (update, grad_left) = lax.scan(
            step,
            (
                jnp.zeros((flat, pair_width), jnp.float32),
                jnp.zeros((seq_count, col_count, proj), jnp.float32),
            ),
            (
                left.reshape(seq_count, blocks, block, proj).transpose(1, 0, 2, 3),
                upstream_sensitivity.reshape(blocks, block, col_count, pair_width),
            ),
        )
        grad_left = grad_left.transpose(1, 0, 2, 3).reshape(seq_count, row_count, proj)
    pair_delta = update.reshape(row_count, col_count, pair_width)

    grad_left = (grad_left / seq_count).astype(jnp.bfloat16)
    grad_right = (grad_right / seq_count).astype(jnp.bfloat16)

    def weight_part(normed, grads):
        return jnp.einsum("stc,stp->cp", normed, grads, preferred_element_type=jnp.float32)

    side_part = jnp.concatenate(
        [weight_part(row_normed, grad_left), weight_part(col_normed, grad_right)], axis=1
    )
    share_rows = flat // devices
    side_rows = -(-features * 2 * proj // (pair_width * devices))
    side_flat = side_part.reshape(-1, pair_width)
    side_flat = jnp.pad(side_flat, ((0, side_rows * devices - side_flat.shape[0]), (0, 0)))
    shares = jnp.concatenate(
        [
            grad_out.reshape(devices, share_rows, pair_width),
            side_flat.reshape(devices, side_rows, pair_width),
        ],
        axis=1,
    ).astype(jnp.bfloat16)
    shares = lax.all_to_all(shares, axes, 0, 0)

    def chunks_of(grads, count):
        grads = grads.reshape(seq_count, count // tokens, tokens * proj)
        return grads.transpose(1, 0, 2)

    left_back = lax.all_to_all(chunks_of(grad_left, row_count), "pcol", 0, 0)
    right_back = lax.all_to_all(chunks_of(grad_right, col_count), "prow", 0, 0)
    left_back = jnp.sum(left_back.astype(jnp.float32), axis=0).astype(jnp.bfloat16)
    right_back = jnp.sum(right_back.astype(jnp.float32), axis=0).astype(jnp.bfloat16)
    left_back = lax.ppermute(left_back, axes, to_tokens)

    share = jnp.sum(shares.astype(jnp.float32), axis=0).astype(jnp.bfloat16)
    message = spread(share, axes, devices)
    output_weight_gradient = (
        message[:, :share_rows].reshape(flat, pair_width).astype(jnp.float32)
    )
    side = message[:, share_rows:].reshape(-1, pair_width).astype(jnp.float32)
    side = side[: features * 2 * proj // pair_width].reshape(features, 2 * proj)
    left_weight_gradient, right_weight_gradient = side[:, :proj], side[:, proj:]

    normed, inverse_spread = normalize(picked)
    both = jnp.concatenate(
        [
            left_back.reshape(seq_count, tokens, proj),
            right_back.reshape(seq_count, tokens, proj),
        ],
        axis=-1,
    )
    sides = jnp.concatenate([first_side_matrix, second_side_matrix], axis=1)
    grad_normed = jnp.einsum("stp,cp->stc", both, sides, preferred_element_type=jnp.float32)
    mean_factor = jnp.mean(grad_normed, axis=-1, keepdims=True)
    projected = jnp.mean(grad_normed * normed, axis=-1, keepdims=True)
    alignment_gradient = (
        inverse_spread * (grad_normed - mean_factor - normed * projected)
    ).astype(jnp.bfloat16)
    return (
        pair_delta,
        alignment_gradient,
        left_weight_gradient,
        right_weight_gradient,
        output_weight_gradient,
    )


def dot(x, y, contract=(1, 0), precision=None):
    return lax.dot_general(
        x, y, (((contract[0],), (contract[1],)), ((), ())),
        precision=precision, preferred_element_type=F32,
    )


def lane_ids(shape):
    return lax.broadcasted_iota(jnp.int32, shape, len(shape) - 1)


def lane_groups(shape, width):
    row = lax.broadcasted_iota(jnp.int32, (1, shape[1]), 1) % LANES // width
    return jnp.broadcast_to(row, shape)


def fold_tokens(parts):
    quarter = LANES // 4
    chunk = lane_groups(parts[0].shape, quarter)
    first, even = chunk < 2, chunk % 2 == 0
    halves = [
        jnp.where(first, parts[t], parts[t + 2])
        + pltpu.roll(jnp.where(first, parts[t + 2], parts[t]), 2 * quarter, 1)
        for t in range(2)
    ]
    other = jnp.where(even, halves[1], halves[0])
    moved = jnp.where(even, pltpu.roll(other, 3 * quarter, 1), pltpu.roll(other, quarter, 1))
    return jnp.where(even, halves[0], halves[1]) + moved


def group_mean(x, group):
    rows, lanes = x.shape
    rows_id = lax.broadcasted_iota(jnp.int32, (lanes, lanes), 0) // group
    cols_id = lax.broadcasted_iota(jnp.int32, (lanes, lanes), 1) // group
    block = (rows_id == cols_id).astype(BF16)
    pieces = [x.astype(BF16)]
    if x.dtype == F32:
        for _ in range(2):
            x = x - pieces[-1].astype(F32)
            pieces.append(x.astype(BF16))
    total = dot(jnp.concatenate(pieces, axis=0), block)
    total = functools.reduce(
        jnp.add, [total[n * rows : (n + 1) * rows] for n in reversed(range(len(pieces)))]
    )
    return total * (1.0 / group)


def pick_kernel(
    positions_ref,
    features_ref,
    cot_ref,
    normed_ref,
    inverse_ref,
    message_ref,
    positions,
    features,
    in_sems,
):
    pairs = cot_ref.shape[0]
    inputs = [
        pltpu.make_async_copy(source, target, in_sems.at[n])
        for n, (source, target) in enumerate(
            [
                (positions_ref, positions),
                (features_ref, features),
                (cot_ref, message_ref.at[pl.ds(0, pairs)]),
            ]
        )
    ]
    for copy in inputs:
        copy.start()
    heads = features_ref.shape[1]
    seqs, packed = normed_ref.shape
    channels = packed // 4
    for copy in inputs:
        copy.wait()
    wanted = positions[...] == lax.broadcasted_iota(jnp.int32, (heads, seqs), 0)
    chosen = dot(wanted.astype(BF16), features[...], contract=(0, 1))
    mean_factor = group_mean(chosen.astype(BF16), channels)
    centered = chosen - mean_factor
    variance = group_mean(centered * centered, channels)
    inverse = lax.rsqrt(variance + 1e-05)
    normed = centered * inverse
    for n in range(packed // LANES):
        message_ref[pairs + n * seqs : pairs + (n + 1) * seqs] = normed[
            :, n * LANES : (n + 1) * LANES
        ].astype(BF16)
    normed_ref[...] = normed
    inverse_ref[...] = inverse


def setup_kernel(
    first_ref,
    own_ref,
    mapping_ref,
    turned_mapping_ref,
    left_ref,
    right_ref,
    offset_ref,
    first_out_ref,
    own_out_ref,
    left_wide_ref,
    left_one_ref,
    right_one_ref,
    offset_out_ref,
    shuffle_ref,
):
    del mapping_ref, turned_mapping_ref
    first_out_ref[...] = first_ref[...]
    own_out_ref[...] = own_ref[...]
    offset_out_ref[...] = offset_ref[...]
    proj, channels = left_ref.shape
    tokens = left_one_ref.shape[0] // channels
    wide, highs = shuffle_ref.shape[0], proj // tokens
    block_cols = wide // proj
    target = lax.broadcasted_iota(jnp.int32, (1, wide), 1)
    jj, qh = target % block_cols, target // block_cols % highs
    source = jj * proj + qh * tokens + target // (highs * block_cols)
    rows_id = lax.broadcasted_iota(jnp.int32, (wide, wide), 0)
    shuffle_ref[...] = (rows_id == jnp.broadcast_to(source, (wide, wide))).astype(BF16)
    repeat = lane_ids((proj, LANES)) % proj
    repeat = (repeat == lax.broadcasted_iota(jnp.int32, (proj, LANES), 0)).astype(BF16)
    left_row = dot(left_ref[...], repeat, contract=(0, 0))
    right_row = dot(right_ref[...], repeat, contract=(0, 0))
    slot = lane_ids(left_row.shape) // proj
    nothing = jnp.zeros(left_row.shape, BF16)
    for t in range(tokens):
        here = slice(t * channels, (t + 1) * channels)
        left_one_ref[here] = jnp.where(slot == t, left_row, 0.0).astype(BF16)
        right_one_ref[here] = jnp.where(slot == t, right_row, 0.0).astype(BF16)
        for other in range(tokens):
            left_wide_ref[here, other * LANES : (other + 1) * LANES] = (
                left_row.astype(BF16) if other == t else nothing
            )


def place_blocks(place_ref, offsets, blocks, out_ref):
    for (down, across), block in zip(offsets, blocks, strict=True):
        out_ref[place_ref[0] ^ down, place_ref[1] ^ across] = block


def pull_blocks(cot, mapping_ref, pulled_ref, r, at):
    block_rows = pulled_ref.shape[2] // LANES
    block_cols = cot.shape[0] // block_rows
    grad = dot(cot, mapping_ref[...])
    for h in range(mapping_ref.shape[1] // LANES):
        there = pl.ds(pl.multiple_of(at + h * block_cols, block_cols), block_cols)
        for t in range(block_rows):
            pulled_ref[r, there, t * LANES : (t + 1) * LANES] = grad[
                t * block_cols : (t + 1) * block_cols, h * LANES : (h + 1) * LANES
            ].astype(BF16)


def pull_own_kernel(downs, place_ref, mapping_ref, *refs):
    *message_refs, pulled_ref, rows_ref = refs
    pairs = message_refs[0].shape[0] - rows_ref.shape[1]
    for n, (down, ref) in enumerate(zip(downs, message_refs, strict=True)):
        rows_ref[n] = ref[pairs:]
        pull_blocks(ref[:pairs], mapping_ref, pulled_ref, place_ref[0] ^ down, 0)


def pull_kernel(offsets, place_ref, mapping_ref, own_ref, *refs):
    *message_refs, cot_ref, pulled_ref = refs
    rows, groups, pairs, _ = cot_ref.shape
    place_blocks(place_ref, offsets, [ref[:pairs] for ref in message_refs], cot_ref)
    share = own_ref.shape[1]
    for r in range(rows):
        for across in range(1, groups):
            group = place_ref[1] ^ across
            pull_blocks(cot_ref[r, group], mapping_ref, pulled_ref, r, group * share)
        at = pl.multiple_of(place_ref[1] * share, share)
        pulled_ref[r, pl.ds(at, share)] = own_ref[r]


def owner_order(places, prow_n, core):
    mine = [(2 * g + core) * prow_n + r for g, r in places]
    return mine + [(2 * g + 1 - core) * prow_n + r for g, r in places]


def left_block(expanded, row, step_owners, tokens):
    ahead = jnp.concatenate([expanded[row * step_owners + o] for o in range(step_owners)], axis=1)
    low = lane_groups(ahead.shape, LANES // tokens)
    return jnp.concatenate(
        [jnp.where(low == l, ahead, jnp.zeros_like(ahead)) for l in range(tokens)], axis=0
    )


def pair_kernel(
    offsets,
    place_ref,
    mine_from_ref,
    theirs_from_ref,
    mapping_ref,
    left_ref,
    right_ref,
    offset_ref,
    shuffle_ref,
    cot_ref,
    pulled_ref,
    pair_ref,
    grads_ref,
    message_ref,
    rows_ref,
    expanded,
    swapped,
    outer_ref,
    mine_ref,
    theirs_ref,
    turned,
    left_back,
    right_back,
    sums,
    weights,
):
    for source, target in ((mine_from_ref, mine_ref), (theirs_from_ref, theirs_ref)):
        place_blocks(place_ref, offsets, [source[n] for n in range(source.shape[0])], target)
    prow_n, groups = mine_ref.shape[:2]
    block_rows, block_cols, pair_width = pair_ref.shape
    owners, seqs = expanded.shape[:2]
    packed = left_ref.shape[0]
    tokens = left_ref.shape[1] // LANES
    proj = LANES // tokens
    highs = proj // tokens
    span = highs * block_cols
    own_row, own_group, core = place_ref[0], place_ref[1], place_ref[2]

    def rows_of(ref, g, r):
        return jnp.concatenate(
            [ref[r, g, n * seqs : (n + 1) * seqs] for n in range(packed // LANES)], axis=1
        )

    places = [(g, r) for g in range(groups) for r in range(prow_n)]
    rows_mine = [rows_of(mine_ref, g, r) for g, r in places]
    rows_all = jnp.concatenate(
        rows_mine + [rows_of(theirs_ref, g, r) for g, r in places], axis=0
    )
    rows_ref[...] = rows_all
    wide_left = dot(rows_all, left_ref[...]).astype(BF16)
    for n, owner in enumerate(owner_order(places, prow_n, core)):
        expanded[owner] = wide_left[n * seqs : (n + 1) * seqs]

    side_rows = []
    for g in range(groups):
        chunks = rows_mine[g * prow_n : (g + 1) * prow_n]
        side_rows.append(
            jnp.concatenate([dot(x, right_ref[...]).astype(BF16) for x in chunks], axis=1)
        )
    right = dot(jnp.concatenate(side_rows, axis=0), shuffle_ref[...])
    for g in range(groups):
        for l in range(tokens):
            swapped[l * seqs : (l + 1) * seqs, g * span : (g + 1) * span] = (
                right[g * seqs : (g + 1) * seqs, l * span : (l + 1) * span] * (1.0 / seqs)
            ).astype(BF16)
    turned[...] = swapped[...].astype(F32).T.astype(BF16)

    order = owner_order(places, prow_n, core)
    pairs = block_rows * block_cols
    step_owners = owners // prow_n
    for row in range(prow_n):
        block = left_block(expanded, row, step_owners, tokens)
        made = dot(turned[...], block)
        for g in range(groups):
            for t in range(block_rows):
                start = (g * block_rows + t) * block_cols
                lanes = slice(t * LANES, (t + 1) * LANES)
                for h in range(highs):
                    there = slice((g * highs + h) * block_cols, (g * highs + h + 1) * block_cols)
                    outer_ref[row, start : start + block_cols, h * LANES : (h + 1) * LANES] = made[
                        there, lanes
                    ].astype(BF16)
        cot = cot_ref[row].reshape(groups * pairs, pair_width)
        weight_part = dot(cot, outer_ref[row], contract=(0, 0))
        weights[...] = weight_part if row == 0 else weights[...] + weight_part
        if row == prow_n - 1:
            share = block_rows * block_cols
            mine = outer_ref[own_row, pl.ds(pl.multiple_of(own_group * share, share), share)]
            update = dot(mine, mapping_ref[...]) + offset_ref[...]
            pair_ref[...] = update.astype(BF16).reshape(pair_ref.shape)
            flat = weights.shape[1]
            outer_f = weights[...].T
            weight_rows = outer_f.reshape(proj, proj, pair_width).swapaxes(0, 1).reshape(flat, pair_width)

            message_ref[:flat] = weight_rows.astype(BF16)
        pulled = pulled_ref[row]
        back = dot(swapped[...], pulled)
        low = lane_groups((seqs, back.shape[1]), proj)
        back = functools.reduce(
            jnp.add,
            [
                jnp.where(low == l, back[l * seqs : (l + 1) * seqs], 0.0)
                for l in range(tokens)
            ],
        )
        for o in range(step_owners):
            parts = [
                back[:, (o * tokens + t) * LANES : (o * tokens + t + 1) * LANES]
                for t in range(tokens)
            ]
            left_back[row * step_owners + o] = fold_tokens(parts).astype(BF16)
        sum_part = dot(pulled, block, contract=(1, 1))
        sums[...] = sum_part if row == 0 else sums[...] + sum_part

    back = (sums[...].T * (1.0 / seqs)).astype(BF16)
    back = jnp.concatenate(
        [
            jnp.concatenate(
                [
                    back[l * seqs : (l + 1) * seqs, g * span : (g + 1) * span]
                    for l in range(tokens)
                ],
                axis=1,
            )
            for g in range(groups)
        ],
        axis=0,
    )
    back = dot(back, shuffle_ref[...], contract=(1, 1)).astype(BF16)
    for g, r in places:
        right_back[g * prow_n + r] = back[g * seqs : (g + 1) * seqs, r * LANES : (r + 1) * LANES]

    def side(grads, rows):
        total = dot(grads, rows, contract=(0, 0))
        features = rows.shape[1] // tokens
        return functools.reduce(
            jnp.add,
            [
                total[t * proj : (t + 1) * proj, t * features : (t + 1) * features]
                for t in range(tokens)
            ],
        )

    left_side = side(
        jnp.concatenate([left_back[owner] for owner in order], axis=0), rows_ref[...]
    )
    columns = groups * prow_n * seqs
    right_side = side(right_back[...].reshape(columns, LANES), rows_ref[:columns])
    both = jnp.concatenate([left_side, right_side], axis=0).astype(BF16)
    both = jnp.concatenate([both, jnp.zeros_like(both)], axis=1)

    message_ref[flat : flat + 2 * proj] = both
    message_ref[flat + 2 * proj :] = left_back[(2 * own_group + 1 - core) * prow_n + own_row]
    grads_ref[0] = left_back[(2 * own_group + core) * prow_n + own_row]
    grads_ref[1] = right_back[own_group * prow_n + own_row]


def close_kernel(
    grads_ref,
    own_ref,
    message_ref,
    normed_ref,
    inverse_ref,
    left_ref,
    right_ref,
    out_ref,
    left_out_ref,
    right_out_ref,
    rows_out_ref,
):
    flat = out_ref.shape[0]
    proj, features = left_out_ref.shape
    out_ref[...] = own_ref[:flat].astype(F32) + message_ref[:flat].astype(F32)
    sides = slice(flat, flat + 2 * proj)
    both = own_ref[sides, :features].astype(F32) + message_ref[sides, :features].astype(F32)
    left_out_ref[...] = both[:proj]
    right_out_ref[...] = both[proj:]
    left_back = grads_ref[0].astype(F32) + message_ref[flat + 2 * proj :].astype(F32)
    grad_normed = dot(left_back.astype(BF16), left_ref[...], contract=(1, 1))
    grad_normed = grad_normed + dot(grads_ref[1], right_ref[...], contract=(1, 1))
    normed = normed_ref[...]
    means = jnp.concatenate([grad_normed, grad_normed * normed], axis=0)
    means = group_mean(means, features)
    mean_factor, projected = means[: normed.shape[0]], means[normed.shape[0] :]
    result = inverse_ref[...] * (grad_normed - mean_factor - normed * projected)
    rows_out_ref[...] = jnp.stack(
        [result[:, t * features : (t + 1) * features] for t in range(rows_out_ref.shape[1])],
        axis=1,
    ).astype(BF16)


def local_gathered(
    homolog_features,
    subset_homolog_positions,
    first_side_matrix,
    second_side_matrix,
    final_mapping_matrix,
    final_offset_vector,
    upstream_sensitivity,
):
    prow_n, groups = lax.axis_size("prow"), lax.axis_size("px")
    owners = prow_n * groups * 2
    heads, tokens, features = homolog_features.shape
    seqs = subset_homolog_positions.shape[0]
    block_rows, block_cols, pair_width = upstream_sensitivity.shape
    proj = first_side_matrix.shape[1]
    flat = proj * proj
    packed = tokens * features
    shape = jax.ShapeDtypeStruct
    vmem = pl.BlockSpec(memory_space=pltpu.VMEM)
    smem = pl.BlockSpec(memory_space=pltpu.SMEM)
    params = pltpu.CompilerParams(vmem_limit_bytes=36 * 1024 * 1024)

    pairs = block_rows * block_cols
    length = seqs * packed // LANES
    hbm = pl.BlockSpec(memory_space=pltpu.HBM)
    normed, inverse, sent = pl.pallas_call(
        pick_kernel,
        out_shape=(
            shape((seqs, packed), F32),
            shape((seqs, packed), F32),
            shape((pairs + length, LANES), BF16),
        ),
        in_specs=[hbm] * 3,
        out_specs=(vmem,) * 3,
        scratch_shapes=[
            pltpu.VMEM((1, seqs), jnp.int32),
            pltpu.VMEM((packed, heads), BF16),
            pltpu.SemaphoreType.DMA((3,)),
        ],
        compiler_params=pltpu.CompilerParams(vmem_limit_bytes=60 * 1024 * 1024),
        name="pick_rows",
    )(
        subset_homolog_positions.reshape(1, seqs),
        homolog_features.transpose(1, 2, 0).reshape(packed, heads),
        upstream_sensitivity.reshape(pairs, pair_width),
    )

    mapping = final_mapping_matrix.reshape(proj, proj, pair_width)
    mapping = mapping.swapaxes(0, 1).reshape(flat, pair_width)
    turned_mapping = mapping.T

    def swapped_with(values, axis, size, mask):
        return lax.ppermute(values, axis, [(n, n ^ mask) for n in range(size)])

    messages = [sent] + [
        swapped_with(sent, "prow", prow_n, down) for down in range(1, prow_n)
    ]
    messages[1], own, left_wide, left_one, right_one, offset, shuffle = pl.pallas_call(
        setup_kernel,
        out_shape=(
            shape(sent.shape, BF16),
            shape(sent.shape, BF16),
            shape((packed, tokens * LANES), BF16),
            shape((packed, LANES), BF16),
            shape((packed, LANES), BF16),
            shape((1, pair_width), F32),
            shape((block_cols * proj, block_cols * proj), BF16),
        ),
        in_specs=[vmem] * 7,
        out_specs=(vmem,) * 7,
        compiler_params=params,
        name="setup",
    )(
        messages[1],
        sent,
        mapping,
        turned_mapping,
        first_side_matrix.T,
        second_side_matrix.T,
        final_offset_vector.reshape(1, pair_width),
    )
    messages += [
        swapped_with(one, "px", groups, across) for across in range(1, groups) for one in messages
    ]
    messages[0] = own
    offsets = [(down, across) for across in range(groups) for down in range(prow_n)]
    place = jnp.stack([lax.axis_index("prow"), lax.axis_index("px"), lax.axis_index("pc")])

    columns = groups * proj // tokens * block_cols
    pull_cost = pl.CostEstimate(
        flops=prow_n * groups * pairs * pair_width * flat,
        bytes_accessed=prow_n * groups * pairs * (2 * pair_width + flat),
        transcendentals=0,
    )
    pulled_own, rows_own = pl.pallas_call(
        functools.partial(pull_own_kernel, [down for down, _ in offsets[:prow_n]]),
        out_shape=(
            shape((prow_n, columns // groups, block_rows * LANES), BF16),
            shape((prow_n, length, LANES), BF16),
        ),
        in_specs=[smem] + [vmem] * (1 + prow_n),
        out_specs=(vmem,) * 2,
        compiler_params=params,
        cost_estimate=pull_cost,
        name="pull_own",
    )(place, turned_mapping, *messages[:prow_n])
    rows = jnp.concatenate(
        [rows_own] + [one[None, pairs:] for one in messages[prow_n:]], axis=0
    )
    theirs = lax.ppermute(rows, "pc", [(0, 1), (1, 0)])
    cot, pulled = pl.pallas_call(
        functools.partial(pull_kernel, offsets),
        out_shape=(
            shape((prow_n, groups, pairs, pair_width), BF16),
            shape((prow_n, columns, block_rows * LANES), BF16),
        ),
        in_specs=[smem] + [vmem] * (2 + len(messages)),
        out_specs=(vmem,) * 2,
        compiler_params=params,
        cost_estimate=pull_cost,
        name="pull_back",
    )(place, turned_mapping, pulled_own, *messages)
    pair_delta, grads, message = pl.pallas_call(
        functools.partial(pair_kernel, offsets),
        out_shape=(
            shape(upstream_sensitivity.shape, BF16),
            shape((2, seqs, LANES), BF16),
            shape((flat + 2 * proj + seqs, LANES), BF16),
        ),
        in_specs=[smem] + [vmem] * 9,
        out_specs=(vmem,) * 3,
        scratch_shapes=[
            pltpu.VMEM((owners * seqs, packed), BF16),
            pltpu.VMEM((owners, seqs, tokens * LANES), BF16),
            pltpu.VMEM((tokens * seqs, columns), BF16),
            pltpu.VMEM((prow_n, groups * pairs, flat), BF16),
            pltpu.VMEM((prow_n, groups, length, LANES), BF16),
            pltpu.VMEM((prow_n, groups, length, LANES), BF16),
            pltpu.VMEM((columns, tokens * seqs), BF16),
            pltpu.VMEM((owners, seqs, LANES), BF16),
            pltpu.VMEM((groups * prow_n, seqs, LANES), BF16),
            pltpu.VMEM((columns, tokens * seqs), F32),
            pltpu.VMEM((pair_width, flat), F32),
        ],
        compiler_params=params,
        name="pair_work",
    )(place, rows, theirs, mapping, left_wide, right_one, offset, shuffle, cot, pulled)

    theirs = lax.ppermute(message, "pc", [(0, 1), (1, 0)])
    output_weight_gradient, left_weight_gradient, right_weight_gradient, alignment = pl.pallas_call(
        close_kernel,
        out_shape=(
            shape((flat, pair_width), F32),
            shape((proj, features), F32),
            shape((proj, features), F32),
            shape((seqs, tokens, features), BF16),
        ),
        in_specs=[vmem] * 7,
        out_specs=(vmem,) * 4,
        compiler_params=params,
        name="close",
    )(grads, message, theirs, normed, inverse, left_one, right_one)
    return (
        pair_delta,
        alignment,
        left_weight_gradient.T,
        right_weight_gradient.T,
        output_weight_gradient,
    )


def shapes_allow_gathering(
    mesh_shape, features, positions, first_side, second_side, mapping, offset, cot
):
    rows_n, cols_n = mesh_shape["prow"], mesh_shape["pcol"]
    parts = mesh_shape["rep"]
    tokens = features.shape[1] // (rows_n * cols_n)
    block_rows, block_cols = cot.shape[0] // (parts * rows_n), cot.shape[1] // cols_n
    proj, width = first_side.shape[1], cot.shape[2]
    return (
        cols_n % 2 == 0
        and cot.shape[1] * cot.shape[1] <= GATHERED_PAIRS
        and tokens * proj == LANES
        and tokens == 4
        and block_rows % tokens == 0
        and block_cols == rows_n * tokens == 16
        and rows_n & (rows_n - 1) == 0
        and cols_n & (cols_n - 1) == 0
        and width == LANES
        and features.shape[2] >= 2 * proj
        and positions.shape[0] // parts % 16 == 0
        and features.shape[2] * tokens % LANES == 0
    )


def solution(mesh):
    def run(local, over, columns, *args):
        tokens_split = P("rep", columns + ("prow",), None)
        pairs_split = P(("rep", "prow"), columns, None)
        return jax.shard_map(
            local,
            mesh=over,
            in_specs=(tokens_split, P("rep"), P(), P(), P(), P(), pairs_split),
            out_specs=(pairs_split, tokens_split, P("rep", None), P("rep", None), P("rep", None)),
            check_vma=False,
        )(*args)

    def program(*args):
        if not shapes_allow_gathering(mesh.shape, *args):
            return run(local_phased, mesh, ("pcol",), *args)
        reps, rows_n, cols_n = (mesh.shape[name] for name in ("rep", "prow", "pcol"))
        chips = Mesh(
            mesh.devices.reshape(reps, rows_n, cols_n // 2, 2), ("rep", "prow", "px", "pc")
        )
        return run(local_gathered, chips, ("px", "pc"), *args)

    return program
```

```python
import functools

import jax
import jax.numpy as jnp
from jax import lax
from jax.experimental import pallas as pl
from jax.experimental.pallas import tpu as pltpu
from jax.sharding import Mesh
from jax.sharding import PartitionSpec as P

BF16, F32 = jnp.bfloat16, jnp.float32
LANES = 128
GATHERED_PAIRS = 4096

PAIRS_AT_ONCE = 1024


def normalize(values):
    values = values.astype(jnp.float32)
    mean_factor = jnp.mean(values, axis=-1, keepdims=True)
    centered = values - mean_factor
    variance = jnp.mean(centered * centered, axis=-1, keepdims=True)
    inverse_spread = lax.rsqrt(variance + 1e-05)
    return (centered * inverse_spread, inverse_spread)


def transposed(rows_n, cols_n):
    return [
        (r * cols_n + c, c * rows_n + r) for r in range(rows_n) for c in range(cols_n)
    ]


def spread(values, axes, count):
    return lax.all_to_all(jnp.broadcast_to(values[None], (count,) + values.shape), axes, 0, 0)


def local_phased(
    homolog_features,
    subset_homolog_positions,
    first_side_matrix,
    second_side_matrix,
    final_mapping_matrix,
    final_offset_vector,
    upstream_sensitivity,
):
    axes = ("prow", "pcol")
    rows_n, cols_n = lax.axis_size("prow"), lax.axis_size("pcol")
    devices = rows_n * cols_n
    seq_count = subset_homolog_positions.shape[0]
    tokens, features = homolog_features.shape[1:]
    row_count, col_count, pair_width = upstream_sensitivity.shape
    proj = first_side_matrix.shape[1]
    flat = proj * proj
    to_rows = transposed(rows_n, cols_n)
    to_tokens = [(target, source) for source, target in to_rows]

    picked = jnp.take(homolog_features, subset_homolog_positions, axis=0)
    packed = picked.reshape(seq_count, tokens * features)
    row_own = lax.ppermute(packed, axes, to_rows)
    col_all = spread(packed, "prow", rows_n)
    row_all = spread(row_own, "pcol", cols_n)

    def side_of(chunks, count, matrix):
        chunks = chunks.reshape(count // tokens, seq_count, tokens, features)
        chunks = chunks.transpose(1, 0, 2, 3).reshape(seq_count, count, features)
        normed_low = normalize(chunks)[0].astype(jnp.bfloat16)
        side = jnp.einsum("stc,cp->stp", normed_low, matrix, preferred_element_type=jnp.float32)
        return normed_low, side.astype(jnp.bfloat16)

    row_normed, left = side_of(row_all, row_count, first_side_matrix)
    col_normed, right = side_of(col_all, col_count, second_side_matrix)

    def block_step(left_blk, cot_blk):
        rows = left_blk.shape[1]
        outer = jnp.einsum("sip,sjq->ijpq", left_blk, right, preferred_element_type=jnp.float32)
        outer = (outer / seq_count).astype(jnp.bfloat16).reshape(rows * col_count, flat)
        update = jnp.dot(outer, final_mapping_matrix, preferred_element_type=jnp.float32)
        update = (update + final_offset_vector).astype(jnp.bfloat16)
        cot_flat = cot_blk.reshape(rows * col_count, pair_width)
        grad_out = jnp.dot(outer.T, cot_flat, preferred_element_type=jnp.float32)
        grad_outer = jnp.dot(cot_flat, final_mapping_matrix.T, preferred_element_type=jnp.float32)
        grad_outer = grad_outer.astype(jnp.bfloat16).reshape(rows, col_count, proj, proj)
        grad_left = jnp.einsum(
            "ijpq,sjq->sip", grad_outer, right, preferred_element_type=jnp.float32
        )
        grad_right = jnp.einsum(
            "ijpq,sip->sjq", grad_outer, left_blk, preferred_element_type=jnp.float32
        )
        return update.reshape(rows, col_count, pair_width), grad_out, grad_left, grad_right

    block = max(1, min(row_count, PAIRS_AT_ONCE // col_count))
    blocks = row_count // block
    if blocks == 1:
        update, grad_out, grad_left, grad_right = block_step(left, upstream_sensitivity)
    else:
        def step(totals, inputs):
            update, grad_out, grad_left, grad_right = block_step(*inputs)
            return (totals[0] + grad_out, totals[1] + grad_right), (update, grad_left)

        (grad_out, grad_right), (update, grad_left) = lax.scan(
            step,
            (
                jnp.zeros((flat, pair_width), jnp.float32),
                jnp.zeros((seq_count, col_count, proj), jnp.float32),
            ),
            (
                left.reshape(seq_count, blocks, block, proj).transpose(1, 0, 2, 3),
                upstream_sensitivity.reshape(blocks, block, col_count, pair_width),
            ),
        )
        grad_left = grad_left.transpose(1, 0, 2, 3).reshape(seq_count, row_count, proj)
    pair_delta = update.reshape(row_count, col_count, pair_width)

    grad_left = (grad_left / seq_count).astype(jnp.bfloat16)
    grad_right = (grad_right / seq_count).astype(jnp.bfloat16)

    def weight_part(normed, grads):
        return jnp.einsum("stc,stp->cp", normed, grads, preferred_element_type=jnp.float32)

    side_part = jnp.concatenate(
        [weight_part(row_normed, grad_left), weight_part(col_normed, grad_right)], axis=1
    )
    share_rows = flat // devices
    side_rows = -(-features * 2 * proj // (pair_width * devices))
    side_flat = side_part.reshape(-1, pair_width)
    side_flat = jnp.pad(side_flat, ((0, side_rows * devices - side_flat.shape[0]), (0, 0)))
    shares = jnp.concatenate(
        [
            grad_out.reshape(devices, share_rows, pair_width),
            side_flat.reshape(devices, side_rows, pair_width),
        ],
        axis=1,
    ).astype(jnp.bfloat16)
    shares = lax.all_to_all(shares, axes, 0, 0)

    def chunks_of(grads, count):
        grads = grads.reshape(seq_count, count // tokens, tokens * proj)
        return grads.transpose(1, 0, 2)

    left_back = lax.all_to_all(chunks_of(grad_left, row_count), "pcol", 0, 0)
    right_back = lax.all_to_all(chunks_of(grad_right, col_count), "prow", 0, 0)
    left_back = jnp.sum(left_back.astype(jnp.float32), axis=0).astype(jnp.bfloat16)
    right_back = jnp.sum(right_back.astype(jnp.float32), axis=0).astype(jnp.bfloat16)
    left_back = lax.ppermute(left_back, axes, to_tokens)

    share = jnp.sum(shares.astype(jnp.float32), axis=0).astype(jnp.bfloat16)
    message = spread(share, axes, devices)
    output_weight_gradient = (
        message[:, :share_rows].reshape(flat, pair_width).astype(jnp.float32)
    )
    side = message[:, share_rows:].reshape(-1, pair_width).astype(jnp.float32)
    side = side[: features * 2 * proj // pair_width].reshape(features, 2 * proj)
    left_weight_gradient, right_weight_gradient = side[:, :proj], side[:, proj:]

    normed, inverse_spread = normalize(picked)
    both = jnp.concatenate(
        [
            left_back.reshape(seq_count, tokens, proj),
            right_back.reshape(seq_count, tokens, proj),
        ],
        axis=-1,
    )
    sides = jnp.concatenate([first_side_matrix, second_side_matrix], axis=1)
    grad_normed = jnp.einsum("stp,cp->stc", both, sides, preferred_element_type=jnp.float32)
    mean_factor = jnp.mean(grad_normed, axis=-1, keepdims=True)
    projected = jnp.mean(grad_normed * normed, axis=-1, keepdims=True)
    alignment_gradient = (
        inverse_spread * (grad_normed - mean_factor - normed * projected)
    ).astype(jnp.bfloat16)
    return (
        pair_delta,
        alignment_gradient,
        left_weight_gradient,
        right_weight_gradient,
        output_weight_gradient,
    )


def dot(x, y, contract=(1, 0), precision=None):
    return lax.dot_general(
        x, y, (((contract[0],), (contract[1],)), ((), ())),
        precision=precision, preferred_element_type=F32,
    )


def lane_ids(shape):
    return lax.broadcasted_iota(jnp.int32, shape, len(shape) - 1)


def lane_groups(shape, width):
    row = lax.broadcasted_iota(jnp.int32, (1, shape[1]), 1) % LANES // width
    return jnp.broadcast_to(row, shape)


def fold_tokens(parts):
    quarter = LANES // 4
    chunk = lane_groups(parts[0].shape, quarter)
    first, even = chunk < 2, chunk % 2 == 0
    halves = [
        jnp.where(first, parts[t], parts[t + 2])
        + pltpu.roll(jnp.where(first, parts[t + 2], parts[t]), 2 * quarter, 1)
        for t in range(2)
    ]
    other = jnp.where(even, halves[1], halves[0])
    moved = jnp.where(even, pltpu.roll(other, 3 * quarter, 1), pltpu.roll(other, quarter, 1))
    return jnp.where(even, halves[0], halves[1]) + moved


def group_mean(x, group):
    rows, lanes = x.shape
    rows_id = lax.broadcasted_iota(jnp.int32, (lanes, lanes), 0) // group
    cols_id = lax.broadcasted_iota(jnp.int32, (lanes, lanes), 1) // group
    block = (rows_id == cols_id).astype(BF16)
    pieces = [x.astype(BF16)]
    if x.dtype == F32:
        for _ in range(2):
            x = x - pieces[-1].astype(F32)
            pieces.append(x.astype(BF16))
    total = dot(jnp.concatenate(pieces, axis=0), block)
    total = functools.reduce(
        jnp.add, [total[n * rows : (n + 1) * rows] for n in reversed(range(len(pieces)))]
    )
    return total * (1.0 / group)


def pick_kernel(
    positions_ref,
    features_ref,
    cot_ref,
    normed_ref,
    inverse_ref,
    message_ref,
    positions,
    features,
    in_sems,
):
    pairs = cot_ref.shape[0]
    inputs = [
        pltpu.make_async_copy(source, target, in_sems.at[n])
        for n, (source, target) in enumerate(
            [
                (positions_ref, positions),
                (features_ref, features),
                (cot_ref, message_ref.at[pl.ds(0, pairs)]),
            ]
        )
    ]
    for copy in inputs:
        copy.start()
    heads = features_ref.shape[1]
    seqs, packed = normed_ref.shape
    channels = packed // 4
    for copy in inputs:
        copy.wait()
    wanted = positions[...] == lax.broadcasted_iota(jnp.int32, (heads, seqs), 0)
    chosen = dot(wanted.astype(BF16), features[...], contract=(0, 1))
    mean_factor = group_mean(chosen.astype(BF16), channels)
    centered = chosen - mean_factor
    variance = group_mean(centered * centered, channels)
    inverse = lax.rsqrt(variance + 1e-05)
    normed = centered * inverse
    for n in range(packed // LANES):
        message_ref[pairs + n * seqs : pairs + (n + 1) * seqs] = normed[
            :, n * LANES : (n + 1) * LANES
        ].astype(BF16)
    normed_ref[...] = normed
    inverse_ref[...] = inverse


def setup_kernel(
    first_ref,
    own_ref,
    mapping_ref,
    turned_mapping_ref,
    left_ref,
    right_ref,
    offset_ref,
    first_out_ref,
    own_out_ref,
    left_wide_ref,
    left_one_ref,
    right_one_ref,
    offset_out_ref,
    shuffle_ref,
):
    del mapping_ref, turned_mapping_ref
    first_out_ref[...] = first_ref[...]
    own_out_ref[...] = own_ref[...]
    offset_out_ref[...] = offset_ref[...]
    proj, channels = left_ref.shape
    tokens = left_one_ref.shape[0] // channels
    wide, highs = shuffle_ref.shape[0], proj // tokens
    block_cols = wide // proj
    target = lax.broadcasted_iota(jnp.int32, (1, wide), 1)
    jj, qh = target % block_cols, target // block_cols % highs
    source = jj * proj + qh * tokens + target // (highs * block_cols)
    rows_id = lax.broadcasted_iota(jnp.int32, (wide, wide), 0)
    shuffle_ref[...] = (rows_id == jnp.broadcast_to(source, (wide, wide))).astype(BF16)
    repeat = lane_ids((proj, LANES)) % proj
    repeat = (repeat == lax.broadcasted_iota(jnp.int32, (proj, LANES), 0)).astype(BF16)
    left_row = dot(left_ref[...], repeat, contract=(0, 0))
    right_row = dot(right_ref[...], repeat, contract=(0, 0))
    slot = lane_ids(left_row.shape) // proj
    nothing = jnp.zeros(left_row.shape, BF16)
    for t in range(tokens):
        here = slice(t * channels, (t + 1) * channels)
        left_one_ref[here] = jnp.where(slot == t, left_row, 0.0).astype(BF16)
        right_one_ref[here] = jnp.where(slot == t, right_row, 0.0).astype(BF16)
        for other in range(tokens):
            left_wide_ref[here, other * LANES : (other + 1) * LANES] = (
                left_row.astype(BF16) if other == t else nothing
            )


def place_blocks(place_ref, offsets, blocks, out_ref):
    for (down, across), block in zip(offsets, blocks, strict=True):
        out_ref[place_ref[0] ^ down, place_ref[1] ^ across] = block


def pull_blocks(cot, mapping_ref, pulled_ref, r, at):
    block_rows = pulled_ref.shape[2] // LANES
    block_cols = cot.shape[0] // block_rows
    grad = dot(cot, mapping_ref[...])
    for h in range(mapping_ref.shape[1] // LANES):
        there = pl.ds(pl.multiple_of(at + h * block_cols, block_cols), block_cols)
        for t in range(block_rows):
            pulled_ref[r, there, t * LANES : (t + 1) * LANES] = grad[
                t * block_cols : (t + 1) * block_cols, h * LANES : (h + 1) * LANES
            ].astype(BF16)


def pull_own_kernel(downs, place_ref, mapping_ref, *refs):
    *message_refs, pulled_ref, rows_ref = refs
    pairs = message_refs[0].shape[0] - rows_ref.shape[1]
    for n, (down, ref) in enumerate(zip(downs, message_refs, strict=True)):
        rows_ref[n] = ref[pairs:]
        pull_blocks(ref[:pairs], mapping_ref, pulled_ref, place_ref[0] ^ down, 0)


def pull_kernel(offsets, place_ref, mapping_ref, own_ref, *refs):
    *message_refs, cot_ref, pulled_ref = refs
    rows, groups, pairs, _ = cot_ref.shape
    place_blocks(place_ref, offsets, [ref[:pairs] for ref in message_refs], cot_ref)
    share = own_ref.shape[1]
    for r in range(rows):
        for across in range(1, groups):
            group = place_ref[1] ^ across
            pull_blocks(cot_ref[r, group], mapping_ref, pulled_ref, r, group * share)
        at = pl.multiple_of(place_ref[1] * share, share)
        pulled_ref[r, pl.ds(at, share)] = own_ref[r]


def owner_order(places, prow_n, core):
    mine = [(2 * g + core) * prow_n + r for g, r in places]
    return mine + [(2 * g + 1 - core) * prow_n + r for g, r in places]


def left_block(expanded, row, step_owners, tokens):
    ahead = jnp.concatenate([expanded[row * step_owners + o] for o in range(step_owners)], axis=1)
    low = lane_groups(ahead.shape, LANES // tokens)
    return jnp.concatenate(
        [jnp.where(low == l, ahead, jnp.zeros_like(ahead)) for l in range(tokens)], axis=0
    )


def pair_kernel(
    offsets,
    place_ref,
    mine_from_ref,
    theirs_from_ref,
    mapping_ref,
    left_ref,
    right_ref,
    offset_ref,
    shuffle_ref,
    cot_ref,
    pulled_ref,
    pair_ref,
    grads_ref,
    message_ref,
    rows_ref,
    expanded,
    swapped,
    outer_ref,
    mine_ref,
    theirs_ref,
    turned,
    left_back,
    right_back,
    sums,
    weights,
):
    for source, target in ((mine_from_ref, mine_ref), (theirs_from_ref, theirs_ref)):
        place_blocks(place_ref, offsets, [source[n] for n in range(source.shape[0])], target)
    prow_n, groups = mine_ref.shape[:2]
    block_rows, block_cols, pair_width = pair_ref.shape
    owners, seqs = expanded.shape[:2]
    packed = left_ref.shape[0]
    tokens = left_ref.shape[1] // LANES
    proj = LANES // tokens
    highs = proj // tokens
    span = highs * block_cols
    own_row, own_group, core = place_ref[0], place_ref[1], place_ref[2]

    def rows_of(ref, g, r):
        return jnp.concatenate(
            [ref[r, g, n * seqs : (n + 1) * seqs] for n in range(packed // LANES)], axis=1
        )

    places = [(g, r) for g in range(groups) for r in range(prow_n)]
    rows_mine = [rows_of(mine_ref, g, r) for g, r in places]
    rows_all = jnp.concatenate(
        rows_mine + [rows_of(theirs_ref, g, r) for g, r in places], axis=0
    )
    rows_ref[...] = rows_all
    wide_left = dot(rows_all, left_ref[...]).astype(BF16)
    for n, owner in enumerate(owner_order(places, prow_n, core)):
        expanded[owner] = wide_left[n * seqs : (n + 1) * seqs]

    side_rows = []
    for g in range(groups):
        chunks = rows_mine[g * prow_n : (g + 1) * prow_n]
        side_rows.append(
            jnp.concatenate([dot(x, right_ref[...]).astype(BF16) for x in chunks], axis=1)
        )
    right = dot(jnp.concatenate(side_rows, axis=0), shuffle_ref[...])
    for g in range(groups):
        for l in range(tokens):
            swapped[l * seqs : (l + 1) * seqs, g * span : (g + 1) * span] = (
                right[g * seqs : (g + 1) * seqs, l * span : (l + 1) * span] * (1.0 / seqs)
            ).astype(BF16)
    turned[...] = swapped[...].astype(F32).T.astype(BF16)

    order = owner_order(places, prow_n, core)
    pairs = block_rows * block_cols
    step_owners = owners // prow_n
    for row in range(prow_n):
        block = left_block(expanded, row, step_owners, tokens)
        made = dot(turned[...], block)
        for g in range(groups):
            for t in range(block_rows):
                start = (g * block_rows + t) * block_cols
                lanes = slice(t * LANES, (t + 1) * LANES)
                for h in range(highs):
                    there = slice((g * highs + h) * block_cols, (g * highs + h + 1) * block_cols)
                    outer_ref[row, start : start + block_cols, h * LANES : (h + 1) * LANES] = made[
                        there, lanes
                    ].astype(BF16)
        cot = cot_ref[row].reshape(groups * pairs, pair_width)
        weight_part = dot(cot, outer_ref[row], contract=(0, 0))
        weights[...] = weight_part if row == 0 else weights[...] + weight_part
        if row == prow_n - 1:
            share = block_rows * block_cols
            mine = outer_ref[own_row, pl.ds(pl.multiple_of(own_group * share, share), share)]
            update = dot(mine, mapping_ref[...]) + offset_ref[...]
            pair_ref[...] = update.astype(BF16).reshape(pair_ref.shape)
            flat = weights.shape[1]
            outer_f = weights[...].T
            weight_rows = outer_f.reshape(proj, proj, pair_width).swapaxes(0, 1).reshape(flat, pair_width)

            message_ref[:flat] = weight_rows.astype(BF16)
        pulled = pulled_ref[row]
        back = dot(swapped[...], pulled)
        low = lane_groups((seqs, back.shape[1]), proj)
        back = functools.reduce(
            jnp.add,
            [
                jnp.where(low == l, back[l * seqs : (l + 1) * seqs], 0.0)
                for l in range(tokens)
            ],
        )
        for o in range(step_owners):
            parts = [
                back[:, (o * tokens + t) * LANES : (o * tokens + t + 1) * LANES]
                for t in range(tokens)
            ]
            left_back[row * step_owners + o] = fold_tokens(parts).astype(BF16)
        sum_part = dot(block, pulled, contract=(1, 1))
        sums[...] = sum_part if row == 0 else sums[...] + sum_part

    back = (sums[...] * (1.0 / seqs)).astype(BF16)
    back = jnp.concatenate(
        [
            jnp.concatenate(
                [
                    back[l * seqs : (l + 1) * seqs, g * span : (g + 1) * span]
                    for l in range(tokens)
                ],
                axis=1,
            )
            for g in range(groups)
        ],
        axis=0,
    )
    back = dot(back, shuffle_ref[...], contract=(1, 1)).astype(BF16)
    for g, r in places:
        right_back[g * prow_n + r] = back[g * seqs : (g + 1) * seqs, r * LANES : (r + 1) * LANES]

    def side(grads, rows):
        total = dot(grads, rows, contract=(0, 0))
        features = rows.shape[1] // tokens
        return functools.reduce(
            jnp.add,
            [
                total[t * proj : (t + 1) * proj, t * features : (t + 1) * features]
                for t in range(tokens)
            ],
        )

    left_side = side(
        jnp.concatenate([left_back[owner] for owner in order], axis=0), rows_ref[...]
    )
    columns = groups * prow_n * seqs
    right_side = side(right_back[...].reshape(columns, LANES), rows_ref[:columns])
    both = jnp.concatenate([left_side, right_side], axis=0).astype(BF16)
    both = jnp.concatenate([both, jnp.zeros_like(both)], axis=1)

    message_ref[flat : flat + 2 * proj] = both
    message_ref[flat + 2 * proj :] = left_back[(2 * own_group + 1 - core) * prow_n + own_row]
    grads_ref[0] = left_back[(2 * own_group + core) * prow_n + own_row]
    grads_ref[1] = right_back[own_group * prow_n + own_row]


def close_kernel(
    grads_ref,
    own_ref,
    message_ref,
    normed_ref,
    inverse_ref,
    left_ref,
    right_ref,
    out_ref,
    left_out_ref,
    right_out_ref,
    rows_out_ref,
):
    flat = out_ref.shape[0]
    proj, features = left_out_ref.shape
    out_ref[...] = own_ref[:flat].astype(F32) + message_ref[:flat].astype(F32)
    sides = slice(flat, flat + 2 * proj)
    both = own_ref[sides, :features].astype(F32) + message_ref[sides, :features].astype(F32)
    left_out_ref[...] = both[:proj]
    right_out_ref[...] = both[proj:]
    left_back = grads_ref[0].astype(F32) + message_ref[flat + 2 * proj :].astype(F32)
    grad_normed = dot(left_back.astype(BF16), left_ref[...], contract=(1, 1))
    grad_normed = grad_normed + dot(grads_ref[1], right_ref[...], contract=(1, 1))
    normed = normed_ref[...]
    means = jnp.concatenate([grad_normed, grad_normed * normed], axis=0)
    means = group_mean(means, features)
    mean_factor, projected = means[: normed.shape[0]], means[normed.shape[0] :]
    result = inverse_ref[...] * (grad_normed - mean_factor - normed * projected)
    rows_out_ref[...] = jnp.stack(
        [result[:, t * features : (t + 1) * features] for t in range(rows_out_ref.shape[1])],
        axis=1,
    ).astype(BF16)


def local_gathered(
    homolog_features,
    subset_homolog_positions,
    first_side_matrix,
    second_side_matrix,
    final_mapping_matrix,
    final_offset_vector,
    upstream_sensitivity,
):
    prow_n, groups = lax.axis_size("prow"), lax.axis_size("px")
    owners = prow_n * groups * 2
    heads, tokens, features = homolog_features.shape
    seqs = subset_homolog_positions.shape[0]
    block_rows, block_cols, pair_width = upstream_sensitivity.shape
    proj = first_side_matrix.shape[1]
    flat = proj * proj
    packed = tokens * features
    shape = jax.ShapeDtypeStruct
    vmem = pl.BlockSpec(memory_space=pltpu.VMEM)
    smem = pl.BlockSpec(memory_space=pltpu.SMEM)
    params = pltpu.CompilerParams(vmem_limit_bytes=36 * 1024 * 1024)

    pairs = block_rows * block_cols
    length = seqs * packed // LANES
    hbm = pl.BlockSpec(memory_space=pltpu.HBM)
    normed, inverse, sent = pl.pallas_call(
        pick_kernel,
        out_shape=(
            shape((seqs, packed), F32),
            shape((seqs, packed), F32),
            shape((pairs + length, LANES), BF16),
        ),
        in_specs=[hbm] * 3,
        out_specs=(vmem,) * 3,
        scratch_shapes=[
            pltpu.VMEM((1, seqs), jnp.int32),
            pltpu.VMEM((packed, heads), BF16),
            pltpu.SemaphoreType.DMA((3,)),
        ],
        compiler_params=pltpu.CompilerParams(vmem_limit_bytes=60 * 1024 * 1024),
        name="pick_rows",
    )(
        subset_homolog_positions.reshape(1, seqs),
        homolog_features.transpose(1, 2, 0).reshape(packed, heads),
        upstream_sensitivity.reshape(pairs, pair_width),
    )

    mapping = final_mapping_matrix.reshape(proj, proj, pair_width)
    mapping = mapping.swapaxes(0, 1).reshape(flat, pair_width)
    turned_mapping = mapping.T

    def swapped_with(values, axis, size, mask):
        return lax.ppermute(values, axis, [(n, n ^ mask) for n in range(size)])

    messages = [sent] + [
        swapped_with(sent, "prow", prow_n, down) for down in range(1, prow_n)
    ]
    messages[1], own, left_wide, left_one, right_one, offset, shuffle = pl.pallas_call(
        setup_kernel,
        out_shape=(
            shape(sent.shape, BF16),
            shape(sent.shape, BF16),
            shape((packed, tokens * LANES), BF16),
            shape((packed, LANES), BF16),
            shape((packed, LANES), BF16),
            shape((1, pair_width), F32),
            shape((block_cols * proj, block_cols * proj), BF16),
        ),
        in_specs=[vmem] * 7,
        out_specs=(vmem,) * 7,
        compiler_params=params,
        name="setup",
    )(
        messages[1],
        sent,
        mapping,
        turned_mapping,
        first_side_matrix.T,
        second_side_matrix.T,
        final_offset_vector.reshape(1, pair_width),
    )
    messages += [
        swapped_with(one, "px", groups, across) for across in range(1, groups) for one in messages
    ]
    messages[0] = own
    offsets = [(down, across) for across in range(groups) for down in range(prow_n)]
    place = jnp.stack([lax.axis_index("prow"), lax.axis_index("px"), lax.axis_index("pc")])

    columns = groups * proj // tokens * block_cols
    pull_cost = pl.CostEstimate(
        flops=prow_n * groups * pairs * pair_width * flat,
        bytes_accessed=prow_n * groups * pairs * (2 * pair_width + flat),
        transcendentals=0,
    )
    pulled_own, rows_own = pl.pallas_call(
        functools.partial(pull_own_kernel, [down for down, _ in offsets[:prow_n]]),
        out_shape=(
            shape((prow_n, columns // groups, block_rows * LANES), BF16),
            shape((prow_n, length, LANES), BF16),
        ),
        in_specs=[smem] + [vmem] * (1 + prow_n),
        out_specs=(vmem,) * 2,
        compiler_params=params,
        cost_estimate=pull_cost,
        name="pull_own",
    )(place, turned_mapping, *messages[:prow_n])
    rows = jnp.concatenate(
        [rows_own] + [one[None, pairs:] for one in messages[prow_n:]], axis=0
    )
    theirs = lax.ppermute(rows, "pc", [(0, 1), (1, 0)])
    cot, pulled = pl.pallas_call(
        functools.partial(pull_kernel, offsets),
        out_shape=(
            shape((prow_n, groups, pairs, pair_width), BF16),
            shape((prow_n, columns, block_rows * LANES), BF16),
        ),
        in_specs=[smem] + [vmem] * (2 + len(messages)),
        out_specs=(vmem,) * 2,
        compiler_params=params,
        cost_estimate=pull_cost,
        name="pull_back",
    )(place, turned_mapping, pulled_own, *messages)
    pair_delta, grads, message = pl.pallas_call(
        functools.partial(pair_kernel, offsets),
        out_shape=(
            shape(upstream_sensitivity.shape, BF16),
            shape((2, seqs, LANES), BF16),
            shape((flat + 2 * proj + seqs, LANES), BF16),
        ),
        in_specs=[smem] + [vmem] * 9,
        out_specs=(vmem,) * 3,
        scratch_shapes=[
            pltpu.VMEM((owners * seqs, packed), BF16),
            pltpu.VMEM((owners, seqs, tokens * LANES), BF16),
            pltpu.VMEM((tokens * seqs, columns), BF16),
            pltpu.VMEM((prow_n, groups * pairs, flat), BF16),
            pltpu.VMEM((prow_n, groups, length, LANES), BF16),
            pltpu.VMEM((prow_n, groups, length, LANES), BF16),
            pltpu.VMEM((columns, tokens * seqs), BF16),
            pltpu.VMEM((owners, seqs, LANES), BF16),
            pltpu.VMEM((groups * prow_n, seqs, LANES), BF16),
            pltpu.VMEM((tokens * seqs, columns), F32),
            pltpu.VMEM((pair_width, flat), F32),
        ],
        compiler_params=params,
        name="pair_work",
    )(place, rows, theirs, mapping, left_wide, right_one, offset, shuffle, cot, pulled)

    theirs = lax.ppermute(message, "pc", [(0, 1), (1, 0)])
    output_weight_gradient, left_weight_gradient, right_weight_gradient, alignment = pl.pallas_call(
        close_kernel,
        out_shape=(
            shape((flat, pair_width), F32),
            shape((proj, features), F32),
            shape((proj, features), F32),
            shape((seqs, tokens, features), BF16),
        ),
        in_specs=[vmem] * 7,
        out_specs=(vmem,) * 4,
        compiler_params=params,
        name="close",
    )(grads, message, theirs, normed, inverse, left_one, right_one)
    return (
        pair_delta,
        alignment,
        left_weight_gradient.T,
        right_weight_gradient.T,
        output_weight_gradient,
    )


def shapes_allow_gathering(
    mesh_shape, features, positions, first_side, second_side, mapping, offset, cot
):
    rows_n, cols_n = mesh_shape["prow"], mesh_shape["pcol"]
    parts = mesh_shape["rep"]
    tokens = features.shape[1] // (rows_n * cols_n)
    block_rows, block_cols = cot.shape[0] // (parts * rows_n), cot.shape[1] // cols_n
    proj, width = first_side.shape[1], cot.shape[2]
    return (
        cols_n % 2 == 0
        and cot.shape[1] * cot.shape[1] <= GATHERED_PAIRS
        and tokens * proj == LANES
        and tokens == 4
        and block_rows % tokens == 0
        and block_cols == rows_n * tokens == 16
        and rows_n & (rows_n - 1) == 0
        and cols_n & (cols_n - 1) == 0
        and width == LANES
        and features.shape[2] >= 2 * proj
        and positions.shape[0] // parts % 16 == 0
        and features.shape[2] * tokens % LANES == 0
    )


def solution(mesh):
    def run(local, over, columns, *args):
        tokens_split = P("rep", columns + ("prow",), None)
        pairs_split = P(("rep", "prow"), columns, None)
        return jax.shard_map(
            local,
            mesh=over,
            in_specs=(tokens_split, P("rep"), P(), P(), P(), P(), pairs_split),
            out_specs=(pairs_split, tokens_split, P("rep", None), P("rep", None), P("rep", None)),
            check_vma=False,
        )(*args)

    def program(*args):
        if not shapes_allow_gathering(mesh.shape, *args):
            return run(local_phased, mesh, ("pcol",), *args)
        reps, rows_n, cols_n = (mesh.shape[name] for name in ("rep", "prow", "pcol"))
        chips = Mesh(
            mesh.devices.reshape(reps, rows_n, cols_n // 2, 2), ("rep", "prow", "px", "pc")
        )
        return run(local_gathered, chips, ("px", "pc"), *args)

    return program
```
